32 devices in a mesh: rows: 16 (over z, y, x), hid: 2 (over core).
Axes of the slice: x: 2, y: 2, z: 4, core: 2. Of those that a mesh axis runs over, the one named last changes fastest.
Arguments:
- hidden_in: bfloat16 [16, 1024, 768], P('rows', None, 'hid'), may hold values from -6 to 6
- teacher_in: bfloat16 [16, 1024, 768], P('rows', None, 'hid'), may hold values from -6 to 6
- segment_ids: int32 [16, 1024], P('rows'), may hold values from 0 to 7, as said below
- pad_mask: int32 [16, 1024], P('rows'), may hold values from 0 to 1, as said below
- qkv_weight: float32 [3, 768, 768], P(None, None, 'hid'), may hold values from -0.21875 to 0.21875
- qkv_moment1: float32 [3, 768, 768], P(None, None, 'hid'), may hold values from -2.3841858e-07 to 2.3841858e-07
- qkv_moment2: float32 [3, 768, 768], P(None, None, 'hid'), may hold values from 7.055068e-17 to 1.1288108e-15
- out_weight: float32 [768, 768], P('hid'), may hold values from -1.75 to 1.75
- out_moment1: float32 [768, 768], P('hid'), may hold values from -2.3841858e-07 to 2.3841858e-07
- out_moment2: float32 [768, 768], P('hid'), may hold values from 7.055068e-17 to 1.1288108e-15
- up_weight: float32 [768, 3072], P(None, 'hid'), may hold values from -0.21875 to 0.21875
- up_moment1: float32 [768, 3072], P(None, 'hid'), may hold values from -2.3841858e-07 to 2.3841858e-07
- up_moment2: float32 [768, 3072], P(None, 'hid'), may hold values from 7.055068e-17 to 1.1288108e-15
- down_weight: float32 [3072, 768], P('hid'), may hold values from -0.109375 to 0.109375
- down_moment1: float32 [3072, 768], P('hid'), may hold values from -2.3841858e-07 to 2.3841858e-07
- down_moment2: float32 [3072, 768], P('hid'), may hold values from 7.055068e-17 to 1.1288108e-15
- bias_vectors: float32 [6, 768], P(None, 'hid'), may hold values from -1.75 to 1.75
- bias_moment1: float32 [6, 768], P(None, 'hid'), may hold values from -9.536743e-07 to 9.536743e-07
- bias_moment2: float32 [6, 768], P(None, 'hid'), may hold values from 1.1288108e-15 to 1.8060974e-14
- up_bias: float32 [3072], P('hid'), may hold values from -1.75 to 1.75
- up_bias_moment1: float32 [3072], P('hid'), may hold values from -4.7683716e-07 to 4.7683716e-07
- up_bias_moment2: float32 [3072], P('hid'), may hold values from 1.4110136e-16 to 2.2576217e-15
- norm_gains: float32 [2, 768], P(None, 'hid'), may hold values from 0.5 to 1.5
- gain_moment1: float32 [2, 768], P(None, 'hid'), may hold values from -9.536743e-07 to 9.536743e-07
- gain_moment2: float32 [2, 768], P(None, 'hid'), may hold values from 1.1288108e-15 to 1.8060974e-14
- head_gates: float32 [12], P('hid'), may hold values from 0.2 to 1
- layer_gates: float32 [2], replicated, may hold values from 0.5 to 1
- dim_gates: float32 [768], P('hid'), may hold values from 0.2 to 1
- unit_gates: float32 [3072], P('hid'), may hold values from 0.2 to 1
- teacher_qkv: bfloat16 [3, 768, 768], P(None, None, 'hid'), may hold values from -0.21875 to 0.21875
- teacher_out: bfloat16 [768, 768], P('hid'), may hold values from -1.75 to 1.75
- teacher_up: bfloat16 [768, 3072], P(None, 'hid'), may hold values from -0.21875 to 0.21875
- teacher_down: bfloat16 [3072, 768], P('hid'), may hold values from -0.109375 to 0.109375
- teacher_biases: bfloat16 [6, 768], P(None, 'hid'), may hold values from -1.75 to 1.75
- teacher_up_bias: bfloat16 [3072], P('hid'), may hold values from -1.75 to 1.75
- teacher_gains: bfloat16 [2, 768], P(None, 'hid'), may hold values from 0.5 to 1.5
Outputs:
- block_out: bfloat16 [16, 1024, 768], P('rows', None, 'hid')
- input_grad: float32 [16, 1024, 768], P('rows', None, 'hid')
- grad_norm: float32 [], replicated
- qkv_grad: float32 [3, 768, 768], P(None, None, 'hid')
- qkv_new: float32 [3, 768, 768], P(None, None, 'hid')
- qkv_moment2_new: float32 [3, 768, 768], P(None, None, 'hid')
- out_grad: float32 [768, 768], P('hid')
- out_new: float32 [768, 768], P('hid')
- out_moment2_new: float32 [768, 768], P('hid')
- up_grad: float32 [768, 3072], P(None, 'hid')
- up_new: float32 [768, 3072], P(None, 'hid')
- up_moment2_new: float32 [768, 3072], P(None, 'hid')
- down_grad: float32 [3072, 768], P('hid')
- down_new: float32 [3072, 768], P('hid')
- down_moment2_new: float32 [3072, 768], P('hid')
- bias_grad: float32 [6, 768], P(None, 'hid')
- bias_new: float32 [6, 768], P(None, 'hid')
- bias_moment2_new: float32 [6, 768], P(None, 'hid')
- up_bias_grad: float32 [3072], P('hid')
- up_bias_new: float32 [3072], P('hid')
- up_bias_moment2_new: float32 [3072], P('hid')
- gain_grad: float32 [2, 768], P(None, 'hid')
- gain_new: float32 [2, 768], P(None, 'hid')
- gain_moment2_new: float32 [2, 768], P(None, 'hid')
- qkv_copy: bfloat16 [3, 768, 768], P(None, None, 'hid')
- out_copy: bfloat16 [768, 768], P('hid')
- up_copy: bfloat16 [768, 3072], P(None, 'hid')
- down_copy: bfloat16 [3072, 768], P('hid')
The draws below stay inside these ranges and needn't reach their ends.
Inputs may be any that keep to these rules, and one draw needn't show every extreme that they name: `segment_ids`: along each row the ids start at 0, never fall and rise by at most one from a position to the next, so a row holds at most 8 documents; positions with pad_mask 0 keep the id of the row's last real token. `pad_mask`: each row is 1 on a prefix of 307 positions or more and 0 after it.
All inputs are finite; a program needn't handle non-finite values.
Results may differ from the reference program's by a relative error of at most 0.012.
Values may be sent and summed in bfloat16 or wider, within the bound.
A program may use at most 256 MiB of HBM per device.

```python
import math
import jax
import jax.numpy as jnp
from jax import lax

D = 768
HEADS = 12
HEAD = 64
FF = 3072
LEN = 1024
STEP = 10
ROWS = 16


def valid_lengths(key):
    row_index = jnp.arange(ROWS, dtype=jnp.int32)
    span_rows = max(ROWS - 1, 1)
    base_length = LEN * (3 * span_rows + 6 * row_index) // (10 * span_rows)
    return base_length + jax.random.randint(key, (ROWS,), 0, LEN // 10 + 1)


def draw_pad_mask(key, part):
    lengths = valid_lengths(key)
    positions = jnp.arange(LEN, dtype=jnp.int32)
    return (positions[None, :] < lengths[:, None]).astype(jnp.int32)


def draw_segment_ids(key, part):
    lengths = valid_lengths(key)
    key = jax.random.fold_in(key, 7)
    positions = jnp.arange(LEN, dtype=jnp.int32)
    starts = (jax.random.randint(key, (ROWS, LEN), 0, max(LEN // 4, 2)) == 0).astype(jnp.int32)
    marks = jnp.zeros((LEN,), jnp.int32)
    for index in range(1, 8):
        marks = marks + (positions == index * LEN // 10).astype(jnp.int32)
    last_row = (jnp.arange(ROWS, dtype=jnp.int32) == ROWS - 1).astype(jnp.int32)
    starts = jnp.maximum(starts, last_row[:, None] * marks[None, :])
    starts = starts * (positions[None, :] > 0).astype(jnp.int32) * (positions[None, :] < lengths[:, None]).astype(jnp.int32)
    return jnp.minimum(jnp.cumsum(starts, axis=1), 7).astype(jnp.int32)


def draw_dim_gates(key, part):
    key = jax.random.fold_in(key, 11)
    ramp = 1.0 / 3.0 + 2.0 / 3.0 * jnp.arange(D, dtype=jnp.float32) / max(D - 1, 1)
    factor = jax.random.uniform(key, (D,), jnp.float32, 0.8, 1.0)
    return ramp * factor


def steps_of(stream_key, dims, cuts, low, top_value):
    level, own = 1.0, jax.random.fold_in(stream_key, 6)
    for dim, shards_of in cuts:
        heights = jnp.exp(jax.random.uniform(jax.random.fold_in(own, dim), (shards_of,), jnp.float32, low / len(cuts), top_value / len(cuts)))
        level = level * jnp.repeat(heights, dims[dim] // shards_of).reshape([-1 if axis == dim else 1 for axis in range(len(dims))])
    return level


def bell_draw(stream_key, shape, width, most, cuts=(), kind=jnp.bfloat16):
    array = jax.random.normal(stream_key, shape, jnp.float32) * width
    if len(cuts) > 0:
        array = steps_of(stream_key, shape, cuts, -0.22, 0.18) * array
    return jnp.clip(array, min=-most, max=most).astype(kind)


def setup_inputs(seed: int = 0) -> dict:
    arg_keys = jax.random.split(jax.random.key(seed), 37)
    hidden_in = bell_draw(arg_keys[0], (ROWS, LEN, D), 1.0, 6.0, ((0, 16), (2, 2)))
    teacher_in = bell_draw(arg_keys[1], (ROWS, LEN, D), 1.0, 6.0, ((0, 16), (2, 2)))
    segment_ids = draw_segment_ids(jax.random.fold_in(arg_keys[36], 71), 0)
    pad_mask = draw_pad_mask(jax.random.fold_in(arg_keys[36], 71), 0)
    qkv_weight = bell_draw(arg_keys[4], (3, D, D), D ** -0.5, 0.21875, ((2, 2),), jnp.float32)
    qkv_moment1 = bell_draw(arg_keys[5], (3, D, D), (0.00011 / (4 * D * D + 2 * D * FF + FF + 8 * D) ** 0.5), 2.384185791015625e-07, ((2, 2),), jnp.float32)
    qkv_moment2 = jnp.clip(jnp.exp(math.log(1.128810845015297e-15) - 2.7725887 * jax.random.uniform(arg_keys[6], (3, D, D), jnp.float32) ** steps_of(arg_keys[6], (3, D, D), ((2, 2),), -0.2, 0.2)), 7.055067781345606e-17, 1.128810845015297e-15)
    out_weight = bell_draw(arg_keys[7], (D, D), (D // 64 + 1) ** -0.5, 1.75, ((0, 2),), jnp.float32)
    out_moment1 = bell_draw(arg_keys[8], (D, D), (0.00011 / (4 * D * D + 2 * D * FF + FF + 8 * D) ** 0.5), 2.384185791015625e-07, ((0, 2),), jnp.float32)
    out_moment2 = jnp.clip(jnp.exp(math.log(1.128810845015297e-15) - 2.7725887 * jax.random.uniform(arg_keys[9], (D, D), jnp.float32) ** steps_of(arg_keys[9], (D, D), ((0, 2),), -0.2, 0.2)), 7.055067781345606e-17, 1.128810845015297e-15)
    up_weight = bell_draw(arg_keys[10], (D, FF), D ** -0.5, 0.21875, ((1, 2),), jnp.float32)
    up_moment1 = bell_draw(arg_keys[11], (D, FF), (0.00011 / (4 * D * D + 2 * D * FF + FF + 8 * D) ** 0.5), 2.384185791015625e-07, ((1, 2),), jnp.float32)
    up_moment2 = jnp.clip(jnp.exp(math.log(1.128810845015297e-15) - 2.7725887 * jax.random.uniform(arg_keys[12], (D, FF), jnp.float32) ** steps_of(arg_keys[12], (D, FF), ((1, 2),), -0.2, 0.2)), 7.055067781345606e-17, 1.128810845015297e-15)
    down_weight = bell_draw(arg_keys[13], (FF, D), FF ** -0.5, 0.109375, ((0, 2),), jnp.float32)
    down_moment1 = bell_draw(arg_keys[14], (FF, D), (0.00011 / (4 * D * D + 2 * D * FF + FF + 8 * D) ** 0.5), 2.384185791015625e-07, ((0, 2),), jnp.float32)
    down_moment2 = jnp.clip(jnp.exp(math.log(1.128810845015297e-15) - 2.7725887 * jax.random.uniform(arg_keys[15], (FF, D), jnp.float32) ** steps_of(arg_keys[15], (FF, D), ((0, 2),), -0.2, 0.2)), 7.055067781345606e-17, 1.128810845015297e-15)
    bias_vectors = bell_draw(arg_keys[16], (6, D), 0.3, 1.75, ((1, 2),), jnp.float32)
    bias_moment1 = bell_draw(arg_keys[17], (6, D), (0.00044 / (4 * D * D + 2 * D * FF + FF + 8 * D) ** 0.5), 9.5367431640625e-07, ((1, 2),), jnp.float32)
    bias_moment2 = jnp.clip(jnp.exp(math.log(1.806097352024475e-14) - 2.7725887 * jax.random.uniform(arg_keys[18], (6, D), jnp.float32) ** steps_of(arg_keys[18], (6, D), ((1, 2),), -0.2, 0.2)), 1.128810845015297e-15, 1.806097352024475e-14)
    up_bias = bell_draw(arg_keys[19], (FF,), 0.3, 1.75, ((0, 2),), jnp.float32)
    up_bias_moment1 = bell_draw(arg_keys[20], (FF,), (0.00022 / (4 * D * D + 2 * D * FF + FF + 8 * D) ** 0.5), 4.76837158203125e-07, ((0, 2),), jnp.float32)
    up_bias_moment2 = jnp.clip(jnp.exp(math.log(2.257621690030594e-15) - 2.7725887 * jax.random.uniform(arg_keys[21], (FF,), jnp.float32) ** steps_of(arg_keys[21], (FF,), ((0, 2),), -0.2, 0.2)), 1.4110135562691212e-16, 2.257621690030594e-15)
    norm_gains = jnp.clip(1.0 + 0.1 * jax.random.normal(arg_keys[22], (2, D), jnp.float32), 0.5, 1.5)
    gain_moment1 = bell_draw(arg_keys[23], (2, D), (0.00044 / (4 * D * D + 2 * D * FF + FF + 8 * D) ** 0.5), 9.5367431640625e-07, ((1, 2),), jnp.float32)
    gain_moment2 = jnp.clip(jnp.exp(math.log(1.806097352024475e-14) - 2.7725887 * jax.random.uniform(arg_keys[24], (2, D), jnp.float32) ** steps_of(arg_keys[24], (2, D), ((1, 2),), -0.2, 0.2)), 1.128810845015297e-15, 1.806097352024475e-14)
    head_gates = jnp.clip(0.2 + 0.8 * jax.random.uniform(arg_keys[25], (HEADS,), jnp.float32) ** steps_of(arg_keys[25], (HEADS,), ((0, 2),), -0.2, 0.2), 0.2, 1.0)
    layer_gates = jnp.clip(jax.random.uniform(arg_keys[26], (2,), jnp.float32, 0.5, 1.0), 0.5, 1.0)
    dim_gates = draw_dim_gates(jax.random.fold_in(arg_keys[36], 71), 0)
    unit_gates = jnp.clip(0.2 + 0.8 * jax.random.uniform(arg_keys[28], (FF,), jnp.float32) ** steps_of(arg_keys[28], (FF,), ((0, 2),), -0.2, 0.2), 0.2, 1.0)
    teacher_qkv = bell_draw(arg_keys[29], (3, D, D), D ** -0.5, 0.21875, ((2, 2),))
    teacher_out = bell_draw(arg_keys[30], (D, D), (D // 64 + 1) ** -0.5, 1.75, ((0, 2),))
    teacher_up = bell_draw(arg_keys[31], (D, FF), D ** -0.5, 0.21875, ((1, 2),))
    teacher_down = bell_draw(arg_keys[32], (FF, D), FF ** -0.5, 0.109375, ((0, 2),))
    teacher_biases = bell_draw(arg_keys[33], (6, D), 0.3, 1.75, ((1, 2),))
    teacher_up_bias = bell_draw(arg_keys[34], (FF,), 0.3, 1.75, ((0, 2),))
    teacher_gains = jnp.clip(1.0 + 0.1 * jax.random.normal(arg_keys[35], (2, D), jnp.float32), 0.5, 1.5).astype(jnp.bfloat16)
    return dict(hidden_in=hidden_in, teacher_in=teacher_in, segment_ids=segment_ids, pad_mask=pad_mask, qkv_weight=qkv_weight, qkv_moment1=qkv_moment1, qkv_moment2=qkv_moment2, out_weight=out_weight, out_moment1=out_moment1, out_moment2=out_moment2, up_weight=up_weight, up_moment1=up_moment1, up_moment2=up_moment2, down_weight=down_weight, down_moment1=down_moment1, down_moment2=down_moment2, bias_vectors=bias_vectors, bias_moment1=bias_moment1, bias_moment2=bias_moment2, up_bias=up_bias, up_bias_moment1=up_bias_moment1, up_bias_moment2=up_bias_moment2, norm_gains=norm_gains, gain_moment1=gain_moment1, gain_moment2=gain_moment2, head_gates=head_gates, layer_gates=layer_gates, dim_gates=dim_gates, unit_gates=unit_gates, teacher_qkv=teacher_qkv, teacher_out=teacher_out, teacher_up=teacher_up, teacher_down=teacher_down, teacher_biases=teacher_biases, teacher_up_bias=teacher_up_bias, teacher_gains=teacher_gains)


@jax.custom_vjp
def low(v):
    return lax.optimization_barrier(v.astype(jnp.bfloat16)).astype(jnp.float32)

@jax.custom_vjp
def low_back(v):
    return v

def low_keep(v):
    return (low(v), None)

def low_pass(kept, grad):
    return (grad,)

def back_keep(v):
    return (v, None)

def back_low(kept, grad):
    return (low(grad),)
low.defvjp(low_keep, low_pass)
low_back.defvjp(back_keep, back_low)
epsilon_norm = 1e-06
masked_score = -1000000000.0
clip_norm = 0.001
beta_first = 0.9
beta_second = 0.999
adam_epsilon = 1e-08
weight_decay = 0.01
rate_attend = 0.03
rate_output = 0.2
rate_expand = 0.03
rate_reduce = 0.03
rate_vector = 0.3
highest = lax.Precision.HIGHEST

def matmul(left, right):
    return jnp.dot(left, right, precision=highest, preferred_element_type=jnp.float32)

def rounded(value):
    return low(low_back(value))

def layer_norm(resid, gain, shift):
    center = lax.optimization_barrier(jnp.mean(resid, axis=-1, keepdims=True))
    second = lax.optimization_barrier(jnp.mean(resid * resid, axis=-1, keepdims=True)) - center * center
    return (resid - center) * lax.rsqrt(second + epsilon_norm) * gain + shift

def attend_row(inputs):
    queries, keys_in, values, segment, padding = inputs
    scale = HEAD ** (-0.5)
    raw_score = low_back(jnp.einsum('qhd,khd->hqk', queries, keys_in, precision=highest))
    allowed = (segment[:, None] == segment[None, :]) & (padding[None, :] > 0)
    scores = jnp.where(allowed[None], raw_score * scale, masked_score)
    top_score = lax.optimization_barrier(jnp.max(scores, axis=-1, keepdims=True))
    weights = jnp.exp(scores - top_score)
    probs = low(weights / lax.optimization_barrier(jnp.sum(weights, axis=-1, keepdims=True)))
    return jnp.einsum('hqk,khd->qhd', probs, values, precision=highest)

def layer(hidden, qkv_weight, out_weight, up_weight, down_weight, biases, up_bias, gains, head_gates, layer_gates, dim_gates, unit_gates, segment_ids, pad_mask):
    count_rows = hidden.shape[0] * hidden.shape[1]
    flat_rows = hidden.reshape(count_rows, D)
    gathered = low_back(flat_rows)
    qkv_low = low(qkv_weight)
    queries = rounded(matmul(gathered, qkv_low[0]) + biases[0])
    keys_in = rounded(matmul(gathered, qkv_low[1]))
    values = rounded(matmul(gathered, qkv_low[2]) + biases[1])
    head_shape = (hidden.shape[0], hidden.shape[1], HEADS, HEAD)
    context = lax.map(jax.checkpoint(attend_row), (queries.reshape(head_shape), keys_in.reshape(head_shape), values.reshape(head_shape), segment_ids, pad_mask))
    context = low_back(context) * head_gates[None, None, :, None]
    context = low(context.reshape(count_rows, D))
    attended = low_back(matmul(context, low(out_weight)))
    branch_one = layer_gates[0] * (attended + biases[2]) * dim_gates
    first_out = layer_norm(flat_rows + branch_one, gains[0], biases[4])
    expanded = low_back(matmul(rounded(first_out), low(up_weight)) + up_bias)
    activated = rounded(jax.nn.gelu(expanded, approximate=False) * unit_gates)
    reduced = low_back(matmul(activated, low(down_weight)))
    branch_two = layer_gates[1] * (reduced + biases[3]) * dim_gates
    second_out = layer_norm(first_out + branch_two, gains[1], biases[5])
    return (first_out, second_out)

def adam_step(weight, first, second, grad, rate, decay):
    first_new = beta_first * first + (1.0 - beta_first) * grad
    second_new = beta_second * second + (1.0 - beta_second) * grad * grad
    first_hat = first_new / (1.0 - beta_first ** STEP)
    second_hat = second_new / (1.0 - beta_second ** STEP)
    return (weight - rate * (first_hat / (jnp.sqrt(second_hat) + adam_epsilon) + decay * weight), second_new)

def reference(hidden_in, teacher_in, segment_ids, pad_mask, qkv_weight, qkv_moment1, qkv_moment2, out_weight, out_moment1, out_moment2, up_weight, up_moment1, up_moment2, down_weight, down_moment1, down_moment2, bias_vectors, bias_moment1, bias_moment2, up_bias, up_bias_moment1, up_bias_moment2, norm_gains, gain_moment1, gain_moment2, head_gates, layer_gates, dim_gates, unit_gates, teacher_qkv, teacher_out, teacher_up, teacher_down, teacher_biases, teacher_up_bias, teacher_gains):
    unit_heads = jnp.ones_like(head_gates)
    unit_layers = jnp.ones_like(layer_gates)
    unit_dims = jnp.ones_like(dim_gates)
    unit_units = jnp.ones_like(unit_gates)
    teacher_first, teacher_second = layer(teacher_in.astype(jnp.float32), teacher_qkv.astype(jnp.float32), teacher_out.astype(jnp.float32), teacher_up.astype(jnp.float32), teacher_down.astype(jnp.float32), teacher_biases.astype(jnp.float32), teacher_up_bias.astype(jnp.float32), teacher_gains.astype(jnp.float32), unit_heads, unit_layers, unit_dims, unit_units, segment_ids, pad_mask)
    valid = pad_mask.reshape(-1).astype(jnp.float32)
    total_valid = jnp.sum(valid)

    def objective(student_in, qkv_param, out_param, up_param, down_param, bias_param, up_bias_param, gain_param):
        first_out, second_out = layer(student_in, qkv_param, out_param, up_param, down_param, bias_param, up_bias_param, gain_param, head_gates, layer_gates, dim_gates, unit_gates, segment_ids, pad_mask)
        per_token = lax.optimization_barrier(jnp.sum((first_out - teacher_first) ** 2, axis=-1)) + lax.optimization_barrier(jnp.sum((second_out - teacher_second) ** 2, axis=-1))
        return (jnp.sum(valid * per_token) / (D * total_valid), second_out)
    loss_value, pullback, second_out = jax.vjp(objective, hidden_in.astype(jnp.float32), qkv_weight, out_weight, up_weight, down_weight, bias_vectors, up_bias, norm_gains, has_aux=True)
    gradients = pullback(jnp.ones_like(loss_value))
    input_grad = gradients[0].reshape(hidden_in.shape)
    weight_grads = gradients[1:]
    squares = jnp.zeros((), jnp.float32)
    for tensor in weight_grads:
        squares = squares + jnp.sum(tensor * tensor)
    grad_norm = jnp.sqrt(squares)
    factor = clip_norm / jnp.maximum(grad_norm, clip_norm)
    weights = (qkv_weight, out_weight, up_weight, down_weight, bias_vectors, up_bias, norm_gains)
    firsts = (qkv_moment1, out_moment1, up_moment1, down_moment1, bias_moment1, up_bias_moment1, gain_moment1)
    seconds = (qkv_moment2, out_moment2, up_moment2, down_moment2, bias_moment2, up_bias_moment2, gain_moment2)
    rates = (rate_attend, rate_output, rate_expand, rate_reduce, rate_vector, rate_vector, rate_vector)
    decays = (weight_decay, weight_decay, weight_decay, weight_decay, 0.0, 0.0, 0.0)
    results = []
    for index in range(7):
        clipped = weight_grads[index] * factor
        new_weight, new_second = adam_step(weights[index], firsts[index], seconds[index], clipped, rates[index], decays[index])
        results.append((clipped, new_weight, new_second))
    block_out = second_out.reshape(hidden_in.shape).astype(jnp.bfloat16)
    return (block_out, input_grad, grad_norm, results[0][0], results[0][1], results[0][2], results[1][0], results[1][1], results[1][2], results[2][0], results[2][1], results[2][2], results[3][0], results[3][1], results[3][2], results[4][0], results[4][1], results[4][2], results[5][0], results[5][1], results[5][2], results[6][0], results[6][1], results[6][2], results[0][1].astype(jnp.bfloat16), results[1][1].astype(jnp.bfloat16), results[2][1].astype(jnp.bfloat16), results[3][1].astype(jnp.bfloat16))
```

```python
import functools

import jax
import jax.numpy as jnp
from jax import lax
from jax.experimental import pallas as pl
from jax.experimental.pallas import tpu as pltpu
from jax.sharding import PartitionSpec as P

D = 768
HEAD = 64
STEP = 10


epsilon_norm = 1e-06
masked_score = -1000000000.0
clip_norm = 0.001
beta_first = 0.9
beta_second = 0.999
adam_epsilon = 1e-08
weight_decay = 0.01
rate_attend = 0.03
rate_output = 0.2
rate_expand = 0.03
rate_reduce = 0.03
rate_vector = 0.3


def features(value):
    return lax.all_gather(value, "hid", axis=1, tiled=True)


def spread_sum(partial_rows):
    return lax.psum_scatter(partial_rows, "hid", scatter_dimension=1, tiled=True)


def grad_gather(value):
    return lax.all_gather(value, "hid", axis=1, tiled=True)


def grad_spread(partial_rows):
    return lax.psum_scatter(
        partial_rows.astype(jnp.bfloat16), "hid", scatter_dimension=1, tiled=True
    ).astype(jnp.float32)


def gelu_exact(preact):
    return jax.nn.gelu(preact, approximate=False)


def layer_norm(resid, gain, shift):
    totals, squares = lax.psum((jnp.sum(resid, axis=1), jnp.sum(resid * resid, axis=1)), "hid")
    center = totals / D
    inverse = lax.rsqrt(squares / D - center * center + epsilon_norm)
    normed = (resid - center[:, None]) * inverse[:, None]
    return (normed * gain + shift, normed, inverse)


def norm_back(grad_normed, normed, inverse):
    totals, crossed = lax.psum(
        (jnp.sum(grad_normed, axis=1), jnp.sum(grad_normed * normed, axis=1)), "hid"
    )
    return inverse[:, None] * (grad_normed - totals[:, None] / D - normed * crossed[:, None] / D)


def masked_scores(queries, keys_in, segment, padding):
    raw_score = jnp.einsum("qhd,khd->hqk", queries, keys_in, preferred_element_type=jnp.float32)
    allowed = (segment[:, None] == segment[None, :]) & (padding[None, :] > 0)
    return jnp.where(allowed[None], raw_score * HEAD ** (-0.5), masked_score)


def attend_block(inputs):
    queries, keys_in, values, segment, padding = inputs
    scores = masked_scores(queries, keys_in, segment, padding)
    top_score = jnp.max(scores, axis=-1, keepdims=True)
    weights = jnp.exp(scores - top_score)
    totals = jnp.sum(weights, axis=-1, keepdims=True)
    probs = (weights / totals).astype(jnp.bfloat16)
    context = jnp.einsum("hqk,khd->qhd", probs, values, preferred_element_type=jnp.float32)
    return (context, (top_score + jnp.log(totals))[..., 0])


def attend_back(inputs):
    queries, keys_in, values, segment, padding, log_total, grad_context = inputs
    scores = masked_scores(queries, keys_in, segment, padding)
    probs = jnp.exp(scores - log_total[..., None])
    grad_probs = jnp.einsum(
        "qhd,khd->hqk", grad_context, values, preferred_element_type=jnp.float32
    )
    inner_sum = jnp.sum(probs * grad_probs, axis=-1, keepdims=True)
    grad_raw = (probs * (grad_probs - inner_sum) * HEAD ** (-0.5)).astype(jnp.bfloat16)
    grad_query = jnp.einsum("hqk,khd->qhd", grad_raw, keys_in, preferred_element_type=jnp.float32)
    grad_key = jnp.einsum("hqk,qhd->khd", grad_raw, queries, preferred_element_type=jnp.float32)
    grad_value = jnp.einsum(
        "hqk,qhd->khd", probs.astype(jnp.bfloat16), grad_context, preferred_element_type=jnp.float32
    )
    return (grad_query, grad_key, grad_value)


def forward(hidden, weights, gates, segment_ids, pad_mask):
    qkv_low, out_low, up_low, down_low, biases, up_bias, gains = weights
    head_gates, layer_gates, dim_gates, unit_gates = gates
    seqs_here, length = segment_ids.shape
    width_here = hidden.shape[2]
    tokens_here = seqs_here * length
    heads_here = head_gates.shape[0]
    head_size = width_here // heads_here
    head_shape = (seqs_here, length, heads_here, head_size)
    flat_low = hidden.reshape(tokens_here, width_here)
    gathered = features(flat_low)
    zero_bias = jnp.zeros_like(biases[0])
    projected = jnp.einsum("td,jdc->tjc", gathered, qkv_low, preferred_element_type=jnp.float32)
    projected = (projected + jnp.stack([biases[0], zero_bias, biases[1]])[None]).astype(
        jnp.bfloat16
    )
    queries = projected[:, 0].reshape(head_shape)
    keys_in = projected[:, 1].reshape(head_shape)
    values = projected[:, 2].reshape(head_shape)
    context, log_total = lax.map(attend_block, (queries, keys_in, values, segment_ids, pad_mask))
    gated = context.reshape(tokens_here, heads_here, head_size) * head_gates[None, :, None]
    context_low = gated.reshape(tokens_here, width_here).astype(jnp.bfloat16)
    attended = spread_sum(jnp.dot(context_low, out_low, preferred_element_type=jnp.float32))
    resid_one = flat_low.astype(jnp.float32) + layer_gates[0] * (attended + biases[2]) * dim_gates
    first_out, normed_one, inverse_one = layer_norm(resid_one, gains[0], biases[4])
    first_all = features(first_out.astype(jnp.bfloat16))
    expanded = jnp.dot(first_all, up_low, preferred_element_type=jnp.float32) + up_bias
    activated = (gelu_exact(expanded) * unit_gates).astype(jnp.bfloat16)
    reduced = spread_sum(jnp.dot(activated, down_low, preferred_element_type=jnp.float32))
    resid_two = first_out + layer_gates[1] * (reduced + biases[3]) * dim_gates
    second_out, normed_two, inverse_two = layer_norm(resid_two, gains[1], biases[5])
    kept = (
        gathered,
        queries,
        keys_in,
        values,
        log_total,
        context_low,
        normed_one,
        inverse_one,
        first_all,
        expanded,
        activated,
        normed_two,
        inverse_two,
    )
    return (first_out, second_out, kept)


INNER = 16
BATCHES = 3
SHARD = 96


def reduce_kernel(outer, parts_ref, small_ref, sums_ref, small_out_ref, square_ref, *scratch):
    (
        recv_one, send_two, recv_two, keep, send_three, recv_three, shard, outer_recv,
        small_send, small_recv, small_three, small_outer, square_send, square_recv,
        send_sems, recv_sems, local_sems,
    ) = scratch
    place = lax.axis_index("rows")
    inside = place % INNER
    base = place - inside
    x, y, z = inside % 2, (inside // 2) % 2, inside // 4
    group = place // INNER
    core = lax.axis_index("hid")
    to_x = {"rows": place + 1 - 2 * x}
    to_y = {"rows": place + 2 - 4 * y}
    to_z = [{"rows": base + inside % 4 + 4 * ((z + d) % 4)} for d in range(4)]
    to_group = [{"rows": inside + INNER * ((group + d) % outer)} for d in range(outer)]
    to_core = {"hid": 1 - core}
    barrier = pltpu.get_barrier_semaphore()
    peers = [to_x, to_y] + to_z[1:] + to_group[1:] + [to_core]
    for peer in peers:
        pl.semaphore_signal(barrier, inc=1, device_id=peer, device_id_type=pl.DeviceIdType.MESH)
    pl.semaphore_wait(barrier, len(peers))

    counter = [0]
    pending = []

    def send(source, target, peer):
        index = counter[0]
        counter[0] += 1
        copy = pltpu.make_async_remote_copy(
            src_ref=source, dst_ref=target, send_sem=send_sems.at[index],
            recv_sem=recv_sems.at[index], device_id=peer, device_id_type=pl.DeviceIdType.MESH,
        )
        copy.start()
        pending.append(copy)
        return copy

    wide = jnp.float32
    first_bit, second_bit = (x, y), (y, x)
    first_peer, second_peer = (to_x, to_y), (to_y, to_x)

    def rows(start, size):
        return pl.ds(pl.multiple_of(start, SHARD), size)

    half = [768 * first_bit[lane] for lane in range(2)]
    quarter = [half[lane] + 384 * second_bit[lane] for lane in range(2)]
    mine = [quarter[lane] + SHARD * z for lane in range(2)]
    one, two, three, four, five, six = {}, {}, {}, {}, {}, {}

    def start_one(b):
        for lane in range(2):
            one[b, lane] = send(
                parts_ref.at[b, lane, rows(768 - half[lane], 768)], recv_one.at[b, lane], first_peer[lane]
            )

    def start_two(b):
        for lane in range(2):
            one[b, lane].wait_recv()
            other = 384 - 384 * second_bit[lane]
            send_two[b, lane] = (
                parts_ref[b, lane, rows(half[lane] + other, 384)].astype(wide)
                + recv_one[b, lane, rows(other, 384)].astype(wide)
            ).astype(jnp.bfloat16)
            two[b, lane] = send(send_two.at[b, lane], recv_two.at[b, lane], second_peer[lane])
        for lane in range(2):
            keep[b, lane] = parts_ref[b, lane, rows(quarter[lane], 384)].astype(wide) + recv_one[
                b, lane, rows(384 * second_bit[lane], 384)
            ].astype(wide)

    def start_three(b):
        for lane in range(2):
            two[b, lane].wait_recv()
            keep[b, lane] = keep[b, lane] + recv_two[b, lane].astype(wide)
            for d in (2, 1, 3):
                send_three[b, lane, d - 1] = keep[
                    b, lane, rows(SHARD * ((z + d) % 4), SHARD)
                ].astype(jnp.bfloat16)
                three[b, lane, d] = send(
                    send_three.at[b, lane, d - 1], recv_three.at[b, lane, d - 1], to_z[d]
                )

    squares = []

    def start_four(b):
        for lane in range(2):
            total = keep[b, lane, rows(SHARD * z, SHARD)]
            for d in (1, 3, 2):
                three[b, lane, d].wait_recv()
                total = total + recv_three[b, lane, d - 1].astype(wide)
            if outer > 1:
                shard[b, lane] = total.astype(jnp.bfloat16)
                copies = [
                    send(shard.at[b, lane], outer_recv.at[b, lane, d - 1], to_group[d])
                    for d in range(1, outer)
                ]
                for d, copy in enumerate(copies):
                    copy.wait()
                    total = total + outer_recv[b, lane, d].astype(wide)
            squares.append(jnp.sum(total * total, axis=0, keepdims=True))
            shard[b, lane] = total.astype(jnp.bfloat16)
            place_here = sums_ref.at[b, lane, rows(mine[lane], SHARD)]
            local = pltpu.make_async_copy(shard.at[b, lane], place_here, local_sems.at[b, lane])
            local.start()
            four[b, lane] = [send(shard.at[b, lane], place_here, to_z[d]) for d in (2, 1, 3)] + [local]

    def start_five(b):
        for lane in range(2):
            for copy in four[b, lane][:3]:
                copy.wait_recv()
            four[b, lane][3].wait()
            block = sums_ref.at[b, lane, rows(quarter[lane], 384)]
            five[b, lane] = send(block, block, second_peer[lane])

    def start_six(b):
        for lane in range(2):
            five[b, lane].wait_recv()
            block = sums_ref.at[b, lane, rows(half[lane], 768)]
            six[b, lane] = send(block, block, first_peer[lane])

    def finish(b):
        for lane in range(2):
            six[b, lane].wait_recv()

    start_one(0)
    small_one = send(small_ref, small_recv.at[0], to_x)
    start_one(1)
    small_one.wait_recv()
    small_send[0] = small_ref[...] + small_recv[0]
    small_two = send(small_send.at[0], small_recv.at[1], to_y)
    start_two(0)
    start_one(2)
    small_two.wait_recv()
    small_send[1] = small_send[0] + small_recv[1]
    small_three[z] = small_send[1]
    small_z = [send(small_send.at[1], small_three.at[z], to_z[d]) for d in range(1, 4)]
    start_two(1)
    start_three(0)
    for copy in small_z:
        copy.wait_recv()
    small_total = (small_three[0] + small_three[1]) + (small_three[2] + small_three[3])
    if outer > 1:
        small_send[2] = small_total
        small_outer[group] = small_total
        copies = [send(small_send.at[2], small_outer.at[group], to_group[d]) for d in range(1, outer)]
        for copy in copies:
            copy.wait_recv()
        small_total = small_outer[0]
        for index in range(1, outer):
            small_total = small_total + small_outer[index]
    small_out_ref[...] = small_total
    start_two(2)
    start_three(1)
    start_four(0)
    start_three(2)
    start_four(1)
    start_five(0)
    start_four(2)
    total_square = squares[0]
    for value in squares[1:]:
        total_square = total_square + value
    spread = jnp.broadcast_to(jnp.sum(total_square, axis=1, keepdims=True), (8, 128))
    square_send[0] = spread
    square_x = send(square_send.at[0], square_recv.at[0], to_x)
    start_five(1)
    start_six(0)
    square_x.wait_recv()
    square_send[1] = square_send[0] + square_recv[0]
    square_y = send(square_send.at[1], square_recv.at[1], to_y)
    start_five(2)
    square_y.wait_recv()
    square_send[2] = square_send[1] + square_recv[1]
    square_recv[4 + z] = square_send[2]
    square_z = [send(square_send.at[2], square_recv.at[4 + z], to_z[d]) for d in range(1, 4)]
    start_six(1)
    for copy in square_z:
        copy.wait_recv()
    small_square = jnp.sum(small_total * small_total, axis=(0, 1), keepdims=True)
    square_send[3] = (
        (square_recv[4] + square_recv[5]) + (square_recv[6] + square_recv[7])
    ) + jnp.broadcast_to(small_square, (8, 128))
    square_core = send(square_send.at[3], square_recv.at[2], to_core)
    start_six(2)
    square_core.wait_recv()
    square_ref[...] = square_send[3] + square_recv[2]
    for b in range(BATCHES):
        finish(b)
    for copy in pending:
        copy.wait_send()


def reduce_rows(outer, parts, small):
    low = jnp.bfloat16
    lanes = (BATCHES, 2)
    copies = 6 * (1 + 1 + 3 + (outer - 1) + 3 + 1 + 1) + 5 + (outer - 1) + 6
    small_shape = small.shape
    return pl.pallas_call(
        functools.partial(reduce_kernel, outer),
        out_shape=(
            jax.ShapeDtypeStruct(parts.shape, low),
            jax.ShapeDtypeStruct(small_shape, jnp.float32),
            jax.ShapeDtypeStruct((8, 128), jnp.float32),
        ),
        in_specs=[pl.BlockSpec(memory_space=pltpu.VMEM)] * 2,
        out_specs=(
            pl.BlockSpec(memory_space=pl.ANY),
            pl.BlockSpec(memory_space=pltpu.VMEM),
            pl.BlockSpec(memory_space=pltpu.VMEM),
        ),
        scratch_shapes=[
            pltpu.VMEM(lanes + (768, 384), low),
            pltpu.VMEM(lanes + (384, 384), low),
            pltpu.VMEM(lanes + (384, 384), low),
            pltpu.VMEM(lanes + (384, 384), jnp.float32),
            pltpu.VMEM(lanes + (3, SHARD, 384), low),
            pltpu.VMEM(lanes + (3, SHARD, 384), low),
            pltpu.VMEM(lanes + (SHARD, 384), low),
            pltpu.VMEM(lanes + (max(outer - 1, 1), SHARD, 384), low),
            pltpu.VMEM((3,) + small_shape, jnp.float32),
            pltpu.VMEM((2,) + small_shape, jnp.float32),
            pltpu.VMEM((4,) + small_shape, jnp.float32),
            pltpu.VMEM((outer,) + small_shape, jnp.float32),
            pltpu.VMEM((4, 8, 128), jnp.float32),
            pltpu.VMEM((8, 8, 128), jnp.float32),
            pltpu.SemaphoreType.DMA((copies,)),
            pltpu.SemaphoreType.DMA((copies,)),
            pltpu.SemaphoreType.DMA(lanes),
        ],
        compiler_params=pltpu.CompilerParams(
            collective_id=0, has_side_effects=True, vmem_limit_bytes=56 * 2**20
        ),
        cost_estimate=pl.CostEstimate(flops=10**8, bytes_accessed=3 * 10**8, transcendentals=0),
        name="reduce_rows",
    )(parts, small)


def adam_step(weight, first, second, grad, rate, decay):
    first_new = beta_first * first + (1.0 - beta_first) * grad
    second_new = beta_second * second + (1.0 - beta_second) * grad * grad
    first_hat = first_new / (1.0 - beta_first**STEP)
    second_hat = second_new / (1.0 - beta_second**STEP)
    return (
        weight - rate * (first_hat / (jnp.sqrt(second_hat) + adam_epsilon) + decay * weight),
        second_new,
    )


def clip_factor(square):
    return clip_norm / jnp.maximum(jnp.sqrt(square), clip_norm)


def adam_kernel(rate, square_ref, sums_ref, weight_ref, first_ref, second_ref, grad_ref, new_ref, second_new_ref, copy_ref):
    clipped = sums_ref[...].astype(jnp.float32) * clip_factor(square_ref[:1, :1])
    grad_ref[...] = clipped
    new_weight, new_second = adam_step(
        weight_ref[...], first_ref[...], second_ref[...], clipped, rate, weight_decay
    )
    new_ref[...] = new_weight
    second_new_ref[...] = new_second
    copy_ref[...] = new_weight.astype(jnp.bfloat16)


def adam_call(rate, grid, sums_block, sums_map, block, block_map, square, sums, weight, first, second):
    shape = weight.shape
    same = pl.BlockSpec(block, block_map)
    return pl.pallas_call(
        functools.partial(adam_kernel, rate),
        grid=grid,
        out_shape=(
            jax.ShapeDtypeStruct(shape, jnp.float32),
            jax.ShapeDtypeStruct(shape, jnp.float32),
            jax.ShapeDtypeStruct(shape, jnp.float32),
            jax.ShapeDtypeStruct(shape, jnp.bfloat16),
        ),
        in_specs=[
            pl.BlockSpec((8, 128), lambda *index: (0, 0)),
            pl.BlockSpec(sums_block, sums_map),
            same,
            same,
            same,
        ],
        out_specs=(same, same, same, same),
        compiler_params=pltpu.CompilerParams(vmem_limit_bytes=48 * 2**20),
        cost_estimate=pl.CostEstimate(flops=20 * weight.size, bytes_accessed=28 * weight.size, transcendentals=weight.size),
        name="adam",
    )(square, sums, weight, first, second)


def on_device(
    hidden_in,
    teacher_in,
    segment_ids,
    pad_mask,
    qkv_weight,
    qkv_moment1,
    qkv_moment2,
    out_weight,
    out_moment1,
    out_moment2,
    up_weight,
    up_moment1,
    up_moment2,
    down_weight,
    down_moment1,
    down_moment2,
    bias_vectors,
    bias_moment1,
    bias_moment2,
    up_bias,
    up_bias_moment1,
    up_bias_moment2,
    norm_gains,
    gain_moment1,
    gain_moment2,
    head_gates,
    layer_gates,
    dim_gates,
    unit_gates,
    teacher_qkv,
    teacher_out,
    teacher_up,
    teacher_down,
    teacher_biases,
    teacher_up_bias,
    teacher_gains,
):
    seqs_here, length = segment_ids.shape
    width_here = hidden_in.shape[2]
    tokens_here = seqs_here * length
    heads_here = head_gates.shape[0]
    head_size = width_here // heads_here
    head_shape = (seqs_here, length, heads_here, head_size)
    teacher_weights = (
        teacher_qkv,
        teacher_out,
        teacher_up,
        teacher_down,
        teacher_biases.astype(jnp.float32),
        teacher_up_bias.astype(jnp.float32),
        teacher_gains.astype(jnp.float32),
    )
    unit_ones = (
        jnp.ones_like(head_gates),
        jnp.ones_like(layer_gates),
        jnp.ones_like(dim_gates),
        jnp.ones_like(unit_gates),
    )
    teacher_first, teacher_second, teacher_kept = forward(
        teacher_in, teacher_weights, unit_ones, segment_ids, pad_mask
    )
    qkv_low = qkv_weight.astype(jnp.bfloat16)
    out_low = out_weight.astype(jnp.bfloat16)
    up_low = up_weight.astype(jnp.bfloat16)
    down_low = down_weight.astype(jnp.bfloat16)
    student_weights = (qkv_low, out_low, up_low, down_low, bias_vectors, up_bias, norm_gains)
    student_gates = (head_gates, layer_gates, dim_gates, unit_gates)
    first_out, second_out, kept = forward(
        hidden_in, student_weights, student_gates, segment_ids, pad_mask
    )
    (
        gathered,
        queries,
        keys_in,
        values,
        log_total,
        context_low,
        normed_one,
        inverse_one,
        first_all,
        expanded,
        activated,
        normed_two,
        inverse_two,
    ) = kept
    valid = pad_mask.reshape(-1).astype(jnp.float32)
    total_valid = lax.psum(jnp.sum(valid), "rows")
    scale_rows = 2.0 * valid / (D * total_valid)
    grad_second = scale_rows[:, None] * (second_out - teacher_second)
    grad_first = scale_rows[:, None] * (first_out - teacher_first)
    grad_gain_two = jnp.sum(grad_second * normed_two, axis=0)
    grad_shift_two = jnp.sum(grad_second, axis=0)
    grad_resid_two = norm_back(grad_second * norm_gains[1], normed_two, inverse_two)
    grad_reduced = grad_resid_two * (layer_gates[1] * dim_gates)
    grad_down_bias = jnp.sum(grad_reduced, axis=0)
    grad_reduced_all = grad_gather(grad_reduced.astype(jnp.bfloat16))
    grad_activated = (
        jnp.dot(grad_reduced_all, down_low.T, preferred_element_type=jnp.float32)
        .astype(jnp.bfloat16)
        .astype(jnp.float32)
    )
    grad_down = jnp.dot(activated.T, grad_reduced_all, preferred_element_type=jnp.float32)
    gelu_value, gelu_back = jax.vjp(gelu_exact, expanded)
    grad_expanded = gelu_back(grad_activated * unit_gates)[0].astype(jnp.bfloat16)
    grad_up_bias = jnp.sum(grad_expanded.astype(jnp.float32), axis=0)
    grad_up = jnp.dot(first_all.T, grad_expanded, preferred_element_type=jnp.float32)
    grad_first_ffn = grad_spread(
        jnp.dot(grad_expanded, up_low.T, preferred_element_type=jnp.float32)
    )
    grad_first = (
        grad_first + grad_resid_two + grad_first_ffn.astype(jnp.bfloat16).astype(jnp.float32)
    )
    grad_gain_one = jnp.sum(grad_first * normed_one, axis=0)
    grad_shift_one = jnp.sum(grad_first, axis=0)
    grad_resid_one = norm_back(grad_first * norm_gains[0], normed_one, inverse_one)
    grad_attended = grad_resid_one * (layer_gates[0] * dim_gates)
    grad_out_bias = jnp.sum(grad_attended, axis=0)
    grad_attended_all = grad_gather(grad_attended.astype(jnp.bfloat16))
    grad_context = jnp.dot(grad_attended_all, out_low.T, preferred_element_type=jnp.float32)
    grad_out = jnp.dot(context_low.T, grad_attended_all, preferred_element_type=jnp.float32)
    grad_heads = (
        (grad_context.reshape(tokens_here, heads_here, head_size) * head_gates[None, :, None])
        .astype(jnp.bfloat16)
        .reshape(head_shape)
    )
    grad_query, grad_key, grad_value = lax.map(
        attend_back, (queries, keys_in, values, segment_ids, pad_mask, log_total, grad_heads)
    )
    grad_proj = jnp.stack(
        [
            grad_query.reshape(tokens_here, width_here),
            grad_key.reshape(tokens_here, width_here),
            grad_value.reshape(tokens_here, width_here),
        ],
        axis=1,
    ).astype(jnp.bfloat16)
    grad_qkv = jnp.einsum("td,tjc->jdc", gathered, grad_proj, preferred_element_type=jnp.float32)
    bias_sums = jnp.sum(grad_proj.astype(jnp.float32), axis=0)
    grad_input_part = grad_spread(
        jnp.einsum("tjc,jdc->td", grad_proj, qkv_low, preferred_element_type=jnp.float32)
    )
    input_grad = grad_input_part.astype(jnp.bfloat16).astype(jnp.float32) + grad_resid_one
    grad_biases = jnp.stack(
        [bias_sums[0], bias_sums[2], grad_out_bias, grad_down_bias, grad_shift_one, grad_shift_two]
    )
    grad_gains = jnp.stack([grad_gain_one, grad_gain_two])
    parts = jnp.stack(
        [
            jnp.stack([grad_down[:, :384], grad_down[:, 384:]]),
            jnp.stack(
                [
                    jnp.concatenate([grad_up[:, :384], grad_up[:, 384:768]]),
                    jnp.concatenate([grad_up[:, 768:1152], grad_up[:, 1152:]]),
                ]
            ),
            jnp.stack(
                [
                    jnp.concatenate([grad_qkv[0], grad_qkv[1]]),
                    jnp.concatenate([grad_qkv[2], grad_out[:, :384], grad_out[:, 384:]]),
                ]
            ),
        ]
    ).astype(jnp.bfloat16)
    small = jnp.concatenate(
        [
            grad_biases.reshape(-1),
            grad_up_bias,
            grad_gains.reshape(-1),
            jnp.zeros((512,), jnp.float32),
        ]
    ).reshape(40, 128)
    rows_all = lax.axis_size("rows")
    sums, small_sums, square = reduce_rows(rows_all // INNER, parts, small)
    grad_norm = jnp.sqrt(square[0, 0])
    factor = clip_factor(square[0, 0])
    one = pl.squeezed
    down_results = adam_call(
        rate_reduce, (4, 2), (one, one, 384, 384), lambda i, j: (0, j, i, 0), (384, 384), lambda i, j: (i, j),
        square, sums, down_weight, down_moment1, down_moment2,
    )
    up_results = adam_call(
        rate_expand, (2, 4), (one, one, 384, 384), lambda i, j: (1, j // 2, (j % 2) * 2 + i, 0), (384, 384), lambda i, j: (i, j),
        square, sums, up_weight, up_moment1, up_moment2,
    )
    qkv_results = adam_call(
        rate_attend, (3, 2), (one, one, 384, 384), lambda i, j: (2, i // 2, (i % 2) * 2 + j, 0), (one, 384, 384), lambda i, j: (i, j, 0),
        square, sums, qkv_weight, qkv_moment1, qkv_moment2,
    )
    out_results = adam_call(
        rate_output, (2,), (one, one, 384, 384), lambda j: (2, 1, 2 + j, 0), (384, 384), lambda j: (0, j),
        square, sums, out_weight, out_moment1, out_moment2,
    )
    flat_small = small_sums.reshape(-1) * factor
    small_grads = (
        flat_small[:2304].reshape(6, 384), flat_small[2304:3840], flat_small[3840:4608].reshape(2, 384)
    )
    small_states = (
        (bias_vectors, bias_moment1, bias_moment2),
        (up_bias, up_bias_moment1, up_bias_moment2),
        (norm_gains, gain_moment1, gain_moment2),
    )
    results = [qkv_results, out_results, up_results, down_results]
    for (weight, first, second), clipped in zip(small_states, small_grads):
        results.append((clipped,) + adam_step(weight, first, second, clipped, rate_vector, 0.0))
    block_out = second_out.astype(jnp.bfloat16).reshape(hidden_in.shape)
    input_grad = input_grad.reshape(hidden_in.shape)
    return (
        block_out,
        input_grad,
        grad_norm,
        results[0][0],
        results[0][1],
        results[0][2],
        results[1][0],
        results[1][1],
        results[1][2],
        results[2][0],
        results[2][1],
        results[2][2],
        results[3][0],
        results[3][1],
        results[3][2],
        results[4][0],
        results[4][1],
        results[4][2],
        results[5][0],
        results[5][1],
        results[5][2],
        results[6][0],
        results[6][1],
        results[6][2],
        results[0][3],
        results[1][3],
        results[2][3],
        results[3][3],
    )


def solution(mesh):
    in_specs = (
        P("rows", None, "hid"),
        P("rows", None, "hid"),
        P("rows", None),
        P("rows", None),
        P(None, None, "hid"),
        P(None, None, "hid"),
        P(None, None, "hid"),
        P("hid", None),
        P("hid", None),
        P("hid", None),
        P(None, "hid"),
        P(None, "hid"),
        P(None, "hid"),
        P("hid", None),
        P("hid", None),
        P("hid", None),
        P(None, "hid"),
        P(None, "hid"),
        P(None, "hid"),
        P("hid"),
        P("hid"),
        P("hid"),
        P(None, "hid"),
        P(None, "hid"),
        P(None, "hid"),
        P("hid"),
        P(),
        P("hid"),
        P("hid"),
        P(None, None, "hid"),
        P("hid", None),
        P(None, "hid"),
        P("hid", None),
        P(None, "hid"),
        P("hid"),
        P(None, "hid"),
    )
    out_specs = (
        P("rows", None, "hid"),
        P("rows", None, "hid"),
        P(),
        P(None, None, "hid"),
        P(None, None, "hid"),
        P(None, None, "hid"),
        P("hid", None),
        P("hid", None),
        P("hid", None),
        P(None, "hid"),
        P(None, "hid"),
        P(None, "hid"),
        P("hid", None),
        P("hid", None),
        P("hid", None),
        P(None, "hid"),
        P(None, "hid"),
        P(None, "hid"),
        P("hid"),
        P("hid"),
        P("hid"),
        P(None, "hid"),
        P(None, "hid"),
        P(None, "hid"),
        P(None, None, "hid"),
        P("hid", None),
        P(None, "hid"),
        P("hid", None),
    )
    return jax.shard_map(
        on_device, mesh=mesh, in_specs=in_specs, out_specs=out_specs, check_vma=False
    )
```

```python
import functools

import jax
import jax.numpy as jnp
from jax import lax
from jax.experimental import pallas as pl
from jax.experimental.pallas import tpu as pltpu
from jax.sharding import PartitionSpec as P

D = 768
HEAD = 64
STEP = 10


epsilon_norm = 1e-06
masked_score = -1000000000.0
clip_norm = 0.001
beta_first = 0.9
beta_second = 0.999
adam_epsilon = 1e-08
weight_decay = 0.01
rate_attend = 0.03
rate_output = 0.2
rate_expand = 0.03
rate_reduce = 0.03
rate_vector = 0.3


INNER = 16
BATCHES = 3
SHARD = 96


def reduce_kernel(outer, parts_ref, small_ref, sums_ref, small_out_ref, square_ref, *scratch):
    (
        recv_one, send_two, recv_two, keep, send_three, recv_three, shard, outer_recv,
        small_send, small_recv, small_three, small_outer, square_send, square_recv,
        send_sems, recv_sems, local_sems,
    ) = scratch
    place = lax.axis_index("rows")
    inside = place % INNER
    base = place - inside
    x, y, z = inside % 2, (inside // 2) % 2, inside // 4
    group = place // INNER
    core = lax.axis_index("hid")
    to_x = {"rows": place + 1 - 2 * x}
    to_y = {"rows": place + 2 - 4 * y}
    to_z = [{"rows": base + inside % 4 + 4 * ((z + d) % 4)} for d in range(4)]
    to_group = [{"rows": inside + INNER * ((group + d) % outer)} for d in range(outer)]
    to_core = {"hid": 1 - core}
    barrier = pltpu.get_barrier_semaphore()
    peers = [to_x, to_y] + to_z[1:] + to_group[1:] + [to_core]
    for peer in peers:
        pl.semaphore_signal(barrier, inc=1, device_id=peer, device_id_type=pl.DeviceIdType.MESH)
    pl.semaphore_wait(barrier, len(peers))

    counter = [0]
    pending = []

    def send(source, target, peer):
        index = counter[0]
        counter[0] += 1
        copy = pltpu.make_async_remote_copy(
            src_ref=source, dst_ref=target, send_sem=send_sems.at[index],
            recv_sem=recv_sems.at[index], device_id=peer, device_id_type=pl.DeviceIdType.MESH,
        )
        copy.start()
        pending.append(copy)
        return copy

    wide = jnp.float32
    first_bit, second_bit = (x, y), (y, x)
    first_peer, second_peer = (to_x, to_y), (to_y, to_x)

    def rows(start, size):
        return pl.ds(pl.multiple_of(start, SHARD), size)

    half = [768 * first_bit[lane] for lane in range(2)]
    quarter = [half[lane] + 384 * second_bit[lane] for lane in range(2)]
    mine = [quarter[lane] + SHARD * z for lane in range(2)]
    one, two, three, four, five, six = {}, {}, {}, {}, {}, {}

    def start_one(b):
        for lane in range(2):
            one[b, lane] = send(
                parts_ref.at[b, lane, rows(768 - half[lane], 768)], recv_one.at[b, lane], first_peer[lane]
            )

    def start_two(b):
        for lane in range(2):
            one[b, lane].wait_recv()
            other = 384 - 384 * second_bit[lane]
            send_two[b, lane] = (
                parts_ref[b, lane, rows(half[lane] + other, 384)].astype(wide)
                + recv_one[b, lane, rows(other, 384)].astype(wide)
            ).astype(jnp.bfloat16)
            two[b, lane] = send(send_two.at[b, lane], recv_two.at[b, lane], second_peer[lane])
        for lane in range(2):
            keep[b, lane] = parts_ref[b, lane, rows(quarter[lane], 384)].astype(wide) + recv_one[
                b, lane, rows(384 * second_bit[lane], 384)
            ].astype(wide)

    def start_three(b):
        for lane in range(2):
            two[b, lane].wait_recv()
            keep[b, lane] = keep[b, lane] + recv_two[b, lane].astype(wide)
            for d in (2, 1, 3):
                send_three[b, lane, d - 1] = keep[
                    b, lane, rows(SHARD * ((z + d) % 4), SHARD)
                ].astype(jnp.bfloat16)
                three[b, lane, d] = send(
                    send_three.at[b, lane, d - 1], recv_three.at[b, lane, d - 1], to_z[d]
                )

    squares = []

    def start_four(b):
        for lane in range(2):
            total = keep[b, lane, rows(SHARD * z, SHARD)]
            for d in (1, 3, 2):
                three[b, lane, d].wait_recv()
                total = total + recv_three[b, lane, d - 1].astype(wide)
            if outer > 1:
                shard[b, lane] = total.astype(jnp.bfloat16)
                copies = [
                    send(shard.at[b, lane], outer_recv.at[b, lane, d - 1], to_group[d])
                    for d in range(1, outer)
                ]
                for d, copy in enumerate(copies):
                    copy.wait()
                    total = total + outer_recv[b, lane, d].astype(wide)
            squares.append(jnp.sum(total * total, axis=0, keepdims=True))
            shard[b, lane] = total.astype(jnp.bfloat16)
            place_here = sums_ref.at[b, lane, rows(mine[lane], SHARD)]
            local = pltpu.make_async_copy(shard.at[b, lane], place_here, local_sems.at[b, lane])
            local.start()
            four[b, lane] = [send(shard.at[b, lane], place_here, to_z[d]) for d in (2, 1, 3)] + [local]

    def start_five(b):
        for lane in range(2):
            for copy in four[b, lane][:3]:
                copy.wait_recv()
            four[b, lane][3].wait()
            block = sums_ref.at[b, lane, rows(quarter[lane], 384)]
            five[b, lane] = send(block, block, second_peer[lane])

    def start_six(b):
        for lane in range(2):
            five[b, lane].wait_recv()
            block = sums_ref.at[b, lane, rows(half[lane], 768)]
            six[b, lane] = send(block, block, first_peer[lane])

    def finish(b):
        for lane in range(2):
            six[b, lane].wait_recv()

    start_one(0)
    small_one = send(small_ref, small_recv.at[0], to_x)
    start_one(1)
    small_one.wait_recv()
    small_send[0] = small_ref[...] + small_recv[0]
    small_two = send(small_send.at[0], small_recv.at[1], to_y)
    start_two(0)
    start_one(2)
    small_two.wait_recv()
    small_send[1] = small_send[0] + small_recv[1]
    small_three[z] = small_send[1]
    small_z = [send(small_send.at[1], small_three.at[z], to_z[d]) for d in range(1, 4)]
    start_two(1)
    start_three(0)
    for copy in small_z:
        copy.wait_recv()
    small_total = (small_three[0] + small_three[1]) + (small_three[2] + small_three[3])
    if outer > 1:
        small_send[2] = small_total
        small_outer[group] = small_total
        copies = [send(small_send.at[2], small_outer.at[group], to_group[d]) for d in range(1, outer)]
        for copy in copies:
            copy.wait_recv()
        small_total = small_outer[0]
        for index in range(1, outer):
            small_total = small_total + small_outer[index]
    small_out_ref[...] = small_total
    start_two(2)
    start_three(1)
    start_four(0)
    start_three(2)
    start_four(1)
    start_five(0)
    start_four(2)
    total_square = squares[0]
    for value in squares[1:]:
        total_square = total_square + value
    spread = jnp.broadcast_to(jnp.sum(total_square, axis=1, keepdims=True), (8, 128))
    square_send[0] = spread
    square_x = send(square_send.at[0], square_recv.at[0], to_x)
    start_five(1)
    start_six(0)
    square_x.wait_recv()
    square_send[1] = square_send[0] + square_recv[0]
    square_y = send(square_send.at[1], square_recv.at[1], to_y)
    start_five(2)
    square_y.wait_recv()
    square_send[2] = square_send[1] + square_recv[1]
    square_recv[4 + z] = square_send[2]
    square_z = [send(square_send.at[2], square_recv.at[4 + z], to_z[d]) for d in range(1, 4)]
    start_six(1)
    for copy in square_z:
        copy.wait_recv()
    inside_small = lax.broadcasted_iota(jnp.int32, small_total.shape, 0) < 36
    small_square = jnp.sum(jnp.where(inside_small, small_total * small_total, 0.0), axis=(0, 1), keepdims=True)
    square_send[3] = (
        (square_recv[4] + square_recv[5]) + (square_recv[6] + square_recv[7])
    ) + jnp.broadcast_to(small_square, (8, 128))
    square_core = send(square_send.at[3], square_recv.at[2], to_core)
    start_six(2)
    square_core.wait_recv()
    square_ref[...] = square_send[3] + square_recv[2]
    for b in range(BATCHES):
        finish(b)
    for copy in pending:
        copy.wait_send()


def reduce_rows(outer, parts, small):
    low = jnp.bfloat16
    lanes = (BATCHES, 2)
    copies = 6 * (1 + 1 + 3 + (outer - 1) + 3 + 1 + 1) + 5 + (outer - 1) + 6
    small_shape = small.shape
    return pl.pallas_call(
        functools.partial(reduce_kernel, outer),
        out_shape=(
            jax.ShapeDtypeStruct(parts.shape, low),
            jax.ShapeDtypeStruct(small_shape, jnp.float32),
            jax.ShapeDtypeStruct((8, 128), jnp.float32),
        ),
        in_specs=[pl.BlockSpec(memory_space=pltpu.VMEM)] * 2,
        out_specs=(
            pl.BlockSpec(memory_space=pl.ANY),
            pl.BlockSpec(memory_space=pltpu.VMEM),
            pl.BlockSpec(memory_space=pltpu.VMEM),
        ),
        scratch_shapes=[
            pltpu.VMEM(lanes + (768, 384), low),
            pltpu.VMEM(lanes + (384, 384), low),
            pltpu.VMEM(lanes + (384, 384), low),
            pltpu.VMEM(lanes + (384, 384), jnp.float32),
            pltpu.VMEM(lanes + (3, SHARD, 384), low),
            pltpu.VMEM(lanes + (3, SHARD, 384), low),
            pltpu.VMEM(lanes + (SHARD, 384), low),
            pltpu.VMEM(lanes + (max(outer - 1, 1), SHARD, 384), low),
            pltpu.VMEM((3,) + small_shape, jnp.float32),
            pltpu.VMEM((2,) + small_shape, jnp.float32),
            pltpu.VMEM((4,) + small_shape, jnp.float32),
            pltpu.VMEM((outer,) + small_shape, jnp.float32),
            pltpu.VMEM((4, 8, 128), jnp.float32),
            pltpu.VMEM((8, 8, 128), jnp.float32),
            pltpu.SemaphoreType.DMA((copies,)),
            pltpu.SemaphoreType.DMA((copies,)),
            pltpu.SemaphoreType.DMA(lanes),
        ],
        compiler_params=pltpu.CompilerParams(
            collective_id=0, has_side_effects=True, vmem_limit_bytes=56 * 2**20
        ),
        cost_estimate=pl.CostEstimate(flops=10**8, bytes_accessed=3 * 10**8, transcendentals=0),
        name="reduce_rows",
    )(parts, small)


def adam_step(weight, first, second, grad, rate, decay):
    first_new = beta_first * first + (1.0 - beta_first) * grad
    second_new = beta_second * second + (1.0 - beta_second) * grad * grad
    first_hat = first_new / (1.0 - beta_first**STEP)
    second_hat = second_new / (1.0 - beta_second**STEP)
    return (
        weight - rate * (first_hat / (jnp.sqrt(second_hat) + adam_epsilon) + decay * weight),
        second_new,
    )


def adam_kernel(rate, factor_ref, sums_ref, weight_ref, first_ref, second_ref, grad_ref, new_ref, second_new_ref, copy_ref):
    clipped = sums_ref[...].astype(jnp.float32) * factor_ref[:1, :1]
    grad_ref[...] = clipped
    new_weight, new_second = adam_step(
        weight_ref[...], first_ref[...], second_ref[...], clipped, rate, weight_decay
    )
    new_ref[...] = new_weight
    second_new_ref[...] = new_second
    copy_ref[...] = new_weight.astype(jnp.bfloat16)


def adam_call(rate, grid, sums_block, sums_map, block, block_map, factors, sums, weight, first, second):
    shape = weight.shape
    same = pl.BlockSpec(block, block_map)
    return pl.pallas_call(
        functools.partial(adam_kernel, rate),
        grid=grid,
        out_shape=(
            jax.ShapeDtypeStruct(shape, jnp.float32),
            jax.ShapeDtypeStruct(shape, jnp.float32),
            jax.ShapeDtypeStruct(shape, jnp.float32),
            jax.ShapeDtypeStruct(shape, jnp.bfloat16),
        ),
        in_specs=[
            pl.BlockSpec((8, 128), lambda *index: (0, 0)),
            pl.BlockSpec(sums_block, sums_map),
            same,
            same,
            same,
        ],
        out_specs=(same, same, same, same),
        compiler_params=pltpu.CompilerParams(vmem_limit_bytes=48 * 2**20),
        cost_estimate=pl.CostEstimate(flops=20 * weight.size, bytes_accessed=28 * weight.size, transcendentals=weight.size),
        name="adam",
    )(factors, sums, weight, first, second)


MARKS = 128
TILE = 256


def nt_dot(left, right):
    return lax.dot_general(
        left, right, (((1,), (1,)), ((), ())), preferred_element_type=jnp.float32
    )


def nn_dot(left, right):
    return jnp.dot(left, right, preferred_element_type=jnp.float32)


def attend_kernel(keep, own_ref, other_ref, weight_ref, out_weight_ref, vector_ref, query_mark_ref, key_mark_ref, *refs):
    if keep:
        x_ref, part_ref, query_ref, key_ref, value_ref, context_ref, log_ref, total = refs
    else:
        x_ref, part_ref, total = refs
    low = jnp.bfloat16
    core = lax.axis_index("hid")
    step = pl.program_id(0)
    length, width = own_ref.shape

    @pl.when(step == 0)
    def _():
        x_ref[:, pl.ds(pl.multiple_of(core * width, 128), width)] = own_ref[...]
        x_ref[:, pl.ds(pl.multiple_of((1 - core) * width, 128), width)] = other_ref[...]
        total[...] = jnp.zeros_like(total)

    pair = 2 * HEAD
    weights = jnp.concatenate([weight_ref[j].astype(low) for j in range(3)], axis=1)
    projected = nn_dot(x_ref[...], weights)
    queries = (projected[:, :pair] + vector_ref[0:1]).astype(low)
    keys_in = projected[:, pair : 2 * pair].astype(low)
    values = (projected[:, 2 * pair :] + vector_ref[1:2]).astype(low)
    if keep:
        query_ref[...] = queries
        key_ref[...] = keys_in
        value_ref[...] = values
    scaled = queries * jnp.asarray(HEAD ** (-0.5), low)
    key_wide = jnp.concatenate([keys_in, key_mark_ref[...]], axis=1)
    first_head = lax.broadcasted_iota(jnp.int32, (1, pair), 1) < HEAD
    gate = vector_ref[2:3]
    logs = []
    for start in range(0, length, TILE):
        block = slice(start, start + TILE)
        outs = []
        columns = []
        for head in range(2):
            chosen = jnp.where(first_head if head == 0 else ~first_head, scaled[block], jnp.zeros_like(scaled[block]))
            query_wide = jnp.concatenate([chosen, query_mark_ref[block]], axis=1)
            scores = nt_dot(query_wide, key_wide)
            top = jnp.max(scores, axis=1, keepdims=True)
            weights_here = jnp.exp(scores - top)
            sums = jnp.sum(weights_here, axis=1, keepdims=True)
            mixed = nn_dot(weights_here.astype(low), values)
            outs.append(mixed * (1.0 / sums))
            columns.append(top + jnp.log(sums))
        context = (jnp.where(first_head, outs[0], outs[1]) * gate).astype(low)
        total[block] += nn_dot(context, out_weight_ref[...].astype(low))
        if keep:
            context_ref[block] = context
            both = jnp.where(first_head, columns[0], columns[1])
            logs.append(both)
    if keep:
        turned = jnp.concatenate(logs, axis=0).T
        log_ref[...] = jnp.concatenate([turned[0:1], turned[HEAD : HEAD + 1], turned[0:6]], axis=0)

    @pl.when(step == pl.num_programs(0) - 1)
    def _():
        part_ref[...] = total[...].astype(low)


def attend_call(keep, own, other, weight, out_weight, vectors, query_mark, key_mark):
    length, width = own.shape
    full = 2 * width
    pairs = width // (2 * HEAD)
    low = jnp.bfloat16
    whole = lambda *shape: pl.BlockSpec(shape, lambda i: (0,) * len(shape))
    columns = pl.BlockSpec((length, 128), lambda i: (0, i))
    out_shape = [jax.ShapeDtypeStruct((length, full), low)] * 2
    out_specs = [whole(length, full)] * 2
    if keep:
        out_shape += [jax.ShapeDtypeStruct((length, width), low)] * 4
        out_specs += [columns] * 4
        out_shape += [jax.ShapeDtypeStruct((8 * pairs, length), jnp.float32)]
        out_specs += [pl.BlockSpec((8, length), lambda i: (i, 0))]
    return pl.pallas_call(
        functools.partial(attend_kernel, keep),
        grid=(pairs,),
        out_shape=out_shape,
        in_specs=[
            whole(length, width),
            whole(length, width),
            pl.BlockSpec((3, full, 128), lambda i: (0, 0, i)),
            pl.BlockSpec((128, full), lambda i: (i, 0)),
            pl.BlockSpec((8, 128), lambda i: (0, i)),
            whole(length, MARKS),
            whole(length, MARKS),
        ],
        out_specs=out_specs,
        scratch_shapes=[pltpu.VMEM((length, full), jnp.float32)],
        compiler_params=pltpu.CompilerParams(vmem_limit_bytes=48 * 2**20),
        cost_estimate=pl.CostEstimate(flops=6 * 10**9, bytes_accessed=2 * 10**7, transcendentals=7 * 10**6),
        name="attend",
    )(own, other, weight, out_weight, vectors, query_mark, key_mark)


def normal_cdf(value):
    t = 1.0 / (1.0 + 0.3 * jnp.abs(value))
    poly = jnp.float32(0.0356752946972847)
    for term in (
        -0.15720513463020325, 0.20635683834552765, -0.05368649959564209, 0.1285630166530609,
        0.0999131053686142, 0.12075401097536087, 0.11962929368019104,
    ):
        poly = poly * t + jnp.float32(term)
    bell = jnp.exp(-0.5 * value * value)
    tail = bell * t * poly
    return jnp.where(value < 0.0, tail, 1.0 - tail), bell


def norm_parts(resid):
    center = jnp.mean(resid, axis=1, keepdims=True)
    second = jnp.mean(resid * resid, axis=1, keepdims=True)
    inverse = lax.rsqrt(second - center * center + epsilon_norm)
    return (resid - center) * inverse, inverse


def norm_grad(grad_normed, normed, inverse):
    center = jnp.mean(grad_normed, axis=1, keepdims=True)
    crossed = jnp.mean(grad_normed * normed, axis=1, keepdims=True)
    return inverse * (grad_normed - center - normed * crossed)


def sum_parts(part_ref, other_ref):
    return part_ref[...].astype(jnp.float32) + other_ref[...].astype(jnp.float32)


def feed_kernel(keep, x_ref, part_ref, other_ref, vector_ref, unit_ref, up_ref, down_ref, first_ref, reduced_ref, *refs):
    low = jnp.bfloat16
    resid = x_ref[...].astype(jnp.float32) + (sum_parts(part_ref, other_ref) + vector_ref[1:2]) * vector_ref[0:1]
    normed, inverse = norm_parts(resid)
    first_out = normed * vector_ref[2:3] + vector_ref[3:4]
    first_ref[...] = first_out
    first_low = first_out.astype(low)
    expanded = nn_dot(first_low, up_ref[...]) + unit_ref[0:1]
    share, bell = normal_cdf(expanded)
    activated = (expanded * share * unit_ref[1:2]).astype(low)
    reduced_ref[...] = nn_dot(activated, down_ref[...]).astype(low)
    if keep:
        low_ref, activated_ref, slope_ref = refs
        low_ref[...] = first_low
        activated_ref[...] = activated
        slope_ref[...] = ((share + expanded * bell * 0.3989422804014327) * unit_ref[1:2]).astype(low)


def row_spec(width):
    return pl.BlockSpec((TILE, width), lambda i: (i, 0))


def whole_spec(array):
    return pl.BlockSpec(array.shape, lambda i: (0,) * array.ndim)


def feed_call(keep, x_all, part, other, vectors, units, up_low, down_low):
    length, full = x_all.shape
    hidden = up_low.shape[1]
    low = jnp.bfloat16
    out_shape = [jax.ShapeDtypeStruct((length, full), jnp.float32), jax.ShapeDtypeStruct((length, full), low)]
    out_specs = [row_spec(full)] * 2
    if keep:
        out_shape += [jax.ShapeDtypeStruct((length, full), low)] + [jax.ShapeDtypeStruct((length, hidden), low)] * 2
        out_specs += [row_spec(full), row_spec(hidden), row_spec(hidden)]
    return pl.pallas_call(
        functools.partial(feed_kernel, keep),
        grid=(length // TILE,),
        out_shape=out_shape,
        in_specs=[row_spec(full)] * 3 + [whole_spec(a) for a in (vectors, units, up_low, down_low)],
        out_specs=out_specs,
        compiler_params=pltpu.CompilerParams(vmem_limit_bytes=48 * 2**20),
        cost_estimate=pl.CostEstimate(flops=10 * 10**9, bytes_accessed=2 * 10**7, transcendentals=3 * 10**6),
        name="feed",
    )(x_all, part, other, vectors, units, up_low, down_low)


def add_sums(ref, step, rows):
    stacked = jnp.concatenate(rows + [jnp.zeros_like(rows[0])] * (8 - len(rows)), axis=0)

    @pl.when(step == 0)
    def _():
        ref[...] = stacked

    @pl.when(step > 0)
    def _():
        ref[...] += stacked


def column_sum(value):
    return jnp.sum(value, axis=0, keepdims=True)


def feed_back_kernel(
    first_ref, part_ref, other_ref, teacher_first_ref, teacher_part_ref, teacher_other_ref, valid_ref,
    vector_ref, teacher_vector_ref, slope_ref, up_ref, down_ref,
    block_ref, base_ref, grad_reduced_ref, grad_expanded_ref, part_back_ref, sums_ref, unit_sums_ref,
):
    low = jnp.bfloat16
    core = lax.axis_index("hid")
    step = pl.program_id(0)
    full = first_ref.shape[1]
    first_out = first_ref[...]
    teacher_first = teacher_first_ref[...]
    resid = first_out + (sum_parts(part_ref, other_ref) + vector_ref[5:6]) * vector_ref[4:5]
    normed, inverse = norm_parts(resid)
    second_out = normed * vector_ref[6:7] + vector_ref[7:8]
    teacher_resid = teacher_first + sum_parts(teacher_part_ref, teacher_other_ref) + teacher_vector_ref[5:6]
    teacher_normed, _ = norm_parts(teacher_resid)
    teacher_second = teacher_normed * teacher_vector_ref[6:7] + teacher_vector_ref[7:8]
    half = full // 2
    block_ref[...] = jnp.where(core == 0, second_out[:, :half], second_out[:, half:]).astype(low)
    twice = valid_ref[:, :1] * 2.0
    grad_second = twice * (second_out - teacher_second)
    grad_resid = norm_grad(grad_second * vector_ref[6:7], normed, inverse)
    grad_reduced = grad_resid * vector_ref[4:5]
    add_sums(sums_ref, step, [column_sum(grad_second * normed), column_sum(grad_second), column_sum(grad_reduced)])
    grad_reduced_low = grad_reduced.astype(low)
    grad_reduced_ref[...] = grad_reduced_low
    grad_activated = nt_dot(grad_reduced_low, down_ref[...]).astype(low).astype(jnp.float32)
    grad_expanded = (grad_activated * slope_ref[...].astype(jnp.float32)).astype(low)
    grad_expanded_ref[...] = grad_expanded
    add_sums(unit_sums_ref, step, [column_sum(grad_expanded.astype(jnp.float32))])
    part_back_ref[...] = nt_dot(grad_expanded, up_ref[...]).astype(low)
    base_ref[...] = twice * (first_out - teacher_first) + grad_resid


def feed_back_call(first, part, other, teacher_first, teacher_part, teacher_other, valid, vectors, teacher_vectors, slope, up_low, down_low):
    length, full = first.shape
    hidden = slope.shape[1]
    low, wide = jnp.bfloat16, jnp.float32
    shapes = [((length, full // 2), low), ((length, full), wide), ((length, full), low), ((length, hidden), low), ((length, full), low)]
    return pl.pallas_call(
        feed_back_kernel,
        grid=(length // TILE,),
        out_shape=[jax.ShapeDtypeStruct(*shape) for shape in shapes]
        + [jax.ShapeDtypeStruct((8, full), wide), jax.ShapeDtypeStruct((8, hidden), wide)],
        in_specs=[row_spec(full)] * 6
        + [row_spec(128), whole_spec(vectors), whole_spec(teacher_vectors), row_spec(hidden), whole_spec(up_low), whole_spec(down_low)],
        out_specs=[row_spec(shape[0][1]) for shape in shapes]
        + [pl.BlockSpec((8, full), lambda i: (0, 0)), pl.BlockSpec((8, hidden), lambda i: (0, 0))],
        compiler_params=pltpu.CompilerParams(vmem_limit_bytes=48 * 2**20),
        cost_estimate=pl.CostEstimate(flops=10 * 10**9, bytes_accessed=4 * 10**7, transcendentals=10**4),
        name="feed_back",
    )(first, part, other, teacher_first, teacher_part, teacher_other, valid, vectors, teacher_vectors, slope, up_low, down_low)


def heads_back_kernel(
    base_ref, back_ref, back_other_ref, x_ref, part_ref, other_ref, context_ref, vector_ref, gate_ref, out_weight_ref,
    resid_ref, grad_attended_ref, grad_heads_ref, inner_ref, sums_ref,
):
    low = jnp.bfloat16
    core = lax.axis_index("hid")
    step = pl.program_id(0)
    full = base_ref.shape[1]
    half = full // 2
    grad_first = base_ref[...] + sum_parts(back_ref, back_other_ref).astype(low).astype(jnp.float32)
    resid = x_ref[...].astype(jnp.float32) + (sum_parts(part_ref, other_ref) + vector_ref[1:2]) * vector_ref[0:1]
    normed, inverse = norm_parts(resid)
    grad_resid = norm_grad(grad_first * vector_ref[2:3], normed, inverse)
    resid_ref[...] = jnp.where(core == 0, grad_resid[:, :half], grad_resid[:, half:])
    grad_attended = grad_resid * vector_ref[0:1]
    add_sums(sums_ref, step, [column_sum(grad_first * normed), column_sum(grad_first), column_sum(grad_attended)])
    grad_attended_low = grad_attended.astype(low)
    grad_attended_ref[...] = grad_attended_low
    grad_heads = (nt_dot(grad_attended_low, out_weight_ref[...]) * gate_ref[0:1]).astype(low)
    grad_heads_ref[...] = grad_heads
    product = grad_heads.astype(jnp.float32) * context_ref[...].astype(jnp.float32) * gate_ref[1:2]
    lane = lax.broadcasted_iota(jnp.int32, (1, 128), 1)
    columns = jnp.zeros((product.shape[0], 128), jnp.float32)
    for pair in range(half // 128):
        piece = product[:, 128 * pair : 128 * pair + 128]
        low_sum = jnp.sum(jnp.where(lane < HEAD, piece, 0.0), axis=1, keepdims=True)
        high_sum = jnp.sum(jnp.where(lane < HEAD, 0.0, piece), axis=1, keepdims=True)
        columns = jnp.where(lane == 2 * pair, low_sum, jnp.where(lane == 2 * pair + 1, high_sum, columns))
    inner_ref[...] = columns.T[0:8]


def heads_back_call(base, back, back_other, x_all, part, other, context, vectors, gates, out_low):
    length, full = base.shape
    half = full // 2
    low, wide = jnp.bfloat16, jnp.float32
    return pl.pallas_call(
        heads_back_kernel,
        grid=(length // TILE,),
        out_shape=[
            jax.ShapeDtypeStruct((length, half), wide),
            jax.ShapeDtypeStruct((length, full), low),
            jax.ShapeDtypeStruct((length, half), low),
            jax.ShapeDtypeStruct((8, length), wide),
            jax.ShapeDtypeStruct((8, full), wide),
        ],
        in_specs=[row_spec(full)] * 6 + [row_spec(half)] + [whole_spec(a) for a in (vectors, gates, out_low)],
        out_specs=[
            row_spec(half), row_spec(full), row_spec(half),
            pl.BlockSpec((8, TILE), lambda i: (0, i)),
            pl.BlockSpec((8, full), lambda i: (0, 0)),
        ],
        compiler_params=pltpu.CompilerParams(vmem_limit_bytes=48 * 2**20),
        cost_estimate=pl.CostEstimate(flops=2 * 10**9, bytes_accessed=2 * 10**7, transcendentals=10**4),
        name="heads_back",
    )(base, back, back_other, x_all, part, other, context, vectors, gates, out_low)


def attend_back_kernel(
    query_ref, key_ref, value_ref, grad_ref, query_mark_ref, key_mark_ref, log_ref, inner_ref, out_ref, sums_ref, raw_scratch
):
    low = jnp.bfloat16
    step = pl.program_id(0)
    pair = 2 * HEAD
    length = query_ref.shape[0]
    queries, keys_in, values, grads = query_ref[...], key_ref[...], value_ref[...], grad_ref[...]
    first_head = lax.broadcasted_iota(jnp.int32, (1, pair), 1) < HEAD
    query_wide = jnp.concatenate([queries, query_mark_ref[...]], axis=1)
    scale = HEAD ** (-0.5)
    scaled = keys_in * jnp.asarray(scale, low)
    keys_turned = keys_in.T
    grad_query, key_sums, value_sums = [], [], []
    for head in range(2):
        mask = first_head if head == 0 else ~first_head
        logs = log_ref[head : head + 1]
        inner = inner_ref[pl.ds(2 * step + head, 1), :]
        key_here, value_here = [], []
        for start in range(0, length, TILE):
            block = slice(start, start + TILE)
            zero = jnp.zeros((TILE, pair), low)
            key_wide = jnp.concatenate([jnp.where(mask, scaled[block], zero), key_mark_ref[block]], axis=1)
            probs = jnp.exp(nt_dot(key_wide, query_wide) - logs)
            grad_probs = nt_dot(jnp.where(mask, values[block], zero), grads)
            grad_raw = (probs * (grad_probs - inner)).astype(low)
            raw_scratch[block] = grad_raw
            key_here.append(nn_dot(grad_raw, queries))
            value_here.append(nn_dot(probs.astype(low), grads))
        grad_query.append(nn_dot(keys_turned[HEAD * head : HEAD * head + HEAD], raw_scratch[...]))
        key_sums.append(jnp.concatenate(key_here, axis=0))
        value_sums.append(jnp.concatenate(value_here, axis=0))
    query_out = (jnp.concatenate(grad_query, axis=0).T * scale).astype(low)
    value_out = jnp.where(first_head, value_sums[0], value_sums[1]).astype(low)
    out_ref[0] = query_out
    out_ref[1] = (jnp.where(first_head, key_sums[0], key_sums[1]) * scale).astype(low)
    out_ref[2] = value_out
    rows = [column_sum(query_out.astype(jnp.float32)), column_sum(value_out.astype(jnp.float32))]
    sums_ref[...] = jnp.concatenate(rows + [jnp.zeros_like(rows[0])] * 6, axis=0)


def attend_back_call(queries, keys_in, values, grad_heads, query_mark, key_mark, logs, inner):
    length, width = queries.shape
    pairs = width // (2 * HEAD)
    columns = pl.BlockSpec((length, 128), lambda i: (0, i))
    whole = lambda *shape: pl.BlockSpec(shape, lambda i: (0,) * len(shape))
    return pl.pallas_call(
        attend_back_kernel,
        grid=(pairs,),
        out_shape=[
            jax.ShapeDtypeStruct((3, length, width), jnp.bfloat16),
            jax.ShapeDtypeStruct((8, width), jnp.float32),
        ],
        in_specs=[columns] * 4
        + [whole(length, MARKS)] * 2
        + [pl.BlockSpec((8, length), lambda i: (i, 0)), whole(8, length)],
        out_specs=[
            pl.BlockSpec((3, length, 128), lambda i: (0, 0, i)),
            pl.BlockSpec((8, 128), lambda i: (0, i)),
        ],
        scratch_shapes=[pltpu.VMEM((length, length), jnp.bfloat16)],
        compiler_params=pltpu.CompilerParams(vmem_limit_bytes=48 * 2**20),
        cost_estimate=pl.CostEstimate(flops=10 * 10**9, bytes_accessed=10**7, transcendentals=7 * 10**6),
        name="attend_back",
    )(queries, keys_in, values, grad_heads, query_mark, key_mark, logs, inner)


def on_device(
    hidden_in,
    teacher_in,
    segment_ids,
    pad_mask,
    qkv_weight,
    qkv_moment1,
    qkv_moment2,
    out_weight,
    out_moment1,
    out_moment2,
    up_weight,
    up_moment1,
    up_moment2,
    down_weight,
    down_moment1,
    down_moment2,
    bias_vectors,
    bias_moment1,
    bias_moment2,
    up_bias,
    up_bias_moment1,
    up_bias_moment2,
    norm_gains,
    gain_moment1,
    gain_moment2,
    head_gates,
    layer_gates,
    dim_gates,
    unit_gates,
    teacher_qkv,
    teacher_out,
    teacher_up,
    teacher_down,
    teacher_biases,
    teacher_up_bias,
    teacher_gains,
):
    length = segment_ids.shape[1]
    width = hidden_in.shape[2]
    full = 2 * width
    core = lax.axis_index("hid")
    low, wide = jnp.bfloat16, jnp.float32

    def swap(value):
        return lax.ppermute(value, "hid", [(0, 1), (1, 0)])

    def widen(own, other):
        return jnp.where(
            core == 0, jnp.concatenate([own, other], axis=1), jnp.concatenate([other, own], axis=1)
        )

    inputs = jnp.concatenate([teacher_in, hidden_in])
    inputs_other = swap(inputs)
    owned = jnp.concatenate(
        [
            bias_vectors[2:], norm_gains, dim_gates[None], jnp.zeros((1, width), wide),
            teacher_biases[2:].astype(wide), teacher_gains.astype(wide), jnp.zeros((2, width), wide),
        ]
    )
    spread = widen(owned, swap(owned))
    gates = spread[6:7]
    ones = jnp.ones_like(gates)

    def vector_rows(rows, scale_one, scale_two):
        return jnp.concatenate(
            [scale_one, rows[0:1], rows[4:5], rows[2:3], scale_two, rows[1:2], rows[5:6], rows[3:4]]
        )

    vectors = vector_rows(spread[:8], layer_gates[0] * gates, layer_gates[1] * gates)
    teacher_vectors = vector_rows(spread[8:], ones, ones)
    marks = lax.broadcasted_iota(jnp.int32, (1, MARKS), 1)
    segment, padding = segment_ids[0][:, None], pad_mask[0][:, None]
    query_mark = (segment == marks).astype(low)
    key_mark = jnp.where(((segment == marks) & (padding > 0)) | (marks >= 8), 0.0, masked_score).astype(low)
    valid = jnp.broadcast_to(padding.astype(wide), (length, 128))
    head_rows = jnp.repeat(head_gates, HEAD)[None]
    pad_rows = jnp.zeros((5, width), wide)
    head_vectors = jnp.concatenate([bias_vectors[:2], head_rows, pad_rows])
    teacher_head_vectors = jnp.concatenate(
        [teacher_biases[:2].astype(wide), jnp.ones((1, width), wide), pad_rows]
    )
    units = jnp.concatenate([up_bias[None], unit_gates[None], jnp.zeros((6, up_bias.shape[0]), wide)])
    teacher_units = jnp.concatenate(
        [teacher_up_bias[None].astype(wide), jnp.ones((7, up_bias.shape[0]), wide)]
    )
    out_low, up_low, down_low = out_weight.astype(low), up_weight.astype(low), down_weight.astype(low)

    teacher_x, teacher_part = attend_call(
        False, teacher_in[0], inputs_other[0], teacher_qkv, teacher_out, teacher_head_vectors, query_mark, key_mark
    )
    teacher_part_other = swap(teacher_part)
    x_all, part, queries, keys_in, values, context, logs = attend_call(
        True, hidden_in[0], inputs_other[1], qkv_weight, out_low, head_vectors, query_mark, key_mark
    )
    part_other = swap(part)
    teacher_first, teacher_reduced = feed_call(
        False, teacher_x, teacher_part, teacher_part_other, teacher_vectors, teacher_units, teacher_up, teacher_down
    )
    teacher_reduced_other = swap(teacher_reduced)
    first, reduced, first_low, activated, slope = feed_call(
        True, x_all, part, part_other, vectors, units, up_low, down_low
    )
    reduced_other = swap(reduced)
    block_out, base, grad_reduced, grad_expanded, back, sums_two, unit_sums = feed_back_call(
        first, reduced, reduced_other, teacher_first, teacher_reduced, teacher_reduced_other, valid,
        vectors, teacher_vectors, slope, up_low, down_low,
    )
    back_other = swap(back)
    grad_down = nn_dot(activated.T, grad_reduced)
    grad_up = nn_dot(first_low.T, grad_expanded)
    gate_rows = jnp.concatenate([head_rows, 1.0 / head_rows, jnp.zeros((6, width), wide)])
    grad_resid, grad_attended, grad_heads, inner, sums_one = heads_back_call(
        base, back, back_other, x_all, part, part_other, context, vectors, gate_rows, out_low
    )
    grad_out = nn_dot(context.T, grad_attended)
    grad_proj, proj_sums = attend_back_call(
        queries, keys_in, values, grad_heads, query_mark, key_mark, logs, inner
    )
    grad_qkv = [nn_dot(x_all.T, grad_proj[j]) for j in range(3)]
    qkv_low = qkv_weight.astype(low)
    input_part = sum(nt_dot(grad_proj[j], qkv_low[j]) for j in range(3))
    input_own = jnp.where(core == 0, input_part[:, :width], input_part[:, width:])
    input_sent = jnp.where(core == 0, input_part[:, width:], input_part[:, :width])
    input_sum = input_own + swap(input_sent.astype(low)).astype(wide)

    def own_half(rows):
        return jnp.where(core == 0, rows[:, :width], rows[:, width:])

    sums_one, sums_two = own_half(sums_one), own_half(sums_two)
    grad_biases = jnp.concatenate(
        [proj_sums[:2], sums_one[2:3], sums_two[2:3], sums_one[1:2], sums_two[1:2]]
    )
    grad_up_bias = unit_sums[0]
    grad_gains = jnp.concatenate([sums_one[:1], sums_two[:1]])
    count = jnp.sum(padding.astype(wide))
    parts = jnp.stack(
        [
            jnp.stack([grad_down[:, :384], grad_down[:, 384:]]),
            jnp.stack(
                [
                    jnp.concatenate([grad_up[:, :384], grad_up[:, 384:768]]),
                    jnp.concatenate([grad_up[:, 768:1152], grad_up[:, 1152:]]),
                ]
            ),
            jnp.stack(
                [
                    jnp.concatenate([grad_qkv[0], grad_qkv[1]]),
                    jnp.concatenate([grad_qkv[2], grad_out[:, :384], grad_out[:, 384:]]),
                ]
            ),
        ]
    ).astype(jnp.bfloat16)
    small = jnp.concatenate(
        [
            grad_biases.reshape(-1),
            grad_up_bias,
            grad_gains.reshape(-1),
            jnp.broadcast_to(count, (128,)),
            jnp.zeros((384,), jnp.float32),
        ]
    ).reshape(40, 128)
    rows_all = lax.axis_size("rows")
    sums, small_sums, square = reduce_rows(rows_all // INNER, parts, small)
    unit = 1.0 / (D * small_sums[36, 0])
    grad_norm = jnp.sqrt(square[0, 0]) * unit
    factor = unit * clip_norm / jnp.maximum(grad_norm, clip_norm)
    factors = jnp.broadcast_to(factor, (8, 128))
    one = pl.squeezed
    down_results = adam_call(
        rate_reduce, (4, 2), (one, one, 384, 384), lambda i, j: (0, j, i, 0), (384, 384), lambda i, j: (i, j),
        factors, sums, down_weight, down_moment1, down_moment2,
    )
    up_results = adam_call(
        rate_expand, (2, 4), (one, one, 384, 384), lambda i, j: (1, j // 2, (j % 2) * 2 + i, 0), (384, 384), lambda i, j: (i, j),
        factors, sums, up_weight, up_moment1, up_moment2,
    )
    qkv_results = adam_call(
        rate_attend, (3, 2), (one, one, 384, 384), lambda i, j: (2, i // 2, (i % 2) * 2 + j, 0), (one, 384, 384), lambda i, j: (i, j, 0),
        factors, sums, qkv_weight, qkv_moment1, qkv_moment2,
    )
    out_results = adam_call(
        rate_output, (2,), (one, one, 384, 384), lambda j: (2, 1, 2 + j, 0), (384, 384), lambda j: (0, j),
        factors, sums, out_weight, out_moment1, out_moment2,
    )
    flat_small = small_sums.reshape(-1) * factor
    small_grads = (
        flat_small[:2304].reshape(6, 384), flat_small[2304:3840], flat_small[3840:4608].reshape(2, 384)
    )
    small_states = (
        (bias_vectors, bias_moment1, bias_moment2),
        (up_bias, up_bias_moment1, up_bias_moment2),
        (norm_gains, gain_moment1, gain_moment2),
    )
    results = [qkv_results, out_results, up_results, down_results]
    for (weight, first, second), clipped in zip(small_states, small_grads):
        results.append((clipped,) + adam_step(weight, first, second, clipped, rate_vector, 0.0))
    input_grad = (input_sum.astype(low).astype(wide) + grad_resid) * unit
    block_out = block_out.reshape(hidden_in.shape)
    input_grad = input_grad.reshape(hidden_in.shape)
    return (
        block_out,
        input_grad,
        grad_norm,
        results[0][0],
        results[0][1],
        results[0][2],
        results[1][0],
        results[1][1],
        results[1][2],
        results[2][0],
        results[2][1],
        results[2][2],
        results[3][0],
        results[3][1],
        results[3][2],
        results[4][0],
        results[4][1],
        results[4][2],
        results[5][0],
        results[5][1],
        results[5][2],
        results[6][0],
        results[6][1],
        results[6][2],
        results[0][3],
        results[1][3],
        results[2][3],
        results[3][3],
    )


def solution(mesh):
    in_specs = (
        P("rows", None, "hid"),
        P("rows", None, "hid"),
        P("rows", None),
        P("rows", None),
        P(None, None, "hid"),
        P(None, None, "hid"),
        P(None, None, "hid"),
        P("hid", None),
        P("hid", None),
        P("hid", None),
        P(None, "hid"),
        P(None, "hid"),
        P(None, "hid"),
        P("hid", None),
        P("hid", None),
        P("hid", None),
        P(None, "hid"),
        P(None, "hid"),
        P(None, "hid"),
        P("hid"),
        P("hid"),
        P("hid"),
        P(None, "hid"),
        P(None, "hid"),
        P(None, "hid"),
        P("hid"),
        P(),
        P("hid"),
        P("hid"),
        P(None, None, "hid"),
        P("hid", None),
        P(None, "hid"),
        P("hid", None),
        P(None, "hid"),
        P("hid"),
        P(None, "hid"),
    )
    out_specs = (
        P("rows", None, "hid"),
        P("rows", None, "hid"),
        P(),
        P(None, None, "hid"),
        P(None, None, "hid"),
        P(None, None, "hid"),
        P("hid", None),
        P("hid", None),
        P("hid", None),
        P(None, "hid"),
        P(None, "hid"),
        P(None, "hid"),
        P("hid", None),
        P("hid", None),
        P("hid", None),
        P(None, "hid"),
        P(None, "hid"),
        P(None, "hid"),
        P("hid"),
        P("hid"),
        P("hid"),
        P(None, "hid"),
        P(None, "hid"),
        P(None, "hid"),
        P(None, None, "hid"),
        P("hid", None),
        P(None, "hid"),
        P("hid", None),
    )
    return jax.shard_map(
        on_device, mesh=mesh, in_specs=in_specs, out_specs=out_specs, check_vma=False
    )
```

```python
import functools

import jax
import jax.numpy as jnp
from jax import lax
from jax.experimental import pallas as pl
from jax.experimental.pallas import tpu as pltpu
from jax.sharding import PartitionSpec as P

D = 768
HEAD = 64
STEP = 10


epsilon_norm = 1e-06
masked_score = -1000000000.0
clip_norm = 0.001
beta_first = 0.9
beta_second = 0.999
adam_epsilon = 1e-08
weight_decay = 0.01
rate_attend = 0.03
rate_output = 0.2
rate_expand = 0.03
rate_reduce = 0.03
rate_vector = 0.3


def adam_step(weight, first, second, grad, rate, decay):
    first_new = beta_first * first + (1.0 - beta_first) * grad
    second_new = beta_second * second + (1.0 - beta_second) * grad * grad
    first_hat = first_new / (1.0 - beta_first**STEP)
    second_hat = second_new / (1.0 - beta_second**STEP)
    return (
        weight - rate * (first_hat / (jnp.sqrt(second_hat) + adam_epsilon) + decay * weight),
        second_new,
    )


MARKS = 128
TILE = 256


def nt_dot(left, right):
    return lax.dot_general(
        left, right, (((1,), (1,)), ((), ())), preferred_element_type=jnp.float32
    )


def nn_dot(left, right):
    return jnp.dot(left, right, preferred_element_type=jnp.float32)


def attend_kernel(keep, casts, own_ref, other_ref, weight_ref, out_weight_ref, vector_ref, query_mark_ref, key_mark_ref, *refs):
    low = jnp.bfloat16
    core = lax.axis_index("hid")
    length, width = own_ref.shape
    wide_in, refs = refs[:casts], refs[casts:]
    part_ref, x_out, refs = refs[0], refs[1], refs[2:]
    if keep:
        turned_out, query_out, key_out, value_out, context_out, context_turned_out, log_ref = refs[:7]
        refs = refs[7:]
    low_out, refs = refs[:casts], refs[casts:]
    x_ref, query_ref, key_ref, value_ref, context_ref, sems = refs[:6]
    refs = refs[6:]
    if keep:
        turned_ref, context_turned_ref = refs[:2]
        refs = refs[2:]
    wide_held, low_held = refs[:casts], refs[casts : 2 * casts]
    copies = []

    def copy(source, target):
        moved = pltpu.make_async_copy(source, target, sems.at[len(copies)])
        moved.start()
        copies.append(moved)
        return moved

    arriving = [copy(source, target) for source, target in zip(wide_in, wide_held)]
    leaving = []
    x_ref[:, pl.ds(pl.multiple_of(core * width, 128), width)] = own_ref[...]
    x_ref[:, pl.ds(pl.multiple_of((1 - core) * width, 128), width)] = other_ref[...]
    leaving.append(copy(x_ref, x_out))
    x_all = x_ref[...]
    query_ref[...] = (nn_dot(x_all, weight_ref[0]) + vector_ref[0:1]).astype(low)
    key_ref[...] = nn_dot(x_all, weight_ref[1]).astype(low)
    value_ref[...] = (nn_dot(x_all, weight_ref[2]) + vector_ref[1:2]).astype(low)
    if keep:
        turned_ref[...] = x_all.T
        for source, target in ((query_ref, query_out), (key_ref, key_out), (value_ref, value_out), (turned_ref, turned_out)):
            leaving.append(copy(source, target))
    pair = 2 * HEAD
    block_rows = length // 2
    first_head = lax.broadcasted_iota(jnp.int32, (1, pair), 1) < HEAD
    pairs = width // pair
    for number in range(pairs):
        lanes = slice(number * pair, (number + 1) * pair)
        scaled = query_ref[:, lanes] * jnp.asarray(HEAD ** (-0.5), low)
        key_wide = jnp.concatenate([key_ref[:, lanes], key_mark_ref[...]], axis=1)
        values = value_ref[:, lanes]
        logs = []
        for start in range(0, length, block_rows):
            block = slice(start, start + block_rows)
            outs = []
            columns = []
            for head in range(2):
                chosen = jnp.where(first_head if head == 0 else ~first_head, scaled[block], jnp.zeros_like(scaled[block]))
                query_wide = jnp.concatenate([chosen, query_mark_ref[block]], axis=1)
                scores = nt_dot(query_wide, key_wide)
                top = jnp.max(scores, axis=1, keepdims=True)
                weights_here = jnp.exp(scores - top)
                sums = jnp.sum(weights_here, axis=1, keepdims=True)
                outs.append(nn_dot(weights_here.astype(low), values) * (1.0 / sums))
                columns.append(top + jnp.log(sums))
            context = (jnp.where(first_head, outs[0], outs[1]) * vector_ref[2:3, lanes]).astype(low)
            context_ref[block, lanes] = context
            if keep:
                context_turned_ref[lanes, block] = context.T
                logs.append(jnp.where(first_head, columns[0], columns[1]))
        if keep:
            turned = jnp.concatenate(logs, axis=0).T
            log_ref[8 * number : 8 * number + 8] = jnp.concatenate(
                [turned[0:1], turned[HEAD : HEAD + 1], turned[0:6]], axis=0
            )
        for index in range(casts):
            if index % pairs == number:
                arriving[index].wait()
                low_held[index][...] = wide_held[index][...].astype(low)
                leaving.append(copy(low_held[index], low_out[index]))
    if keep:
        leaving.append(copy(context_ref, context_out))
        leaving.append(copy(context_turned_ref, context_turned_out))
    part_ref[...] = nn_dot(context_ref[...], out_weight_ref[...]).astype(low)
    for moved in leaving:
        moved.wait()


def attend_call(keep, own, other, weight, out_weight, vectors, query_mark, key_mark, wide_weights=()):
    length, width = own.shape
    full = 2 * width
    low = jnp.bfloat16
    vmem, anywhere = pl.BlockSpec(memory_space=pltpu.VMEM), pl.BlockSpec(memory_space=pl.ANY)
    narrow = jax.ShapeDtypeStruct((length, width), low)
    out_shape = [jax.ShapeDtypeStruct((length, full), low)] * 2
    out_specs = [vmem, anywhere]
    scratch = [pltpu.VMEM((length, full), low)] + [pltpu.VMEM((length, width), low)] * 4 + [pltpu.SemaphoreType.DMA((16,))]
    if keep:
        out_shape += [jax.ShapeDtypeStruct((full, length), low), narrow, narrow, narrow, narrow]
        out_shape += [jax.ShapeDtypeStruct((width, length), low), jax.ShapeDtypeStruct((8 * (width // (2 * HEAD)), length), jnp.float32)]
        out_specs += [anywhere] * 6 + [vmem]
        scratch += [pltpu.VMEM((full, length), low), pltpu.VMEM((width, length), low)]
    out_shape += [jax.ShapeDtypeStruct(w.shape, low) for w in wide_weights]
    out_specs += [anywhere] * len(wide_weights)
    scratch += [pltpu.VMEM(w.shape, jnp.float32) for w in wide_weights] + [pltpu.VMEM(w.shape, low) for w in wide_weights]
    return pl.pallas_call(
        functools.partial(attend_kernel, keep, len(wide_weights)),
        out_shape=out_shape,
        in_specs=[vmem] * 7 + [anywhere] * len(wide_weights),
        out_specs=out_specs,
        scratch_shapes=scratch,
        compiler_params=pltpu.CompilerParams(vmem_limit_bytes=56 * 2**20),
        cost_estimate=pl.CostEstimate(flops=6 * 10**9, bytes_accessed=2 * 10**7, transcendentals=7 * 10**6),
        name="attend",
    )(own, other, weight, out_weight, vectors, query_mark, key_mark, *wide_weights)


def norm_parts(resid):
    center = jnp.mean(resid, axis=1, keepdims=True)
    second = jnp.mean(resid * resid, axis=1, keepdims=True)
    inverse = lax.rsqrt(second - center * center + epsilon_norm)
    return (resid - center) * inverse, inverse


def norm_grad(grad_normed, normed, inverse):
    center = jnp.mean(grad_normed, axis=1, keepdims=True)
    crossed = jnp.mean(grad_normed * normed, axis=1, keepdims=True)
    return inverse * (grad_normed - center - normed * crossed)


def sum_parts(part_ref, other_ref):
    return part_ref[...].astype(jnp.float32) + other_ref[...].astype(jnp.float32)


def feed_kernel(keep, x_ref, part_ref, other_ref, vector_ref, unit_ref, up_ref, down_ref, first_ref, reduced_ref, *refs):
    low = jnp.bfloat16
    resid = x_ref[...].astype(jnp.float32) + (sum_parts(part_ref, other_ref) + vector_ref[1:2]) * vector_ref[0:1]
    normed, inverse = norm_parts(resid)
    first_out = normed * vector_ref[2:3] + vector_ref[3:4]
    first_ref[...] = first_out
    first_low = first_out.astype(low)
    expanded = nn_dot(first_low, up_ref[...]) + unit_ref[0:1]
    share = 0.5 + 0.5 * lax.erf(expanded * (0.5**0.5))
    activated = (expanded * share * unit_ref[1:2]).astype(low)
    reduced_ref[...] = nn_dot(activated, down_ref[...]).astype(low)
    if keep:
        turned_ref, activated_turned_ref, slope_ref = refs
        turned_ref[...] = first_low.T
        activated_turned_ref[...] = activated.T
        bell = jnp.exp(-0.5 * expanded * expanded)
        slope_ref[...] = ((share + expanded * bell * 0.3989422804014327) * unit_ref[1:2]).astype(low)


def row_spec(width):
    return pl.BlockSpec((TILE, width), lambda i: (i, 0))


def whole_spec(array):
    return pl.BlockSpec(array.shape, lambda i: (0,) * array.ndim)


def feed_call(keep, x_all, part, other, vectors, units, up_low, down_low):
    length, full = x_all.shape
    hidden = up_low.shape[1]
    low = jnp.bfloat16
    out_shape = [jax.ShapeDtypeStruct((length, full), jnp.float32), jax.ShapeDtypeStruct((length, full), low)]
    out_specs = [row_spec(full)] * 2
    if keep:
        out_shape += [jax.ShapeDtypeStruct(shape, low) for shape in ((full, length), (hidden, length), (length, hidden))]
        out_specs += [pl.BlockSpec((rows, TILE), lambda i: (0, i)) for rows in (full, hidden)] + [row_spec(hidden)]
    return pl.pallas_call(
        functools.partial(feed_kernel, keep),
        grid=(length // TILE,),
        out_shape=out_shape,
        in_specs=[row_spec(full)] * 3 + [whole_spec(a) for a in (vectors, units, up_low, down_low)],
        out_specs=out_specs,
        compiler_params=pltpu.CompilerParams(vmem_limit_bytes=48 * 2**20),
        cost_estimate=pl.CostEstimate(flops=10 * 10**9, bytes_accessed=2 * 10**7, transcendentals=3 * 10**6),
        name="feed",
    )(x_all, part, other, vectors, units, up_low, down_low)


def add_sums(ref, step, rows):
    stacked = jnp.concatenate(rows + [jnp.zeros_like(rows[0])] * (8 - len(rows)), axis=0)

    @pl.when(step == 0)
    def _():
        ref[...] = stacked

    @pl.when(step > 0)
    def _():
        ref[...] += stacked


def column_sum(value):
    return jnp.sum(value, axis=0, keepdims=True)


def feed_back_kernel(
    first_ref, part_ref, other_ref, teacher_first_ref, teacher_part_ref, teacher_other_ref, valid_ref,
    vector_ref, teacher_vector_ref, slope_ref, up_ref, down_ref,
    block_ref, base_ref, grad_reduced_ref, grad_expanded_ref, part_back_ref, sums_ref, unit_sums_ref,
):
    low = jnp.bfloat16
    core = lax.axis_index("hid")
    step = pl.program_id(0)
    full = first_ref.shape[1]
    first_out = first_ref[...]
    teacher_first = teacher_first_ref[...]
    resid = first_out + (sum_parts(part_ref, other_ref) + vector_ref[5:6]) * vector_ref[4:5]
    normed, inverse = norm_parts(resid)
    second_out = normed * vector_ref[6:7] + vector_ref[7:8]
    teacher_resid = teacher_first + sum_parts(teacher_part_ref, teacher_other_ref) + teacher_vector_ref[5:6]
    teacher_normed, _ = norm_parts(teacher_resid)
    teacher_second = teacher_normed * teacher_vector_ref[6:7] + teacher_vector_ref[7:8]
    half = full // 2
    block_ref[...] = jnp.where(core == 0, second_out[:, :half], second_out[:, half:]).astype(low)
    twice = valid_ref[:, :1] * 2.0
    grad_second = twice * (second_out - teacher_second)
    grad_resid = norm_grad(grad_second * vector_ref[6:7], normed, inverse)
    grad_reduced = grad_resid * vector_ref[4:5]
    add_sums(sums_ref, step, [column_sum(grad_second * normed), column_sum(grad_second), column_sum(grad_reduced)])
    grad_reduced_low = grad_reduced.astype(low)
    grad_reduced_ref[...] = grad_reduced_low
    grad_activated = nt_dot(grad_reduced_low, down_ref[...]).astype(low).astype(jnp.float32)
    grad_expanded = (grad_activated * slope_ref[...].astype(jnp.float32)).astype(low)
    grad_expanded_ref[...] = grad_expanded
    add_sums(unit_sums_ref, step, [column_sum(grad_expanded.astype(jnp.float32))])
    part_back_ref[...] = nt_dot(grad_expanded, up_ref[...]).astype(low)
    base_ref[...] = twice * (first_out - teacher_first) + grad_resid


def feed_back_call(first, part, other, teacher_first, teacher_part, teacher_other, valid, vectors, teacher_vectors, slope, up_low, down_low):
    length, full = first.shape
    hidden = slope.shape[1]
    low, wide = jnp.bfloat16, jnp.float32
    shapes = [((length, full // 2), low), ((length, full), wide), ((length, full), low), ((length, hidden), low), ((length, full), low)]
    return pl.pallas_call(
        feed_back_kernel,
        grid=(length // TILE,),
        out_shape=[jax.ShapeDtypeStruct(*shape) for shape in shapes]
        + [jax.ShapeDtypeStruct((8, full), wide), jax.ShapeDtypeStruct((8, hidden), wide)],
        in_specs=[row_spec(full)] * 6
        + [row_spec(128), whole_spec(vectors), whole_spec(teacher_vectors), row_spec(hidden), whole_spec(up_low), whole_spec(down_low)],
        out_specs=[row_spec(shape[0][1]) for shape in shapes]
        + [pl.BlockSpec((8, full), lambda i: (0, 0)), pl.BlockSpec((8, hidden), lambda i: (0, 0))],
        compiler_params=pltpu.CompilerParams(vmem_limit_bytes=48 * 2**20),
        cost_estimate=pl.CostEstimate(flops=10 * 10**9, bytes_accessed=4 * 10**7, transcendentals=10**4),
        name="feed_back",
    )(first, part, other, teacher_first, teacher_part, teacher_other, valid, vectors, teacher_vectors, slope, up_low, down_low)


INNER = 16
SMALL_ROWS = 40
COUNT_ROW = 36


class Piece:
    def __init__(self, source, target, first_row, rows, first_column, columns, order, own, halvings):
        self.source, self.target = source, target
        self.first_row, self.rows = first_row, rows
        self.first_column, self.columns = first_column, columns
        self.order, self.own, self.halvings = order, own, halvings


def piece_buffers(rows, columns, halvings):
    low, wide = jnp.bfloat16, jnp.float32
    last = rows // 16 if halvings == 4 else rows // 8
    return [
        pltpu.VMEM((rows // 2, columns), low),
        pltpu.VMEM((rows // 4, columns), low),
        pltpu.VMEM((rows // 8, columns), low),
        pltpu.VMEM((last, columns), low),
        pltpu.VMEM((rows // 4, columns), low),
        pltpu.VMEM((rows // 8, columns), low),
        pltpu.VMEM((last, columns), low),
        pltpu.VMEM((rows // 4, columns), wide),
        pltpu.VMEM((last, columns), low),
    ]


def aligned(start, size):
    return pl.ds(pl.multiple_of(start, 16), size)


def backward_kernel(outer, shapes, *refs):
    low, wide = jnp.bfloat16, jnp.float32
    names = (
        "down", "up", "back", "base", "x", "x_t", "part", "other", "context", "context_t", "query", "key", "value",
        "query_mark", "key_mark", "out_weight", "qkv_weight", "vector", "gate", "log", "sums_two", "unit_sums", "count",
        "down_sum", "up_sum", "qkv_sum", "out_sum", "bias_out", "unit_out", "scalars", "input_grad",
    )
    ref = dict(zip(names, refs))
    refs = refs[len(names) :]
    loaded = names[3:17]
    local = dict(zip(loaded, refs))
    refs = refs[len(loaded) :]
    (
        back_other, back_own, own_down, own_up, attended_grad, heads_grad, inner_rows, sums_one, raw_scratch, turned_keys,
        turned_grad, pair_keys, pair_values, proj, qkv_parts, out_parts, input_send, input_recv, small, small_recv,
        small_outer, squares, square_recv, resid_grad, shard_outer, send_sems, recv_sems, load_sems, shard_sems,
    ) = refs[:29]
    buffers = refs[29:]

    place = lax.axis_index("rows")
    inside = place % INNER
    group = place // INNER
    core = lax.axis_index("hid")
    bits = {"x": inside % 2, "y": (inside // 2) % 2, "v": (inside // 4) % 2, "w": inside // 8}
    steps = {"x": 1, "y": 2, "v": 4, "w": 8}
    peer = {name: {"rows": place + steps[name] - 2 * steps[name] * bits[name]} for name in bits}
    to_group = [{"rows": inside + INNER * ((group + d) % outer)} for d in range(outer)]
    to_core = {"hid": 1 - core}
    barrier = pltpu.get_barrier_semaphore()
    peers = list(peer.values()) + to_group[1:] + [to_core]
    for other in peers:
        pl.semaphore_signal(barrier, inc=1, device_id=other, device_id_type=pl.DeviceIdType.MESH)
    pl.semaphore_wait(barrier, len(peers))

    counter = [0]
    pending = []

    def send(source, target, device):
        index = counter[0]
        counter[0] += 1
        copy = pltpu.make_async_remote_copy(
            src_ref=source, dst_ref=target, send_sem=send_sems.at[index],
            recv_sem=recv_sems.at[index], device_id=device, device_id_type=pl.DeviceIdType.MESH,
        )
        copy.start()
        pending.append(copy)
        return copy

    loads = {}

    def load(name, source, target):
        copy = pltpu.make_async_copy(source, target, load_sems.at[len(loads)])
        copy.start()
        loads[name] = copy

    down, up = ref["down"], ref["up"]
    orders = ("xyvw", "yxvw", "vxyw")
    orders_two = ("xyvw", "yxvw", "vyxw")
    batches = {"down": [], "up": [], "qkv": [], "out": []}
    taken = [0]

    def add_piece(batch, *fields):
        piece = Piece(*fields)
        piece.buffers = buffers[taken[0] : taken[0] + 9]
        taken[0] += 9
        piece.index = sum(len(v) for v in batches.values())
        piece.step = 0
        batches[batch].append(piece)

    for lane in range(3):
        rows = shapes["down"][0] // 3
        add_piece("down", down, ref["down_sum"], rows * lane, rows, 0, shapes["down"][1], orders[lane], own_down.at[lane], 4)
        rows = shapes["up"][0] // 3
        add_piece("up", up, ref["up_sum"], rows * lane, rows, 0, shapes["up"][1], orders_two[lane], own_up.at[lane], 4)
        rows = shapes["qkv"][0] // 3
        add_piece("qkv", qkv_parts, ref["qkv_sum"], rows * lane, rows, 0, shapes["qkv"][1], orders[lane], None, 4)
        columns = shapes["out"][1] // 3
        add_piece("out", out_parts, ref["out_sum"], 0, shapes["out"][0], columns * lane, columns, orders_two[lane], None, 3)

    for pieces in batches.values():
        for piece in pieces:
            piece.offsets = [0]
            size = piece.rows
            for name in piece.order[: piece.halvings]:
                size = size // 2
                piece.offsets.append(piece.offsets[-1] + size * bits[name])

    def first_half(piece):
        return piece.offsets[1]

    square_terms = []

    def advance(batch):
        for piece in batches[batch]:
            advance_piece(piece)

    def advance_piece(piece):
        r1, r2, r3, r4, s2, s3, s4, keep, shard = piece.buffers
        step = piece.step
        piece.step += 1
        order, rows = piece.order, piece.rows
        columns = pl.ds(piece.first_column, piece.columns)
        names_done = order[: piece.halvings]

        def own(start, size):
            if piece.own is not None:
                return piece.own[aligned(start, size), :].astype(wide)
            return piece.source[aligned(piece.first_row + piece.offsets[1] + start, size), columns].astype(wide)

        if step == 0:
            start = piece.first_row + rows // 2 * (1 - bits[order[0]])
            piece.flight = send(piece.source.at[aligned(start, rows // 2), columns], r1, peer[order[0]])
        elif step == 1:
            piece.flight.wait_recv()
            bit = bits[order[1]]
            size = rows // 4
            sent = size * (1 - bit)
            s2[...] = (own(sent, size) + r1[aligned(sent, size), :].astype(wide)).astype(low)
            piece.flight = send(s2, r2, peer[order[1]])
            kept = size * bit
            keep[...] = own(kept, size) + r1[aligned(kept, size), :].astype(wide)
        elif step == 2:
            piece.flight.wait_recv()
            keep[...] = keep[...] + r2[...].astype(wide)
            bit = bits[order[2]]
            size = rows // 8
            s3[...] = keep[aligned(size * (1 - bit), size), :].astype(low)
            piece.flight = send(s3, r3, peer[order[2]])
        elif step == 3:
            piece.flight.wait_recv()
            size = rows // 8
            mine = aligned(size * bits[order[2]], size)
            total = keep[mine, :] + r3[...].astype(wide)
            if piece.halvings == 4:
                keep[mine, :] = total
                small_size = size // 2
                sent = size * bits[order[2]] + small_size * (1 - bits[order[3]])
                s4[...] = keep[aligned(sent, small_size), :].astype(low)
            else:
                s4[...] = total.astype(low)
            piece.flight = send(s4, r4, peer[order[3]])
        elif step == 4:
            piece.flight.wait_recv()
            if piece.halvings == 4:
                size = rows // 16
                kept = rows // 8 * bits[order[2]] + size * bits[order[3]]
                total = keep[aligned(kept, size), :] + r4[...].astype(wide)
                weight = 1.0
            else:
                total = s4[...].astype(wide) + r4[...].astype(wide)
                weight = 0.5
            if outer > 1:
                shard[...] = total.astype(low)
                shard_outer[piece.index][0] = shard[...]
                copies = [send(shard, shard_outer[piece.index].at[d], to_group[d]) for d in range(1, outer)]
                for copy in copies:
                    copy.wait()
                    pending[:] = [entry for entry in pending if entry is not copy]
                total = jnp.zeros_like(total)
                for index in range(outer):
                    total = total + shard_outer[piece.index][(group - index + outer) % outer].astype(wide)
            shard[...] = total.astype(low)
            square_terms.append(weight * jnp.sum(jnp.sum(total * total, axis=0, keepdims=True), axis=1, keepdims=True))
            size = rows // 2**piece.halvings
            here = piece.target.at[aligned(piece.first_row + piece.offsets[-1], size), columns]
            piece.local = pltpu.make_async_copy(shard, here, shard_sems.at[piece.index])
            piece.local.start()
            piece.flight = send(shard, here, peer[names_done[-1]])
        elif step < 4 + piece.halvings:
            level = piece.halvings - (step - 4)
            piece.flight.wait_recv()
            if step == 5:
                piece.local.wait()
            size = rows // 2**level
            block = piece.target.at[aligned(piece.first_row + piece.offsets[level], size), columns]
            piece.flight = send(block, block, peer[names_done[level - 1]])
        elif step == 4 + piece.halvings:
            piece.flight.wait_recv()

    advance("down")
    back_flight = send(ref["back"], back_other, to_core)
    advance("up")
    for name in ("base", "x", "part", "other"):
        load(name, ref[name], local[name])
    load("back", ref["back"], back_own)
    for name in ("context", "out_weight"):
        load(name, ref[name], local[name])
    for lane in range(3):
        piece = batches["down"][lane]
        load(f"down{lane}", down.at[aligned(piece.first_row + piece.offsets[1], piece.rows // 2), :], own_down.at[lane])
        piece = batches["up"][lane]
        load(f"up{lane}", up.at[aligned(piece.first_row + piece.offsets[1], piece.rows // 2), :], own_up.at[lane])
    for name in ("context_t", "query", "key", "value", "query_mark", "key_mark", "x_t", "qkv_weight"):
        load(name, ref[name], local[name])

    vector_ref, gate_ref = ref["vector"], ref["gate"]
    length, full = local["x"].shape
    half = full // 2
    back_flight.wait_recv()
    for name in ("base", "x", "part", "other", "back", "context", "out_weight"):
        loads[name].wait()
    sums_one[...] = jnp.zeros_like(sums_one)

    @pl.loop(0, length // TILE)
    def _(index):
        block = aligned(index * TILE, TILE)
        returned = (back_own[block, :].astype(wide) + back_other[block, :].astype(wide)).astype(low).astype(wide)
        grad_first = local["base"][block, :] + returned
        branch = local["part"][block, :].astype(wide) + local["other"][block, :].astype(wide)
        resid = local["x"][block, :].astype(wide) + (branch + vector_ref[1:2]) * vector_ref[0:1]
        normed, inverse = norm_parts(resid)
        grad_resid = norm_grad(grad_first * vector_ref[2:3], normed, inverse)
        resid_grad[block, :] = jnp.where(core == 0, grad_resid[:, :half], grad_resid[:, half:])
        grad_attended = grad_resid * vector_ref[0:1]
        sums_one[0:1] += column_sum(grad_first * normed)
        sums_one[1:2] += column_sum(grad_first)
        sums_one[2:3] += column_sum(grad_attended)
        grad_attended_low = grad_attended.astype(low)
        attended_grad[block, :] = grad_attended_low
        grad_heads = (nt_dot(grad_attended_low, local["out_weight"][...]) * gate_ref[0:1]).astype(low)
        heads_grad[block, :] = grad_heads
        product = grad_heads.astype(wide) * local["context"][block, :].astype(wide) * gate_ref[1:2]
        lane = lax.broadcasted_iota(jnp.int32, (1, 128), 1)
        columns = jnp.zeros((TILE, 128), wide)
        for pair in range(half // 128):
            part = product[:, 128 * pair : 128 * pair + 128]
            low_sum = jnp.sum(jnp.where(lane < HEAD, part, 0.0), axis=1, keepdims=True)
            high_sum = jnp.sum(jnp.where(lane < HEAD, 0.0, part), axis=1, keepdims=True)
            columns = jnp.where(lane == 2 * pair, low_sum, jnp.where(lane == 2 * pair + 1, high_sum, columns))
        inner_rows[:, pl.ds(pl.multiple_of(index * TILE, 128), TILE)] = columns.T[0:8]

    loads["context_t"].wait()
    out_parts[...] = nn_dot(local["context_t"][...], attended_grad[...]).astype(low)
    advance("out")
    for lane in range(3):
        loads[f"down{lane}"].wait()
        loads[f"up{lane}"].wait()
    advance("down")
    for name in ("query", "key", "value", "query_mark", "key_mark"):
        loads[name].wait()

    pair_width = 2 * HEAD
    scale = HEAD ** (-0.5)
    pair_rows = []

    def attend_pair(number):
        lanes = slice(number * pair_width, (number + 1) * pair_width)
        turned_keys[...] = local["key"][:, lanes].T

        @pl.loop(0, 2)
        def _(head):
            mask = lax.broadcasted_iota(jnp.int32, (1, pair_width), 1) // HEAD == head
            queries, grads = local["query"][:, lanes], heads_grad[:, lanes]
            query_wide = jnp.concatenate([queries, local["query_mark"][...]], axis=1)
            logs = ref["log"][pl.ds(8 * number + head, 1), :]
            inner = inner_rows[pl.ds(2 * number + head, 1), :]
            for start in range(0, length, TILE):
                block = slice(start, start + TILE)
                zero = jnp.zeros((TILE, pair_width), low)
                chosen = jnp.where(mask, local["key"][block, lanes] * jnp.asarray(scale, low), zero)
                key_wide = jnp.concatenate([chosen, local["key_mark"][block, :]], axis=1)
                probs = jnp.exp(nt_dot(key_wide, query_wide) - logs)
                grad_probs = nt_dot(jnp.where(mask, local["value"][block, lanes], zero), grads)
                grad_raw = (probs * (grad_probs - inner)).astype(low)
                raw_scratch[block, :] = grad_raw
                pair_keys[block, :] = jnp.where(mask, nn_dot(grad_raw, queries), pair_keys[block, :])
                pair_values[block, :] = jnp.where(mask, nn_dot(probs.astype(low), grads), pair_values[block, :])
            rows = pl.ds(pl.multiple_of(HEAD * head, HEAD), HEAD)
            turned_grad[rows, :] = nn_dot(turned_keys[rows, :], raw_scratch[...])

        query_out = (turned_grad[...].T * scale).astype(low)
        value_out = pair_values[...].astype(low)
        proj[0, :, lanes] = query_out
        proj[1, :, lanes] = (pair_keys[...] * scale).astype(low)
        proj[2, :, lanes] = value_out
        pair_rows.append((column_sum(query_out.astype(wide)), column_sum(value_out.astype(wide))))

    pair_keys[...] = jnp.zeros_like(pair_keys)
    pair_values[...] = jnp.zeros_like(pair_values)
    attend_pair(0)
    advance("up")
    advance("down")
    attend_pair(1)
    advance("out")
    advance("up")
    advance("down")
    attend_pair(2)
    advance("out")
    advance("up")
    advance("down")
    loads["x_t"].wait()
    for j in range(3):
        rows = slice(j * full, (j + 1) * full)
        qkv_parts[rows, :] = nn_dot(local["x_t"][...], proj[j]).astype(low)
    advance("qkv")
    advance("out")
    advance("up")

    small[...] = jnp.zeros_like(small)
    row = [0]

    def put(vector):
        for start in range(0, vector.shape[1], 128):
            small[row[0] : row[0] + 1, :] = vector[:, start : start + 128]
            row[0] += 1

    def own_half(vector):
        return jnp.where(core == 0, vector[:, :half], vector[:, half:])

    sums_two = ref["sums_two"]
    for which in range(2):
        for rows in pair_rows:
            put(rows[which])
    put(own_half(sums_one[2:3]))
    put(own_half(sums_two[2:3]))
    put(own_half(sums_one[1:2]))
    put(own_half(sums_two[1:2]))
    put(ref["unit_sums"][0:1])
    put(own_half(sums_one[0:1]))
    put(own_half(sums_two[0:1]))
    put(ref["count"][0:1])
    small_flight = send(small, small_recv.at[0], peer["x"])

    loads["qkv_weight"].wait()
    weights = local["qkv_weight"]
    away = aligned(half * (1 - core), half)
    here = aligned(half * core, half)
    leaving = nt_dot(proj[0], weights[0, away, :]) + nt_dot(proj[1], weights[1, away, :]) + nt_dot(proj[2], weights[2, away, :])
    input_send[...] = leaving.astype(low)
    input_flight = send(input_send, input_recv, to_core)
    staying = nt_dot(proj[0], weights[0, here, :]) + nt_dot(proj[1], weights[1, here, :]) + nt_dot(proj[2], weights[2, here, :])
    ref["input_grad"][...] = staying

    small_flight = [small_flight]

    def next_small(index, name):
        small_flight[0].wait_recv()
        slot = small if index == 1 else small_outer.at[index - 2]
        small_outer[index - 1] = slot[...] + small_recv[index - 1]
        small_flight[0] = send(small_outer.at[index - 1], small_recv.at[index], peer[name])

    advance("qkv")
    next_small(1, "y")
    advance("down")
    advance("out")
    advance("up")
    advance("qkv")
    next_small(2, "v")
    advance("down")
    advance("up")
    advance("out")
    advance("qkv")
    next_small(3, "w")
    advance("down")
    input_flight.wait_recv()
    summed = ref["input_grad"][...] + input_recv[...].astype(wide)
    ref["input_grad"][...] = summed.astype(low).astype(wide) + resid_grad[...]
    advance("up")
    advance("qkv")
    small_flight[0].wait_recv()
    small_total = small_outer[2] + small_recv[3]
    if outer > 1:
        small_outer[3] = small_total
        small_outer[4 + group] = small_total
        copies = [send(small_outer.at[3], small_outer.at[4 + group], to_group[d]) for d in range(1, outer)]
        for copy in copies:
            copy.wait_recv()
        small_total = small_outer[4]
        for index in range(1, outer):
            small_total = small_total + small_outer[4 + index]
    unit = 1.0 / (D * small_total[COUNT_ROW : COUNT_ROW + 1, 0:1])
    ref["input_grad"][...] = ref["input_grad"][...] * unit
    ref["bias_out"][...] = jnp.zeros_like(ref["bias_out"])
    for index in range(24):
        row, lane = index // 3, index % 3
        source = 3 * row + lane if row < 6 else 12 + 3 * row + lane
        ref["bias_out"][row : row + 1, 128 * lane : 128 * lane + 128] = small_total[source : source + 1]
    for index in range(12):
        ref["unit_out"][:, 128 * index : 128 * index + 128] = jnp.broadcast_to(small_total[18 + index : 19 + index], (8, 128))
    total_square = square_terms[0]
    for value in square_terms[1:]:
        total_square = total_square + value
    squares[0] = jnp.broadcast_to(total_square, (8, 128))
    square_flight = send(squares.at[0], square_recv.at[0], peer["x"])
    advance("out")
    advance("down")
    square_flight.wait_recv()
    squares[1] = squares[0] + square_recv[0]
    square_flight = send(squares.at[1], square_recv.at[1], peer["y"])
    advance("qkv")
    advance("up")
    square_flight.wait_recv()
    squares[2] = squares[1] + square_recv[1]
    square_flight = send(squares.at[2], square_recv.at[2], peer["v"])
    advance("out")
    advance("qkv")
    square_flight.wait_recv()
    squares[3] = squares[2] + square_recv[2]
    square_flight = send(squares.at[3], square_recv.at[3], peer["w"])
    advance("qkv")
    square_flight.wait_recv()
    inside_small = lax.broadcasted_iota(jnp.int32, small_total.shape, 0) < COUNT_ROW
    small_square = jnp.sum(
        jnp.sum(jnp.where(inside_small, small_total * small_total, 0.0), axis=0, keepdims=True), axis=1, keepdims=True
    )
    squares[4] = squares[3] + square_recv[3] + jnp.broadcast_to(small_square, (8, 128))
    square_flight = send(squares.at[4], square_recv.at[4], to_core)
    square_flight.wait_recv()
    norm = jnp.sqrt(squares[4] + square_recv[4]) * unit
    ref["scalars"][0:8] = unit * clip_norm / jnp.maximum(norm, clip_norm)
    ref["scalars"][8:16] = norm
    for batch, pieces in batches.items():
        for piece in pieces:
            while piece.step <= 4 + piece.halvings:
                advance_piece(piece)
    for copy in pending:
        copy.wait_send()


def backward_call(outer, down, up, back, base, x_all, x_t, part, other, context, context_t, queries, keys_in, values, query_mark, key_mark, out_low, qkv_low, vectors, gates, logs, sums_two, unit_sums, count):
    low, wide = jnp.bfloat16, jnp.float32
    length, full = x_all.shape
    half = full // 2
    qkv_shape = (3 * full, half)
    out_shape = (half, full)
    shapes = {"down": down.shape, "up": up.shape, "qkv": qkv_shape, "out": out_shape}
    big = [down, up, back, base, x_all, x_t, part, other, context, context_t, queries, keys_in, values, query_mark, key_mark, out_low, qkv_low]
    little = [vectors, gates, logs, sums_two, unit_sums, count]
    vmem = pl.BlockSpec(memory_space=pltpu.VMEM)
    hbm = pl.BlockSpec(memory_space=pl.ANY)
    sizes = []
    for _ in range(3):
        sizes += [
            (down.shape[0] // 3, down.shape[1], 4), (up.shape[0] // 3, up.shape[1], 4),
            (full, half, 4), (half, full // 3, 3),
        ]
    copies = sum(4 + halvings + (outer - 1) for _, _, halvings in sizes) + 2 + 4 + (outer - 1) + 5
    lasts = [(rows // 2**halvings, columns) for rows, columns, halvings in sizes]
    spare = [(outer,) + last if outer > 1 else (1, 8, 128) for last in lasts]
    scratch = [pltpu.VMEM(a.shape, a.dtype) for a in big[3:]]
    scratch += [
        pltpu.VMEM(back.shape, low),
        pltpu.VMEM(back.shape, low),
        pltpu.VMEM((3, down.shape[0] // 6, down.shape[1]), low),
        pltpu.VMEM((3, up.shape[0] // 6, up.shape[1]), low),
        pltpu.VMEM((length, full), low),
        pltpu.VMEM((length, half), low),
        pltpu.VMEM((8, length), wide),
        pltpu.VMEM((8, full), wide),
        pltpu.VMEM((length, length), low),
        pltpu.VMEM((2 * HEAD, length), low),
        pltpu.VMEM((2 * HEAD, length), wide),
        pltpu.VMEM((length, 2 * HEAD), wide),
        pltpu.VMEM((length, 2 * HEAD), wide),
        pltpu.VMEM((3, length, half), low),
        pltpu.VMEM(qkv_shape, low),
        pltpu.VMEM(out_shape, low),
        pltpu.VMEM((length, half), low),
        pltpu.VMEM((length, half), low),
        pltpu.VMEM((SMALL_ROWS, 128), wide),
        pltpu.VMEM((4, SMALL_ROWS, 128), wide),
        pltpu.VMEM((4 + outer, SMALL_ROWS, 128), wide),
        pltpu.VMEM((5, 8, 128), wide),
        pltpu.VMEM((5, 8, 128), wide),
        pltpu.VMEM((length, half), wide),
        tuple(pltpu.VMEM(shape, low) for shape in spare),
        pltpu.SemaphoreType.DMA((copies,)),
        pltpu.SemaphoreType.DMA((copies,)),
        pltpu.SemaphoreType.DMA((len(big) + 6,)),
        pltpu.SemaphoreType.DMA((12,)),
    ]
    for size in sizes:
        scratch += piece_buffers(*size)
    return pl.pallas_call(
        functools.partial(backward_kernel, outer, shapes),
        out_shape=[
            jax.ShapeDtypeStruct(down.shape, low),
            jax.ShapeDtypeStruct(up.shape, low),
            jax.ShapeDtypeStruct(qkv_shape, low),
            jax.ShapeDtypeStruct(out_shape, low),
            jax.ShapeDtypeStruct((8, half), wide),
            jax.ShapeDtypeStruct((8, unit_sums.shape[1]), wide),
            jax.ShapeDtypeStruct((16, 128), wide),
            jax.ShapeDtypeStruct((length, half), wide),
        ],
        in_specs=[hbm] * len(big) + [vmem] * len(little),
        out_specs=[hbm] * 4 + [vmem] * 4,
        scratch_shapes=scratch,
        compiler_params=pltpu.CompilerParams(
            collective_id=0, has_side_effects=True, vmem_limit_bytes=60 * 2**20
        ),
        cost_estimate=pl.CostEstimate(flops=2 * 10**10, bytes_accessed=3 * 10**8, transcendentals=7 * 10**6),
        name="backward_rows",
    )(*big, *little)


def on_device(
    hidden_in,
    teacher_in,
    segment_ids,
    pad_mask,
    qkv_weight,
    qkv_moment1,
    qkv_moment2,
    out_weight,
    out_moment1,
    out_moment2,
    up_weight,
    up_moment1,
    up_moment2,
    down_weight,
    down_moment1,
    down_moment2,
    bias_vectors,
    bias_moment1,
    bias_moment2,
    up_bias,
    up_bias_moment1,
    up_bias_moment2,
    norm_gains,
    gain_moment1,
    gain_moment2,
    head_gates,
    layer_gates,
    dim_gates,
    unit_gates,
    teacher_qkv,
    teacher_out,
    teacher_up,
    teacher_down,
    teacher_biases,
    teacher_up_bias,
    teacher_gains,
):
    length = segment_ids.shape[1]
    width = hidden_in.shape[2]
    full = 2 * width
    core = lax.axis_index("hid")
    low, wide = jnp.bfloat16, jnp.float32

    def swap(value):
        return lax.ppermute(value, "hid", [(0, 1), (1, 0)])

    def widen(own, other):
        return jnp.where(
            core == 0, jnp.concatenate([own, other], axis=1), jnp.concatenate([other, own], axis=1)
        )

    teacher_in_other, hidden_in_other = swap(teacher_in[0]), swap(hidden_in[0])
    owned = jnp.concatenate(
        [
            bias_vectors[2:], norm_gains, dim_gates[None], jnp.zeros((1, width), wide),
            teacher_biases[2:].astype(wide), teacher_gains.astype(wide), jnp.zeros((2, width), wide),
        ]
    )
    spread = widen(owned, swap(owned))
    gates = spread[6:7]
    ones = jnp.ones_like(gates)

    def vector_rows(rows, scale_one, scale_two):
        return jnp.concatenate(
            [scale_one, rows[0:1], rows[4:5], rows[2:3], scale_two, rows[1:2], rows[5:6], rows[3:4]]
        )

    vectors = vector_rows(spread[:8], layer_gates[0] * gates, layer_gates[1] * gates)
    teacher_vectors = vector_rows(spread[8:], ones, ones)
    marks = lax.broadcasted_iota(jnp.int32, (1, MARKS), 1)
    segment, padding = segment_ids[0][:, None], pad_mask[0][:, None]
    query_mark = (segment == marks).astype(low)
    key_mark = jnp.where(((segment == marks) & (padding > 0)) | (marks >= 8), 0.0, masked_score).astype(low)
    valid = jnp.broadcast_to(padding.astype(wide), (length, 128))
    head_rows = jnp.repeat(head_gates, HEAD)[None]
    pad_rows = jnp.zeros((5, width), wide)
    head_vectors = jnp.concatenate([bias_vectors[:2], head_rows, pad_rows])
    teacher_head_vectors = jnp.concatenate(
        [teacher_biases[:2].astype(wide), jnp.ones((1, width), wide), pad_rows]
    )
    units = jnp.concatenate([up_bias[None], unit_gates[None], jnp.zeros((6, up_bias.shape[0]), wide)])
    teacher_units = jnp.concatenate(
        [teacher_up_bias[None].astype(wide), jnp.ones((7, up_bias.shape[0]), wide)]
    )

    teacher_part, teacher_x, up_low, down_low, out_low, qkv_low = attend_call(
        False, teacher_in[0], teacher_in_other, teacher_qkv, teacher_out, teacher_head_vectors, query_mark, key_mark,
        (up_weight, down_weight, out_weight, qkv_weight),
    )
    teacher_part_other = swap(teacher_part)
    part, x_all, x_turned, queries, keys_in, values, context, context_turned, logs = attend_call(
        True, hidden_in[0], hidden_in_other, qkv_low, out_low, head_vectors, query_mark, key_mark
    )
    part_other = swap(part)
    teacher_first, teacher_reduced = feed_call(
        False, teacher_x, teacher_part, teacher_part_other, teacher_vectors, teacher_units, teacher_up, teacher_down
    )
    teacher_reduced_other = swap(teacher_reduced)
    first, reduced, first_turned, activated_turned, slope = feed_call(
        True, x_all, part, part_other, vectors, units, up_low, down_low
    )
    reduced_other = swap(reduced)
    block_out, base, grad_reduced, grad_expanded, back, sums_two, unit_sums = feed_back_call(
        first, reduced, reduced_other, teacher_first, teacher_reduced, teacher_reduced_other, valid,
        vectors, teacher_vectors, slope, up_low, down_low,
    )
    grad_down = nn_dot(activated_turned, grad_reduced).astype(low)
    grad_up = nn_dot(first_turned, grad_expanded).astype(low)
    gate_rows = jnp.concatenate([head_rows, 1.0 / head_rows, jnp.zeros((6, width), wide)])
    count = jnp.broadcast_to(jnp.sum(padding.astype(wide)), (8, 128))
    rows_all = lax.axis_size("rows")
    down_sum, up_sum, qkv_sum, out_sum, bias_sum, unit_sum, scalars, input_grad = backward_call(
        rows_all // INNER, grad_down, grad_up, back, base, x_all, x_turned, part, part_other, context, context_turned,
        queries, keys_in, values, query_mark, key_mark, out_low, qkv_low, vectors, gate_rows, logs,
        sums_two, unit_sums, count,
    )
    grad_norm = scalars[8, 0]
    factor = scalars[0:1, 0:1]
    weight_sums = (
        qkv_sum.reshape(qkv_weight.shape), out_sum, up_sum, down_sum, bias_sum[:6], unit_sum[0], bias_sum[6:8]
    )
    weights = (qkv_weight, out_weight, up_weight, down_weight, bias_vectors, up_bias, norm_gains)
    firsts = (
        qkv_moment1, out_moment1, up_moment1, down_moment1, bias_moment1, up_bias_moment1, gain_moment1
    )
    seconds = (
        qkv_moment2, out_moment2, up_moment2, down_moment2, bias_moment2, up_bias_moment2, gain_moment2
    )
    rates = (rate_attend, rate_output, rate_expand, rate_reduce, rate_vector, rate_vector, rate_vector)
    results = []
    for index in range(7):
        weight = weights[index]
        scale = factor[0] if weight.ndim == 1 else factor
        clipped = weight_sums[index].astype(wide) * scale
        new_weight, new_second = adam_step(
            weight, firsts[index], seconds[index], clipped, rates[index], weight_decay if index < 4 else 0.0
        )
        results.append((clipped, new_weight, new_second))
    block_out = block_out.reshape(hidden_in.shape)
    input_grad = input_grad.reshape(hidden_in.shape)
    return (
        block_out,
        input_grad,
        grad_norm,
        results[0][0],
        results[0][1],
        results[0][2],
        results[1][0],
        results[1][1],
        results[1][2],
        results[2][0],
        results[2][1],
        results[2][2],
        results[3][0],
        results[3][1],
        results[3][2],
        results[4][0],
        results[4][1],
        results[4][2],
        results[5][0],
        results[5][1],
        results[5][2],
        results[6][0],
        results[6][1],
        results[6][2],
        results[0][1].astype(jnp.bfloat16),
        results[1][1].astype(jnp.bfloat16),
        results[2][1].astype(jnp.bfloat16),
        results[3][1].astype(jnp.bfloat16),
    )


def solution(mesh):
    in_specs = (
        P("rows", None, "hid"),
        P("rows", None, "hid"),
        P("rows", None),
        P("rows", None),
        P(None, None, "hid"),
        P(None, None, "hid"),
        P(None, None, "hid"),
        P("hid", None),
        P("hid", None),
        P("hid", None),
        P(None, "hid"),
        P(None, "hid"),
        P(None, "hid"),
        P("hid", None),
        P("hid", None),
        P("hid", None),
        P(None, "hid"),
        P(None, "hid"),
        P(None, "hid"),
        P("hid"),
        P("hid"),
        P("hid"),
        P(None, "hid"),
        P(None, "hid"),
        P(None, "hid"),
        P("hid"),
        P(),
        P("hid"),
        P("hid"),
        P(None, None, "hid"),
        P("hid", None),
        P(None, "hid"),
        P("hid", None),
        P(None, "hid"),
        P("hid"),
        P(None, "hid"),
    )
    out_specs = (
        P("rows", None, "hid"),
        P("rows", None, "hid"),
        P(),
        P(None, None, "hid"),
        P(None, None, "hid"),
        P(None, None, "hid"),
        P("hid", None),
        P("hid", None),
        P("hid", None),
        P(None, "hid"),
        P(None, "hid"),
        P(None, "hid"),
        P("hid", None),
        P("hid", None),
        P("hid", None),
        P(None, "hid"),
        P(None, "hid"),
        P(None, "hid"),
        P("hid"),
        P("hid"),
        P("hid"),
        P(None, "hid"),
        P(None, "hid"),
        P(None, "hid"),
        P(None, None, "hid"),
        P("hid", None),
        P(None, "hid"),
        P("hid", None),
    )
    return jax.shard_map(
        on_device, mesh=mesh, in_specs=in_specs, out_specs=out_specs, check_vma=False
    )
```

```python
import functools

import jax
import jax.numpy as jnp
from jax import lax
from jax.experimental import pallas as pl
from jax.experimental.pallas import tpu as pltpu
from jax.sharding import PartitionSpec as P

D = 768
HEAD = 64
STEP = 10


epsilon_norm = 1e-06
masked_score = -1000000000.0
clip_norm = 0.001
beta_first = 0.9
beta_second = 0.999
adam_epsilon = 1e-08
weight_decay = 0.01
rate_attend = 0.03
rate_output = 0.2
rate_expand = 0.03
rate_reduce = 0.03
rate_vector = 0.3


def adam_step(weight, first, second, grad, rate, decay):
    first_new = beta_first * first + (1.0 - beta_first) * grad
    second_new = beta_second * second + (1.0 - beta_second) * grad * grad
    first_hat = first_new / (1.0 - beta_first**STEP)
    second_hat = second_new / (1.0 - beta_second**STEP)
    return (
        weight - rate * (first_hat / (jnp.sqrt(second_hat) + adam_epsilon) + decay * weight),
        second_new,
    )


MARKS = 128
TILE = 256


def nt_dot(left, right):
    return lax.dot_general(
        left, right, (((1,), (1,)), ((), ())), preferred_element_type=jnp.float32
    )


def nn_dot(left, right):
    return jnp.dot(left, right, preferred_element_type=jnp.float32)


def aligned(start, size):
    return pl.ds(pl.multiple_of(start, 16), size)


def lanes_of(core, width):
    return pl.ds(pl.multiple_of(core * width, 128), width)


class Mover:
    def __init__(self, local_sems, send_sems, recv_sems):
        self.local_sems, self.send_sems, self.recv_sems = local_sems, send_sems, recv_sems
        self.local_count = self.remote_count = 0
        self.sent = []

    def copy(self, source, target):
        moved = pltpu.make_async_copy(source, target, self.local_sems.at[self.local_count])
        self.local_count += 1
        moved.start()
        return moved

    def send(self, source, target, device):
        index = self.remote_count
        self.remote_count += 1
        moved = pltpu.make_async_remote_copy(
            src_ref=source, dst_ref=target, send_sem=self.send_sems.at[index],
            recv_sem=self.recv_sems.at[index], device_id=device, device_id_type=pl.DeviceIdType.MESH,
        )
        moved.start()
        self.sent.append(moved)
        return moved


def greet(core):
    barrier = pltpu.get_barrier_semaphore()
    to_core = {"hid": 1 - core}
    pl.semaphore_signal(barrier, inc=1, device_id=to_core, device_id_type=pl.DeviceIdType.MESH)
    pl.semaphore_wait(barrier, 1)
    return to_core


def attend_rows_kernel(
    teacher_in, hidden_in, teacher_qkv, teacher_out, qkv_weight, out_weight, up_weight, down_weight,
    segment_ref, padding_ref, bias_ref, gain_ref, line_ref, teacher_bias_ref, teacher_gain_ref, head_gates, layer_gates,
    teacher_part_out, teacher_other_out, teacher_x_out, part_out, x_out, turned_out, query_out, key_out, value_out,
    context_out, context_turned_out, up_out, down_out, out_out, qkv_out,
    log_ref, query_mark_ref, key_mark_ref, valid_ref, vector_ref, teacher_vector_ref, gate_ref, count_ref,
    teacher_x, x_all, turned, query, key, value, context, context_turned, teacher_part, part,
    teacher_qkv_held, teacher_out_held, qkv_wide, out_wide, up_wide, down_wide, qkv_low, out_low, up_low, down_low,
    pack, spread, local_sems, send_sems, recv_sems,
):
    low, wide = jnp.bfloat16, jnp.float32
    core = lax.axis_index("hid")
    mover = Mover(local_sems, send_sems, recv_sems)
    length, width = hidden_in.shape
    here = lanes_of(core, width)
    to_core = greet(core)

    arriving = [mover.copy(teacher_in, teacher_x.at[:, here]), mover.send(teacher_in, teacher_x.at[:, here], to_core)]
    arriving_weights = [mover.copy(teacher_qkv, teacher_qkv_held), mover.copy(teacher_out, teacher_out_held)]
    arriving_student = [mover.copy(hidden_in, x_all.at[:, here]), mover.send(hidden_in, x_all.at[:, here], to_core)]
    casts = [
        (mover.copy(qkv_weight, qkv_wide), qkv_wide, qkv_low, qkv_out),
        (mover.copy(out_weight, out_wide), out_wide, out_low, out_out),
        (mover.copy(up_weight, up_wide), up_wide, up_low, up_out),
        (mover.copy(down_weight, down_wide), down_wide, down_low, down_out),
    ]
    leaving = []

    def cast(index):
        arrived, source, target, output = casts[index]
        arrived.wait()
        target[...] = source[...].astype(low)
        leaving.append(mover.copy(target, output))

    pack[0:4] = bias_ref[2:6]
    pack[4:6] = gain_ref[...]
    pack[6:7] = line_ref[3:4, :width]
    pack[7:8] = jnp.zeros_like(pack[7:8])
    pack[8:12] = teacher_bias_ref[2:6].astype(wide)
    pack[12:14] = teacher_gain_ref[...].astype(wide)
    pack[14:16] = jnp.zeros_like(pack[14:16])
    pack_flight = mover.send(pack, spread.at[:, here], to_core)
    spread[:, here] = pack[...]

    marks = lax.broadcasted_iota(jnp.int32, (MARKS, length), 0)
    same = jnp.broadcast_to(segment_ref[...], (MARKS, length)) == marks
    padding = jnp.broadcast_to(padding_ref[...], (MARKS, length))
    query_mark_ref[...] = jnp.where(same, 1.0, 0.0).T.astype(low)
    key_mark_ref[...] = jnp.where((same & (padding > 0)) | (marks >= 8), 0.0, masked_score).T.astype(low)
    valid_ref[...] = padding.astype(wide).T
    count_ref[...] = jnp.broadcast_to(jnp.sum(padding[0:8].astype(wide), axis=1, keepdims=True), (8, 128))

    pair = 2 * HEAD
    pairs = width // pair
    block_rows = length // 2
    first_head = lax.broadcasted_iota(jnp.int32, (1, pair), 1) < HEAD
    gate_ref[...] = jnp.zeros_like(gate_ref)
    for number in range(pairs):
        row = jnp.where(first_head, head_gates[2 * number], head_gates[2 * number + 1])
        gate_ref[0:1, number * pair : (number + 1) * pair] = row
        gate_ref[1:2, number * pair : (number + 1) * pair] = 1.0 / row

    def project(x_ref, weights, query_bias, value_bias):
        rows = x_ref[...]
        query[...] = (nn_dot(rows, weights[0]) + query_bias).astype(low)
        key[...] = nn_dot(rows, weights[1]).astype(low)
        value[...] = (nn_dot(rows, weights[2]) + value_bias).astype(low)

    def attend(number, keep):
        lanes = slice(number * pair, (number + 1) * pair)
        scaled = query[:, lanes] * jnp.asarray(HEAD ** (-0.5), low)
        key_wide = jnp.concatenate([key[:, lanes], key_mark_ref[...]], axis=1)
        values = value[:, lanes]
        logs = []
        for start in range(0, length, block_rows):
            block = slice(start, start + block_rows)
            outs, columns = [], []
            for head in range(2):
                chosen = jnp.where(first_head if head == 0 else ~first_head, scaled[block], jnp.zeros_like(scaled[block]))
                query_wide = jnp.concatenate([chosen, query_mark_ref[block]], axis=1)
                scores = nt_dot(query_wide, key_wide)
                top = jnp.max(scores, axis=1, keepdims=True)
                weights = jnp.exp(scores - top)
                sums = jnp.sum(weights, axis=1, keepdims=True)
                outs.append(nn_dot(weights.astype(low), values) * (1.0 / sums))
                if keep:
                    columns.append(top + jnp.log(sums))
            mixed = jnp.where(first_head, outs[0], outs[1])
            if keep:
                mixed = mixed * gate_ref[0:1, lanes]
                logs.append(jnp.where(first_head, columns[0], columns[1]))
            mixed = mixed.astype(low)
            context[block, lanes] = mixed
            if keep:
                context_turned[lanes, block] = mixed.T
        if keep:
            log_turned = jnp.concatenate(logs, axis=0).T
            log_ref[8 * number : 8 * number + 8] = jnp.concatenate(
                [log_turned[0:1], log_turned[HEAD : HEAD + 1], log_turned[0:6]], axis=0
            )

    for moved in arriving[:1] + arriving_weights[:1]:
        moved.wait()
    arriving[1].wait_recv()
    leaving.append(mover.copy(teacher_x, teacher_x_out))
    project(teacher_x, teacher_qkv_held, teacher_bias_ref[0:1].astype(wide), teacher_bias_ref[1:2].astype(wide))
    for number in range(pairs):
        attend(number, False)
        cast(number)
    arriving_weights[1].wait()
    teacher_part[...] = nn_dot(context[...], teacher_out_held[...]).astype(low)
    teacher_flight = mover.send(teacher_part, teacher_other_out, to_core)
    leaving.append(mover.copy(teacher_part, teacher_part_out))

    arriving_student[0].wait()
    arriving_student[1].wait_recv()
    leaving.append(mover.copy(x_all, x_out))
    project(x_all, qkv_low, bias_ref[0:1], bias_ref[1:2])
    leaving.append(mover.copy(query, query_out))
    leaving.append(mover.copy(key, key_out))
    leaving.append(mover.copy(value, value_out))
    turned[...] = x_all[...].T
    leaving.append(mover.copy(turned, turned_out))
    for number in range(pairs):
        attend(number, True)
        if number == 0:
            cast(3)
    part[...] = nn_dot(context[...], out_low[...]).astype(low)
    leaving.append(mover.copy(part, part_out))
    leaving.append(mover.copy(context, context_out))
    leaving.append(mover.copy(context_turned, context_turned_out))

    pack_flight.wait_recv()
    dims = spread[6:7]
    ones = jnp.ones_like(dims)
    for target, rows, scales in (
        (vector_ref, spread[0:8], (layer_gates[0] * dims, layer_gates[1] * dims)),
        (teacher_vector_ref, spread[8:16], (ones, ones)),
    ):
        target[...] = jnp.concatenate(
            [scales[0], rows[0:1], rows[4:5], rows[2:3], scales[1], rows[1:2], rows[5:6], rows[3:4]], axis=0
        )
    teacher_flight.wait_recv()
    for moved in leaving:
        moved.wait()
    for moved in mover.sent:
        moved.wait_send()


def attend_rows_call(teacher_in, hidden_in, teacher_qkv, teacher_out, qkv_weight, out_weight, up_weight, down_weight, segment, padding, biases, gains, lines, teacher_biases, teacher_gains, head_gates, layer_gates):
    low, wide = jnp.bfloat16, jnp.float32
    length, width = hidden_in.shape
    full = 2 * width
    pairs = width // (2 * HEAD)
    hidden = up_weight.shape[1]
    vmem, anywhere = pl.BlockSpec(memory_space=pltpu.VMEM), pl.BlockSpec(memory_space=pl.ANY)
    smem = pl.BlockSpec(memory_space=pltpu.SMEM)
    rows_full, rows_half = (length, full), (length, width)
    far = [rows_full] * 5 + [(full, length)] + [rows_half] * 4 + [(width, length)]
    far += [up_weight.shape, down_weight.shape, out_weight.shape, qkv_weight.shape]
    near = [
        ((8 * pairs, length), wide), ((length, MARKS), low), ((length, MARKS), low), ((length, MARKS), wide),
        ((8, full), wide), ((8, full), wide), ((8, width), wide), ((8, 128), wide),
    ]
    held = [rows_full, rows_full, (full, length), rows_half, rows_half, rows_half, rows_half, (width, length), rows_full, rows_full]
    return pl.pallas_call(
        attend_rows_kernel,
        out_shape=[jax.ShapeDtypeStruct(shape, low) for shape in far] + [jax.ShapeDtypeStruct(*pair) for pair in near],
        in_specs=[anywhere] * 8 + [vmem] * 7 + [smem] * 2,
        out_specs=[anywhere] * len(far) + [vmem] * len(near),
        scratch_shapes=[pltpu.VMEM(shape, low) for shape in held]
        + [pltpu.VMEM(teacher_qkv.shape, low), pltpu.VMEM(teacher_out.shape, low)]
        + [pltpu.VMEM(w.shape, wide) for w in (qkv_weight, out_weight, up_weight, down_weight)]
        + [pltpu.VMEM(w.shape, low) for w in (qkv_weight, out_weight, up_weight, down_weight)]
        + [pltpu.VMEM((16, width), wide), pltpu.VMEM((16, full), wide)]
        + [pltpu.SemaphoreType.DMA((24,)), pltpu.SemaphoreType.DMA((4,)), pltpu.SemaphoreType.DMA((4,))],
        compiler_params=pltpu.CompilerParams(collective_id=1, has_side_effects=True, vmem_limit_bytes=60 * 2**20),
        cost_estimate=pl.CostEstimate(flops=2 * 10**10, bytes_accessed=5 * 10**7, transcendentals=14 * 10**6),
        name="attend_rows",
    )(
        teacher_in, hidden_in, teacher_qkv, teacher_out, qkv_weight, out_weight, up_weight, down_weight,
        segment, padding, biases, gains, lines, teacher_biases, teacher_gains, head_gates, layer_gates,
    )


def norm_parts(resid):
    center = jnp.mean(resid, axis=1, keepdims=True)
    second = jnp.mean(resid * resid, axis=1, keepdims=True)
    inverse = lax.rsqrt(second - center * center + epsilon_norm)
    return (resid - center) * inverse, inverse


def norm_grad(grad_normed, normed, inverse):
    center = jnp.mean(grad_normed, axis=1, keepdims=True)
    crossed = jnp.mean(grad_normed * normed, axis=1, keepdims=True)
    return inverse * (grad_normed - center - normed * crossed)


def column_sum(value):
    return jnp.sum(value, axis=0, keepdims=True)


def feed_rows_kernel(
    teacher_x_in, teacher_part_in, teacher_other_in, x_in, part_in, teacher_up_in, teacher_down_in, up_in, down_in,
    valid_ref, vector_ref, teacher_vector_ref, line_ref,
    other_out, base_out, back_out, grad_down_out, grad_up_out, block_ref, sums_ref, unit_sums_ref,
    teacher_x, teacher_part, teacher_other, x_all, part, other, teacher_up, teacher_down, up, down,
    teacher_first, first, teacher_reduced, teacher_reduced_other, reduced, reduced_other, slope, activated_turned,
    first_turned, grad_reduced, grad_expanded, base, back, grad_down, grad_up, local_sems, send_sems, recv_sems,
):
    low, wide = jnp.bfloat16, jnp.float32
    core = lax.axis_index("hid")
    mover = Mover(local_sems, send_sems, recv_sems)
    length, full = x_in.shape
    half = full // 2
    to_core = greet(core)
    part_flight = mover.send(part_in, other, to_core)
    tiles = [slice(start, start + TILE) for start in range(0, length, TILE)]
    teacher_rows = ((teacher_x_in, teacher_x), (teacher_part_in, teacher_part), (teacher_other_in, teacher_other))
    tile_loads = [[mover.copy(source.at[tiles[0]], target.at[tiles[0]]) for source, target in teacher_rows]]
    up_load = mover.copy(teacher_up_in, teacher_up)
    down_load = mover.copy(teacher_down_in, teacher_down)
    rest = slice(TILE, length)
    tile_loads.append([mover.copy(source.at[rest], target.at[rest]) for source, target in teacher_rows])
    loads = [
        mover.copy(source, target) for source, target in ((x_in, x_all), (part_in, part), (up_in, up), (down_in, down))
    ]

    def norm_one(x_ref, own_ref, far_ref, vectors, block):
        branch = own_ref[block].astype(wide) + far_ref[block].astype(wide)
        normed, _ = norm_parts(x_ref[block].astype(wide) + (branch + vectors[1:2]) * vectors[0:1])
        return normed * vectors[2:3] + vectors[3:4]

    def gelu_share(expanded):
        return 0.5 + 0.5 * lax.erf(expanded * (0.5**0.5))

    teacher_flights = []
    for index, block in enumerate(tiles):
        if index < 2:
            for moved in tile_loads[index]:
                moved.wait()
        out = norm_one(teacher_x, teacher_part, teacher_other, teacher_vector_ref, block)
        teacher_first[block] = out
        if index == 0:
            up_load.wait()
        expanded = nn_dot(out.astype(low), teacher_up[...]) + line_ref[2:3]
        activated = (expanded * gelu_share(expanded)).astype(low)
        if index == 0:
            down_load.wait()
        teacher_reduced[block] = nn_dot(activated, teacher_down[...]).astype(low)
        teacher_flights.append(mover.send(teacher_reduced.at[block], teacher_reduced_other.at[block], to_core))
    for moved in loads:
        moved.wait()
    part_flight.wait_recv()
    leaving = [mover.copy(other, other_out)]
    flights = []
    for block in tiles:
        out = norm_one(x_all, part, other, vector_ref, block)
        first[block] = out
        out_low = out.astype(low)
        first_turned[:, block] = out_low.T
        expanded = nn_dot(out_low, up[...]) + line_ref[0:1]
        share = gelu_share(expanded)
        activated = (expanded * share * line_ref[1:2]).astype(low)
        reduced[block] = nn_dot(activated, down[...]).astype(low)
        flights.append(mover.send(reduced.at[block], reduced_other.at[block], to_core))
        activated_turned[:, block] = activated.T
        bell = jnp.exp(-0.5 * expanded * expanded)
        slope[block] = ((share + expanded * bell * 0.3989422804014327) * line_ref[1:2]).astype(low)

    sums_ref[...] = jnp.zeros_like(sums_ref)
    unit_sums_ref[...] = jnp.zeros_like(unit_sums_ref)
    for index, block in enumerate(tiles):
        teacher_flights[index].wait_recv()
        flights[index].wait_recv()
        student_first, target_first = first[block], teacher_first[block]
        branch = reduced[block].astype(wide) + reduced_other[block].astype(wide)
        normed, inverse = norm_parts(student_first + (branch + vector_ref[5:6]) * vector_ref[4:5])
        second = normed * vector_ref[6:7] + vector_ref[7:8]
        target_branch = teacher_reduced[block].astype(wide) + teacher_reduced_other[block].astype(wide)
        target_normed, _ = norm_parts(target_first + target_branch + teacher_vector_ref[5:6])
        target = target_normed * teacher_vector_ref[6:7] + teacher_vector_ref[7:8]
        block_ref[block] = jnp.where(core == 0, second[:, :half], second[:, half:]).astype(low)
        twice = valid_ref[block, 0:1] * 2.0
        grad_second = twice * (second - target)
        grad_resid = norm_grad(grad_second * vector_ref[6:7], normed, inverse)
        grad_branch = grad_resid * vector_ref[4:5]
        sums_ref[0:1] += column_sum(grad_second * normed)
        sums_ref[1:2] += column_sum(grad_second)
        sums_ref[2:3] += column_sum(grad_branch)
        grad_branch_low = grad_branch.astype(low)
        grad_reduced[block] = grad_branch_low
        grad_activated = nt_dot(grad_branch_low, down[...]).astype(low).astype(wide)
        grad_unit = (grad_activated * slope[block].astype(wide)).astype(low)
        grad_expanded[block] = grad_unit
        unit_sums_ref[0:1] += column_sum(grad_unit.astype(wide))
        back[block] = nt_dot(grad_unit, up[...]).astype(low)
        base[block] = twice * (student_first - target_first) + grad_resid
        leaving.append(mover.copy(back.at[block], back_out.at[block]))
        leaving.append(mover.copy(base.at[block], base_out.at[block]))
    parts = 3
    rows = grad_down.shape[0] // parts
    for index in range(parts):
        block = slice(index * rows, (index + 1) * rows)
        grad_down[block] = nn_dot(activated_turned[block], grad_reduced[...]).astype(low)
        leaving.append(mover.copy(grad_down.at[block], grad_down_out.at[block]))
    rows = grad_up.shape[0] // parts
    for index in range(parts):
        block = slice(index * rows, (index + 1) * rows)
        grad_up[block] = nn_dot(first_turned[block], grad_expanded[...]).astype(low)
        leaving.append(mover.copy(grad_up.at[block], grad_up_out.at[block]))
    for moved in leaving:
        moved.wait()
    for moved in mover.sent:
        moved.wait_send()


def feed_rows_call(teacher_x, teacher_part, teacher_other, x_all, part, teacher_up, teacher_down, up_low, down_low, valid, vectors, teacher_vectors, lines):
    low, wide = jnp.bfloat16, jnp.float32
    length, full = x_all.shape
    hidden = up_low.shape[1]
    vmem, anywhere = pl.BlockSpec(memory_space=pltpu.VMEM), pl.BlockSpec(memory_space=pl.ANY)
    rows = (length, full)
    up_shape, down_shape = up_low.shape, down_low.shape
    far = [(rows, low), (rows, wide), (rows, low), (down_shape, low), (up_shape, low)]
    near = [((length, full // 2), low), ((8, full), wide), ((8, hidden), wide)]
    held = [(rows, low)] * 6 + [(up_shape, low), (down_shape, low)] * 2
    held += [(rows, wide)] * 2 + [(rows, low)] * 4 + [((length, hidden), low), ((hidden, length), low), ((full, length), low)]
    held += [(rows, low), ((length, hidden), low), (rows, wide), (rows, low), (down_shape, low), (up_shape, low)]
    return pl.pallas_call(
        feed_rows_kernel,
        out_shape=[jax.ShapeDtypeStruct(*pair) for pair in far + near],
        in_specs=[anywhere] * 9 + [vmem] * 4,
        out_specs=[anywhere] * len(far) + [vmem] * len(near),
        scratch_shapes=[pltpu.VMEM(*pair) for pair in held]
        + [pltpu.SemaphoreType.DMA((32,)), pltpu.SemaphoreType.DMA((12,)), pltpu.SemaphoreType.DMA((12,))],
        compiler_params=pltpu.CompilerParams(collective_id=2, has_side_effects=True, vmem_limit_bytes=62 * 2**20),
        cost_estimate=pl.CostEstimate(flops=3 * 10**10, bytes_accessed=5 * 10**7, transcendentals=6 * 10**6),
        name="feed_rows",
    )(
        teacher_x, teacher_part, teacher_other, x_all, part, teacher_up, teacher_down, up_low, down_low,
        valid, vectors, teacher_vectors, lines,
    )


def vector_adam_kernel(
    scalar_ref, bias_sum, unit_sum, bias, bias_first, bias_second, unit, unit_first, unit_second, gain, gain_first, gain_second,
    bias_grad, bias_new, bias_second_new, unit_grad, unit_new, unit_second_new, gain_grad, gain_new, gain_second_new,
):
    factor = scalar_ref[0:1, 0:1]
    for total, states, outs in (
        (bias_sum[0:6], (bias, bias_first, bias_second), (bias_grad, bias_new, bias_second_new)),
        (bias_sum[6:8], (gain, gain_first, gain_second), (gain_grad, gain_new, gain_second_new)),
        (unit_sum[0:1], (unit, unit_first, unit_second), (unit_grad, unit_new, unit_second_new)),
    ):
        clipped = total * factor
        values = [state[...].reshape(clipped.shape) for state in states]
        new_weight, new_second = adam_step(*values, clipped, rate_vector, 0.0)
        for target, value in zip(outs, (clipped, new_weight, new_second)):
            target[...] = value.reshape(target.shape)


def vector_adam(*arrays):
    shapes = [a.shape for a in arrays[3:12:3] for _ in range(3)]
    return pl.pallas_call(
        vector_adam_kernel,
        out_shape=[jax.ShapeDtypeStruct(shape, jnp.float32) for shape in shapes],
        cost_estimate=pl.CostEstimate(flops=10**5, bytes_accessed=3 * 10**5, transcendentals=10**4),
        name="vector_adam",
    )(*arrays)


INNER = 16
SMALL_ROWS = 40
COUNT_ROW = 36


class Piece:
    def __init__(self, source, target, first_row, rows, first_column, columns, order, own, halvings):
        self.source, self.target = source, target
        self.first_row, self.rows = first_row, rows
        self.first_column, self.columns = first_column, columns
        self.order, self.own, self.halvings = order, own, halvings


def piece_buffers(rows, columns, halvings):
    low, wide = jnp.bfloat16, jnp.float32
    last = rows // 16 if halvings == 4 else rows // 8
    return [
        pltpu.VMEM((rows // 2, columns), low),
        pltpu.VMEM((rows // 4, columns), low),
        pltpu.VMEM((rows // 8, columns), low),
        pltpu.VMEM((last, columns), low),
        pltpu.VMEM((rows // 4, columns), low),
        pltpu.VMEM((rows // 8, columns), low),
        pltpu.VMEM((last, columns), low),
        pltpu.VMEM((rows // 4, columns), wide),
        pltpu.VMEM((last, columns), low),
    ]


SCHEDULE = (
    0, 4, 5, 2, "l", "n", "n", 0, 4, "n", "n", "o", 5, 3, "a", 0, 1, 4, 9, "a", 5, 0, "a", 4, 8, 2, 3, 0, "a", 5, 4,
    "a", 1, 0, "a", 5, 4, 9, 2, "q", "q", 0, 6, 1, 3, 2, 9, "q", 7, 1, 8, "i", 4, 3, 5, 2, "s", 6, 1, 8, 7, 3, 0, 4, 1,
    "i", 6, "s", 3, 8, 2, 7, 3, 6, 1, 7, 8, 2, 5, 6, 9, 4, 7, 8, 3, "s", 1, 6, "s", 9, 7, 5, 8, "S", 6, 9, 2, 7, "S", 9,
    8, 3, 6, 7, 1, "S", 5, "S", 0, 9, "S", 2, 6, 7,
)


def backward_kernel(
    outer, down, up, back, base_in, x_in, x_t_in, part_in, other_in, context_in, context_t_in, query_in,
    key_in, value_in, query_mark_in, key_mark_in, out_weight_in, qkv_weight_in,
    vector_ref, gate_ref, log_ref, sums_two, unit_sums, count,
    down_sum, up_sum, qkv_sum, out_sum, bias_out, unit_out, scalars, input_grad,
    base, x, x_t, part, other, context, context_t, query,
    key, value, query_mark, key_mark, out_weight, qkv_weight,
    back_other, back_own, own_down, own_up, attended_grad, heads_grad, inner_rows, sums_one, raw_scratch, turned_keys,
    turned_grad, pair_keys, pair_values, proj, qkv_parts, out_parts, input_send, input_recv, small, small_recv,
    small_outer, squares, square_recv, resid_grad, shard_outer, send_sems, recv_sems, load_sems, shard_sems, *buffers,
):
    low, wide = jnp.bfloat16, jnp.float32
    place = lax.axis_index("rows")
    inside = place % INNER
    group = place // INNER
    core = lax.axis_index("hid")
    bits = {"x": inside % 2, "y": (inside // 2) % 2, "v": (inside // 4) % 2, "w": inside // 8}
    steps = {"x": 1, "y": 2, "v": 4, "w": 8}
    peer = {name: {"rows": place + steps[name] - 2 * steps[name] * bits[name]} for name in bits}
    to_group = [{"rows": inside + INNER * ((group + d) % outer)} for d in range(outer)]
    to_core = {"hid": 1 - core}
    barrier = pltpu.get_barrier_semaphore()
    peers = list(peer.values()) + to_group[1:] + [to_core]
    for there in peers:
        pl.semaphore_signal(barrier, inc=1, device_id=there, device_id_type=pl.DeviceIdType.MESH)
    pl.semaphore_wait(barrier, len(peers))

    counter = [0]
    pending = []

    def send(source, target, device):
        index = counter[0]
        counter[0] += 1
        copy = pltpu.make_async_remote_copy(
            src_ref=source, dst_ref=target, send_sem=send_sems.at[index],
            recv_sem=recv_sems.at[index], device_id=device, device_id_type=pl.DeviceIdType.MESH,
        )
        copy.start()
        pending.append(copy)
        return copy

    loads = []

    def load(source, target):
        copy = pltpu.make_async_copy(source, target, load_sems.at[len(loads)])
        copy.start()
        loads.append(copy)

    def wait_loads(first, last):
        for copy in loads[first:last]:
            copy.wait()

    orders = ("xyvw", "yxvw", "vxyw")
    pieces = []

    def add_piece(*fields):
        piece = Piece(*fields)
        piece.index, piece.step = len(pieces), 0
        piece.buffers = buffers[9 * piece.index : 9 * piece.index + 9]
        piece.offsets = [0]
        size = piece.rows
        for name in piece.order[: piece.halvings]:
            size = size // 2
            piece.offsets.append(piece.offsets[-1] + size * bits[name])
        pieces.append(piece)

    for source, target, held in ((down, down_sum, own_down), (up, up_sum, own_up)):
        rows = source.shape[0] // 3
        for lane in range(3):
            add_piece(source, target, rows * lane, rows, 0, source.shape[1], orders[lane], held.at[lane], 4)
    columns = qkv_parts.shape[1]
    split = qkv_parts.shape[0] * 5 // 9
    add_piece(qkv_parts, qkv_sum, 0, split, 0, columns, orders[0], None, 4)
    add_piece(qkv_parts, qkv_sum, split, qkv_parts.shape[0] - split, 0, columns, orders[1], None, 4)
    split = out_parts.shape[1] // 3
    add_piece(out_parts, out_sum, 0, out_parts.shape[0], 0, split, orders[0], None, 3)
    add_piece(out_parts, out_sum, 0, out_parts.shape[0], split, 2 * split, orders[1], None, 3)

    square_terms = []

    def advance_piece(piece):
        r1, r2, r3, r4, s2, s3, s4, keep, shard = piece.buffers
        step = piece.step
        piece.step += 1
        order, rows = piece.order, piece.rows
        columns = pl.ds(piece.first_column, piece.columns)
        names_done = order[: piece.halvings]

        def own(start, size):
            if piece.own is not None:
                return piece.own[aligned(start, size), :].astype(wide)
            return piece.source[aligned(piece.first_row + piece.offsets[1] + start, size), columns].astype(wide)

        if step == 0:
            start = piece.first_row + rows // 2 * (1 - bits[order[0]])
            piece.flight = send(piece.source.at[aligned(start, rows // 2), columns], r1, peer[order[0]])
        elif step == 1:
            if piece.own is not None:
                wait_loads(piece.loaded, piece.loaded + 1)
            piece.flight.wait_recv()
            bit = bits[order[1]]
            size = rows // 4
            sent = size * (1 - bit)
            s2[...] = (own(sent, size) + r1[aligned(sent, size), :].astype(wide)).astype(low)
            piece.flight = send(s2, r2, peer[order[1]])
            kept = size * bit
            keep[...] = own(kept, size) + r1[aligned(kept, size), :].astype(wide)
        elif step == 2:
            piece.flight.wait_recv()
            keep[...] = keep[...] + r2[...].astype(wide)
            bit = bits[order[2]]
            size = rows // 8
            s3[...] = keep[aligned(size * (1 - bit), size), :].astype(low)
            piece.flight = send(s3, r3, peer[order[2]])
        elif step == 3:
            piece.flight.wait_recv()
            size = rows // 8
            mine = aligned(size * bits[order[2]], size)
            total = keep[mine, :] + r3[...].astype(wide)
            if piece.halvings == 4:
                keep[mine, :] = total
                small_size = size // 2
                sent = size * bits[order[2]] + small_size * (1 - bits[order[3]])
                s4[...] = keep[aligned(sent, small_size), :].astype(low)
            else:
                s4[...] = total.astype(low)
            piece.flight = send(s4, r4, peer[order[3]])
        elif step == 4:
            piece.flight.wait_recv()
            if piece.halvings == 4:
                size = rows // 16
                kept = rows // 8 * bits[order[2]] + size * bits[order[3]]
                total = keep[aligned(kept, size), :] + r4[...].astype(wide)
                weight = 1.0
            else:
                total = s4[...].astype(wide) + r4[...].astype(wide)
                weight = 0.5
            if outer > 1:
                shard[...] = total.astype(low)
                shard_outer[piece.index][0] = shard[...]
                copies = [send(shard, shard_outer[piece.index].at[d], to_group[d]) for d in range(1, outer)]
                for copy in copies:
                    copy.wait()
                    pending[:] = [entry for entry in pending if entry is not copy]
                total = jnp.zeros_like(total)
                for index in range(outer):
                    total = total + shard_outer[piece.index][(group - index + outer) % outer].astype(wide)
            shard[...] = total.astype(low)
            square_terms.append(weight * jnp.sum(jnp.sum(total * total, axis=0, keepdims=True), axis=1, keepdims=True))
            size = rows // 2**piece.halvings
            here = piece.target.at[aligned(piece.first_row + piece.offsets[-1], size), columns]
            piece.local = pltpu.make_async_copy(shard, here, shard_sems.at[piece.index])
            piece.local.start()
            piece.flight = send(shard, here, peer[names_done[-1]])
        elif step < 4 + piece.halvings:
            level = piece.halvings - (step - 4)
            piece.flight.wait_recv()
            if step == 5:
                piece.local.wait()
            size = rows // 2**level
            block = piece.target.at[aligned(piece.first_row + piece.offsets[level], size), columns]
            piece.flight = send(block, block, peer[names_done[level - 1]])
        elif step == 4 + piece.halvings:
            piece.flight.wait_recv()

    back_flight = []
    length, full = x.shape
    half = full // 2
    head_loads = ((base_in, base), (x_in, x), (part_in, part), (other_in, other), (back, back_own), (context_in, context), (out_weight_in, out_weight))
    mid_loads = ((context_t_in, context_t), (query_in, query), (key_in, key), (value_in, value), (query_mark_in, query_mark), (key_mark_in, key_mark))
    late_loads = ((x_t_in, x_t), (qkv_weight_in, qkv_weight))

    def start_loads():
        back_flight.append(send(back, back_other, to_core))
        for pair in head_loads:
            load(*pair)
        for piece in pieces:
            if piece.own is not None:
                piece.loaded = len(loads)
                load(piece.source.at[aligned(piece.first_row + piece.offsets[1], piece.rows // 2), :], piece.own)
        for pair in mid_loads + late_loads:
            load(*pair)
        back_flight[0].wait_recv()
        wait_loads(0, 7)
        sums_one[...] = jnp.zeros_like(sums_one)
        pair_keys[...] = jnp.zeros_like(pair_keys)
        pair_values[...] = jnp.zeros_like(pair_values)

    def norm_back(index):
        block = slice(index * TILE, (index + 1) * TILE)
        returned = (back_own[block, :].astype(wide) + back_other[block, :].astype(wide)).astype(low).astype(wide)
        grad_first = base[block, :] + returned
        branch = part[block, :].astype(wide) + other[block, :].astype(wide)
        resid = x[block, :].astype(wide) + (branch + vector_ref[1:2]) * vector_ref[0:1]
        normed, inverse = norm_parts(resid)
        grad_resid = norm_grad(grad_first * vector_ref[2:3], normed, inverse)
        resid_grad[block, :] = jnp.where(core == 0, grad_resid[:, :half], grad_resid[:, half:])
        grad_attended = grad_resid * vector_ref[0:1]
        sums_one[0:1] += column_sum(grad_first * normed)
        sums_one[1:2] += column_sum(grad_first)
        sums_one[2:3] += column_sum(grad_attended)
        grad_attended_low = grad_attended.astype(low)
        attended_grad[block, :] = grad_attended_low
        grad_heads = (nt_dot(grad_attended_low, out_weight[...]) * gate_ref[0:1]).astype(low)
        heads_grad[block, :] = grad_heads
        product = grad_heads.astype(wide) * context[block, :].astype(wide) * gate_ref[1:2]
        lane = lax.broadcasted_iota(jnp.int32, (1, 128), 1)
        columns = jnp.zeros((TILE, 128), wide)
        for pair in range(half // 128):
            some = product[:, 128 * pair : 128 * pair + 128]
            low_sum = jnp.sum(jnp.where(lane < HEAD, some, 0.0), axis=1, keepdims=True)
            high_sum = jnp.sum(jnp.where(lane < HEAD, 0.0, some), axis=1, keepdims=True)
            columns = jnp.where(lane == 2 * pair, low_sum, jnp.where(lane == 2 * pair + 1, high_sum, columns))
        inner_rows[:, block] = columns.T[0:8]

    def out_gradient():
        wait_loads(13, 19)
        out_parts[...] = nn_dot(context_t[...], attended_grad[...]).astype(low)

    pair_width = 2 * HEAD
    scale = HEAD ** (-0.5)
    vector_rows = [[], []]

    def attend_head(number, head):
        lanes = slice(number * pair_width, (number + 1) * pair_width)
        if head == 0:
            turned_keys[...] = key[:, lanes].T
        lane = lax.broadcasted_iota(jnp.int32, (1, pair_width), 1)
        mask = lane < HEAD if head == 0 else lane >= HEAD
        queries, grads = query[:, lanes], heads_grad[:, lanes]
        query_wide = jnp.concatenate([queries, query_mark[...]], axis=1)
        logs = log_ref[8 * number + head : 8 * number + head + 1, :]
        inner = inner_rows[2 * number + head : 2 * number + head + 1, :]

        for start in range(0, length, TILE):
            block = slice(start, start + TILE)
            zero = jnp.zeros((TILE, pair_width), low)
            chosen = jnp.where(mask, key[block, lanes] * jnp.asarray(scale, low), zero)
            key_wide = jnp.concatenate([chosen, key_mark[block, :]], axis=1)
            probs = jnp.exp(nt_dot(key_wide, query_wide) - logs)
            grad_probs = nt_dot(jnp.where(mask, value[block, lanes], zero), grads)
            grad_raw = (probs * (grad_probs - inner)).astype(low)
            raw_scratch[block, :] = grad_raw
            pair_keys[block, :] = jnp.where(mask, nn_dot(grad_raw, queries), pair_keys[block, :])
            pair_values[block, :] = jnp.where(mask, nn_dot(probs.astype(low), grads), pair_values[block, :])

        rows = slice(HEAD * head, HEAD * head + HEAD)
        turned_grad[rows, :] = nn_dot(turned_keys[rows, :], raw_scratch[...])
        if head == 1:
            query_out = (turned_grad[...].T * scale).astype(low)
            value_out = pair_values[...].astype(low)
            proj[0, :, lanes] = query_out
            proj[1, :, lanes] = (pair_keys[...] * scale).astype(low)
            proj[2, :, lanes] = value_out
            vector_rows[0].append(column_sum(query_out.astype(wide)))
            vector_rows[1].append(column_sum(value_out.astype(wide)))

    def projection_gradient(index):
        if index == 0:
            wait_loads(19, 21)
        rows = slice(index * full, (index + 1) * full)
        qkv_parts[rows, :] = nn_dot(x_t[...], proj[index]).astype(low)

    small_flight = []

    def own_half(vector):
        return jnp.where(core == 0, vector[:, :half], vector[:, half:])

    def start_small():
        small[...] = jnp.zeros_like(small)
        vectors = vector_rows[0] + vector_rows[1]
        vectors += [own_half(sums_one[2:3]), own_half(sums_two[2:3]), own_half(sums_one[1:2]), own_half(sums_two[1:2])]
        vectors += [unit_sums[0:1], own_half(sums_one[0:1]), own_half(sums_two[0:1]), count[0:1]]
        row = 0
        for vector in vectors:
            for start in range(0, vector.shape[1], 128):
                small[row : row + 1, :] = vector[:, start : start + 128]
                row += 1
        small_flight.append(send(small, small_recv.at[0], peer["x"]))

    def next_small():
        index = len(small_flight)
        if index == 0:
            start_small()
            return
        small_flight[-1].wait_recv()
        last = small if index == 1 else small_outer.at[index - 2]
        small_outer[index - 1] = last[...] + small_recv[index - 1]
        small_flight.append(send(small_outer.at[index - 1], small_recv.at[index], peer["xyvw"[index]]))

    input_flight = []

    def input_half(side):
        columns = aligned(half * side, half)
        return (
            nt_dot(proj[0], qkv_weight[0, columns, :])
            + nt_dot(proj[1], qkv_weight[1, columns, :])
            + nt_dot(proj[2], qkv_weight[2, columns, :])
        )

    def input_gradient(index):
        if index == 0:
            input_send[...] = input_half(1 - core).astype(low)
            input_flight.append(send(input_send, input_recv, to_core))
        else:
            input_grad[...] = input_half(core)

    small_totals = []
    square_flights = []

    def finish_small():
        small_flight[-1].wait_recv()
        small_total = small_outer[2] + small_recv[3]
        if outer > 1:
            small_outer[3] = small_total
            small_outer[4 + group] = small_total
            copies = [send(small_outer.at[3], small_outer.at[4 + group], to_group[d]) for d in range(1, outer)]
            for copy in copies:
                copy.wait_recv()
            small_total = small_outer[4]
            for index in range(1, outer):
                small_total = small_total + small_outer[4 + index]
        unit = 1.0 / (D * small_total[COUNT_ROW : COUNT_ROW + 1, 0:1])
        for index in range(24):
            row, lane = index // 3, index % 3
            source = 3 * row + lane if row < 6 else 12 + 3 * row + lane
            bias_out[row : row + 1, 128 * lane : 128 * lane + 128] = small_total[source : source + 1]
        for index in range(12):
            unit_out[:, 128 * index : 128 * index + 128] = jnp.broadcast_to(small_total[18 + index : 19 + index], (8, 128))
        inside_small = lax.broadcasted_iota(jnp.int32, small_total.shape, 0) < COUNT_ROW
        square = jnp.sum(
            jnp.sum(jnp.where(inside_small, small_total * small_total, 0.0), axis=0, keepdims=True), axis=1, keepdims=True
        )
        small_totals.extend([unit, square])
        input_flight[0].wait_recv()
        summed = input_grad[...] + input_recv[...].astype(wide)
        input_grad[...] = (summed.astype(low).astype(wide) + resid_grad[...]) * unit

    def next_square():
        index = len(square_flights)
        if index == 0:
            total_square = square_terms[0]
            for term in square_terms[1:]:
                total_square = total_square + term
            squares[0] = jnp.broadcast_to(total_square, (8, 128))
        else:
            square_flights[-1].wait_recv()
            squares[index] = squares[index - 1] + square_recv[index - 1]
        if index == 4:
            squares[4] = squares[4] + jnp.broadcast_to(small_totals[1], (8, 128))
        device = to_core if index == 4 else peer["xyvw"[index]]
        square_flights.append(send(squares.at[index], square_recv.at[index], device))
        if index == 0:
            finish_small()

    done = {"n": 0, "a": 0, "q": 0, "i": 0}
    for entry in SCHEDULE:
        if isinstance(entry, int):
            advance_piece(pieces[entry])
        elif entry == "l":
            start_loads()
        elif entry == "n":
            norm_back(done["n"])
        elif entry == "o":
            out_gradient()
        elif entry == "a":
            attend_head(done["a"] // 2, done["a"] % 2)
        elif entry == "q":
            projection_gradient(done["q"])
        elif entry == "i":
            input_gradient(done["i"])
        elif entry == "s":
            next_small()
        else:
            next_square()
        if entry in done:
            done[entry] += 1
    square_flights[-1].wait_recv()
    norm = jnp.sqrt(squares[4] + square_recv[4]) * small_totals[0]
    scalars[0:8] = small_totals[0] * clip_norm / jnp.maximum(norm, clip_norm)
    scalars[8:16] = norm
    for copy in pending:
        copy.wait_send()


def backward_call(outer, down, up, back, base, x_all, x_t, part, other, context, context_t, queries, keys_in, values, query_mark, key_mark, out_low, qkv_low, vectors, gates, logs, sums_two, unit_sums, count):
    low, wide = jnp.bfloat16, jnp.float32
    length, full = x_all.shape
    half = full // 2
    qkv_shape = (3 * full, half)
    out_shape = (half, full)
    big = [down, up, back, base, x_all, x_t, part, other, context, context_t, queries, keys_in, values, query_mark, key_mark, out_low, qkv_low]
    little = [vectors, gates, logs, sums_two, unit_sums, count]
    vmem = pl.BlockSpec(memory_space=pltpu.VMEM)
    hbm = pl.BlockSpec(memory_space=pl.ANY)
    sizes = [(shape[0] // 3, shape[1], 4) for shape in (down.shape, up.shape) for _ in range(3)]
    split = qkv_shape[0] * 5 // 9
    sizes += [(split, half, 4), (qkv_shape[0] - split, half, 4), (half, full // 3, 3), (half, full // 3 * 2, 3)]
    copies = sum(4 + halvings + (outer - 1) for _, _, halvings in sizes) + 2 + 4 + (outer - 1) + 5
    lasts = [(rows // 2**halvings, columns) for rows, columns, halvings in sizes]
    spare = [(outer,) + last if outer > 1 else (1, 8, 128) for last in lasts]
    scratch = [pltpu.VMEM(a.shape, a.dtype) for a in big[3:]]
    scratch += [
        pltpu.VMEM(back.shape, low),
        pltpu.VMEM(back.shape, low),
        pltpu.VMEM((3, down.shape[0] // 6, down.shape[1]), low),
        pltpu.VMEM((3, up.shape[0] // 6, up.shape[1]), low),
        pltpu.VMEM((length, full), low),
        pltpu.VMEM((length, half), low),
        pltpu.VMEM((8, length), wide),
        pltpu.VMEM((8, full), wide),
        pltpu.VMEM((length, length), low),
        pltpu.VMEM((2 * HEAD, length), low),
        pltpu.VMEM((2 * HEAD, length), wide),
        pltpu.VMEM((length, 2 * HEAD), wide),
        pltpu.VMEM((length, 2 * HEAD), wide),
        pltpu.VMEM((3, length, half), low),
        pltpu.VMEM(qkv_shape, low),
        pltpu.VMEM(out_shape, low),
        pltpu.VMEM((length, half), low),
        pltpu.VMEM((length, half), low),
        pltpu.VMEM((SMALL_ROWS, 128), wide),
        pltpu.VMEM((4, SMALL_ROWS, 128), wide),
        pltpu.VMEM((4 + outer, SMALL_ROWS, 128), wide),
        pltpu.VMEM((5, 8, 128), wide),
        pltpu.VMEM((5, 8, 128), wide),
        pltpu.VMEM((length, half), wide),
        tuple(pltpu.VMEM(shape, low) for shape in spare),
        pltpu.SemaphoreType.DMA((copies,)),
        pltpu.SemaphoreType.DMA((copies,)),
        pltpu.SemaphoreType.DMA((len(big) + 6,)),
        pltpu.SemaphoreType.DMA((12,)),
    ]
    for size in sizes:
        scratch += piece_buffers(*size)
    return pl.pallas_call(
        functools.partial(backward_kernel, outer),
        out_shape=[
            jax.ShapeDtypeStruct(down.shape, low),
            jax.ShapeDtypeStruct(up.shape, low),
            jax.ShapeDtypeStruct(qkv_shape, low),
            jax.ShapeDtypeStruct(out_shape, low),
            jax.ShapeDtypeStruct((8, half), wide),
            jax.ShapeDtypeStruct((8, unit_sums.shape[1]), wide),
            jax.ShapeDtypeStruct((16, 128), wide),
            jax.ShapeDtypeStruct((length, half), wide),
        ],
        in_specs=[hbm] * len(big) + [vmem] * len(little),
        out_specs=[hbm] * 4 + [vmem] * 4,
        scratch_shapes=scratch,
        compiler_params=pltpu.CompilerParams(
            collective_id=0, has_side_effects=True, vmem_limit_bytes=(51 if outer == 1 else 60) * 2**20
        ),
        cost_estimate=pl.CostEstimate(flops=2 * 10**10, bytes_accessed=3 * 10**8, transcendentals=7 * 10**6),
        name="backward_rows",
    )(*big, *little)


def on_device(
    hidden_in,
    teacher_in,
    segment_ids,
    pad_mask,
    qkv_weight,
    qkv_moment1,
    qkv_moment2,
    out_weight,
    out_moment1,
    out_moment2,
    up_weight,
    up_moment1,
    up_moment2,
    down_weight,
    down_moment1,
    down_moment2,
    bias_vectors,
    bias_moment1,
    bias_moment2,
    up_bias,
    up_bias_moment1,
    up_bias_moment2,
    norm_gains,
    gain_moment1,
    gain_moment2,
    head_gates,
    layer_gates,
    dim_gates,
    unit_gates,
    teacher_qkv,
    teacher_out,
    teacher_up,
    teacher_down,
    teacher_biases,
    teacher_up_bias,
    teacher_gains,
):
    length = segment_ids.shape[1]
    width = hidden_in.shape[2]
    wide = jnp.float32
    hidden = up_bias.shape[0]
    lines = jnp.stack([up_bias, unit_gates, teacher_up_bias.astype(wide), jnp.pad(dim_gates, (0, hidden - width))])
    (
        teacher_part, teacher_other, teacher_x, part, x_all, x_turned, queries, keys_in, values, context, context_turned,
        up_low, down_low, out_low, qkv_low, logs, query_mark, key_mark, valid, vectors, teacher_vectors, gate_rows, count,
    ) = attend_rows_call(
        teacher_in[0], hidden_in[0], teacher_qkv, teacher_out, qkv_weight, out_weight, up_weight, down_weight,
        segment_ids, pad_mask, bias_vectors, norm_gains, lines, teacher_biases, teacher_gains, head_gates, layer_gates,
    )
    part_other, base, back, grad_down, grad_up, block_out, sums_two, unit_sums = feed_rows_call(
        teacher_x, teacher_part, teacher_other, x_all, part, teacher_up, teacher_down, up_low, down_low,
        valid, vectors, teacher_vectors, lines,
    )
    rows_all = lax.axis_size("rows")
    down_sum, up_sum, qkv_sum, out_sum, bias_sum, unit_sum, scalars, input_grad = backward_call(
        rows_all // INNER, grad_down, grad_up, back, base, x_all, x_turned, part, part_other, context, context_turned,
        queries, keys_in, values, query_mark, key_mark, out_low, qkv_low, vectors, gate_rows, logs,
        sums_two, unit_sums, count,
    )
    grad_norm = scalars[8, 0]
    factor = scalars[0:1, 0:1]
    weight_sums = (qkv_sum.reshape(qkv_weight.shape), out_sum, up_sum, down_sum)
    weights = (qkv_weight, out_weight, up_weight, down_weight)
    firsts = (qkv_moment1, out_moment1, up_moment1, down_moment1)
    seconds = (qkv_moment2, out_moment2, up_moment2, down_moment2)
    rates = (rate_attend, rate_output, rate_expand, rate_reduce)
    results = []
    for index in range(4):
        clipped = weight_sums[index].astype(wide) * factor
        new_weight, new_second = adam_step(
            weights[index], firsts[index], seconds[index], clipped, rates[index], weight_decay
        )
        results.append((clipped, new_weight, new_second))
    vector_results = vector_adam(
        scalars, bias_sum, unit_sum, bias_vectors, bias_moment1, bias_moment2, up_bias, up_bias_moment1, up_bias_moment2,
        norm_gains, gain_moment1, gain_moment2,
    )
    results += [vector_results[0:3], vector_results[3:6], vector_results[6:9]]
    block_out = block_out.reshape(hidden_in.shape)
    input_grad = input_grad.reshape(hidden_in.shape)
    return (
        block_out,
        input_grad,
        grad_norm,
        results[0][0],
        results[0][1],
        results[0][2],
        results[1][0],
        results[1][1],
        results[1][2],
        results[2][0],
        results[2][1],
        results[2][2],
        results[3][0],
        results[3][1],
        results[3][2],
        results[4][0],
        results[4][1],
        results[4][2],
        results[5][0],
        results[5][1],
        results[5][2],
        results[6][0],
        results[6][1],
        results[6][2],
        results[0][1].astype(jnp.bfloat16),
        results[1][1].astype(jnp.bfloat16),
        results[2][1].astype(jnp.bfloat16),
        results[3][1].astype(jnp.bfloat16),
    )


def solution(mesh):
    in_specs = (
        P("rows", None, "hid"),
        P("rows", None, "hid"),
        P("rows", None),
        P("rows", None),
        P(None, None, "hid"),
        P(None, None, "hid"),
        P(None, None, "hid"),
        P("hid", None),
        P("hid", None),
        P("hid", None),
        P(None, "hid"),
        P(None, "hid"),
        P(None, "hid"),
        P("hid", None),
        P("hid", None),
        P("hid", None),
        P(None, "hid"),
        P(None, "hid"),
        P(None, "hid"),
        P("hid"),
        P("hid"),
        P("hid"),
        P(None, "hid"),
        P(None, "hid"),
        P(None, "hid"),
        P("hid"),
        P(),
        P("hid"),
        P("hid"),
        P(None, None, "hid"),
        P("hid", None),
        P(None, "hid"),
        P("hid", None),
        P(None, "hid"),
        P("hid"),
        P(None, "hid"),
    )
    out_specs = (
        P("rows", None, "hid"),
        P("rows", None, "hid"),
        P(),
        P(None, None, "hid"),
        P(None, None, "hid"),
        P(None, None, "hid"),
        P("hid", None),
        P("hid", None),
        P("hid", None),
        P(None, "hid"),
        P(None, "hid"),
        P(None, "hid"),
        P("hid", None),
        P("hid", None),
        P("hid", None),
        P(None, "hid"),
        P(None, "hid"),
        P(None, "hid"),
        P("hid"),
        P("hid"),
        P("hid"),
        P(None, "hid"),
        P(None, "hid"),
        P(None, "hid"),
        P(None, None, "hid"),
        P("hid", None),
        P(None, "hid"),
        P("hid", None),
    )
    return jax.shard_map(
        on_device, mesh=mesh, in_specs=in_specs, out_specs=out_specs, check_vma=False
    )
```

```python
import functools

import jax
import jax.numpy as jnp
from jax import lax
from jax.experimental import pallas as pl
from jax.experimental.pallas import tpu as pltpu
from jax.sharding import PartitionSpec as P

D = 768
HEAD = 64
STEP = 10


epsilon_norm = 1e-06
masked_score = -1000000000.0
clip_norm = 0.001
beta_first = 0.9
beta_second = 0.999
adam_epsilon = 1e-08
weight_decay = 0.01
rate_attend = 0.03
rate_output = 0.2
rate_expand = 0.03
rate_reduce = 0.03
rate_vector = 0.3


def adam_step(weight, first, second, grad, rate, decay):
    first_new = beta_first * first + (1.0 - beta_first) * grad
    second_new = beta_second * second + (1.0 - beta_second) * grad * grad
    first_hat = first_new / (1.0 - beta_first**STEP)
    second_hat = second_new / (1.0 - beta_second**STEP)
    return (
        weight - rate * (first_hat / (jnp.sqrt(second_hat) + adam_epsilon) + decay * weight),
        second_new,
    )


MARKS = 128
TILE = 256


def nt_dot(left, right):
    return lax.dot_general(
        left, right, (((1,), (1,)), ((), ())), preferred_element_type=jnp.float32
    )


def nn_dot(left, right):
    return jnp.dot(left, right, preferred_element_type=jnp.float32)


def aligned(start, size):
    return pl.ds(pl.multiple_of(start, 16), size)


def lanes_of(core, width):
    return pl.ds(pl.multiple_of(core * width, 128), width)


class Mover:
    def __init__(self, local_sems, send_sems, recv_sems):
        self.local_sems, self.send_sems, self.recv_sems = local_sems, send_sems, recv_sems
        self.local_count = self.remote_count = 0
        self.sent = []

    def copy(self, source, target):
        moved = pltpu.make_async_copy(source, target, self.local_sems.at[self.local_count])
        self.local_count += 1
        moved.start()
        return moved

    def send(self, source, target, device):
        index = self.remote_count
        self.remote_count += 1
        moved = pltpu.make_async_remote_copy(
            src_ref=source, dst_ref=target, send_sem=self.send_sems.at[index],
            recv_sem=self.recv_sems.at[index], device_id=device, device_id_type=pl.DeviceIdType.MESH,
        )
        moved.start()
        self.sent.append(moved)
        return moved


def greet(core):
    barrier = pltpu.get_barrier_semaphore()
    to_core = {"hid": 1 - core}
    pl.semaphore_signal(barrier, inc=1, device_id=to_core, device_id_type=pl.DeviceIdType.MESH)
    pl.semaphore_wait(barrier, 1)
    return to_core


def attend_rows_kernel(
    teacher_in, hidden_in, teacher_qkv, teacher_out, qkv_weight, out_weight, up_weight, down_weight,
    segment_ref, padding_ref, bias_ref, gain_ref, dim_ref, teacher_bias_ref, teacher_gain_ref, head_gates, layer_gates,
    teacher_part_out, teacher_other_out, teacher_x_out, part_out, x_out, turned_out, query_out, key_out, value_out,
    context_out, context_turned_out, up_out, down_out, out_out, qkv_out,
    log_ref, query_mark_ref, key_mark_ref, valid_ref, vector_ref, teacher_vector_ref, gate_ref, count_ref,
    teacher_x, x_all, turned, query, key, value, context, context_turned, teacher_part, part,
    teacher_qkv_held, teacher_out_held, qkv_wide, out_wide, up_wide, down_wide, qkv_low, out_low, up_low, down_low,
    pack, spread, local_sems, send_sems, recv_sems,
):
    low, wide = jnp.bfloat16, jnp.float32
    core = lax.axis_index("hid")
    mover = Mover(local_sems, send_sems, recv_sems)
    length, width = hidden_in.shape
    here = lanes_of(core, width)
    to_core = greet(core)

    arriving = [mover.copy(teacher_in, teacher_x.at[:, here]), mover.send(teacher_in, teacher_x.at[:, here], to_core)]
    arriving_weights = [mover.copy(teacher_qkv, teacher_qkv_held), mover.copy(teacher_out, teacher_out_held)]
    arriving_student = [mover.copy(hidden_in, x_all.at[:, here]), mover.send(hidden_in, x_all.at[:, here], to_core)]
    casts = [
        (mover.copy(qkv_weight, qkv_wide), qkv_wide, qkv_low, qkv_out),
        (mover.copy(out_weight, out_wide), out_wide, out_low, out_out),
        (mover.copy(up_weight, up_wide), up_wide, up_low, up_out),
        (mover.copy(down_weight, down_wide), down_wide, down_low, down_out),
    ]
    leaving = []

    def cast(index):
        arrived, source, target, output = casts[index]
        arrived.wait()
        target[...] = source[...].astype(low)
        leaving.append(mover.copy(target, output))

    pack[0:4] = bias_ref[2:6]
    pack[4:6] = gain_ref[...]
    pack[6:7] = dim_ref[...].reshape(1, width)
    pack[7:8] = jnp.zeros_like(pack[7:8])
    pack[8:12] = teacher_bias_ref[2:6].astype(wide)
    pack[12:14] = teacher_gain_ref[...].astype(wide)
    pack[14:16] = jnp.zeros_like(pack[14:16])
    pack_flight = mover.send(pack, spread.at[:, here], to_core)
    spread[:, here] = pack[...]

    marks = lax.broadcasted_iota(jnp.int32, (MARKS, length), 0)
    same = jnp.broadcast_to(segment_ref[...], (MARKS, length)) == marks
    padding = jnp.broadcast_to(padding_ref[...], (MARKS, length))
    query_mark_ref[...] = jnp.where(same, 1.0, 0.0).T.astype(low)
    key_mark_ref[...] = jnp.where((same & (padding > 0)) | (marks >= 8), 0.0, masked_score).T.astype(low)
    valid_ref[...] = padding.astype(wide).T
    count_ref[...] = jnp.broadcast_to(jnp.sum(padding[0:8].astype(wide), axis=1, keepdims=True), (8, 128))

    pair = 2 * HEAD
    pairs = width // pair
    block_rows = length // 2
    first_head = lax.broadcasted_iota(jnp.int32, (1, pair), 1) < HEAD
    gate_ref[...] = jnp.zeros_like(gate_ref)
    for number in range(pairs):
        row = jnp.where(first_head, head_gates[2 * number], head_gates[2 * number + 1])
        gate_ref[0:1, number * pair : (number + 1) * pair] = row
        gate_ref[1:2, number * pair : (number + 1) * pair] = 1.0 / row

    def project(x_ref, weights, query_bias, value_bias):
        rows = x_ref[...]
        query[...] = (nn_dot(rows, weights[0]) + query_bias).astype(low)
        key[...] = nn_dot(rows, weights[1]).astype(low)
        value[...] = (nn_dot(rows, weights[2]) + value_bias).astype(low)

    def attend(number, keep):
        lanes = slice(number * pair, (number + 1) * pair)
        scaled = query[:, lanes] * jnp.asarray(HEAD ** (-0.5), low)
        key_wide = jnp.concatenate([key[:, lanes], key_mark_ref[...]], axis=1)
        values = value[:, lanes]
        logs = []
        for start in range(0, length, block_rows):
            block = slice(start, start + block_rows)
            outs, columns = [], []
            for head in range(2):
                chosen = jnp.where(first_head if head == 0 else ~first_head, scaled[block], jnp.zeros_like(scaled[block]))
                query_wide = jnp.concatenate([chosen, query_mark_ref[block]], axis=1)
                scores = nt_dot(query_wide, key_wide)
                top = jnp.max(scores, axis=1, keepdims=True)
                weights = jnp.exp(scores - top)
                sums = jnp.sum(weights, axis=1, keepdims=True)
                outs.append(nn_dot(weights.astype(low), values) * (1.0 / sums))
                if keep:
                    columns.append(top + jnp.log(sums))
            mixed = jnp.where(first_head, outs[0], outs[1])
            if keep:
                mixed = mixed * gate_ref[0:1, lanes]
                logs.append(jnp.where(first_head, columns[0], columns[1]))
            mixed = mixed.astype(low)
            context[block, lanes] = mixed
            if keep:
                context_turned[lanes, block] = mixed.T
        if keep:
            log_turned = jnp.concatenate(logs, axis=0).T
            log_ref[8 * number : 8 * number + 8] = jnp.concatenate(
                [log_turned[0:1], log_turned[HEAD : HEAD + 1], log_turned[0:6]], axis=0
            )

    for moved in arriving[:1] + arriving_weights[:1]:
        moved.wait()
    arriving[1].wait_recv()
    leaving.append(mover.copy(teacher_x, teacher_x_out))
    project(teacher_x, teacher_qkv_held, teacher_bias_ref[0:1].astype(wide), teacher_bias_ref[1:2].astype(wide))
    for number in range(pairs):
        attend(number, False)
        cast(number)
    arriving_weights[1].wait()
    teacher_part[...] = nn_dot(context[...], teacher_out_held[...]).astype(low)
    teacher_flight = mover.send(teacher_part, teacher_other_out, to_core)
    leaving.append(mover.copy(teacher_part, teacher_part_out))

    arriving_student[0].wait()
    arriving_student[1].wait_recv()
    leaving.append(mover.copy(x_all, x_out))
    project(x_all, qkv_low, bias_ref[0:1], bias_ref[1:2])
    leaving.append(mover.copy(query, query_out))
    leaving.append(mover.copy(key, key_out))
    leaving.append(mover.copy(value, value_out))
    turned[...] = x_all[...].T
    leaving.append(mover.copy(turned, turned_out))
    for number in range(pairs):
        attend(number, True)
        if number == 0:
            cast(3)
    part[...] = nn_dot(context[...], out_low[...]).astype(low)
    leaving.append(mover.copy(part, part_out))
    leaving.append(mover.copy(context, context_out))
    leaving.append(mover.copy(context_turned, context_turned_out))

    pack_flight.wait_recv()
    dims = spread[6:7]
    ones = jnp.ones_like(dims)
    for target, rows, scales in (
        (vector_ref, spread[0:8], (layer_gates[0] * dims, layer_gates[1] * dims)),
        (teacher_vector_ref, spread[8:16], (ones, ones)),
    ):
        target[...] = jnp.concatenate(
            [scales[0], rows[0:1], rows[4:5], rows[2:3], scales[1], rows[1:2], rows[5:6], rows[3:4]], axis=0
        )
    teacher_flight.wait_recv()
    for moved in leaving:
        moved.wait()
    for moved in mover.sent:
        moved.wait_send()


def attend_rows_call(teacher_in, hidden_in, teacher_qkv, teacher_out, qkv_weight, out_weight, up_weight, down_weight, segment, padding, biases, gains, dims, teacher_biases, teacher_gains, head_gates, layer_gates):
    low, wide = jnp.bfloat16, jnp.float32
    length, width = hidden_in.shape
    full = 2 * width
    pairs = width // (2 * HEAD)
    hidden = up_weight.shape[1]
    vmem, anywhere = pl.BlockSpec(memory_space=pltpu.VMEM), pl.BlockSpec(memory_space=pl.ANY)
    smem = pl.BlockSpec(memory_space=pltpu.SMEM)
    rows_full, rows_half = (length, full), (length, width)
    far = [rows_full] * 5 + [(full, length)] + [rows_half] * 4 + [(width, length)]
    far += [up_weight.shape, down_weight.shape, out_weight.shape, qkv_weight.shape]
    near = [
        ((8 * pairs, length), wide), ((length, MARKS), low), ((length, MARKS), low), ((length, MARKS), wide),
        ((8, full), wide), ((8, full), wide), ((8, width), wide), ((8, 128), wide),
    ]
    held = [rows_full, rows_full, (full, length), rows_half, rows_half, rows_half, rows_half, (width, length), rows_full, rows_full]
    return pl.pallas_call(
        attend_rows_kernel,
        out_shape=[jax.ShapeDtypeStruct(shape, low) for shape in far] + [jax.ShapeDtypeStruct(*pair) for pair in near],
        in_specs=[anywhere] * 8 + [vmem] * 7 + [smem] * 2,
        out_specs=[anywhere] * len(far) + [vmem] * len(near),
        scratch_shapes=[pltpu.VMEM(shape, low) for shape in held]
        + [pltpu.VMEM(teacher_qkv.shape, low), pltpu.VMEM(teacher_out.shape, low)]
        + [pltpu.VMEM(w.shape, wide) for w in (qkv_weight, out_weight, up_weight, down_weight)]
        + [pltpu.VMEM(w.shape, low) for w in (qkv_weight, out_weight, up_weight, down_weight)]
        + [pltpu.VMEM((16, width), wide), pltpu.VMEM((16, full), wide)]
        + [pltpu.SemaphoreType.DMA((24,)), pltpu.SemaphoreType.DMA((4,)), pltpu.SemaphoreType.DMA((4,))],
        compiler_params=pltpu.CompilerParams(collective_id=1, has_side_effects=True, vmem_limit_bytes=60 * 2**20),
        cost_estimate=pl.CostEstimate(flops=2 * 10**10, bytes_accessed=5 * 10**7, transcendentals=14 * 10**6),
        name="attend_rows",
    )(
        teacher_in, hidden_in, teacher_qkv, teacher_out, qkv_weight, out_weight, up_weight, down_weight,
        segment, padding, biases, gains, dims, teacher_biases, teacher_gains, head_gates, layer_gates,
    )


def norm_parts(resid):
    center = jnp.mean(resid, axis=1, keepdims=True)
    second = jnp.mean(resid * resid, axis=1, keepdims=True)
    inverse = lax.rsqrt(second - center * center + epsilon_norm)
    return (resid - center) * inverse, inverse


def norm_grad(grad_normed, normed, inverse):
    center = jnp.mean(grad_normed, axis=1, keepdims=True)
    crossed = jnp.mean(grad_normed * normed, axis=1, keepdims=True)
    return inverse * (grad_normed - center - normed * crossed)


def column_sum(value):
    return jnp.sum(value, axis=0, keepdims=True)


def feed_rows_kernel(
    teacher_x_in, teacher_part_in, teacher_other_in, x_in, part_in, teacher_up_in, teacher_down_in, up_in, down_in,
    valid_ref, vector_ref, teacher_vector_ref, up_bias_ref, unit_gate_ref, teacher_up_bias_ref,
    other_out, base_out, back_out, grad_down_out, grad_up_out, block_ref, sums_ref, unit_sums_ref,
    teacher_x, teacher_part, teacher_other, x_all, part, other, teacher_up, teacher_down, up, down,
    teacher_first, first, teacher_reduced, teacher_reduced_other, reduced, reduced_other, slope, activated_turned,
    first_turned, grad_reduced, grad_expanded, base, back, grad_down, grad_up, local_sems, send_sems, recv_sems,
):
    low, wide = jnp.bfloat16, jnp.float32
    core = lax.axis_index("hid")
    mover = Mover(local_sems, send_sems, recv_sems)
    length, full = x_in.shape
    half = full // 2
    up_bias, unit_gate, teacher_up_bias = (r[...].reshape(1, r.shape[0]) for r in (up_bias_ref, unit_gate_ref, teacher_up_bias_ref))
    to_core = greet(core)
    part_flight = mover.send(part_in, other, to_core)
    tiles = [slice(start, start + TILE) for start in range(0, length, TILE)]
    teacher_rows = ((teacher_x_in, teacher_x), (teacher_part_in, teacher_part), (teacher_other_in, teacher_other))
    tile_loads = [[mover.copy(source.at[tiles[0]], target.at[tiles[0]]) for source, target in teacher_rows]]
    up_load = mover.copy(teacher_up_in, teacher_up)
    down_load = mover.copy(teacher_down_in, teacher_down)
    rest = slice(TILE, length)
    tile_loads.append([mover.copy(source.at[rest], target.at[rest]) for source, target in teacher_rows])
    loads = [
        mover.copy(source, target) for source, target in ((x_in, x_all), (part_in, part), (up_in, up), (down_in, down))
    ]

    def norm_one(x_ref, own_ref, far_ref, vectors, block):
        branch = own_ref[block].astype(wide) + far_ref[block].astype(wide)
        normed, _ = norm_parts(x_ref[block].astype(wide) + (branch + vectors[1:2]) * vectors[0:1])
        return normed * vectors[2:3] + vectors[3:4]

    def gelu_share(expanded):
        return 0.5 + 0.5 * lax.erf(expanded * (0.5**0.5))

    teacher_flights = []
    for index, block in enumerate(tiles):
        if index < 2:
            for moved in tile_loads[index]:
                moved.wait()
        out = norm_one(teacher_x, teacher_part, teacher_other, teacher_vector_ref, block)
        teacher_first[block] = out
        if index == 0:
            up_load.wait()
        expanded = nn_dot(out.astype(low), teacher_up[...]) + teacher_up_bias
        activated = (expanded * gelu_share(expanded)).astype(low)
        if index == 0:
            down_load.wait()
        teacher_reduced[block] = nn_dot(activated, teacher_down[...]).astype(low)
        teacher_flights.append(mover.send(teacher_reduced.at[block], teacher_reduced_other.at[block], to_core))
    for moved in loads:
        moved.wait()
    part_flight.wait_recv()
    leaving = [mover.copy(other, other_out)]
    flights = []
    for block in tiles:
        out = norm_one(x_all, part, other, vector_ref, block)
        first[block] = out
        out_low = out.astype(low)
        first_turned[:, block] = out_low.T
        expanded = nn_dot(out_low, up[...]) + up_bias
        share = gelu_share(expanded)
        activated = (expanded * share * unit_gate).astype(low)
        reduced[block] = nn_dot(activated, down[...]).astype(low)
        flights.append(mover.send(reduced.at[block], reduced_other.at[block], to_core))
        activated_turned[:, block] = activated.T
        bell = jnp.exp(-0.5 * expanded * expanded)
        slope[block] = ((share + expanded * bell * 0.3989422804014327) * unit_gate).astype(low)

    sums_ref[...] = jnp.zeros_like(sums_ref)
    unit_sums_ref[...] = jnp.zeros_like(unit_sums_ref)
    for index, block in enumerate(tiles):
        teacher_flights[index].wait_recv()
        flights[index].wait_recv()
        student_first, target_first = first[block], teacher_first[block]
        branch = reduced[block].astype(wide) + reduced_other[block].astype(wide)
        normed, inverse = norm_parts(student_first + (branch + vector_ref[5:6]) * vector_ref[4:5])
        second = normed * vector_ref[6:7] + vector_ref[7:8]
        target_branch = teacher_reduced[block].astype(wide) + teacher_reduced_other[block].astype(wide)
        target_normed, _ = norm_parts(target_first + target_branch + teacher_vector_ref[5:6])
        target = target_normed * teacher_vector_ref[6:7] + teacher_vector_ref[7:8]
        block_ref[block] = jnp.where(core == 0, second[:, :half], second[:, half:]).astype(low)
        twice = valid_ref[block, 0:1] * 2.0
        grad_second = twice * (second - target)
        grad_resid = norm_grad(grad_second * vector_ref[6:7], normed, inverse)
        grad_branch = grad_resid * vector_ref[4:5]
        sums_ref[0:1] += column_sum(grad_second * normed)
        sums_ref[1:2] += column_sum(grad_second)
        sums_ref[2:3] += column_sum(grad_branch)
        grad_branch_low = grad_branch.astype(low)
        grad_reduced[block] = grad_branch_low
        grad_activated = nt_dot(grad_branch_low, down[...]).astype(low).astype(wide)
        grad_unit = (grad_activated * slope[block].astype(wide)).astype(low)
        grad_expanded[block] = grad_unit
        unit_sums_ref[0:1] += column_sum(grad_unit.astype(wide))
        back[block] = nt_dot(grad_unit, up[...]).astype(low)
        base[block] = twice * (student_first - target_first) + grad_resid
        leaving.append(mover.copy(back.at[block], back_out.at[block]))
        leaving.append(mover.copy(base.at[block], base_out.at[block]))
    parts = 3
    rows = grad_down.shape[0] // parts
    for index in range(parts):
        block = slice(index * rows, (index + 1) * rows)
        grad_down[block] = nn_dot(activated_turned[block], grad_reduced[...]).astype(low)
        leaving.append(mover.copy(grad_down.at[block], grad_down_out.at[block]))
    rows = grad_up.shape[0] // parts
    for index in range(parts):
        block = slice(index * rows, (index + 1) * rows)
        grad_up[block] = nn_dot(first_turned[block], grad_expanded[...]).astype(low)
        leaving.append(mover.copy(grad_up.at[block], grad_up_out.at[block]))
    for moved in leaving:
        moved.wait()
    for moved in mover.sent:
        moved.wait_send()


def feed_rows_call(teacher_x, teacher_part, teacher_other, x_all, part, teacher_up, teacher_down, up_low, down_low, valid, vectors, teacher_vectors, up_bias, unit_gates, teacher_up_bias):
    low, wide = jnp.bfloat16, jnp.float32
    length, full = x_all.shape
    hidden = up_low.shape[1]
    vmem, anywhere = pl.BlockSpec(memory_space=pltpu.VMEM), pl.BlockSpec(memory_space=pl.ANY)
    rows = (length, full)
    up_shape, down_shape = up_low.shape, down_low.shape
    far = [(rows, low), (rows, wide), (rows, low), (down_shape, low), (up_shape, low)]
    near = [((length, full // 2), low), ((8, full), wide), ((8, hidden), wide)]
    held = [(rows, low)] * 6 + [(up_shape, low), (down_shape, low)] * 2
    held += [(rows, wide)] * 2 + [(rows, low)] * 4 + [((length, hidden), low), ((hidden, length), low), ((full, length), low)]
    held += [(rows, low), ((length, hidden), low), (rows, wide), (rows, low), (down_shape, low), (up_shape, low)]
    return pl.pallas_call(
        feed_rows_kernel,
        out_shape=[jax.ShapeDtypeStruct(*pair) for pair in far + near],
        in_specs=[anywhere] * 9 + [vmem] * 6,
        out_specs=[anywhere] * len(far) + [vmem] * len(near),
        scratch_shapes=[pltpu.VMEM(*pair) for pair in held]
        + [pltpu.SemaphoreType.DMA((32,)), pltpu.SemaphoreType.DMA((12,)), pltpu.SemaphoreType.DMA((12,))],
        compiler_params=pltpu.CompilerParams(collective_id=2, has_side_effects=True, vmem_limit_bytes=62 * 2**20),
        cost_estimate=pl.CostEstimate(flops=3 * 10**10, bytes_accessed=5 * 10**7, transcendentals=6 * 10**6),
        name="feed_rows",
    )(
        teacher_x, teacher_part, teacher_other, x_all, part, teacher_up, teacher_down, up_low, down_low,
        valid, vectors, teacher_vectors, up_bias, unit_gates, teacher_up_bias,
    )


def vector_adam_kernel(
    scalar_ref, bias_sum, unit_sum, bias, bias_first, bias_second, unit, unit_first, unit_second, gain, gain_first, gain_second,
    bias_grad, bias_new, bias_second_new, unit_grad, unit_new, unit_second_new, gain_grad, gain_new, gain_second_new,
):
    factor = scalar_ref[0:1, 0:1]
    for total, states, outs in (
        (bias_sum[0:6], (bias, bias_first, bias_second), (bias_grad, bias_new, bias_second_new)),
        (bias_sum[6:8], (gain, gain_first, gain_second), (gain_grad, gain_new, gain_second_new)),
        (unit_sum[0:1], (unit, unit_first, unit_second), (unit_grad, unit_new, unit_second_new)),
    ):
        clipped = total * factor
        values = [state[...].reshape(clipped.shape) for state in states]
        new_weight, new_second = adam_step(*values, clipped, rate_vector, 0.0)
        for target, value in zip(outs, (clipped, new_weight, new_second)):
            target[...] = value.reshape(target.shape)


def vector_adam(*arrays):
    shapes = [a.shape for a in arrays[3:12:3] for _ in range(3)]
    return pl.pallas_call(
        vector_adam_kernel,
        out_shape=[jax.ShapeDtypeStruct(shape, jnp.float32) for shape in shapes],
        cost_estimate=pl.CostEstimate(flops=10**5, bytes_accessed=3 * 10**5, transcendentals=10**4),
        name="vector_adam",
    )(*arrays)


INNER = 16
SMALL_ROWS = 40
COUNT_ROW = 36


class Piece:
    def __init__(self, source, target, first_row, rows, first_column, columns, order, own, halvings):
        self.source, self.target = source, target
        self.first_row, self.rows = first_row, rows
        self.first_column, self.columns = first_column, columns
        self.order, self.own, self.halvings = order, own, halvings


def piece_buffers(rows, columns, halvings):
    low, wide = jnp.bfloat16, jnp.float32
    last = rows // 16 if halvings == 4 else rows // 8
    return [
        pltpu.VMEM((rows // 2, columns), low),
        pltpu.VMEM((rows // 4, columns), low),
        pltpu.VMEM((rows // 8, columns), low),
        pltpu.VMEM((last, columns), low),
        pltpu.VMEM((rows // 4, columns), low),
        pltpu.VMEM((rows // 8, columns), low),
        pltpu.VMEM((last, columns), low),
        pltpu.VMEM((rows // 4, columns), wide),
        pltpu.VMEM((last, columns), low),
    ]


SCHEDULE = (
    3, 5, 4, 1, 0, "l", 2, "n", "n", "n", 3, 4, "n", "o", "a", "a", 1, 9, "a", 4, 3, 0, "a", 1, 2, 4, "a", 3, 8, 9, 5,
    0, 1, "a", 3, "q", 2, "q", 0, 6, 8, 1, "q", 7, 5, 4, 3, 1, 8, 4, 0, 2, 3, 1, "i", 6, "s", 9, 7, 4, 5, 2, 0, 1, 8, 6,
    7, 3, "s", 5, 2, 0, 6, 4, 7, 9, 8, "s", 5, 2, 6, 1, "s", 7, 0, 9, "i", 6, 8, 5, "S", 7, 2, "S", 9, 6, 7, 0, 8, 9, 5,
    6, 4, 7, 8, 9, "S", "S", "S", 2, 5, 7, 3, 6,
)


def backward_kernel(
    outer, down, up, back, base_in, x_in, x_t_in, part_in, other_in, context_in, context_t_in, query_in,
    key_in, value_in, query_mark_in, key_mark_in, out_weight_in, qkv_weight_in,
    vector_ref, gate_ref, log_ref, sums_two, unit_sums, count,
    down_sum, up_sum, qkv_sum, out_sum, bias_out, unit_out, scalars, input_grad,
    base, x, x_t, part, other, context, context_t, query,
    key, value, query_mark, key_mark, out_weight, qkv_weight,
    back_other, back_own, own_down, own_up, attended_grad, heads_grad, inner_rows, sums_one, raw_scratch, turned_keys,
    turned_grad, pair_keys, pair_values, proj, qkv_parts, out_parts, input_send, input_recv, small, small_recv,
    small_outer, squares, square_recv, resid_grad, shard_outer, send_sems, recv_sems, load_sems, shard_sems, *buffers,
):
    low, wide = jnp.bfloat16, jnp.float32
    place = lax.axis_index("rows")
    inside = place % INNER
    group = place // INNER
    core = lax.axis_index("hid")
    bits = {"x": inside % 2, "y": (inside // 2) % 2, "v": (inside // 4) % 2, "w": inside // 8}
    steps = {"x": 1, "y": 2, "v": 4, "w": 8}
    peer = {name: {"rows": place + steps[name] - 2 * steps[name] * bits[name]} for name in bits}
    to_group = [{"rows": inside + INNER * ((group + d) % outer)} for d in range(outer)]
    to_core = {"hid": 1 - core}
    barrier = pltpu.get_barrier_semaphore()
    peers = list(peer.values()) + to_group[1:] + [to_core]
    for there in peers:
        pl.semaphore_signal(barrier, inc=1, device_id=there, device_id_type=pl.DeviceIdType.MESH)
    pl.semaphore_wait(barrier, len(peers))

    counter = [0]
    pending = []

    def send(source, target, device):
        index = counter[0]
        counter[0] += 1
        copy = pltpu.make_async_remote_copy(
            src_ref=source, dst_ref=target, send_sem=send_sems.at[index],
            recv_sem=recv_sems.at[index], device_id=device, device_id_type=pl.DeviceIdType.MESH,
        )
        copy.start()
        pending.append(copy)
        return copy

    loads = []

    def load(source, target):
        copy = pltpu.make_async_copy(source, target, load_sems.at[len(loads)])
        copy.start()
        loads.append(copy)

    def wait_loads(first, last):
        for copy in loads[first:last]:
            copy.wait()

    orders = ("xyvw", "yxvw", "vxyw")
    orders_two = ("xyvw", "yxvw", "vyxw")
    pieces = []

    def add_piece(*fields):
        piece = Piece(*fields)
        piece.index, piece.step = len(pieces), 0
        piece.buffers = buffers[9 * piece.index : 9 * piece.index + 9]
        piece.offsets = [0]
        size = piece.rows
        for name in piece.order[: piece.halvings]:
            size = size // 2
            piece.offsets.append(piece.offsets[-1] + size * bits[name])
        pieces.append(piece)

    for source, target, held, lanes in ((down, down_sum, own_down, orders), (up, up_sum, own_up, orders_two)):
        rows = source.shape[0] // 3
        for lane in range(3):
            add_piece(source, target, rows * lane, rows, 0, source.shape[1], lanes[lane], held.at[lane], 4)
    columns = qkv_parts.shape[1]
    split = qkv_parts.shape[0] * 5 // 9
    add_piece(qkv_parts, qkv_sum, 0, split, 0, columns, orders[0], None, 4)
    add_piece(qkv_parts, qkv_sum, split, qkv_parts.shape[0] - split, 0, columns, orders[1], None, 4)
    split = out_parts.shape[1] // 3
    add_piece(out_parts, out_sum, 0, out_parts.shape[0], 0, split, orders[0], None, 3)
    add_piece(out_parts, out_sum, 0, out_parts.shape[0], split, 2 * split, orders[1], None, 3)

    square_terms = []

    def advance_piece(piece):
        r1, r2, r3, r4, s2, s3, s4, keep, shard = piece.buffers
        step = piece.step
        piece.step += 1
        order, rows = piece.order, piece.rows
        columns = pl.ds(piece.first_column, piece.columns)
        names_done = order[: piece.halvings]

        def own(start, size):
            if piece.own is not None:
                return piece.own[aligned(start, size), :].astype(wide)
            return piece.source[aligned(piece.first_row + piece.offsets[1] + start, size), columns].astype(wide)

        if step == 0:
            start = piece.first_row + rows // 2 * (1 - bits[order[0]])
            piece.flight = send(piece.source.at[aligned(start, rows // 2), columns], r1, peer[order[0]])
        elif step == 1:
            if piece.own is not None:
                wait_loads(piece.loaded, piece.loaded + 1)
            piece.flight.wait_recv()
            bit = bits[order[1]]
            size = rows // 4
            sent = size * (1 - bit)
            s2[...] = (own(sent, size) + r1[aligned(sent, size), :].astype(wide)).astype(low)
            piece.flight = send(s2, r2, peer[order[1]])
            kept = size * bit
            keep[...] = own(kept, size) + r1[aligned(kept, size), :].astype(wide)
        elif step == 2:
            piece.flight.wait_recv()
            keep[...] = keep[...] + r2[...].astype(wide)
            bit = bits[order[2]]
            size = rows // 8
            s3[...] = keep[aligned(size * (1 - bit), size), :].astype(low)
            piece.flight = send(s3, r3, peer[order[2]])
        elif step == 3:
            piece.flight.wait_recv()
            size = rows // 8
            mine = aligned(size * bits[order[2]], size)
            total = keep[mine, :] + r3[...].astype(wide)
            if piece.halvings == 4:
                keep[mine, :] = total
                small_size = size // 2
                sent = size * bits[order[2]] + small_size * (1 - bits[order[3]])
                s4[...] = keep[aligned(sent, small_size), :].astype(low)
            else:
                s4[...] = total.astype(low)
            piece.flight = send(s4, r4, peer[order[3]])
        elif step == 4:
            piece.flight.wait_recv()
            if piece.halvings == 4:
                size = rows // 16
                kept = rows // 8 * bits[order[2]] + size * bits[order[3]]
                total = keep[aligned(kept, size), :] + r4[...].astype(wide)
                weight = 1.0
            else:
                total = s4[...].astype(wide) + r4[...].astype(wide)
                weight = 0.5
            if outer > 1:
                shard[...] = total.astype(low)
                shard_outer[piece.index][0] = shard[...]
                copies = [send(shard, shard_outer[piece.index].at[d], to_group[d]) for d in range(1, outer)]
                for copy in copies:
                    copy.wait()
                    pending[:] = [entry for entry in pending if entry is not copy]
                total = jnp.zeros_like(total)
                for index in range(outer):
                    total = total + shard_outer[piece.index][(group - index + outer) % outer].astype(wide)
            shard[...] = total.astype(low)
            square_terms.append(weight * jnp.sum(jnp.sum(total * total, axis=0, keepdims=True), axis=1, keepdims=True))
            size = rows // 2**piece.halvings
            here = piece.target.at[aligned(piece.first_row + piece.offsets[-1], size), columns]
            piece.local = pltpu.make_async_copy(shard, here, shard_sems.at[piece.index])
            piece.local.start()
            piece.flight = send(shard, here, peer[names_done[-1]])
        elif step < 4 + piece.halvings:
            level = piece.halvings - (step - 4)
            piece.flight.wait_recv()
            if step == 5:
                piece.local.wait()
            size = rows // 2**level
            block = piece.target.at[aligned(piece.first_row + piece.offsets[level], size), columns]
            piece.flight = send(block, block, peer[names_done[level - 1]])
        elif step == 4 + piece.halvings:
            piece.flight.wait_recv()

    back_flight = []
    length, full = x.shape
    half = full // 2
    head_loads = ((base_in, base), (x_in, x), (part_in, part), (other_in, other), (back, back_own), (context_in, context), (out_weight_in, out_weight))
    mid_loads = ((context_t_in, context_t), (query_in, query), (key_in, key), (value_in, value), (query_mark_in, query_mark), (key_mark_in, key_mark))
    late_loads = ((x_t_in, x_t), (qkv_weight_in, qkv_weight))

    def start_loads():
        back_flight.append(send(back, back_other, to_core))
        for pair in head_loads:
            load(*pair)
        for piece in pieces:
            if piece.own is not None:
                piece.loaded = len(loads)
                load(piece.source.at[aligned(piece.first_row + piece.offsets[1], piece.rows // 2), :], piece.own)
        for pair in mid_loads + late_loads:
            load(*pair)
        back_flight[0].wait_recv()
        wait_loads(0, 7)
        sums_one[...] = jnp.zeros_like(sums_one)
        pair_keys[...] = jnp.zeros_like(pair_keys)
        pair_values[...] = jnp.zeros_like(pair_values)

    def norm_back(index):
        block = slice(index * TILE, (index + 1) * TILE)
        returned = (back_own[block, :].astype(wide) + back_other[block, :].astype(wide)).astype(low).astype(wide)
        grad_first = base[block, :] + returned
        branch = part[block, :].astype(wide) + other[block, :].astype(wide)
        resid = x[block, :].astype(wide) + (branch + vector_ref[1:2]) * vector_ref[0:1]
        normed, inverse = norm_parts(resid)
        grad_resid = norm_grad(grad_first * vector_ref[2:3], normed, inverse)
        resid_grad[block, :] = jnp.where(core == 0, grad_resid[:, :half], grad_resid[:, half:])
        grad_attended = grad_resid * vector_ref[0:1]
        sums_one[0:1] += column_sum(grad_first * normed)
        sums_one[1:2] += column_sum(grad_first)
        sums_one[2:3] += column_sum(grad_attended)
        grad_attended_low = grad_attended.astype(low)
        attended_grad[block, :] = grad_attended_low
        grad_heads = (nt_dot(grad_attended_low, out_weight[...]) * gate_ref[0:1]).astype(low)
        heads_grad[block, :] = grad_heads
        product = grad_heads.astype(wide) * context[block, :].astype(wide) * gate_ref[1:2]
        lane = lax.broadcasted_iota(jnp.int32, (1, 128), 1)
        columns = jnp.zeros((TILE, 128), wide)
        for pair in range(half // 128):
            some = product[:, 128 * pair : 128 * pair + 128]
            low_sum = jnp.sum(jnp.where(lane < HEAD, some, 0.0), axis=1, keepdims=True)
            high_sum = jnp.sum(jnp.where(lane < HEAD, 0.0, some), axis=1, keepdims=True)
            columns = jnp.where(lane == 2 * pair, low_sum, jnp.where(lane == 2 * pair + 1, high_sum, columns))
        inner_rows[:, block] = columns.T[0:8]

    def out_gradient():
        wait_loads(13, 19)
        out_parts[...] = nn_dot(context_t[...], attended_grad[...]).astype(low)

    pair_width = 2 * HEAD
    scale = HEAD ** (-0.5)
    vector_rows = [[], []]

    def attend_head(number, head):
        lanes = slice(number * pair_width, (number + 1) * pair_width)
        if head == 0:
            turned_keys[...] = key[:, lanes].T
        lane = lax.broadcasted_iota(jnp.int32, (1, pair_width), 1)
        mask = lane < HEAD if head == 0 else lane >= HEAD
        queries, grads = query[:, lanes], heads_grad[:, lanes]
        query_wide = jnp.concatenate([queries, query_mark[...]], axis=1)
        logs = log_ref[8 * number + head : 8 * number + head + 1, :]
        inner = inner_rows[2 * number + head : 2 * number + head + 1, :]

        for start in range(0, length, TILE):
            block = slice(start, start + TILE)
            zero = jnp.zeros((TILE, pair_width), low)
            chosen = jnp.where(mask, key[block, lanes] * jnp.asarray(scale, low), zero)
            key_wide = jnp.concatenate([chosen, key_mark[block, :]], axis=1)
            probs = jnp.exp(nt_dot(key_wide, query_wide) - logs)
            grad_probs = nt_dot(jnp.where(mask, value[block, lanes], zero), grads)
            grad_raw = (probs * (grad_probs - inner)).astype(low)
            raw_scratch[block, :] = grad_raw
            pair_keys[block, :] = jnp.where(mask, nn_dot(grad_raw, queries), pair_keys[block, :])
            pair_values[block, :] = jnp.where(mask, nn_dot(probs.astype(low), grads), pair_values[block, :])

        rows = slice(HEAD * head, HEAD * head + HEAD)
        turned_grad[rows, :] = nn_dot(turned_keys[rows, :], raw_scratch[...])
        if head == 1:
            query_out = (turned_grad[...].T * scale).astype(low)
            value_out = pair_values[...].astype(low)
            proj[0, :, lanes] = query_out
            proj[1, :, lanes] = (pair_keys[...] * scale).astype(low)
            proj[2, :, lanes] = value_out
            vector_rows[0].append(column_sum(query_out.astype(wide)))
            vector_rows[1].append(column_sum(value_out.astype(wide)))

    def projection_gradient(index):
        if index == 0:
            wait_loads(19, 21)
        rows = slice(index * full, (index + 1) * full)
        qkv_parts[rows, :] = nn_dot(x_t[...], proj[index]).astype(low)

    small_flight = []

    def own_half(vector):
        return jnp.where(core == 0, vector[:, :half], vector[:, half:])

    def start_small():
        small[...] = jnp.zeros_like(small)
        vectors = vector_rows[0] + vector_rows[1]
        vectors += [own_half(sums_one[2:3]), own_half(sums_two[2:3]), own_half(sums_one[1:2]), own_half(sums_two[1:2])]
        vectors += [unit_sums[0:1], own_half(sums_one[0:1]), own_half(sums_two[0:1]), count[0:1]]
        row = 0
        for vector in vectors:
            for start in range(0, vector.shape[1], 128):
                small[row : row + 1, :] = vector[:, start : start + 128]
                row += 1
        small_flight.append(send(small, small_recv.at[0], peer["x"]))

    def next_small():
        index = len(small_flight)
        if index == 0:
            start_small()
            return
        small_flight[-1].wait_recv()
        last = small if index == 1 else small_outer.at[index - 2]
        small_outer[index - 1] = last[...] + small_recv[index - 1]
        small_flight.append(send(small_outer.at[index - 1], small_recv.at[index], peer["xyvw"[index]]))

    input_flight = []

    def input_half(side):
        columns = aligned(half * side, half)
        return (
            nt_dot(proj[0], qkv_weight[0, columns, :])
            + nt_dot(proj[1], qkv_weight[1, columns, :])
            + nt_dot(proj[2], qkv_weight[2, columns, :])
        )

    def input_gradient(index):
        if index == 0:
            input_send[...] = input_half(1 - core).astype(low)
            input_flight.append(send(input_send, input_recv, to_core))
        else:
            input_grad[...] = input_half(core)

    small_totals = []
    square_flights = []

    def finish_small():
        small_flight[-1].wait_recv()
        small_total = small_outer[2] + small_recv[3]
        if outer > 1:
            small_outer[3] = small_total
            small_outer[4 + group] = small_total
            copies = [send(small_outer.at[3], small_outer.at[4 + group], to_group[d]) for d in range(1, outer)]
            for copy in copies:
                copy.wait_recv()
            small_total = small_outer[4]
            for index in range(1, outer):
                small_total = small_total + small_outer[4 + index]
        unit = 1.0 / (D * small_total[COUNT_ROW : COUNT_ROW + 1, 0:1])
        for index in range(24):
            row, lane = index // 3, index % 3
            source = 3 * row + lane if row < 6 else 12 + 3 * row + lane
            bias_out[row : row + 1, 128 * lane : 128 * lane + 128] = small_total[source : source + 1]
        for index in range(12):
            unit_out[:, 128 * index : 128 * index + 128] = jnp.broadcast_to(small_total[18 + index : 19 + index], (8, 128))
        inside_small = lax.broadcasted_iota(jnp.int32, small_total.shape, 0) < COUNT_ROW
        square = jnp.sum(
            jnp.sum(jnp.where(inside_small, small_total * small_total, 0.0), axis=0, keepdims=True), axis=1, keepdims=True
        )
        small_totals.extend([unit, square])
        input_flight[0].wait_recv()
        summed = input_grad[...] + input_recv[...].astype(wide)
        input_grad[...] = (summed.astype(low).astype(wide) + resid_grad[...]) * unit

    def next_square():
        index = len(square_flights)
        if index == 0:
            total_square = square_terms[0]
            for term in square_terms[1:]:
                total_square = total_square + term
            squares[0] = jnp.broadcast_to(total_square, (8, 128))
        else:
            square_flights[-1].wait_recv()
            squares[index] = squares[index - 1] + square_recv[index - 1]
        if index == 4:
            squares[4] = squares[4] + jnp.broadcast_to(small_totals[1], (8, 128))
        device = to_core if index == 4 else peer["xyvw"[index]]
        square_flights.append(send(squares.at[index], square_recv.at[index], device))
        if index == 0:
            finish_small()

    done = {"n": 0, "a": 0, "q": 0, "i": 0}
    for entry in SCHEDULE:
        if isinstance(entry, int):
            advance_piece(pieces[entry])
        elif entry == "l":
            start_loads()
        elif entry == "n":
            norm_back(done["n"])
        elif entry == "o":
            out_gradient()
        elif entry == "a":
            attend_head(done["a"] // 2, done["a"] % 2)
        elif entry == "q":
            projection_gradient(done["q"])
        elif entry == "i":
            input_gradient(done["i"])
        elif entry == "s":
            next_small()
        else:
            next_square()
        if entry in done:
            done[entry] += 1
    square_flights[-1].wait_recv()
    norm = jnp.sqrt(squares[4] + square_recv[4]) * small_totals[0]
    scalars[0:8] = small_totals[0] * clip_norm / jnp.maximum(norm, clip_norm)
    scalars[8:16] = norm
    for copy in pending:
        copy.wait_send()


def backward_call(outer, down, up, back, base, x_all, x_t, part, other, context, context_t, queries, keys_in, values, query_mark, key_mark, out_low, qkv_low, vectors, gates, logs, sums_two, unit_sums, count):
    low, wide = jnp.bfloat16, jnp.float32
    length, full = x_all.shape
    half = full // 2
    qkv_shape = (3 * full, half)
    out_shape = (half, full)
    big = [down, up, back, base, x_all, x_t, part, other, context, context_t, queries, keys_in, values, query_mark, key_mark, out_low, qkv_low]
    little = [vectors, gates, logs, sums_two, unit_sums, count]
    vmem = pl.BlockSpec(memory_space=pltpu.VMEM)
    hbm = pl.BlockSpec(memory_space=pl.ANY)
    sizes = [(shape[0] // 3, shape[1], 4) for shape in (down.shape, up.shape) for _ in range(3)]
    split = qkv_shape[0] * 5 // 9
    sizes += [(split, half, 4), (qkv_shape[0] - split, half, 4), (half, full // 3, 3), (half, full // 3 * 2, 3)]
    copies = sum(4 + halvings + (outer - 1) for _, _, halvings in sizes) + 2 + 4 + (outer - 1) + 5
    lasts = [(rows // 2**halvings, columns) for rows, columns, halvings in sizes]
    spare = [(outer,) + last if outer > 1 else (1, 8, 128) for last in lasts]
    scratch = [pltpu.VMEM(a.shape, a.dtype) for a in big[3:]]
    scratch += [
        pltpu.VMEM(back.shape, low),
        pltpu.VMEM(back.shape, low),
        pltpu.VMEM((3, down.shape[0] // 6, down.shape[1]), low),
        pltpu.VMEM((3, up.shape[0] // 6, up.shape[1]), low),
        pltpu.VMEM((length, full), low),
        pltpu.VMEM((length, half), low),
        pltpu.VMEM((8, length), wide),
        pltpu.VMEM((8, full), wide),
        pltpu.VMEM((length, length), low),
        pltpu.VMEM((2 * HEAD, length), low),
        pltpu.VMEM((2 * HEAD, length), wide),
        pltpu.VMEM((length, 2 * HEAD), wide),
        pltpu.VMEM((length, 2 * HEAD), wide),
        pltpu.VMEM((3, length, half), low),
        pltpu.VMEM(qkv_shape, low),
        pltpu.VMEM(out_shape, low),
        pltpu.VMEM((length, half), low),
        pltpu.VMEM((length, half), low),
        pltpu.VMEM((SMALL_ROWS, 128), wide),
        pltpu.VMEM((4, SMALL_ROWS, 128), wide),
        pltpu.VMEM((4 + outer, SMALL_ROWS, 128), wide),
        pltpu.VMEM((5, 8, 128), wide),
        pltpu.VMEM((5, 8, 128), wide),
        pltpu.VMEM((length, half), wide),
        tuple(pltpu.VMEM(shape, low) for shape in spare),
        pltpu.SemaphoreType.DMA((copies,)),
        pltpu.SemaphoreType.DMA((copies,)),
        pltpu.SemaphoreType.DMA((len(big) + 6,)),
        pltpu.SemaphoreType.DMA((12,)),
    ]
    for size in sizes:
        scratch += piece_buffers(*size)
    return pl.pallas_call(
        functools.partial(backward_kernel, outer),
        out_shape=[
            jax.ShapeDtypeStruct(down.shape, low),
            jax.ShapeDtypeStruct(up.shape, low),
            jax.ShapeDtypeStruct(qkv_shape, low),
            jax.ShapeDtypeStruct(out_shape, low),
            jax.ShapeDtypeStruct((8, half), wide),
            jax.ShapeDtypeStruct((8, unit_sums.shape[1]), wide),
            jax.ShapeDtypeStruct((16, 128), wide),
            jax.ShapeDtypeStruct((length, half), wide),
        ],
        in_specs=[hbm] * len(big) + [vmem] * len(little),
        out_specs=[hbm] * 4 + [vmem] * 4,
        scratch_shapes=scratch,
        compiler_params=pltpu.CompilerParams(
            collective_id=0, has_side_effects=True, vmem_limit_bytes=61 * 2**20
        ),
        cost_estimate=pl.CostEstimate(flops=2 * 10**10, bytes_accessed=3 * 10**8, transcendentals=7 * 10**6),
        name="backward_rows",
    )(*big, *little)


def on_device(
    hidden_in,
    teacher_in,
    segment_ids,
    pad_mask,
    qkv_weight,
    qkv_moment1,
    qkv_moment2,
    out_weight,
    out_moment1,
    out_moment2,
    up_weight,
    up_moment1,
    up_moment2,
    down_weight,
    down_moment1,
    down_moment2,
    bias_vectors,
    bias_moment1,
    bias_moment2,
    up_bias,
    up_bias_moment1,
    up_bias_moment2,
    norm_gains,
    gain_moment1,
    gain_moment2,
    head_gates,
    layer_gates,
    dim_gates,
    unit_gates,
    teacher_qkv,
    teacher_out,
    teacher_up,
    teacher_down,
    teacher_biases,
    teacher_up_bias,
    teacher_gains,
):
    length = segment_ids.shape[1]
    width = hidden_in.shape[2]
    wide = jnp.float32
    (
        teacher_part, teacher_other, teacher_x, part, x_all, x_turned, queries, keys_in, values, context, context_turned,
        up_low, down_low, out_low, qkv_low, logs, query_mark, key_mark, valid, vectors, teacher_vectors, gate_rows, count,
    ) = attend_rows_call(
        teacher_in[0], hidden_in[0], teacher_qkv, teacher_out, qkv_weight, out_weight, up_weight, down_weight,
        segment_ids, pad_mask, bias_vectors, norm_gains, dim_gates, teacher_biases, teacher_gains, head_gates, layer_gates,
    )
    part_other, base, back, grad_down, grad_up, block_out, sums_two, unit_sums = feed_rows_call(
        teacher_x, teacher_part, teacher_other, x_all, part, teacher_up, teacher_down, up_low, down_low,
        valid, vectors, teacher_vectors, up_bias, unit_gates, teacher_up_bias.astype(wide),
    )
    rows_all = lax.axis_size("rows")
    down_sum, up_sum, qkv_sum, out_sum, bias_sum, unit_sum, scalars, input_grad = backward_call(
        rows_all // INNER, grad_down, grad_up, back, base, x_all, x_turned, part, part_other, context, context_turned,
        queries, keys_in, values, query_mark, key_mark, out_low, qkv_low, vectors, gate_rows, logs,
        sums_two, unit_sums, count,
    )
    grad_norm = scalars[8, 0]
    factor = scalars[0:1, 0:1]
    weight_sums = (qkv_sum, out_sum, up_sum, down_sum)
    weights = (qkv_weight.reshape(qkv_sum.shape), out_weight, up_weight, down_weight)
    firsts = (qkv_moment1.reshape(qkv_sum.shape), out_moment1, up_moment1, down_moment1)
    seconds = (qkv_moment2.reshape(qkv_sum.shape), out_moment2, up_moment2, down_moment2)
    rates = (rate_attend, rate_output, rate_expand, rate_reduce)
    results = []
    for index in range(4):
        clipped = weight_sums[index].astype(wide) * factor
        new_weight, new_second = adam_step(
            weights[index], firsts[index], seconds[index], clipped, rates[index], weight_decay
        )
        results.append((clipped, new_weight, new_second, new_weight.astype(jnp.bfloat16)))
    results[0] = [value.reshape(qkv_weight.shape) for value in results[0]]
    vector_results = vector_adam(
        scalars, bias_sum, unit_sum, bias_vectors, bias_moment1, bias_moment2, up_bias, up_bias_moment1, up_bias_moment2,
        norm_gains, gain_moment1, gain_moment2,
    )
    results += [vector_results[0:3], vector_results[3:6], vector_results[6:9]]
    block_out = block_out.reshape(hidden_in.shape)
    input_grad = input_grad.reshape(hidden_in.shape)
    return (
        block_out,
        input_grad,
        grad_norm,
        results[0][0],
        results[0][1],
        results[0][2],
        results[1][0],
        results[1][1],
        results[1][2],
        results[2][0],
        results[2][1],
        results[2][2],
        results[3][0],
        results[3][1],
        results[3][2],
        results[4][0],
        results[4][1],
        results[4][2],
        results[5][0],
        results[5][1],
        results[5][2],
        results[6][0],
        results[6][1],
        results[6][2],
        results[0][3],
        results[1][3],
        results[2][3],
        results[3][3],
    )


def solution(mesh):
    in_specs = (
        P("rows", None, "hid"),
        P("rows", None, "hid"),
        P("rows", None),
        P("rows", None),
        P(None, None, "hid"),
        P(None, None, "hid"),
        P(None, None, "hid"),
        P("hid", None),
        P("hid", None),
        P("hid", None),
        P(None, "hid"),
        P(None, "hid"),
        P(None, "hid"),
        P("hid", None),
        P("hid", None),
        P("hid", None),
        P(None, "hid"),
        P(None, "hid"),
        P(None, "hid"),
        P("hid"),
        P("hid"),
        P("hid"),
        P(None, "hid"),
        P(None, "hid"),
        P(None, "hid"),
        P("hid"),
        P(),
        P("hid"),
        P("hid"),
        P(None, None, "hid"),
        P("hid", None),
        P(None, "hid"),
        P("hid", None),
        P(None, "hid"),
        P("hid"),
        P(None, "hid"),
    )
    out_specs = (
        P("rows", None, "hid"),
        P("rows", None, "hid"),
        P(),
        P(None, None, "hid"),
        P(None, None, "hid"),
        P(None, None, "hid"),
        P("hid", None),
        P("hid", None),
        P("hid", None),
        P(None, "hid"),
        P(None, "hid"),
        P(None, "hid"),
        P("hid", None),
        P("hid", None),
        P("hid", None),
        P(None, "hid"),
        P(None, "hid"),
        P(None, "hid"),
        P("hid"),
        P("hid"),
        P("hid"),
        P(None, "hid"),
        P(None, "hid"),
        P(None, "hid"),
        P(None, None, "hid"),
        P("hid", None),
        P(None, "hid"),
        P("hid", None),
    )
    return jax.shard_map(
        on_device, mesh=mesh, in_specs=in_specs, out_specs=out_specs, check_vma=False
    )
```

```python
import functools

import jax
import jax.numpy as jnp
from jax import lax
from jax.experimental import pallas as pl
from jax.experimental.pallas import tpu as pltpu
from jax.sharding import PartitionSpec as P

D = 768
HEAD = 64
STEP = 10


epsilon_norm = 1e-06
masked_score = -1000000000.0
clip_norm = 0.001
beta_first = 0.9
beta_second = 0.999
adam_epsilon = 1e-08
weight_decay = 0.01
rate_attend = 0.03
rate_output = 0.2
rate_expand = 0.03
rate_reduce = 0.03
rate_vector = 0.3


def adam_step(weight, first, second, grad, rate, decay):
    first_new = beta_first * first + (1.0 - beta_first) * grad
    second_new = beta_second * second + (1.0 - beta_second) * grad * grad
    first_hat = first_new / (1.0 - beta_first**STEP)
    second_hat = second_new / (1.0 - beta_second**STEP)
    return (
        weight - rate * (first_hat / (jnp.sqrt(second_hat) + adam_epsilon) + decay * weight),
        second_new,
    )


MARKS = 128
TILE = 256


def nt_dot(left, right):
    return lax.dot_general(
        left, right, (((1,), (1,)), ((), ())), preferred_element_type=jnp.float32
    )


def nn_dot(left, right):
    return jnp.dot(left, right, preferred_element_type=jnp.float32)


def aligned(start, size):
    return pl.ds(pl.multiple_of(start, 16), size)


def lanes_of(core, width):
    return pl.ds(pl.multiple_of(core * width, 128), width)


class Mover:
    def __init__(self, local_sems, send_sems, recv_sems):
        self.local_sems, self.send_sems, self.recv_sems = local_sems, send_sems, recv_sems
        self.local_count = self.remote_count = 0
        self.sent = []

    def copy(self, source, target):
        moved = pltpu.make_async_copy(source, target, self.local_sems.at[self.local_count])
        self.local_count += 1
        moved.start()
        return moved

    def send(self, source, target, device):
        index = self.remote_count
        self.remote_count += 1
        moved = pltpu.make_async_remote_copy(
            src_ref=source, dst_ref=target, send_sem=self.send_sems.at[index],
            recv_sem=self.recv_sems.at[index], device_id=device, device_id_type=pl.DeviceIdType.MESH,
        )
        moved.start()
        self.sent.append(moved)
        return moved


def greet(core):
    barrier = pltpu.get_barrier_semaphore()
    to_core = {"hid": 1 - core}
    pl.semaphore_signal(barrier, inc=1, device_id=to_core, device_id_type=pl.DeviceIdType.MESH)
    pl.semaphore_wait(barrier, 1)
    return to_core


def attend_rows_kernel(
    teacher_in, hidden_in, teacher_qkv, teacher_out, qkv_weight, out_weight, up_weight, down_weight,
    segment_ref, padding_ref, bias_ref, gain_ref, dim_ref, teacher_bias_ref, teacher_gain_ref, head_gates, layer_gates,
    teacher_part_out, teacher_other_out, teacher_x_out, part_out, x_out, turned_out, query_out, key_out, value_out,
    context_out, context_turned_out, up_out, down_out, out_out, qkv_out,
    log_ref, query_mark_ref, key_mark_ref, valid_ref, vector_ref, teacher_vector_ref, gate_ref, count_ref,
    teacher_x, x_all, turned, query, key, value, context, context_turned, teacher_part, part,
    teacher_qkv_held, teacher_out_held, qkv_wide, out_wide, up_wide, down_wide, qkv_low, out_low, up_low, down_low,
    pack, spread, local_sems, send_sems, recv_sems,
):
    low, wide = jnp.bfloat16, jnp.float32
    core = lax.axis_index("hid")
    mover = Mover(local_sems, send_sems, recv_sems)
    length, width = hidden_in.shape
    here = lanes_of(core, width)
    to_core = greet(core)

    arriving = [mover.copy(teacher_in, teacher_x.at[:, here]), mover.send(teacher_in, teacher_x.at[:, here], to_core)]
    arriving_weights = [mover.copy(teacher_qkv, teacher_qkv_held), mover.copy(teacher_out, teacher_out_held)]
    arriving_student = [mover.copy(hidden_in, x_all.at[:, here]), mover.send(hidden_in, x_all.at[:, here], to_core)]
    casts = [
        (mover.copy(qkv_weight, qkv_wide), qkv_wide, qkv_low, qkv_out),
        (mover.copy(out_weight, out_wide), out_wide, out_low, out_out),
        (mover.copy(up_weight, up_wide), up_wide, up_low, up_out),
        (mover.copy(down_weight, down_wide), down_wide, down_low, down_out),
    ]
    leaving = []

    def cast(index):
        arrived, source, target, output = casts[index]
        arrived.wait()
        target[...] = source[...].astype(low)
        leaving.append(mover.copy(target, output))

    pack[0:4] = bias_ref[2:6]
    pack[4:6] = gain_ref[...]
    pack[6:7] = dim_ref[...].reshape(1, width)
    pack[7:8] = jnp.zeros_like(pack[7:8])
    pack[8:12] = teacher_bias_ref[2:6].astype(wide)
    pack[12:14] = teacher_gain_ref[...].astype(wide)
    pack[14:16] = jnp.zeros_like(pack[14:16])
    pack_flight = mover.send(pack, spread.at[:, here], to_core)
    spread[:, here] = pack[...]

    marks = lax.broadcasted_iota(jnp.int32, (MARKS, length), 0)
    same = jnp.broadcast_to(segment_ref[...], (MARKS, length)) == marks
    padding = jnp.broadcast_to(padding_ref[...], (MARKS, length))
    query_mark_ref[...] = jnp.where(same, 1.0, 0.0).T.astype(low)
    key_mark_ref[...] = jnp.where((same & (padding > 0)) | (marks >= 8), 0.0, masked_score).T.astype(low)
    valid_ref[...] = padding.astype(wide).T
    count_ref[...] = jnp.broadcast_to(jnp.sum(padding[0:8].astype(wide), axis=1, keepdims=True), (8, 128))

    pair = 2 * HEAD
    pairs = width // pair
    block_rows = length // 2
    first_head = lax.broadcasted_iota(jnp.int32, (1, pair), 1) < HEAD
    gate_ref[...] = jnp.zeros_like(gate_ref)
    for number in range(pairs):
        row = jnp.where(first_head, head_gates[2 * number], head_gates[2 * number + 1])
        gate_ref[0:1, number * pair : (number + 1) * pair] = row
        gate_ref[1:2, number * pair : (number + 1) * pair] = 1.0 / row

    def project(x_ref, weights, query_bias, value_bias):
        rows = x_ref[...]
        query[...] = (nn_dot(rows, weights[0]) + query_bias).astype(low)
        key[...] = nn_dot(rows, weights[1]).astype(low)
        value[...] = (nn_dot(rows, weights[2]) + value_bias).astype(low)

    def attend(number, keep):
        lanes = slice(number * pair, (number + 1) * pair)
        scaled = query[:, lanes] * jnp.asarray(HEAD ** (-0.5), low)
        key_wide = jnp.concatenate([key[:, lanes], key_mark_ref[...]], axis=1)
        values = value[:, lanes]
        logs = []
        for start in range(0, length, block_rows):
            block = slice(start, start + block_rows)
            outs, columns = [], []
            for head in range(2):
                chosen = jnp.where(first_head if head == 0 else ~first_head, scaled[block], jnp.zeros_like(scaled[block]))
                query_wide = jnp.concatenate([chosen, query_mark_ref[block]], axis=1)
                scores = nt_dot(query_wide, key_wide)
                top = jnp.max(scores, axis=1, keepdims=True)
                weights = jnp.exp(scores - top)
                sums = jnp.sum(weights, axis=1, keepdims=True)
                outs.append(nn_dot(weights.astype(low), values) * (1.0 / sums))
                if keep:
                    columns.append(top + jnp.log(sums))
            mixed = jnp.where(first_head, outs[0], outs[1])
            if keep:
                mixed = mixed * gate_ref[0:1, lanes]
                logs.append(jnp.where(first_head, columns[0], columns[1]))
            mixed = mixed.astype(low)
            context[block, lanes] = mixed
            if keep:
                context_turned[lanes, block] = mixed.T
        if keep:
            log_turned = jnp.concatenate(logs, axis=0).T
            log_ref[8 * number : 8 * number + 8] = jnp.concatenate(
                [log_turned[0:1], log_turned[HEAD : HEAD + 1], log_turned[0:6]], axis=0
            )

    for moved in arriving[:1] + arriving_weights[:1]:
        moved.wait()
    arriving[1].wait_recv()
    leaving.append(mover.copy(teacher_x, teacher_x_out))
    project(teacher_x, teacher_qkv_held, teacher_bias_ref[0:1].astype(wide), teacher_bias_ref[1:2].astype(wide))
    for number in range(pairs):
        attend(number, False)
        cast(number)
    arriving_weights[1].wait()
    teacher_part[...] = nn_dot(context[...], teacher_out_held[...]).astype(low)
    teacher_flight = mover.send(teacher_part, teacher_other_out, to_core)
    leaving.append(mover.copy(teacher_part, teacher_part_out))

    arriving_student[0].wait()
    arriving_student[1].wait_recv()
    leaving.append(mover.copy(x_all, x_out))
    project(x_all, qkv_low, bias_ref[0:1], bias_ref[1:2])
    leaving.append(mover.copy(query, query_out))
    leaving.append(mover.copy(key, key_out))
    leaving.append(mover.copy(value, value_out))
    turned[...] = x_all[...].T
    leaving.append(mover.copy(turned, turned_out))
    for number in range(pairs):
        attend(number, True)
        if number == 0:
            cast(3)
    part[...] = nn_dot(context[...], out_low[...]).astype(low)
    leaving.append(mover.copy(part, part_out))
    leaving.append(mover.copy(context, context_out))
    leaving.append(mover.copy(context_turned, context_turned_out))

    pack_flight.wait_recv()
    dims = spread[6:7]
    ones = jnp.ones_like(dims)
    for target, rows, scales in (
        (vector_ref, spread[0:8], (layer_gates[0] * dims, layer_gates[1] * dims)),
        (teacher_vector_ref, spread[8:16], (ones, ones)),
    ):
        target[...] = jnp.concatenate(
            [scales[0], rows[0:1], rows[4:5], rows[2:3], scales[1], rows[1:2], rows[5:6], rows[3:4]], axis=0
        )
    teacher_flight.wait_recv()
    for moved in leaving:
        moved.wait()
    for moved in mover.sent:
        moved.wait_send()


def attend_rows_call(teacher_in, hidden_in, teacher_qkv, teacher_out, qkv_weight, out_weight, up_weight, down_weight, segment, padding, biases, gains, dims, teacher_biases, teacher_gains, head_gates, layer_gates):
    low, wide = jnp.bfloat16, jnp.float32
    length, width = hidden_in.shape
    full = 2 * width
    pairs = width // (2 * HEAD)
    hidden = up_weight.shape[1]
    vmem, anywhere = pl.BlockSpec(memory_space=pltpu.VMEM), pl.BlockSpec(memory_space=pl.ANY)
    smem = pl.BlockSpec(memory_space=pltpu.SMEM)
    rows_full, rows_half = (length, full), (length, width)
    far = [rows_full] * 5 + [(full, length)] + [rows_half] * 4 + [(width, length)]
    far += [up_weight.shape, down_weight.shape, out_weight.shape, qkv_weight.shape]
    near = [
        ((8 * pairs, length), wide), ((length, MARKS), low), ((length, MARKS), low), ((length, MARKS), wide),
        ((8, full), wide), ((8, full), wide), ((8, width), wide), ((8, 128), wide),
    ]
    held = [rows_full, rows_full, (full, length), rows_half, rows_half, rows_half, rows_half, (width, length), rows_full, rows_full]
    return pl.pallas_call(
        attend_rows_kernel,
        out_shape=[jax.ShapeDtypeStruct(shape, low) for shape in far] + [jax.ShapeDtypeStruct(*pair) for pair in near],
        in_specs=[anywhere] * 8 + [vmem] * 7 + [smem] * 2,
        out_specs=[anywhere] * len(far) + [vmem] * len(near),
        scratch_shapes=[pltpu.VMEM(shape, low) for shape in held]
        + [pltpu.VMEM(teacher_qkv.shape, low), pltpu.VMEM(teacher_out.shape, low)]
        + [pltpu.VMEM(w.shape, wide) for w in (qkv_weight, out_weight, up_weight, down_weight)]
        + [pltpu.VMEM(w.shape, low) for w in (qkv_weight, out_weight, up_weight, down_weight)]
        + [pltpu.VMEM((16, width), wide), pltpu.VMEM((16, full), wide)]
        + [pltpu.SemaphoreType.DMA((24,)), pltpu.SemaphoreType.DMA((4,)), pltpu.SemaphoreType.DMA((4,))],
        compiler_params=pltpu.CompilerParams(collective_id=1, has_side_effects=True, vmem_limit_bytes=60 * 2**20),
        cost_estimate=pl.CostEstimate(flops=2 * 10**10, bytes_accessed=5 * 10**7, transcendentals=14 * 10**6),
        name="attend_rows",
    )(
        teacher_in, hidden_in, teacher_qkv, teacher_out, qkv_weight, out_weight, up_weight, down_weight,
        segment, padding, biases, gains, dims, teacher_biases, teacher_gains, head_gates, layer_gates,
    )


def norm_parts(resid):
    center = jnp.mean(resid, axis=1, keepdims=True)
    second = jnp.mean(resid * resid, axis=1, keepdims=True)
    inverse = lax.rsqrt(second - center * center + epsilon_norm)
    return (resid - center) * inverse, inverse


def norm_grad(grad_normed, normed, inverse):
    center = jnp.mean(grad_normed, axis=1, keepdims=True)
    crossed = jnp.mean(grad_normed * normed, axis=1, keepdims=True)
    return inverse * (grad_normed - center - normed * crossed)


def column_sum(value):
    return jnp.sum(value, axis=0, keepdims=True)


def feed_rows_kernel(
    teacher_x_in, teacher_part_in, teacher_other_in, x_in, part_in, teacher_up_in, teacher_down_in, up_in, down_in,
    valid_ref, vector_ref, teacher_vector_ref, up_bias_ref, unit_gate_ref, teacher_up_bias_ref,
    other_out, base_out, back_out, activated_out, first_out, reduced_out, expanded_out, block_ref, sums_ref, unit_sums_ref,
    teacher_x, teacher_part, teacher_other, x_all, part, other, teacher_up, teacher_down, up, down,
    teacher_first, first, teacher_reduced, teacher_reduced_other, reduced, reduced_other, slope, activated_turned,
    first_turned, grad_reduced, grad_expanded, base, back, local_sems, send_sems, recv_sems,
):
    low, wide = jnp.bfloat16, jnp.float32
    core = lax.axis_index("hid")
    mover = Mover(local_sems, send_sems, recv_sems)
    length, full = x_in.shape
    half = full // 2
    up_bias, unit_gate, teacher_up_bias = (r[...].reshape(1, r.shape[0]) for r in (up_bias_ref, unit_gate_ref, teacher_up_bias_ref))
    to_core = greet(core)
    part_flight = mover.send(part_in, other, to_core)
    tiles = [slice(start, start + TILE) for start in range(0, length, TILE)]
    teacher_rows = ((teacher_x_in, teacher_x), (teacher_part_in, teacher_part), (teacher_other_in, teacher_other))
    tile_loads = [[mover.copy(source.at[tiles[0]], target.at[tiles[0]]) for source, target in teacher_rows]]
    up_load = mover.copy(teacher_up_in, teacher_up)
    down_load = mover.copy(teacher_down_in, teacher_down)
    rest = slice(TILE, length)
    tile_loads.append([mover.copy(source.at[rest], target.at[rest]) for source, target in teacher_rows])
    loads = [
        mover.copy(source, target) for source, target in ((x_in, x_all), (part_in, part), (up_in, up), (down_in, down))
    ]

    def norm_one(x_ref, own_ref, far_ref, vectors, block):
        branch = own_ref[block].astype(wide) + far_ref[block].astype(wide)
        normed, _ = norm_parts(x_ref[block].astype(wide) + (branch + vectors[1:2]) * vectors[0:1])
        return normed * vectors[2:3] + vectors[3:4]

    def gelu_share(expanded):
        return 0.5 + 0.5 * lax.erf(expanded * (0.5**0.5))

    teacher_flights = []
    for index, block in enumerate(tiles):
        if index < 2:
            for moved in tile_loads[index]:
                moved.wait()
        out = norm_one(teacher_x, teacher_part, teacher_other, teacher_vector_ref, block)
        teacher_first[block] = out
        if index == 0:
            up_load.wait()
        expanded = nn_dot(out.astype(low), teacher_up[...]) + teacher_up_bias
        activated = (expanded * gelu_share(expanded)).astype(low)
        if index == 0:
            down_load.wait()
        teacher_reduced[block] = nn_dot(activated, teacher_down[...]).astype(low)
        teacher_flights.append(mover.send(teacher_reduced.at[block], teacher_reduced_other.at[block], to_core))
    for moved in loads:
        moved.wait()
    part_flight.wait_recv()
    leaving = [mover.copy(other, other_out)]
    flights = []
    for block in tiles:
        out = norm_one(x_all, part, other, vector_ref, block)
        first[block] = out
        out_low = out.astype(low)
        first_turned[:, block] = out_low.T
        expanded = nn_dot(out_low, up[...]) + up_bias
        share = gelu_share(expanded)
        activated = (expanded * share * unit_gate).astype(low)
        reduced[block] = nn_dot(activated, down[...]).astype(low)
        flights.append(mover.send(reduced.at[block], reduced_other.at[block], to_core))
        activated_turned[:, block] = activated.T
        bell = jnp.exp(-0.5 * expanded * expanded)
        slope[block] = ((share + expanded * bell * 0.3989422804014327) * unit_gate).astype(low)
        leaving.append(mover.copy(activated_turned.at[:, block], activated_out.at[:, block]))
        leaving.append(mover.copy(first_turned.at[:, block], first_out.at[:, block]))

    sums_ref[...] = jnp.zeros_like(sums_ref)
    unit_sums_ref[...] = jnp.zeros_like(unit_sums_ref)
    for index, block in enumerate(tiles):
        teacher_flights[index].wait_recv()
        flights[index].wait_recv()
        student_first, target_first = first[block], teacher_first[block]
        branch = reduced[block].astype(wide) + reduced_other[block].astype(wide)
        normed, inverse = norm_parts(student_first + (branch + vector_ref[5:6]) * vector_ref[4:5])
        second = normed * vector_ref[6:7] + vector_ref[7:8]
        target_branch = teacher_reduced[block].astype(wide) + teacher_reduced_other[block].astype(wide)
        target_normed, _ = norm_parts(target_first + target_branch + teacher_vector_ref[5:6])
        target = target_normed * teacher_vector_ref[6:7] + teacher_vector_ref[7:8]
        block_ref[block] = jnp.where(core == 0, second[:, :half], second[:, half:]).astype(low)
        twice = valid_ref[block, 0:1] * 2.0
        grad_second = twice * (second - target)
        grad_resid = norm_grad(grad_second * vector_ref[6:7], normed, inverse)
        grad_branch = grad_resid * vector_ref[4:5]
        sums_ref[0:1] += column_sum(grad_second * normed)
        sums_ref[1:2] += column_sum(grad_second)
        sums_ref[2:3] += column_sum(grad_branch)
        grad_branch_low = grad_branch.astype(low)
        grad_reduced[block] = grad_branch_low
        grad_activated = nt_dot(grad_branch_low, down[...]).astype(low).astype(wide)
        grad_unit = (grad_activated * slope[block].astype(wide)).astype(low)
        grad_expanded[block] = grad_unit
        unit_sums_ref[0:1] += column_sum(grad_unit.astype(wide))
        back[block] = nt_dot(grad_unit, up[...]).astype(low)
        base[block] = twice * (student_first - target_first) + grad_resid
        leaving.append(mover.copy(back.at[block], back_out.at[block]))
        leaving.append(mover.copy(base.at[block], base_out.at[block]))
        leaving.append(mover.copy(grad_reduced.at[block], reduced_out.at[block]))
        leaving.append(mover.copy(grad_expanded.at[block], expanded_out.at[block]))
    for moved in leaving:
        moved.wait()
    for moved in mover.sent:
        moved.wait_send()


def feed_rows_call(teacher_x, teacher_part, teacher_other, x_all, part, teacher_up, teacher_down, up_low, down_low, valid, vectors, teacher_vectors, up_bias, unit_gates, teacher_up_bias):
    low, wide = jnp.bfloat16, jnp.float32
    length, full = x_all.shape
    hidden = up_low.shape[1]
    vmem, anywhere = pl.BlockSpec(memory_space=pltpu.VMEM), pl.BlockSpec(memory_space=pl.ANY)
    rows = (length, full)
    up_shape, down_shape = up_low.shape, down_low.shape
    far = [(rows, low), (rows, wide), (rows, low), ((hidden, length), low), ((full, length), low), (rows, low), ((length, hidden), low)]
    near = [((length, full // 2), low), ((8, full), wide), ((8, hidden), wide)]
    held = [(rows, low)] * 6 + [(up_shape, low), (down_shape, low)] * 2
    held += [(rows, wide)] * 2 + [(rows, low)] * 4 + [((length, hidden), low), ((hidden, length), low), ((full, length), low)]
    held += [(rows, low), ((length, hidden), low), (rows, wide), (rows, low)]
    return pl.pallas_call(
        feed_rows_kernel,
        out_shape=[jax.ShapeDtypeStruct(*pair) for pair in far + near],
        in_specs=[anywhere] * 9 + [vmem] * 6,
        out_specs=[anywhere] * len(far) + [vmem] * len(near),
        scratch_shapes=[pltpu.VMEM(*pair) for pair in held]
        + [pltpu.SemaphoreType.DMA((48,)), pltpu.SemaphoreType.DMA((12,)), pltpu.SemaphoreType.DMA((12,))],
        compiler_params=pltpu.CompilerParams(collective_id=2, has_side_effects=True, vmem_limit_bytes=62 * 2**20),
        cost_estimate=pl.CostEstimate(flops=3 * 10**10, bytes_accessed=5 * 10**7, transcendentals=6 * 10**6),
        name="feed_rows",
    )(
        teacher_x, teacher_part, teacher_other, x_all, part, teacher_up, teacher_down, up_low, down_low,
        valid, vectors, teacher_vectors, up_bias, unit_gates, teacher_up_bias,
    )


def vector_adam_kernel(
    factor_ref, norm_in, block_in, input_grad_in, bias_sum, unit_sum, bias, bias_first, bias_second,
    unit, unit_first, unit_second, gain, gain_first, gain_second,
    norm_out, block_out, input_grad_out, bias_grad, bias_new, bias_second_new, unit_grad, unit_new, unit_second_new, gain_grad, gain_new, gain_second_new,
):
    block_out[...] = block_in[...]
    input_grad_out[...] = input_grad_in[...]
    norm_out[...] = norm_in[...]
    factor = factor_ref[...]
    for total, states, outs in (
        (bias_sum[0:6], (bias, bias_first, bias_second), (bias_grad, bias_new, bias_second_new)),
        (bias_sum[6:8], (gain, gain_first, gain_second), (gain_grad, gain_new, gain_second_new)),
        (unit_sum[0:1], (unit, unit_first, unit_second), (unit_grad, unit_new, unit_second_new)),
    ):
        clipped = total * factor
        values = [state[...].reshape(clipped.shape) for state in states]
        new_weight, new_second = adam_step(*values, clipped, rate_vector, 0.0)
        for target, value in zip(outs, (clipped, new_weight, new_second)):
            target[...] = value.reshape(target.shape)


def vector_adam(*arrays):
    same = [jax.ShapeDtypeStruct(a.shape, a.dtype) for a in arrays[1:4]]
    shapes = [a.shape for a in arrays[6:15:3] for _ in range(3)]
    vmem = pl.BlockSpec(memory_space=pltpu.VMEM)
    return pl.pallas_call(
        vector_adam_kernel,
        out_shape=same + [jax.ShapeDtypeStruct(shape, jnp.float32) for shape in shapes],
        in_specs=[vmem] * 15,
        out_specs=[vmem] * 12,
        cost_estimate=pl.CostEstimate(flops=10**5, bytes_accessed=5 * 10**6, transcendentals=10**4),
        name="vector_adam",
    )(*arrays)


INNER = 16
SMALL_ROWS = 40
COUNT_ROW = 36


class Piece:
    def __init__(self, source, target, first_row, rows, first_column, columns, order, own, halvings):
        self.source, self.target = source, target
        self.first_row, self.rows = first_row, rows
        self.first_column, self.columns = first_column, columns
        self.order, self.own, self.halvings = order, own, halvings


def piece_buffers(rows, columns, halvings):
    low, wide = jnp.bfloat16, jnp.float32
    last = rows // 16 if halvings == 4 else rows // 8
    return [
        pltpu.VMEM((rows // 2, columns), low),
        pltpu.VMEM((rows // 4, columns), low),
        pltpu.VMEM((rows // 8, columns), low),
        pltpu.VMEM((last, columns), low),
        pltpu.VMEM((rows // 4, columns), low),
        pltpu.VMEM((rows // 8, columns), low),
        pltpu.VMEM((last, columns), low),
        pltpu.VMEM((rows // 4, columns), wide),
        pltpu.VMEM((last, columns), low),
    ]


SCHEDULE = (
    "D", 0, 1, 2, "F", 5, 3, "E", "G", "l", "n", "n", 0, "n", 1, "n", "o", 4, "a", 0, "a", "a", 0, 3, 1, 2, "a", 8, 5,
    0, "a", 1, 4, 3, 9, 2, 0, "a", 5, 1, "q", "q", 3, 6, 0, 4, "q", 5, 1, "i", 7, "s", 9, 4, "s", 5, 8, 3, "i", 1, 4, 2,
    6, "s", 9, 7, 8, 4, 3, 5, 0, 1, 2, 6, 7, 8, 4, 3, 6, 9, 5, 7, 3, 2, 6, 9, 4, "s", 7, 8, 6, 9, "S", 7, 2, 8, 0, 5,
    "S", 6, 7, 8, 9, 4, "S", 2, 6, 7, 3, 5, 1, 9, "S", 8, 2, "S", 7, 6,
)


def backward_kernel(
    outer, unit_t_in, first_t_in, branch_in, expanded_in, back, base_in, x_in, x_t_in, part_in, other_in, context_in, context_t_in, query_in,
    key_in, value_in, query_mark_in, key_mark_in, out_weight_in, qkv_weight_in,
    vector_ref, gate_ref, log_ref, sums_two, unit_sums, count,
    down_sum, up_sum, qkv_sum, out_sum, bias_out, unit_out, factor_out, norm_out, input_grad,
    base, x, part, other, context, context_t, query,
    key, value, query_mark, key_mark, out_weight, qkv_weight,
    unit_t, first_t, branch_grad, expanded, down, up, back_other, back_own, heads_grad, inner_rows, sums_one, turned_keys,
    turned_grad, pair_keys, pair_values, qkv_parts, out_parts, input_send, input_recv, small, small_recv,
    small_outer, squares, square_recv, resid_grad, shard_outer, send_sems, recv_sems, load_sems, shard_sems, *buffers,
):
    low, wide = jnp.bfloat16, jnp.float32
    place = lax.axis_index("rows")
    inside = place % INNER
    group = place // INNER
    core = lax.axis_index("hid")
    bits = {"x": inside % 2, "y": (inside // 2) % 2, "v": (inside // 4) % 2, "w": inside // 8}
    steps = {"x": 1, "y": 2, "v": 4, "w": 8}
    peer = {name: {"rows": place + steps[name] - 2 * steps[name] * bits[name]} for name in bits}
    to_group = [{"rows": inside + INNER * ((group + d) % outer)} for d in range(outer)]
    to_core = {"hid": 1 - core}
    barrier = pltpu.get_barrier_semaphore()
    peers = list(peer.values()) + to_group[1:] + [to_core]
    for there in peers:
        pl.semaphore_signal(barrier, inc=1, device_id=there, device_id_type=pl.DeviceIdType.MESH)
    pl.semaphore_wait(barrier, len(peers))

    counter = [0]
    pending = []

    def send(source, target, device):
        index = counter[0]
        counter[0] += 1
        copy = pltpu.make_async_remote_copy(
            src_ref=source, dst_ref=target, send_sem=send_sems.at[index],
            recv_sem=recv_sems.at[index], device_id=device, device_id_type=pl.DeviceIdType.MESH,
        )
        copy.start()
        pending.append(copy)
        return copy

    loads = []

    def load(source, target):
        copy = pltpu.make_async_copy(source, target, load_sems.at[len(loads)])
        copy.start()
        loads.append(copy)

    def wait_loads(first, last):
        for copy in loads[first:last]:
            copy.wait()

    orders = ("xyvw", "yxvw", "vxyw")
    orders_two = ("xyvw", "yxvw", "vyxw")
    pieces = []

    def add_piece(*fields):
        piece = Piece(*fields)
        piece.index, piece.step = len(pieces), 0
        piece.buffers = buffers[9 * piece.index : 9 * piece.index + 9]
        piece.offsets = [0]
        size = piece.rows
        for name in piece.order[: piece.halvings]:
            size = size // 2
            piece.offsets.append(piece.offsets[-1] + size * bits[name])
        pieces.append(piece)

    for source, target, lanes in ((down, down_sum, orders), (up, up_sum, orders_two)):
        rows = source.shape[0] // 3
        for lane in range(3):
            add_piece(source, target, rows * lane, rows, 0, source.shape[1], lanes[lane], None, 4)
    columns = qkv_parts.shape[1]
    split = qkv_parts.shape[0] * 5 // 9
    add_piece(qkv_parts, qkv_sum, 0, split, 0, columns, orders[0], None, 4)
    add_piece(qkv_parts, qkv_sum, split, qkv_parts.shape[0] - split, 0, columns, orders[1], None, 4)
    split = out_parts.shape[1] // 3
    add_piece(out_parts, out_sum, 0, out_parts.shape[0], 0, split, orders[0], None, 3)
    add_piece(out_parts, out_sum, 0, out_parts.shape[0], split, 2 * split, orders[1], None, 3)

    square_terms = []

    def advance_piece(piece):
        r1, r2, r3, r4, s2, s3, s4, keep, shard = piece.buffers
        step = piece.step
        piece.step += 1
        order, rows = piece.order, piece.rows
        columns = pl.ds(piece.first_column, piece.columns)
        names_done = order[: piece.halvings]

        def own(start, size):
            if piece.own is not None:
                return piece.own[aligned(start, size), :].astype(wide)
            return piece.source[aligned(piece.first_row + piece.offsets[1] + start, size), columns].astype(wide)

        if step == 0:
            start = piece.first_row + rows // 2 * (1 - bits[order[0]])
            piece.flight = send(piece.source.at[aligned(start, rows // 2), columns], r1, peer[order[0]])
        elif step == 1:
            if piece.own is not None:
                wait_loads(piece.loaded, piece.loaded + 1)
            piece.flight.wait_recv()
            bit = bits[order[1]]
            size = rows // 4
            sent = size * (1 - bit)
            s2[...] = (own(sent, size) + r1[aligned(sent, size), :].astype(wide)).astype(low)
            piece.flight = send(s2, r2, peer[order[1]])
            kept = size * bit
            keep[...] = own(kept, size) + r1[aligned(kept, size), :].astype(wide)
        elif step == 2:
            piece.flight.wait_recv()
            keep[...] = keep[...] + r2[...].astype(wide)
            bit = bits[order[2]]
            size = rows // 8
            s3[...] = keep[aligned(size * (1 - bit), size), :].astype(low)
            piece.flight = send(s3, r3, peer[order[2]])
        elif step == 3:
            piece.flight.wait_recv()
            size = rows // 8
            mine = aligned(size * bits[order[2]], size)
            total = keep[mine, :] + r3[...].astype(wide)
            if piece.halvings == 4:
                keep[mine, :] = total
                small_size = size // 2
                sent = size * bits[order[2]] + small_size * (1 - bits[order[3]])
                s4[...] = keep[aligned(sent, small_size), :].astype(low)
            else:
                s4[...] = total.astype(low)
            piece.flight = send(s4, r4, peer[order[3]])
        elif step == 4:
            piece.flight.wait_recv()
            if piece.halvings == 4:
                size = rows // 16
                kept = rows // 8 * bits[order[2]] + size * bits[order[3]]
                total = keep[aligned(kept, size), :] + r4[...].astype(wide)
                weight = 1.0
            else:
                total = s4[...].astype(wide) + r4[...].astype(wide)
                weight = 0.5
            if outer > 1:
                shard[...] = total.astype(low)
                shard_outer[piece.index][0] = shard[...]
                copies = [send(shard, shard_outer[piece.index].at[d], to_group[d]) for d in range(1, outer)]
                for copy in copies:
                    copy.wait()
                    pending[:] = [entry for entry in pending if entry is not copy]
                total = jnp.zeros_like(total)
                for index in range(outer):
                    total = total + shard_outer[piece.index][(group - index + outer) % outer].astype(wide)
            shard[...] = total.astype(low)
            square_terms.append(weight * jnp.sum(jnp.sum(total * total, axis=0, keepdims=True), axis=1, keepdims=True))
            size = rows // 2**piece.halvings
            here = piece.target.at[aligned(piece.first_row + piece.offsets[-1], size), columns]
            piece.local = pltpu.make_async_copy(shard, here, shard_sems.at[piece.index])
            piece.local.start()
            piece.flight = send(shard, here, peer[names_done[-1]])
        elif step < 4 + piece.halvings:
            level = piece.halvings - (step - 4)
            piece.flight.wait_recv()
            if step == 5:
                piece.local.wait()
            size = rows // 2**level
            block = piece.target.at[aligned(piece.first_row + piece.offsets[level], size), columns]
            piece.flight = send(block, block, peer[names_done[level - 1]])
        elif step == 4 + piece.halvings:
            piece.flight.wait_recv()

    back_flight = []
    length, full = x.shape
    half = full // 2
    head_loads = ((base_in, base), (x_in, x), (part_in, part), (other_in, other), (back, back_own), (context_in, context), (out_weight_in, out_weight))
    mid_loads = ((context_t_in, context_t), (query_in, query), (key_in, key), (value_in, value), (query_mark_in, query_mark), (key_mark_in, key_mark))

    def start_loads():
        for pair in ((unit_t_in, unit_t), (branch_in, branch_grad), (first_t_in, first_t), (expanded_in, expanded)):
            load(*pair)
        back_flight.append(send(back, back_other, to_core))
        for pair in head_loads + mid_loads + ((qkv_weight_in, qkv_weight),):
            load(*pair)

    def weight_gradient(first, turned, grads, leaves):
        for piece in pieces[first : first + 3]:
            bit = bits[piece.order[0]]
            size = piece.rows // 2
            block = aligned(piece.first_row + size * (1 - bit if leaves else bit), size)
            piece.source[block, :] = nn_dot(turned[block, :], grads[...]).astype(low)

    def wait_head_loads():
        back_flight[0].wait_recv()
        wait_loads(4, 11)
        sums_one[...] = jnp.zeros_like(sums_one)
        pair_keys[...] = jnp.zeros_like(pair_keys)
        pair_values[...] = jnp.zeros_like(pair_values)

    def norm_back(index):
        block = slice(index * TILE, (index + 1) * TILE)
        returned = (back_own[block, :].astype(wide) + back_other[block, :].astype(wide)).astype(low).astype(wide)
        grad_first = base[block, :] + returned
        branch = part[block, :].astype(wide) + other[block, :].astype(wide)
        resid = x[block, :].astype(wide) + (branch + vector_ref[1:2]) * vector_ref[0:1]
        normed, inverse = norm_parts(resid)
        grad_resid = norm_grad(grad_first * vector_ref[2:3], normed, inverse)
        resid_grad[block, :] = jnp.where(core == 0, grad_resid[:, :half], grad_resid[:, half:])
        grad_attended = grad_resid * vector_ref[0:1]
        sums_one[0:1] += column_sum(grad_first * normed)
        sums_one[1:2] += column_sum(grad_first)
        sums_one[2:3] += column_sum(grad_attended)
        grad_attended_low = grad_attended.astype(low)
        branch_grad[block, :] = grad_attended_low
        grad_heads = (nt_dot(grad_attended_low, out_weight[...]) * gate_ref[0:1]).astype(low)
        heads_grad[block, :] = grad_heads
        product = grad_heads.astype(wide) * context[block, :].astype(wide) * gate_ref[1:2]
        lane = lax.broadcasted_iota(jnp.int32, (1, 128), 1)
        columns = jnp.zeros((TILE, 128), wide)
        for pair in range(half // 128):
            some = product[:, 128 * pair : 128 * pair + 128]
            low_sum = jnp.sum(jnp.where(lane < HEAD, some, 0.0), axis=1, keepdims=True)
            high_sum = jnp.sum(jnp.where(lane < HEAD, 0.0, some), axis=1, keepdims=True)
            columns = jnp.where(lane == 2 * pair, low_sum, jnp.where(lane == 2 * pair + 1, high_sum, columns))
        inner_rows[:, block] = columns.T[0:8]

    def out_gradient():
        wait_loads(11, 17)
        out_parts[...] = nn_dot(context_t[...], branch_grad[...]).astype(low)

    pair_width = 2 * HEAD
    scale = HEAD ** (-0.5)
    vector_rows = [[], []]

    def attend_head(number, head):
        lanes = slice(number * pair_width, (number + 1) * pair_width)
        if head == 0:
            turned_keys[...] = key[:, lanes].T
        lane = lax.broadcasted_iota(jnp.int32, (1, pair_width), 1)
        mask = lane < HEAD if head == 0 else lane >= HEAD
        queries, grads = query[:, lanes], heads_grad[:, lanes]
        query_wide = jnp.concatenate([queries, query_mark[...]], axis=1)
        logs = log_ref[8 * number + head : 8 * number + head + 1, :]
        inner = inner_rows[2 * number + head : 2 * number + head + 1, :]

        for start in range(0, length, TILE):
            block = slice(start, start + TILE)
            zero = jnp.zeros((TILE, pair_width), low)
            chosen = jnp.where(mask, key[block, lanes] * jnp.asarray(scale, low), zero)
            key_wide = jnp.concatenate([chosen, key_mark[block, :]], axis=1)
            probs = jnp.exp(nt_dot(key_wide, query_wide) - logs)
            grad_probs = nt_dot(jnp.where(mask, value[block, lanes], zero), grads)
            grad_raw = (probs * (grad_probs - inner)).astype(low)
            unit_t[block, :] = grad_raw
            pair_keys[block, :] = jnp.where(mask, nn_dot(grad_raw, queries), pair_keys[block, :])
            pair_values[block, :] = jnp.where(mask, nn_dot(probs.astype(low), grads), pair_values[block, :])

        rows = slice(HEAD * head, HEAD * head + HEAD)
        turned_grad[rows, :] = nn_dot(turned_keys[rows, :], unit_t[0:length, :])
        if head == 1:
            query_out = (turned_grad[...].T * scale).astype(low)
            value_out = pair_values[...].astype(low)
            for index, value_here in enumerate((query_out, (pair_keys[...] * scale).astype(low), value_out)):
                expanded[:, index * half + number * pair_width : index * half + (number + 1) * pair_width] = value_here
            vector_rows[0].append(column_sum(query_out.astype(wide)))
            vector_rows[1].append(column_sum(value_out.astype(wide)))

    def proj(index):
        return expanded[:, index * half : (index + 1) * half]

    def projection_gradient(index):
        if index == 0:
            wait_loads(17, 19)
        rows = slice(index * full, (index + 1) * full)
        qkv_parts[rows, :] = nn_dot(first_t[...], proj(index)).astype(low)

    small_flight = []

    def own_half(vector):
        return jnp.where(core == 0, vector[:, :half], vector[:, half:])

    def start_small():
        small[...] = jnp.zeros_like(small)
        vectors = vector_rows[0] + vector_rows[1]
        vectors += [own_half(sums_one[2:3]), own_half(sums_two[2:3]), own_half(sums_one[1:2]), own_half(sums_two[1:2])]
        vectors += [unit_sums[0:1], own_half(sums_one[0:1]), own_half(sums_two[0:1]), count[0:1]]
        row = 0
        for vector in vectors:
            for start in range(0, vector.shape[1], 128):
                small[row : row + 1, :] = vector[:, start : start + 128]
                row += 1
        small_flight.append(send(small, small_recv.at[0], peer["x"]))

    def next_small():
        index = len(small_flight)
        if index == 0:
            start_small()
            return
        small_flight[-1].wait_recv()
        last = small if index == 1 else small_outer.at[index - 2]
        small_outer[index - 1] = last[...] + small_recv[index - 1]
        small_flight.append(send(small_outer.at[index - 1], small_recv.at[index], peer["xyvw"[index]]))

    input_flight = []

    def input_half(side):
        columns = aligned(half * side, half)
        return (
            nt_dot(proj(0), qkv_weight[0, columns, :])
            + nt_dot(proj(1), qkv_weight[1, columns, :])
            + nt_dot(proj(2), qkv_weight[2, columns, :])
        )

    def input_gradient(index):
        if index == 0:
            input_send[...] = input_half(1 - core).astype(low)
            input_flight.append(send(input_send, input_recv, to_core))
        else:
            input_grad[...] = input_half(core)

    small_totals = []
    square_flights = []

    def finish_small():
        small_flight[-1].wait_recv()
        small_total = small_outer[2] + small_recv[3]
        if outer > 1:
            small_outer[3] = small_total
            small_outer[4 + group] = small_total
            copies = [send(small_outer.at[3], small_outer.at[4 + group], to_group[d]) for d in range(1, outer)]
            for copy in copies:
                copy.wait_recv()
            small_total = small_outer[4]
            for index in range(1, outer):
                small_total = small_total + small_outer[4 + index]
        unit = 1.0 / (D * small_total[COUNT_ROW : COUNT_ROW + 1, 0:1])
        for index in range(24):
            row, lane = index // 3, index % 3
            source = 3 * row + lane if row < 6 else 12 + 3 * row + lane
            bias_out[row : row + 1, 128 * lane : 128 * lane + 128] = small_total[source : source + 1]
        for index in range(12):
            unit_out[:, 128 * index : 128 * index + 128] = jnp.broadcast_to(small_total[18 + index : 19 + index], (8, 128))
        inside_small = lax.broadcasted_iota(jnp.int32, small_total.shape, 0) < COUNT_ROW
        square = jnp.sum(
            jnp.sum(jnp.where(inside_small, small_total * small_total, 0.0), axis=0, keepdims=True), axis=1, keepdims=True
        )
        small_totals.extend([unit, square])
        input_flight[0].wait_recv()
        summed = input_grad[...] + input_recv[...].astype(wide)
        input_grad[...] = (summed.astype(low).astype(wide) + resid_grad[...]) * unit

    def next_square():
        index = len(square_flights)
        if index == 0:
            total_square = square_terms[0]
            for term in square_terms[1:]:
                total_square = total_square + term
            squares[0] = jnp.broadcast_to(total_square, (8, 128))
        else:
            square_flights[-1].wait_recv()
            squares[index] = squares[index - 1] + square_recv[index - 1]
        if index == 4:
            squares[4] = squares[4] + jnp.broadcast_to(small_totals[1], (8, 128))
        device = to_core if index == 4 else peer["xyvw"[index]]
        square_flights.append(send(squares.at[index], square_recv.at[index], device))
        if index == 0:
            finish_small()

    start_loads()
    done = {"n": 0, "a": 0, "q": 0, "i": 0}
    for entry in SCHEDULE:
        if isinstance(entry, int):
            advance_piece(pieces[entry])
        elif entry == "D":
            wait_loads(0, 2)
            weight_gradient(0, unit_t, branch_grad, True)
        elif entry == "E":
            weight_gradient(0, unit_t, branch_grad, False)
        elif entry == "F":
            wait_loads(2, 4)
            weight_gradient(3, first_t, expanded, True)
        elif entry == "G":
            weight_gradient(3, first_t, expanded, False)
            load(x_t_in, first_t)
        elif entry == "l":
            wait_head_loads()
        elif entry == "n":
            norm_back(done["n"])
        elif entry == "o":
            out_gradient()
        elif entry == "a":
            attend_head(done["a"] // 2, done["a"] % 2)
        elif entry == "q":
            projection_gradient(done["q"])
        elif entry == "i":
            input_gradient(done["i"])
        elif entry == "s":
            next_small()
        else:
            next_square()
        if entry in done:
            done[entry] += 1
    square_flights[-1].wait_recv()
    norm = jnp.sqrt(squares[4] + square_recv[4]) * small_totals[0]
    factor_out[...] = (small_totals[0] * clip_norm / jnp.maximum(norm, clip_norm))[0:1, 0:1]
    norm_out[...] = norm[0:1, 0:1]
    for copy in pending:
        copy.wait_send()


def backward_call(outer, unit_t, first_t, branch_grad, expanded, back, base, x_all, x_t, part, other, context, context_t, queries, keys_in, values, query_mark, key_mark, out_low, qkv_low, vectors, gates, logs, sums_two, unit_sums, count):
    low, wide = jnp.bfloat16, jnp.float32
    length, full = x_all.shape
    half = full // 2
    qkv_shape = (3 * full, half)
    out_shape = (half, full)
    down_shape, up_shape = (unit_t.shape[0], full), (full, expanded.shape[1])
    big = [unit_t, first_t, branch_grad, expanded, back, base, x_all, x_t, part, other, context, context_t, queries, keys_in, values, query_mark, key_mark, out_low, qkv_low]
    little = [vectors, gates, logs, sums_two, unit_sums, count]
    vmem = pl.BlockSpec(memory_space=pltpu.VMEM)
    hbm = pl.BlockSpec(memory_space=pl.ANY)
    sizes = [(shape[0] // 3, shape[1], 4) for shape in (down_shape, up_shape) for _ in range(3)]
    split = qkv_shape[0] * 5 // 9
    sizes += [(split, half, 4), (qkv_shape[0] - split, half, 4), (half, full // 3, 3), (half, full // 3 * 2, 3)]
    copies = sum(4 + halvings + (outer - 1) for _, _, halvings in sizes) + 2 + 4 + (outer - 1) + 5
    lasts = [(rows // 2**halvings, columns) for rows, columns, halvings in sizes]
    spare = [(outer,) + last if outer > 1 else (1, 8, 128) for last in lasts]
    scratch = [pltpu.VMEM(a.shape, a.dtype) for a in big[5:7] + big[8:]]
    scratch += [pltpu.VMEM(shape, low) for shape in (unit_t.shape, first_t.shape, branch_grad.shape, expanded.shape, down_shape, up_shape)]
    scratch += [
        pltpu.VMEM(back.shape, low),
        pltpu.VMEM(back.shape, low),
        pltpu.VMEM((length, half), low),
        pltpu.VMEM((8, length), wide),
        pltpu.VMEM((8, full), wide),
        pltpu.VMEM((2 * HEAD, length), low),
        pltpu.VMEM((2 * HEAD, length), wide),
        pltpu.VMEM((length, 2 * HEAD), wide),
        pltpu.VMEM((length, 2 * HEAD), wide),
        pltpu.VMEM(qkv_shape, low),
        pltpu.VMEM(out_shape, low),
        pltpu.VMEM((length, half), low),
        pltpu.VMEM((length, half), low),
        pltpu.VMEM((SMALL_ROWS, 128), wide),
        pltpu.VMEM((4, SMALL_ROWS, 128), wide),
        pltpu.VMEM((4 + outer, SMALL_ROWS, 128), wide),
        pltpu.VMEM((5, 8, 128), wide),
        pltpu.VMEM((5, 8, 128), wide),
        pltpu.VMEM((length, half), wide),
        tuple(pltpu.VMEM(shape, low) for shape in spare),
        pltpu.SemaphoreType.DMA((copies,)),
        pltpu.SemaphoreType.DMA((copies,)),
        pltpu.SemaphoreType.DMA((len(big) + 6,)),
        pltpu.SemaphoreType.DMA((12,)),
    ]
    for size in sizes:
        scratch += piece_buffers(*size)
    return pl.pallas_call(
        functools.partial(backward_kernel, outer),
        out_shape=[
            jax.ShapeDtypeStruct(down_shape, low),
            jax.ShapeDtypeStruct(up_shape, low),
            jax.ShapeDtypeStruct(qkv_shape, low),
            jax.ShapeDtypeStruct(out_shape, low),
            jax.ShapeDtypeStruct((8, half), wide),
            jax.ShapeDtypeStruct((8, unit_sums.shape[1]), wide),
            jax.ShapeDtypeStruct((1, 1), wide),
            jax.ShapeDtypeStruct((1, 1), wide),
            jax.ShapeDtypeStruct((length, half), wide),
        ],
        in_specs=[hbm] * len(big) + [vmem] * len(little),
        out_specs=[hbm] * 4 + [vmem] * 5,
        scratch_shapes=scratch,
        compiler_params=pltpu.CompilerParams(
            collective_id=0, has_side_effects=True, vmem_limit_bytes=61 * 2**20
        ),
        cost_estimate=pl.CostEstimate(flops=2 * 10**10, bytes_accessed=3 * 10**8, transcendentals=7 * 10**6),
        name="backward_rows",
    )(*big, *little)


def on_device(
    hidden_in,
    teacher_in,
    segment_ids,
    pad_mask,
    qkv_weight,
    qkv_moment1,
    qkv_moment2,
    out_weight,
    out_moment1,
    out_moment2,
    up_weight,
    up_moment1,
    up_moment2,
    down_weight,
    down_moment1,
    down_moment2,
    bias_vectors,
    bias_moment1,
    bias_moment2,
    up_bias,
    up_bias_moment1,
    up_bias_moment2,
    norm_gains,
    gain_moment1,
    gain_moment2,
    head_gates,
    layer_gates,
    dim_gates,
    unit_gates,
    teacher_qkv,
    teacher_out,
    teacher_up,
    teacher_down,
    teacher_biases,
    teacher_up_bias,
    teacher_gains,
):
    length = segment_ids.shape[1]
    width = hidden_in.shape[2]
    wide = jnp.float32
    (
        teacher_part, teacher_other, teacher_x, part, x_all, x_turned, queries, keys_in, values, context, context_turned,
        up_low, down_low, out_low, qkv_low, logs, query_mark, key_mark, valid, vectors, teacher_vectors, gate_rows, count,
    ) = attend_rows_call(
        teacher_in[0], hidden_in[0], teacher_qkv, teacher_out, qkv_weight, out_weight, up_weight, down_weight,
        segment_ids, pad_mask, bias_vectors, norm_gains, dim_gates, teacher_biases, teacher_gains, head_gates, layer_gates,
    )
    part_other, base, back, activated, first, reduced, expanded, block_out, sums_two, unit_sums = feed_rows_call(
        teacher_x, teacher_part, teacher_other, x_all, part, teacher_up, teacher_down, up_low, down_low,
        valid, vectors, teacher_vectors, up_bias, unit_gates, teacher_up_bias.astype(wide),
    )
    rows_all = lax.axis_size("rows")
    down_sum, up_sum, qkv_sum, out_sum, bias_sum, unit_sum, factor, norm, input_grad = backward_call(
        rows_all // INNER, activated, first, reduced, expanded, back, base, x_all, x_turned, part, part_other, context, context_turned,
        queries, keys_in, values, query_mark, key_mark, out_low, qkv_low, vectors, gate_rows, logs,
        sums_two, unit_sums, count,
    )
    weight_sums = (lax.optimization_barrier(qkv_sum.reshape(qkv_weight.shape)), out_sum, up_sum, down_sum)
    weights = (qkv_weight, out_weight, up_weight, down_weight)
    firsts = (qkv_moment1, out_moment1, up_moment1, down_moment1)
    seconds = (qkv_moment2, out_moment2, up_moment2, down_moment2)
    rates = (rate_attend, rate_output, rate_expand, rate_reduce)
    results = []
    for index in range(4):
        clipped = weight_sums[index].astype(wide) * factor
        new_weight, new_second = adam_step(
            weights[index], firsts[index], seconds[index], clipped, rates[index], weight_decay
        )
        results.append((clipped, new_weight, new_second, new_weight.astype(jnp.bfloat16)))
    vector_results = vector_adam(
        factor, norm, block_out, input_grad, bias_sum, unit_sum, bias_vectors, bias_moment1, bias_moment2, up_bias, up_bias_moment1, up_bias_moment2,
        norm_gains, gain_moment1, gain_moment2,
    )
    norm, block_out, input_grad = vector_results[:3]
    grad_norm = norm.reshape(())
    results += [vector_results[3:6], vector_results[6:9], vector_results[9:12]]
    block_out = block_out.reshape(hidden_in.shape)
    input_grad = input_grad.reshape(hidden_in.shape)
    return (
        block_out,
        input_grad,
        grad_norm,
        results[0][0],
        results[0][1],
        results[0][2],
        results[1][0],
        results[1][1],
        results[1][2],
        results[2][0],
        results[2][1],
        results[2][2],
        results[3][0],
        results[3][1],
        results[3][2],
        results[4][0],
        results[4][1],
        results[4][2],
        results[5][0],
        results[5][1],
        results[5][2],
        results[6][0],
        results[6][1],
        results[6][2],
        results[0][3],
        results[1][3],
        results[2][3],
        results[3][3],
    )


def solution(mesh):
    in_specs = (
        P("rows", None, "hid"),
        P("rows", None, "hid"),
        P("rows", None),
        P("rows", None),
        P(None, None, "hid"),
        P(None, None, "hid"),
        P(None, None, "hid"),
        P("hid", None),
        P("hid", None),
        P("hid", None),
        P(None, "hid"),
        P(None, "hid"),
        P(None, "hid"),
        P("hid", None),
        P("hid", None),
        P("hid", None),
        P(None, "hid"),
        P(None, "hid"),
        P(None, "hid"),
        P("hid"),
        P("hid"),
        P("hid"),
        P(None, "hid"),
        P(None, "hid"),
        P(None, "hid"),
        P("hid"),
        P(),
        P("hid"),
        P("hid"),
        P(None, None, "hid"),
        P("hid", None),
        P(None, "hid"),
        P("hid", None),
        P(None, "hid"),
        P("hid"),
        P(None, "hid"),
    )
    out_specs = (
        P("rows", None, "hid"),
        P("rows", None, "hid"),
        P(),
        P(None, None, "hid"),
        P(None, None, "hid"),
        P(None, None, "hid"),
        P("hid", None),
        P("hid", None),
        P("hid", None),
        P(None, "hid"),
        P(None, "hid"),
        P(None, "hid"),
        P("hid", None),
        P("hid", None),
        P("hid", None),
        P(None, "hid"),
        P(None, "hid"),
        P(None, "hid"),
        P("hid"),
        P("hid"),
        P("hid"),
        P(None, "hid"),
        P(None, "hid"),
        P(None, "hid"),
        P(None, None, "hid"),
        P("hid", None),
        P(None, "hid"),
        P("hid", None),
    )
    return jax.shard_map(
        on_device, mesh=mesh, in_specs=in_specs, out_specs=out_specs, check_vma=False
    )
```

```python
import functools

import jax
import jax.numpy as jnp
from jax import lax
from jax.experimental import pallas as pl
from jax.experimental.pallas import tpu as pltpu
from jax.sharding import PartitionSpec as P

D = 768
HEAD = 64
STEP = 10


epsilon_norm = 1e-06
masked_score = -1000000000.0
clip_norm = 0.001
beta_first = 0.9
beta_second = 0.999
adam_epsilon = 1e-08
weight_decay = 0.01
rate_attend = 0.03
rate_output = 0.2
rate_expand = 0.03
rate_reduce = 0.03
rate_vector = 0.3


def adam_step(weight, first, second, grad, rate, decay):
    first_new = beta_first * first + (1.0 - beta_first) * grad
    second_new = beta_second * second + (1.0 - beta_second) * grad * grad
    first_hat = first_new / (1.0 - beta_first**STEP)
    second_hat = second_new / (1.0 - beta_second**STEP)
    return (
        weight - rate * (first_hat / (jnp.sqrt(second_hat) + adam_epsilon) + decay * weight),
        second_new,
    )


MARKS = 128
TILE = 256


def nt_dot(left, right):
    return lax.dot_general(
        left, right, (((1,), (1,)), ((), ())), preferred_element_type=jnp.float32
    )


def nn_dot(left, right):
    return jnp.dot(left, right, preferred_element_type=jnp.float32)


def aligned(start, size):
    return pl.ds(pl.multiple_of(start, 16), size)


def lanes_of(core, width):
    return pl.ds(pl.multiple_of(core * width, 128), width)


class Mover:
    def __init__(self, local_sems, send_sems, recv_sems):
        self.local_sems, self.send_sems, self.recv_sems = local_sems, send_sems, recv_sems
        self.local_count = self.remote_count = 0
        self.sent = []

    def copy(self, source, target):
        moved = pltpu.make_async_copy(source, target, self.local_sems.at[self.local_count])
        self.local_count += 1
        moved.start()
        return moved

    def send(self, source, target, device):
        index = self.remote_count
        self.remote_count += 1
        moved = pltpu.make_async_remote_copy(
            src_ref=source, dst_ref=target, send_sem=self.send_sems.at[index],
            recv_sem=self.recv_sems.at[index], device_id=device, device_id_type=pl.DeviceIdType.MESH,
        )
        moved.start()
        self.sent.append(moved)
        return moved


def greet(core):
    barrier = pltpu.get_barrier_semaphore()
    to_core = {"hid": 1 - core}
    pl.semaphore_signal(barrier, inc=1, device_id=to_core, device_id_type=pl.DeviceIdType.MESH)
    pl.semaphore_wait(barrier, 1)
    return to_core


def attend_rows_kernel(
    teacher_in, hidden_in, teacher_qkv, teacher_out, qkv_weight, out_weight, up_weight, down_weight,
    segment_ref, padding_ref, bias_ref, gain_ref, dim_ref, teacher_bias_ref, teacher_gain_ref, head_gates, layer_gates,
    teacher_part_out, teacher_other_out, teacher_x_out, part_out, x_out, turned_out, query_out, key_out, value_out,
    context_out, context_turned_out, up_out, down_out, out_out, qkv_out,
    log_ref, query_mark_ref, key_mark_ref, valid_ref, vector_ref, teacher_vector_ref, gate_ref, count_ref,
    teacher_x, x_all, turned, query, key, value, context, context_turned, teacher_part, part,
    teacher_qkv_held, teacher_out_held, qkv_wide, out_wide, up_wide, down_wide, qkv_low, out_low, up_low, down_low,
    pack, spread, local_sems, send_sems, recv_sems,
):
    low, wide = jnp.bfloat16, jnp.float32
    core = lax.axis_index("hid")
    mover = Mover(local_sems, send_sems, recv_sems)
    length, width = hidden_in.shape
    here = lanes_of(core, width)
    to_core = greet(core)

    arriving = [mover.copy(teacher_in, teacher_x.at[:, here]), mover.send(teacher_in, teacher_x.at[:, here], to_core)]
    arriving_weights = [mover.copy(teacher_qkv, teacher_qkv_held), mover.copy(teacher_out, teacher_out_held)]
    arriving_student = [mover.copy(hidden_in, x_all.at[:, here]), mover.send(hidden_in, x_all.at[:, here], to_core)]
    casts = [
        (mover.copy(qkv_weight, qkv_wide), qkv_wide, qkv_low, qkv_out),
        (mover.copy(out_weight, out_wide), out_wide, out_low, out_out),
        (mover.copy(up_weight, up_wide), up_wide, up_low, up_out),
        (mover.copy(down_weight, down_wide), down_wide, down_low, down_out),
    ]
    leaving = []

    def cast(index):
        arrived, source, target, output = casts[index]
        arrived.wait()
        target[...] = source[...].astype(low)
        leaving.append(mover.copy(target, output))

    pack[0:4] = bias_ref[2:6]
    pack[4:6] = gain_ref[...]
    pack[6:7] = dim_ref[...].reshape(1, width)
    pack[7:8] = jnp.zeros_like(pack[7:8])
    pack[8:12] = teacher_bias_ref[2:6].astype(wide)
    pack[12:14] = teacher_gain_ref[...].astype(wide)
    pack[14:16] = jnp.zeros_like(pack[14:16])
    pack_flight = mover.send(pack, spread.at[:, here], to_core)
    spread[:, here] = pack[...]

    marks = lax.broadcasted_iota(jnp.int32, (MARKS, length), 0)
    same = jnp.broadcast_to(segment_ref[...], (MARKS, length)) == marks
    padding = jnp.broadcast_to(padding_ref[...], (MARKS, length))
    query_mark_ref[...] = jnp.where(same, 1.0, 0.0).T.astype(low)
    key_mark_ref[...] = jnp.where((same & (padding > 0)) | (marks >= 8), 0.0, masked_score).T.astype(low)
    valid_ref[...] = padding.astype(wide).T
    count_ref[...] = jnp.broadcast_to(jnp.sum(padding[0:8].astype(wide), axis=1, keepdims=True), (8, 128))

    pair = 2 * HEAD
    pairs = width // pair
    block_rows = length // 2
    first_head = lax.broadcasted_iota(jnp.int32, (1, pair), 1) < HEAD
    gate_ref[...] = jnp.zeros_like(gate_ref)
    for number in range(pairs):
        row = jnp.where(first_head, head_gates[2 * number], head_gates[2 * number + 1])
        gate_ref[0:1, number * pair : (number + 1) * pair] = row
        gate_ref[1:2, number * pair : (number + 1) * pair] = 1.0 / row

    def project(x_ref, weights, query_bias, value_bias):
        rows = x_ref[...]
        query[...] = (nn_dot(rows, weights[0]) + query_bias).astype(low)
        key[...] = nn_dot(rows, weights[1]).astype(low)
        value[...] = (nn_dot(rows, weights[2]) + value_bias).astype(low)

    def attend(number, keep):
        lanes = slice(number * pair, (number + 1) * pair)
        scaled = query[:, lanes] * jnp.asarray(HEAD ** (-0.5), low)
        key_wide = jnp.concatenate([key[:, lanes], key_mark_ref[...]], axis=1)
        values = jnp.concatenate([value[:, lanes], jnp.ones((length, pair), low)], axis=1)
        logs = []
        for start in range(0, length, block_rows):
            block = slice(start, start + block_rows)
            outs, columns = [], []
            for head in range(2):
                chosen = jnp.where(first_head if head == 0 else ~first_head, scaled[block], jnp.zeros_like(scaled[block]))
                query_wide = jnp.concatenate([chosen, query_mark_ref[block]], axis=1)
                scores = nt_dot(query_wide, key_wide)
                top = jnp.max(scores, axis=1, keepdims=True)
                weights = jnp.exp(scores - top)
                mixed = nn_dot(weights.astype(low), values)
                sums = mixed[:, pair:]
                outs.append(mixed[:, :pair] * (1.0 / sums))
                if keep:
                    columns.append(top + jnp.log(sums))
            mixed = jnp.where(first_head, outs[0], outs[1])
            if keep:
                mixed = mixed * gate_ref[0:1, lanes]
                logs.append(jnp.where(first_head, columns[0], columns[1]))
            mixed = mixed.astype(low)
            context[block, lanes] = mixed
            if keep:
                context_turned[lanes, block] = mixed.T
        if keep:
            log_turned = jnp.concatenate(logs, axis=0).T
            log_ref[8 * number : 8 * number + 8] = jnp.concatenate(
                [log_turned[0:1], log_turned[HEAD : HEAD + 1], log_turned[0:6]], axis=0
            )

    for moved in arriving[:1] + arriving_weights[:1]:
        moved.wait()
    arriving[1].wait_recv()
    leaving.append(mover.copy(teacher_x, teacher_x_out))
    project(teacher_x, teacher_qkv_held, teacher_bias_ref[0:1].astype(wide), teacher_bias_ref[1:2].astype(wide))
    for number in range(pairs):
        attend(number, False)
        cast(number)
    arriving_weights[1].wait()
    teacher_part[...] = nn_dot(context[...], teacher_out_held[...]).astype(low)
    teacher_flight = mover.send(teacher_part, teacher_other_out, to_core)
    leaving.append(mover.copy(teacher_part, teacher_part_out))

    arriving_student[0].wait()
    arriving_student[1].wait_recv()
    leaving.append(mover.copy(x_all, x_out))
    project(x_all, qkv_low, bias_ref[0:1], bias_ref[1:2])
    leaving.append(mover.copy(query, query_out))
    leaving.append(mover.copy(key, key_out))
    leaving.append(mover.copy(value, value_out))
    turned[...] = x_all[...].T
    leaving.append(mover.copy(turned, turned_out))
    for number in range(pairs):
        attend(number, True)
        if number == 0:
            cast(3)
    part[...] = nn_dot(context[...], out_low[...]).astype(low)
    leaving.append(mover.copy(part, part_out))
    leaving.append(mover.copy(context, context_out))
    leaving.append(mover.copy(context_turned, context_turned_out))

    pack_flight.wait_recv()
    dims = spread[6:7]
    ones = jnp.ones_like(dims)
    for target, rows, scales in (
        (vector_ref, spread[0:8], (layer_gates[0] * dims, layer_gates[1] * dims)),
        (teacher_vector_ref, spread[8:16], (ones, ones)),
    ):
        target[...] = jnp.concatenate(
            [scales[0], rows[0:1], rows[4:5], rows[2:3], scales[1], rows[1:2], rows[5:6], rows[3:4]], axis=0
        )
    teacher_flight.wait_recv()
    for moved in leaving:
        moved.wait()
    for moved in mover.sent:
        moved.wait_send()


def attend_rows_call(teacher_in, hidden_in, teacher_qkv, teacher_out, qkv_weight, out_weight, up_weight, down_weight, segment, padding, biases, gains, dims, teacher_biases, teacher_gains, head_gates, layer_gates):
    low, wide = jnp.bfloat16, jnp.float32
    length, width = hidden_in.shape
    full = 2 * width
    pairs = width // (2 * HEAD)
    hidden = up_weight.shape[1]
    vmem, anywhere = pl.BlockSpec(memory_space=pltpu.VMEM), pl.BlockSpec(memory_space=pl.ANY)
    smem = pl.BlockSpec(memory_space=pltpu.SMEM)
    rows_full, rows_half = (length, full), (length, width)
    far = [rows_full] * 5 + [(full, length)] + [rows_half] * 4 + [(width, length)]
    far += [up_weight.shape, down_weight.shape, out_weight.shape, qkv_weight.shape]
    near = [
        ((8 * pairs, length), wide), ((length, MARKS), low), ((length, MARKS), low), ((length, MARKS), wide),
        ((8, full), wide), ((8, full), wide), ((8, width), wide), ((8, 128), wide),
    ]
    held = [rows_full, rows_full, (full, length), rows_half, rows_half, rows_half, rows_half, (width, length), rows_full, rows_full]
    return pl.pallas_call(
        attend_rows_kernel,
        out_shape=[jax.ShapeDtypeStruct(shape, low) for shape in far] + [jax.ShapeDtypeStruct(*pair) for pair in near],
        in_specs=[anywhere] * 8 + [vmem] * 7 + [smem] * 2,
        out_specs=[anywhere] * len(far) + [vmem] * len(near),
        scratch_shapes=[pltpu.VMEM(shape, low) for shape in held]
        + [pltpu.VMEM(teacher_qkv.shape, low), pltpu.VMEM(teacher_out.shape, low)]
        + [pltpu.VMEM(w.shape, wide) for w in (qkv_weight, out_weight, up_weight, down_weight)]
        + [pltpu.VMEM(w.shape, low) for w in (qkv_weight, out_weight, up_weight, down_weight)]
        + [pltpu.VMEM((16, width), wide), pltpu.VMEM((16, full), wide)]
        + [pltpu.SemaphoreType.DMA((24,)), pltpu.SemaphoreType.DMA((4,)), pltpu.SemaphoreType.DMA((4,))],
        compiler_params=pltpu.CompilerParams(collective_id=1, has_side_effects=True, vmem_limit_bytes=60 * 2**20),
        cost_estimate=pl.CostEstimate(flops=2 * 10**10, bytes_accessed=5 * 10**7, transcendentals=14 * 10**6),
        name="attend_rows",
    )(
        teacher_in, hidden_in, teacher_qkv, teacher_out, qkv_weight, out_weight, up_weight, down_weight,
        segment, padding, biases, gains, dims, teacher_biases, teacher_gains, head_gates, layer_gates,
    )


def norm_parts(resid):
    center = jnp.mean(resid, axis=1, keepdims=True)
    second = jnp.mean(resid * resid, axis=1, keepdims=True)
    inverse = lax.rsqrt(second - center * center + epsilon_norm)
    return (resid - center) * inverse, inverse


def norm_grad(grad_normed, normed, inverse):
    center = jnp.mean(grad_normed, axis=1, keepdims=True)
    crossed = jnp.mean(grad_normed * normed, axis=1, keepdims=True)
    return inverse * (grad_normed - center - normed * crossed)


def column_sum(value):
    return jnp.sum(value, axis=0, keepdims=True)


def feed_rows_kernel(
    teacher_x_in, teacher_part_in, teacher_other_in, x_in, part_in, teacher_up_in, teacher_down_in, up_in, down_in,
    valid_ref, vector_ref, teacher_vector_ref, up_bias_ref, unit_gate_ref, teacher_up_bias_ref,
    other_out, base_out, back_out, activated_out, first_out, reduced_out, expanded_out, block_ref, sums_ref, unit_sums_ref,
    teacher_x, teacher_part, teacher_other, x_all, part, other, teacher_up, teacher_down, up, down,
    teacher_first, first, teacher_reduced, teacher_reduced_other, reduced, reduced_other, slope, activated_turned,
    first_turned, grad_reduced, grad_expanded, base, back, local_sems, send_sems, recv_sems,
):
    low, wide = jnp.bfloat16, jnp.float32
    core = lax.axis_index("hid")
    mover = Mover(local_sems, send_sems, recv_sems)
    length, full = x_in.shape
    half = full // 2
    up_bias, unit_gate, teacher_up_bias = (r[...].astype(wide).reshape(1, r.shape[0]) for r in (up_bias_ref, unit_gate_ref, teacher_up_bias_ref))
    to_core = greet(core)
    part_flight = mover.send(part_in, other, to_core)
    tiles = [slice(start, start + TILE) for start in range(0, length, TILE)]
    teacher_rows = ((teacher_x_in, teacher_x), (teacher_part_in, teacher_part), (teacher_other_in, teacher_other))
    tile_loads = [[mover.copy(source.at[tiles[0]], target.at[tiles[0]]) for source, target in teacher_rows]]
    up_load = mover.copy(teacher_up_in, teacher_up)
    down_load = mover.copy(teacher_down_in, teacher_down)
    rest = slice(TILE, length)
    tile_loads.append([mover.copy(source.at[rest], target.at[rest]) for source, target in teacher_rows])
    loads = [
        mover.copy(source, target) for source, target in ((x_in, x_all), (part_in, part), (up_in, up), (down_in, down))
    ]

    def norm_one(x_ref, own_ref, far_ref, vectors, block):
        branch = own_ref[block].astype(wide) + far_ref[block].astype(wide)
        normed, _ = norm_parts(x_ref[block].astype(wide) + (branch + vectors[1:2]) * vectors[0:1])
        return normed * vectors[2:3] + vectors[3:4]

    def gelu_share(expanded):
        return 0.5 + 0.5 * lax.erf(expanded * (0.5**0.5))

    teacher_flights = []
    for index, block in enumerate(tiles):
        if index < 2:
            for moved in tile_loads[index]:
                moved.wait()
        out = norm_one(teacher_x, teacher_part, teacher_other, teacher_vector_ref, block)
        teacher_first[block] = out
        if index == 0:
            up_load.wait()
        expanded = nn_dot(out.astype(low), teacher_up[...]) + teacher_up_bias
        activated = (expanded * gelu_share(expanded)).astype(low)
        if index == 0:
            down_load.wait()
        teacher_reduced[block] = nn_dot(activated, teacher_down[...]).astype(low)
        teacher_flights.append(mover.send(teacher_reduced.at[block], teacher_reduced_other.at[block], to_core))
    for moved in loads:
        moved.wait()
    part_flight.wait_recv()
    leaving = [mover.copy(other, other_out)]
    flights = []
    for block in tiles:
        out = norm_one(x_all, part, other, vector_ref, block)
        first[block] = out
        out_low = out.astype(low)
        first_turned[:, block] = out_low.T
        expanded = nn_dot(out_low, up[...]) + up_bias
        share = gelu_share(expanded)
        activated = (expanded * share * unit_gate).astype(low)
        reduced[block] = nn_dot(activated, down[...]).astype(low)
        flights.append(mover.send(reduced.at[block], reduced_other.at[block], to_core))
        activated_turned[:, block] = activated.T
        bell = jnp.exp(-0.5 * expanded * expanded)
        slope[block] = ((share + expanded * bell * 0.3989422804014327) * unit_gate).astype(low)
        leaving.append(mover.copy(activated_turned.at[:, block], activated_out.at[:, block]))
        leaving.append(mover.copy(first_turned.at[:, block], first_out.at[:, block]))

    sums_ref[...] = jnp.zeros_like(sums_ref)
    unit_sums_ref[...] = jnp.zeros_like(unit_sums_ref)
    for index, block in enumerate(tiles):
        teacher_flights[index].wait_recv()
        flights[index].wait_recv()
        student_first, target_first = first[block], teacher_first[block]
        branch = reduced[block].astype(wide) + reduced_other[block].astype(wide)
        normed, inverse = norm_parts(student_first + (branch + vector_ref[5:6]) * vector_ref[4:5])
        second = normed * vector_ref[6:7] + vector_ref[7:8]
        target_branch = teacher_reduced[block].astype(wide) + teacher_reduced_other[block].astype(wide)
        target_normed, _ = norm_parts(target_first + target_branch + teacher_vector_ref[5:6])
        target = target_normed * teacher_vector_ref[6:7] + teacher_vector_ref[7:8]
        block_ref[block] = jnp.where(core == 0, second[:, :half], second[:, half:]).astype(low)
        twice = valid_ref[block, 0:1] * 2.0
        grad_second = twice * (second - target)
        grad_resid = norm_grad(grad_second * vector_ref[6:7], normed, inverse)
        grad_branch = grad_resid * vector_ref[4:5]
        sums_ref[0:1] += column_sum(grad_second * normed)
        sums_ref[1:2] += column_sum(grad_second)
        sums_ref[2:3] += column_sum(grad_branch)
        grad_branch_low = grad_branch.astype(low)
        grad_reduced[block] = grad_branch_low
        grad_activated = nt_dot(grad_branch_low, down[...]).astype(low).astype(wide)
        grad_unit = (grad_activated * slope[block].astype(wide)).astype(low)
        grad_expanded[block] = grad_unit
        unit_sums_ref[0:1] += column_sum(grad_unit.astype(wide))
        back[block] = nt_dot(grad_unit, up[...]).astype(low)
        base[block] = twice * (student_first - target_first) + grad_resid
        leaving.append(mover.copy(back.at[block], back_out.at[block]))
        leaving.append(mover.copy(base.at[block], base_out.at[block]))
        leaving.append(mover.copy(grad_reduced.at[block], reduced_out.at[block]))
        leaving.append(mover.copy(grad_expanded.at[block], expanded_out.at[block]))
    for moved in leaving:
        moved.wait()
    for moved in mover.sent:
        moved.wait_send()


def feed_rows_call(teacher_x, teacher_part, teacher_other, x_all, part, teacher_up, teacher_down, up_low, down_low, valid, vectors, teacher_vectors, up_bias, unit_gates, teacher_up_bias):
    low, wide = jnp.bfloat16, jnp.float32
    length, full = x_all.shape
    hidden = up_low.shape[1]
    vmem, anywhere = pl.BlockSpec(memory_space=pltpu.VMEM), pl.BlockSpec(memory_space=pl.ANY)
    rows = (length, full)
    up_shape, down_shape = up_low.shape, down_low.shape
    far = [(rows, low), (rows, wide), (rows, low), ((hidden, length), low), ((full, length), low), (rows, low), ((length, hidden), low)]
    near = [((length, full // 2), low), ((8, full), wide), ((8, hidden), wide)]
    held = [(rows, low)] * 6 + [(up_shape, low), (down_shape, low)] * 2
    held += [(rows, wide)] * 2 + [(rows, low)] * 4 + [((length, hidden), low), ((hidden, length), low), ((full, length), low)]
    held += [(rows, low), ((length, hidden), low), (rows, wide), (rows, low)]
    return pl.pallas_call(
        feed_rows_kernel,
        out_shape=[jax.ShapeDtypeStruct(*pair) for pair in far + near],
        in_specs=[anywhere] * 9 + [vmem] * 6,
        out_specs=[anywhere] * len(far) + [vmem] * len(near),
        scratch_shapes=[pltpu.VMEM(*pair) for pair in held]
        + [pltpu.SemaphoreType.DMA((48,)), pltpu.SemaphoreType.DMA((12,)), pltpu.SemaphoreType.DMA((12,))],
        compiler_params=pltpu.CompilerParams(collective_id=2, has_side_effects=True, vmem_limit_bytes=62 * 2**20),
        cost_estimate=pl.CostEstimate(flops=3 * 10**10, bytes_accessed=5 * 10**7, transcendentals=6 * 10**6),
        name="feed_rows",
    )(
        teacher_x, teacher_part, teacher_other, x_all, part, teacher_up, teacher_down, up_low, down_low,
        valid, vectors, teacher_vectors, up_bias, unit_gates, teacher_up_bias,
    )


def vector_adam_kernel(
    factor_ref, norm_in, block_in, input_grad_in, bias_sum, unit_sum, bias, bias_first, bias_second,
    unit, unit_first, unit_second, gain, gain_first, gain_second,
    norm_out, block_out, input_grad_out, bias_grad, bias_new, bias_second_new, unit_grad, unit_new, unit_second_new, gain_grad, gain_new, gain_second_new,
):
    block_out[...] = block_in[...]
    input_grad_out[...] = input_grad_in[...]
    norm_out[...] = norm_in[...]
    factor = factor_ref[...]
    for total, states, outs in (
        (bias_sum[0:6], (bias, bias_first, bias_second), (bias_grad, bias_new, bias_second_new)),
        (bias_sum[6:8], (gain, gain_first, gain_second), (gain_grad, gain_new, gain_second_new)),
        (unit_sum[0:1], (unit, unit_first, unit_second), (unit_grad, unit_new, unit_second_new)),
    ):
        clipped = total * factor
        values = [state[...].reshape(clipped.shape) for state in states]
        new_weight, new_second = adam_step(*values, clipped, rate_vector, 0.0)
        for target, value in zip(outs, (clipped, new_weight, new_second)):
            target[...] = value.reshape(target.shape)


def vector_adam(*arrays):
    same = [jax.ShapeDtypeStruct(a.shape, a.dtype) for a in arrays[1:4]]
    shapes = [a.shape for a in arrays[6:15:3] for _ in range(3)]
    vmem = pl.BlockSpec(memory_space=pltpu.VMEM)
    return pl.pallas_call(
        vector_adam_kernel,
        out_shape=same + [jax.ShapeDtypeStruct(shape, jnp.float32) for shape in shapes],
        in_specs=[vmem] * 15,
        out_specs=[vmem] * 12,
        cost_estimate=pl.CostEstimate(flops=10**5, bytes_accessed=5 * 10**6, transcendentals=10**4),
        name="vector_adam",
    )(*arrays)


INNER = 16
SMALL_ROWS = 40
COUNT_ROW = 36


class Piece:
    def __init__(self, source, target, first_row, rows, first_column, columns, order, own, halvings):
        self.source, self.target = source, target
        self.first_row, self.rows = first_row, rows
        self.first_column, self.columns = first_column, columns
        self.order, self.own, self.halvings = order, own, halvings


def piece_buffers(rows, columns, halvings):
    low, wide = jnp.bfloat16, jnp.float32
    last = rows // 16 if halvings == 4 else rows // 8
    return [
        pltpu.VMEM((rows // 2, columns), low),
        pltpu.VMEM((rows // 4, columns), low),
        pltpu.VMEM((rows // 8, columns), low),
        pltpu.VMEM((last, columns), low),
        pltpu.VMEM((rows // 4, columns), low),
        pltpu.VMEM((rows // 8, columns), low),
        pltpu.VMEM((last, columns), low),
        pltpu.VMEM((rows // 4, columns), wide),
        pltpu.VMEM((last, columns), low),
    ]


SCHEDULE = (
    "D", 1, 0, "F", 2, "E", "G", "l", 5, "n", "n", 1, 0, "n", "n", 4, 2, "o", 3, "a", 0, 1, "a", "a", 0, 2, 9, 5, 1,
    "a", 4, 8, 0, 2, "a", 1, 3, "a", 0, 9, 2, 4, "q", 5, "q", 6, 8, "q", 7, 1, "i", 3, 4, 5, 2, 3, 0, 9, 1, 4, "i", 7,
    6, 3, 8, "s", 5, "s", 4, 0, 3, 8, 1, 6, 5, 4, "s", 9, 2, 7, 3, "s", 6, 5, 8, 7, 6, 0, 8, 3, 4, 7, 9, 6, 7, 2, 9, 6,
    "S", 7, 8, 4, 9, "S", 6, 5, "S", 7, "S", 2, 1, 9, 8, "S", 3, 5, 7, 6,
)


def backward_kernel(
    outer, unit_t_in, first_t_in, branch_in, expanded_in, back, base_in, x_in, x_t_in, part_in, other_in, context_in, context_t_in, query_in,
    key_in, value_in, query_mark_in, key_mark_in, out_weight_in, qkv_weight_in,
    vector_ref, gate_ref, log_ref, sums_two, unit_sums, count,
    down_sum, up_sum, qkv_sum, out_sum, bias_out, unit_out, factor_out, norm_out, input_grad,
    base, x, part, other, context, context_t, query,
    key, value, query_mark, key_mark, out_weight, qkv_weight,
    unit_t, first_t, branch_grad, expanded, down, up, back_other, back_own, heads_grad, inner_rows, sums_one, turned_keys,
    turned_grad, pair_keys, pair_values, qkv_parts, out_parts, input_send, input_recv, small, small_recv,
    small_outer, squares, square_recv, resid_grad, shard_outer, send_sems, recv_sems, load_sems, shard_sems, *buffers,
):
    low, wide = jnp.bfloat16, jnp.float32
    place = lax.axis_index("rows")
    inside = place % INNER
    group = place // INNER
    core = lax.axis_index("hid")
    bits = {"x": inside % 2, "y": (inside // 2) % 2, "v": (inside // 4) % 2, "w": inside // 8}
    steps = {"x": 1, "y": 2, "v": 4, "w": 8}
    peer = {name: {"rows": place + steps[name] - 2 * steps[name] * bits[name]} for name in bits}
    to_group = [{"rows": inside + INNER * ((group + d) % outer)} for d in range(outer)]
    to_core = {"hid": 1 - core}
    barrier = pltpu.get_barrier_semaphore()
    peers = list(peer.values()) + to_group[1:] + [to_core]
    for there in peers:
        pl.semaphore_signal(barrier, inc=1, device_id=there, device_id_type=pl.DeviceIdType.MESH)
    pl.semaphore_wait(barrier, len(peers))

    counter = [0]
    pending = []

    def send(source, target, device):
        index = counter[0]
        counter[0] += 1
        copy = pltpu.make_async_remote_copy(
            src_ref=source, dst_ref=target, send_sem=send_sems.at[index],
            recv_sem=recv_sems.at[index], device_id=device, device_id_type=pl.DeviceIdType.MESH,
        )
        copy.start()
        pending.append(copy)
        return copy

    loads = []

    def load(source, target):
        copy = pltpu.make_async_copy(source, target, load_sems.at[len(loads)])
        copy.start()
        loads.append(copy)

    def wait_loads(first, last):
        for copy in loads[first:last]:
            copy.wait()

    orders = ("xyvw", "yxvw", "vxyw")
    orders_two = ("xyvw", "yxvw", "vyxw")
    pieces = []

    def add_piece(*fields):
        piece = Piece(*fields)
        piece.index, piece.step = len(pieces), 0
        piece.buffers = buffers[9 * piece.index : 9 * piece.index + 9]
        piece.offsets = [0]
        size = piece.rows
        for name in piece.order[: piece.halvings]:
            size = size // 2
            piece.offsets.append(piece.offsets[-1] + size * bits[name])
        pieces.append(piece)

    for source, target, lanes in ((down, down_sum, orders), (up, up_sum, orders_two)):
        rows = source.shape[0] // 3
        for lane in range(3):
            add_piece(source, target, rows * lane, rows, 0, source.shape[1], lanes[lane], None, 4)
    columns = qkv_parts.shape[1]
    split = qkv_parts.shape[0] * 5 // 9
    add_piece(qkv_parts, qkv_sum, 0, split, 0, columns, orders[0], None, 4)
    add_piece(qkv_parts, qkv_sum, split, qkv_parts.shape[0] - split, 0, columns, orders[1], None, 4)
    split = out_parts.shape[1] // 3
    add_piece(out_parts, out_sum, 0, out_parts.shape[0], 0, split, orders[0], None, 3)
    add_piece(out_parts, out_sum, 0, out_parts.shape[0], split, 2 * split, orders[1], None, 3)

    square_terms = []

    def advance_piece(piece):
        r1, r2, r3, r4, s2, s3, s4, keep, shard = piece.buffers
        step = piece.step
        piece.step += 1
        order, rows = piece.order, piece.rows
        columns = pl.ds(piece.first_column, piece.columns)
        names_done = order[: piece.halvings]

        def own(start, size):
            if piece.own is not None:
                return piece.own[aligned(start, size), :].astype(wide)
            return piece.source[aligned(piece.first_row + piece.offsets[1] + start, size), columns].astype(wide)

        if step == 0:
            start = piece.first_row + rows // 2 * (1 - bits[order[0]])
            piece.flight = send(piece.source.at[aligned(start, rows // 2), columns], r1, peer[order[0]])
        elif step == 1:
            if piece.own is not None:
                wait_loads(piece.loaded, piece.loaded + 1)
            piece.flight.wait_recv()
            bit = bits[order[1]]
            size = rows // 4
            sent = size * (1 - bit)
            s2[...] = (own(sent, size) + r1[aligned(sent, size), :].astype(wide)).astype(low)
            piece.flight = send(s2, r2, peer[order[1]])
            kept = size * bit
            keep[...] = own(kept, size) + r1[aligned(kept, size), :].astype(wide)
        elif step == 2:
            piece.flight.wait_recv()
            keep[...] = keep[...] + r2[...].astype(wide)
            bit = bits[order[2]]
            size = rows // 8
            s3[...] = keep[aligned(size * (1 - bit), size), :].astype(low)
            piece.flight = send(s3, r3, peer[order[2]])
        elif step == 3:
            piece.flight.wait_recv()
            size = rows // 8
            mine = aligned(size * bits[order[2]], size)
            total = keep[mine, :] + r3[...].astype(wide)
            if piece.halvings == 4:
                keep[mine, :] = total
                small_size = size // 2
                sent = size * bits[order[2]] + small_size * (1 - bits[order[3]])
                s4[...] = keep[aligned(sent, small_size), :].astype(low)
            else:
                s4[...] = total.astype(low)
            piece.flight = send(s4, r4, peer[order[3]])
        elif step == 4:
            piece.flight.wait_recv()
            if piece.halvings == 4:
                size = rows // 16
                kept = rows // 8 * bits[order[2]] + size * bits[order[3]]
                total = keep[aligned(kept, size), :] + r4[...].astype(wide)
                weight = 1.0
            else:
                total = s4[...].astype(wide) + r4[...].astype(wide)
                weight = 0.5
            if outer > 1:
                shard[...] = total.astype(low)
                shard_outer[piece.index][0] = shard[...]
                copies = [send(shard, shard_outer[piece.index].at[d], to_group[d]) for d in range(1, outer)]
                for copy in copies:
                    copy.wait()
                    pending[:] = [entry for entry in pending if entry is not copy]
                total = jnp.zeros_like(total)
                for index in range(outer):
                    total = total + shard_outer[piece.index][(group - index + outer) % outer].astype(wide)
            shard[...] = total.astype(low)
            square_terms.append(weight * jnp.sum(jnp.sum(total * total, axis=0, keepdims=True), axis=1, keepdims=True))
            size = rows // 2**piece.halvings
            here = piece.target.at[aligned(piece.first_row + piece.offsets[-1], size), columns]
            piece.local = pltpu.make_async_copy(shard, here, shard_sems.at[piece.index])
            piece.local.start()
            piece.flight = send(shard, here, peer[names_done[-1]])
        elif step < 4 + piece.halvings:
            level = piece.halvings - (step - 4)
            piece.flight.wait_recv()
            if step == 5:
                piece.local.wait()
            size = rows // 2**level
            block = piece.target.at[aligned(piece.first_row + piece.offsets[level], size), columns]
            piece.flight = send(block, block, peer[names_done[level - 1]])
        elif step == 4 + piece.halvings:
            piece.flight.wait_recv()

    back_flight = []
    length, full = x.shape
    half = full // 2
    head_loads = ((base_in, base), (x_in, x), (part_in, part), (other_in, other), (back, back_own), (context_in, context), (out_weight_in, out_weight))
    mid_loads = ((context_t_in, context_t), (query_in, query), (key_in, key), (value_in, value), (query_mark_in, query_mark), (key_mark_in, key_mark))

    def start_loads():
        for pair in ((unit_t_in, unit_t), (branch_in, branch_grad), (first_t_in, first_t), (expanded_in, expanded)):
            load(*pair)
        back_flight.append(send(back, back_other, to_core))
        for pair in head_loads + mid_loads + ((qkv_weight_in, qkv_weight),):
            load(*pair)

    def weight_gradient(first, turned, grads, leaves):
        for piece in pieces[first : first + 3]:
            bit = bits[piece.order[0]]
            size = piece.rows // 2
            block = aligned(piece.first_row + size * (1 - bit if leaves else bit), size)
            piece.source[block, :] = nn_dot(turned[block, :], grads[...]).astype(low)

    def wait_head_loads():
        back_flight[0].wait_recv()
        wait_loads(4, 11)
        sums_one[...] = jnp.zeros_like(sums_one)
        pair_keys[...] = jnp.zeros_like(pair_keys)
        pair_values[...] = jnp.zeros_like(pair_values)

    def norm_back(index):
        block = slice(index * TILE, (index + 1) * TILE)
        returned = (back_own[block, :].astype(wide) + back_other[block, :].astype(wide)).astype(low).astype(wide)
        grad_first = base[block, :] + returned
        branch = part[block, :].astype(wide) + other[block, :].astype(wide)
        resid = x[block, :].astype(wide) + (branch + vector_ref[1:2]) * vector_ref[0:1]
        normed, inverse = norm_parts(resid)
        grad_resid = norm_grad(grad_first * vector_ref[2:3], normed, inverse)
        resid_grad[block, :] = jnp.where(core == 0, grad_resid[:, :half], grad_resid[:, half:])
        grad_attended = grad_resid * vector_ref[0:1]
        sums_one[0:1] += column_sum(grad_first * normed)
        sums_one[1:2] += column_sum(grad_first)
        sums_one[2:3] += column_sum(grad_attended)
        grad_attended_low = grad_attended.astype(low)
        branch_grad[block, :] = grad_attended_low
        grad_heads = (nt_dot(grad_attended_low, out_weight[...]) * gate_ref[0:1]).astype(low)
        heads_grad[block, :] = grad_heads
        product = grad_heads.astype(wide) * context[block, :].astype(wide) * gate_ref[1:2]
        lane = lax.broadcasted_iota(jnp.int32, (1, 128), 1)
        columns = jnp.zeros((TILE, 128), wide)
        for pair in range(half // 128):
            some = product[:, 128 * pair : 128 * pair + 128]
            low_sum = jnp.sum(jnp.where(lane < HEAD, some, 0.0), axis=1, keepdims=True)
            high_sum = jnp.sum(jnp.where(lane < HEAD, 0.0, some), axis=1, keepdims=True)
            columns = jnp.where(lane == 2 * pair, low_sum, jnp.where(lane == 2 * pair + 1, high_sum, columns))
        inner_rows[:, block] = columns.T[0:8]

    def out_gradient():
        wait_loads(11, 17)
        out_parts[...] = nn_dot(context_t[...], branch_grad[...]).astype(low)

    pair_width = 2 * HEAD
    scale = HEAD ** (-0.5)
    vector_rows = [[], []]

    def attend_head(number, head):
        lanes = slice(number * pair_width, (number + 1) * pair_width)
        if head == 0:
            turned_keys[...] = key[:, lanes].T
        lane = lax.broadcasted_iota(jnp.int32, (1, pair_width), 1)
        mask = lane < HEAD if head == 0 else lane >= HEAD
        queries, grads = query[:, lanes], heads_grad[:, lanes]
        query_wide = jnp.concatenate([queries, query_mark[...]], axis=1)
        logs = log_ref[8 * number + head : 8 * number + head + 1, :]
        inner = inner_rows[2 * number + head : 2 * number + head + 1, :]

        for start in range(0, length, TILE):
            block = slice(start, start + TILE)
            zero = jnp.zeros((TILE, pair_width), low)
            chosen = jnp.where(mask, key[block, lanes] * jnp.asarray(scale, low), zero)
            key_wide = jnp.concatenate([chosen, key_mark[block, :]], axis=1)
            probs = jnp.exp(nt_dot(key_wide, query_wide) - logs)
            grad_probs = nt_dot(jnp.where(mask, value[block, lanes], zero), grads)
            grad_raw = (probs * (grad_probs - inner)).astype(low)
            unit_t[block, :] = grad_raw
            pair_keys[block, :] = jnp.where(mask, nn_dot(grad_raw, queries), pair_keys[block, :])
            pair_values[block, :] = jnp.where(mask, nn_dot(probs.astype(low), grads), pair_values[block, :])

        rows = slice(HEAD * head, HEAD * head + HEAD)
        turned_grad[rows, :] = nn_dot(turned_keys[rows, :], unit_t[0:length, :])
        if head == 1:
            query_out = (turned_grad[...].T * scale).astype(low)
            value_out = pair_values[...].astype(low)
            for index, value_here in enumerate((query_out, (pair_keys[...] * scale).astype(low), value_out)):
                expanded[:, index * half + number * pair_width : index * half + (number + 1) * pair_width] = value_here
            vector_rows[0].append(column_sum(query_out.astype(wide)))
            vector_rows[1].append(column_sum(value_out.astype(wide)))

    def proj(index):
        return expanded[:, index * half : (index + 1) * half]

    def projection_gradient(index):
        if index == 0:
            wait_loads(17, 19)
        rows = slice(index * full, (index + 1) * full)
        qkv_parts[rows, :] = nn_dot(first_t[...], proj(index)).astype(low)

    small_flight = []

    def own_half(vector):
        return jnp.where(core == 0, vector[:, :half], vector[:, half:])

    def start_small():
        small[...] = jnp.zeros_like(small)
        vectors = vector_rows[0] + vector_rows[1]
        vectors += [own_half(sums_one[2:3]), own_half(sums_two[2:3]), own_half(sums_one[1:2]), own_half(sums_two[1:2])]
        vectors += [unit_sums[0:1], own_half(sums_one[0:1]), own_half(sums_two[0:1]), count[0:1]]
        row = 0
        for vector in vectors:
            for start in range(0, vector.shape[1], 128):
                small[row : row + 1, :] = vector[:, start : start + 128]
                row += 1
        small_flight.append(send(small, small_recv.at[0], peer["x"]))

    def next_small():
        index = len(small_flight)
        if index == 0:
            start_small()
            return
        small_flight[-1].wait_recv()
        last = small if index == 1 else small_outer.at[index - 2]
        small_outer[index - 1] = last[...] + small_recv[index - 1]
        small_flight.append(send(small_outer.at[index - 1], small_recv.at[index], peer["xyvw"[index]]))

    input_flight = []

    def input_half(side):
        columns = aligned(half * side, half)
        return (
            nt_dot(proj(0), qkv_weight[0, columns, :])
            + nt_dot(proj(1), qkv_weight[1, columns, :])
            + nt_dot(proj(2), qkv_weight[2, columns, :])
        )

    def input_gradient(index):
        if index == 0:
            input_send[...] = input_half(1 - core).astype(low)
            input_flight.append(send(input_send, input_recv, to_core))
        else:
            input_grad[...] = input_half(core)

    small_totals = []
    square_flights = []

    def finish_small():
        small_flight[-1].wait_recv()
        small_total = small_outer[2] + small_recv[3]
        if outer > 1:
            small_outer[3] = small_total
            small_outer[4 + group] = small_total
            copies = [send(small_outer.at[3], small_outer.at[4 + group], to_group[d]) for d in range(1, outer)]
            for copy in copies:
                copy.wait_recv()
            small_total = small_outer[4]
            for index in range(1, outer):
                small_total = small_total + small_outer[4 + index]
        unit = 1.0 / (D * small_total[COUNT_ROW : COUNT_ROW + 1, 0:1])
        for index in range(24):
            row, lane = index // 3, index % 3
            source = 3 * row + lane if row < 6 else 12 + 3 * row + lane
            bias_out[row : row + 1, 128 * lane : 128 * lane + 128] = small_total[source : source + 1]
        for index in range(12):
            unit_out[:, 128 * index : 128 * index + 128] = jnp.broadcast_to(small_total[18 + index : 19 + index], (8, 128))
        inside_small = lax.broadcasted_iota(jnp.int32, small_total.shape, 0) < COUNT_ROW
        square = jnp.sum(
            jnp.sum(jnp.where(inside_small, small_total * small_total, 0.0), axis=0, keepdims=True), axis=1, keepdims=True
        )
        small_totals.extend([unit, square])
        input_flight[0].wait_recv()
        summed = input_grad[...] + input_recv[...].astype(wide)
        input_grad[...] = (summed.astype(low).astype(wide) + resid_grad[...]) * unit

    def next_square():
        index = len(square_flights)
        if index == 0:
            total_square = square_terms[0]
            for term in square_terms[1:]:
                total_square = total_square + term
            squares[0] = jnp.broadcast_to(total_square, (8, 128))
        else:
            square_flights[-1].wait_recv()
            squares[index] = squares[index - 1] + square_recv[index - 1]
        if index == 4:
            squares[4] = squares[4] + jnp.broadcast_to(small_totals[1], (8, 128))
        device = to_core if index == 4 else peer["xyvw"[index]]
        square_flights.append(send(squares.at[index], square_recv.at[index], device))
        if index == 0:
            finish_small()

    start_loads()
    done = {"n": 0, "a": 0, "q": 0, "i": 0}
    for entry in SCHEDULE:
        if isinstance(entry, int):
            advance_piece(pieces[entry])
        elif entry == "D":
            wait_loads(0, 2)
            weight_gradient(0, unit_t, branch_grad, True)
        elif entry == "E":
            weight_gradient(0, unit_t, branch_grad, False)
        elif entry == "F":
            wait_loads(2, 4)
            weight_gradient(3, first_t, expanded, True)
        elif entry == "G":
            weight_gradient(3, first_t, expanded, False)
            load(x_t_in, first_t)
        elif entry == "l":
            wait_head_loads()
        elif entry == "n":
            norm_back(done["n"])
        elif entry == "o":
            out_gradient()
        elif entry == "a":
            attend_head(done["a"] // 2, done["a"] % 2)
        elif entry == "q":
            projection_gradient(done["q"])
        elif entry == "i":
            input_gradient(done["i"])
        elif entry == "s":
            next_small()
        else:
            next_square()
        if entry in done:
            done[entry] += 1
    square_flights[-1].wait_recv()
    norm = jnp.sqrt(squares[4] + square_recv[4]) * small_totals[0]
    factor_out[...] = (small_totals[0] * clip_norm / jnp.maximum(norm, clip_norm))[0:1, 0:1]
    norm_out[...] = norm[0:1, 0:1]
    for copy in pending:
        copy.wait_send()


def backward_call(outer, unit_t, first_t, branch_grad, expanded, back, base, x_all, x_t, part, other, context, context_t, queries, keys_in, values, query_mark, key_mark, out_low, qkv_low, vectors, gates, logs, sums_two, unit_sums, count):
    low, wide = jnp.bfloat16, jnp.float32
    length, full = x_all.shape
    half = full // 2
    qkv_shape = (3 * full, half)
    out_shape = (half, full)
    down_shape, up_shape = (unit_t.shape[0], full), (full, expanded.shape[1])
    big = [unit_t, first_t, branch_grad, expanded, back, base, x_all, x_t, part, other, context, context_t, queries, keys_in, values, query_mark, key_mark, out_low, qkv_low]
    little = [vectors, gates, logs, sums_two, unit_sums, count]
    vmem = pl.BlockSpec(memory_space=pltpu.VMEM)
    hbm = pl.BlockSpec(memory_space=pl.ANY)
    sizes = [(shape[0] // 3, shape[1], 4) for shape in (down_shape, up_shape) for _ in range(3)]
    split = qkv_shape[0] * 5 // 9
    sizes += [(split, half, 4), (qkv_shape[0] - split, half, 4), (half, full // 3, 3), (half, full // 3 * 2, 3)]
    copies = sum(4 + halvings + (outer - 1) for _, _, halvings in sizes) + 2 + 4 + (outer - 1) + 5
    lasts = [(rows // 2**halvings, columns) for rows, columns, halvings in sizes]
    spare = [(outer,) + last if outer > 1 else (1, 8, 128) for last in lasts]
    scratch = [pltpu.VMEM(a.shape, a.dtype) for a in big[5:7] + big[8:]]
    scratch += [pltpu.VMEM(shape, low) for shape in (unit_t.shape, first_t.shape, branch_grad.shape, expanded.shape, down_shape, up_shape)]
    scratch += [
        pltpu.VMEM(back.shape, low),
        pltpu.VMEM(back.shape, low),
        pltpu.VMEM((length, half), low),
        pltpu.VMEM((8, length), wide),
        pltpu.VMEM((8, full), wide),
        pltpu.VMEM((2 * HEAD, length), low),
        pltpu.VMEM((2 * HEAD, length), wide),
        pltpu.VMEM((length, 2 * HEAD), wide),
        pltpu.VMEM((length, 2 * HEAD), wide),
        pltpu.VMEM(qkv_shape, low),
        pltpu.VMEM(out_shape, low),
        pltpu.VMEM((length, half), low),
        pltpu.VMEM((length, half), low),
        pltpu.VMEM((SMALL_ROWS, 128), wide),
        pltpu.VMEM((4, SMALL_ROWS, 128), wide),
        pltpu.VMEM((4 + outer, SMALL_ROWS, 128), wide),
        pltpu.VMEM((5, 8, 128), wide),
        pltpu.VMEM((5, 8, 128), wide),
        pltpu.VMEM((length, half), wide),
        tuple(pltpu.VMEM(shape, low) for shape in spare),
        pltpu.SemaphoreType.DMA((copies,)),
        pltpu.SemaphoreType.DMA((copies,)),
        pltpu.SemaphoreType.DMA((len(big) + 6,)),
        pltpu.SemaphoreType.DMA((12,)),
    ]
    for size in sizes:
        scratch += piece_buffers(*size)
    return pl.pallas_call(
        functools.partial(backward_kernel, outer),
        out_shape=[
            jax.ShapeDtypeStruct(down_shape, low),
            jax.ShapeDtypeStruct(up_shape, low),
            jax.ShapeDtypeStruct(qkv_shape, low),
            jax.ShapeDtypeStruct(out_shape, low),
            jax.ShapeDtypeStruct((8, half), wide),
            jax.ShapeDtypeStruct((8, unit_sums.shape[1]), wide),
            jax.ShapeDtypeStruct((1, 1), wide),
            jax.ShapeDtypeStruct((1, 1), wide),
            jax.ShapeDtypeStruct((length, half), wide),
        ],
        in_specs=[hbm] * len(big) + [vmem] * len(little),
        out_specs=[hbm] * 4 + [vmem] * 5,
        scratch_shapes=scratch,
        compiler_params=pltpu.CompilerParams(
            collective_id=0, has_side_effects=True, vmem_limit_bytes=61 * 2**20
        ),
        cost_estimate=pl.CostEstimate(flops=2 * 10**10, bytes_accessed=3 * 10**8, transcendentals=7 * 10**6),
        name="backward_rows",
    )(*big, *little)


def on_device(
    hidden_in,
    teacher_in,
    segment_ids,
    pad_mask,
    qkv_weight,
    qkv_moment1,
    qkv_moment2,
    out_weight,
    out_moment1,
    out_moment2,
    up_weight,
    up_moment1,
    up_moment2,
    down_weight,
    down_moment1,
    down_moment2,
    bias_vectors,
    bias_moment1,
    bias_moment2,
    up_bias,
    up_bias_moment1,
    up_bias_moment2,
    norm_gains,
    gain_moment1,
    gain_moment2,
    head_gates,
    layer_gates,
    dim_gates,
    unit_gates,
    teacher_qkv,
    teacher_out,
    teacher_up,
    teacher_down,
    teacher_biases,
    teacher_up_bias,
    teacher_gains,
):
    length = segment_ids.shape[1]
    width = hidden_in.shape[2]
    wide = jnp.float32
    (
        teacher_part, teacher_other, teacher_x, part, x_all, x_turned, queries, keys_in, values, context, context_turned,
        up_low, down_low, out_low, qkv_low, logs, query_mark, key_mark, valid, vectors, teacher_vectors, gate_rows, count,
    ) = attend_rows_call(
        teacher_in[0], hidden_in[0], teacher_qkv, teacher_out, qkv_weight, out_weight, up_weight, down_weight,
        segment_ids, pad_mask, bias_vectors, norm_gains, dim_gates, teacher_biases, teacher_gains, head_gates, layer_gates,
    )
    part_other, base, back, activated, first, reduced, expanded, block_out, sums_two, unit_sums = feed_rows_call(
        teacher_x, teacher_part, teacher_other, x_all, part, teacher_up, teacher_down, up_low, down_low,
        valid, vectors, teacher_vectors, up_bias, unit_gates, teacher_up_bias,
    )
    rows_all = lax.axis_size("rows")
    down_sum, up_sum, qkv_sum, out_sum, bias_sum, unit_sum, factor, norm, input_grad = backward_call(
        rows_all // INNER, activated, first, reduced, expanded, back, base, x_all, x_turned, part, part_other, context, context_turned,
        queries, keys_in, values, query_mark, key_mark, out_low, qkv_low, vectors, gate_rows, logs,
        sums_two, unit_sums, count,
    )
    weight_sums = (lax.optimization_barrier(qkv_sum.reshape(qkv_weight.shape)), out_sum, up_sum, down_sum)
    weights = (qkv_weight, out_weight, up_weight, down_weight)
    firsts = (qkv_moment1, out_moment1, up_moment1, down_moment1)
    seconds = (qkv_moment2, out_moment2, up_moment2, down_moment2)
    rates = (rate_attend, rate_output, rate_expand, rate_reduce)
    results = []
    for index in range(4):
        clipped = weight_sums[index].astype(wide) * factor
        new_weight, new_second = adam_step(
            weights[index], firsts[index], seconds[index], clipped, rates[index], weight_decay
        )
        results.append((clipped, new_weight, new_second, new_weight.astype(jnp.bfloat16)))
    vector_results = vector_adam(
        factor, norm, block_out, input_grad, bias_sum, unit_sum, bias_vectors, bias_moment1, bias_moment2, up_bias, up_bias_moment1, up_bias_moment2,
        norm_gains, gain_moment1, gain_moment2,
    )
    norm, block_out, input_grad = vector_results[:3]
    grad_norm = norm.reshape(())
    results += [vector_results[3:6], vector_results[6:9], vector_results[9:12]]
    block_out = block_out.reshape(hidden_in.shape)
    input_grad = input_grad.reshape(hidden_in.shape)
    return (
        block_out,
        input_grad,
        grad_norm,
        results[0][0],
        results[0][1],
        results[0][2],
        results[1][0],
        results[1][1],
        results[1][2],
        results[2][0],
        results[2][1],
        results[2][2],
        results[3][0],
        results[3][1],
        results[3][2],
        results[4][0],
        results[4][1],
        results[4][2],
        results[5][0],
        results[5][1],
        results[5][2],
        results[6][0],
        results[6][1],
        results[6][2],
        results[0][3],
        results[1][3],
        results[2][3],
        results[3][3],
    )


def solution(mesh):
    in_specs = (
        P("rows", None, "hid"),
        P("rows", None, "hid"),
        P("rows", None),
        P("rows", None),
        P(None, None, "hid"),
        P(None, None, "hid"),
        P(None, None, "hid"),
        P("hid", None),
        P("hid", None),
        P("hid", None),
        P(None, "hid"),
        P(None, "hid"),
        P(None, "hid"),
        P("hid", None),
        P("hid", None),
        P("hid", None),
        P(None, "hid"),
        P(None, "hid"),
        P(None, "hid"),
        P("hid"),
        P("hid"),
        P("hid"),
        P(None, "hid"),
        P(None, "hid"),
        P(None, "hid"),
        P("hid"),
        P(),
        P("hid"),
        P("hid"),
        P(None, None, "hid"),
        P("hid", None),
        P(None, "hid"),
        P("hid", None),
        P(None, "hid"),
        P("hid"),
        P(None, "hid"),
    )
    out_specs = (
        P("rows", None, "hid"),
        P("rows", None, "hid"),
        P(),
        P(None, None, "hid"),
        P(None, None, "hid"),
        P(None, None, "hid"),
        P("hid", None),
        P("hid", None),
        P("hid", None),
        P(None, "hid"),
        P(None, "hid"),
        P(None, "hid"),
        P("hid", None),
        P("hid", None),
        P("hid", None),
        P(None, "hid"),
        P(None, "hid"),
        P(None, "hid"),
        P("hid"),
        P("hid"),
        P("hid"),
        P(None, "hid"),
        P(None, "hid"),
        P(None, "hid"),
        P(None, None, "hid"),
        P("hid", None),
        P(None, "hid"),
        P("hid", None),
    )
    return jax.shard_map(
        on_device, mesh=mesh, in_specs=in_specs, out_specs=out_specs, check_vma=False
    )
```

```python
import functools

import jax
import jax.numpy as jnp
from jax import lax
from jax.experimental import pallas as pl
from jax.experimental.pallas import tpu as pltpu
from jax.sharding import PartitionSpec as P

D = 768
HEAD = 64
STEP = 10


epsilon_norm = 1e-06
masked_score = -1000000000.0
clip_norm = 0.001
beta_first = 0.9
beta_second = 0.999
adam_epsilon = 1e-08
weight_decay = 0.01
rate_attend = 0.03
rate_output = 0.2
rate_expand = 0.03
rate_reduce = 0.03
rate_vector = 0.3


def adam_step(weight, first, second, grad, rate, decay):
    first_new = beta_first * first + (1.0 - beta_first) * grad
    second_new = beta_second * second + (1.0 - beta_second) * grad * grad
    first_hat = first_new / (1.0 - beta_first**STEP)
    second_hat = second_new / (1.0 - beta_second**STEP)
    return (
        weight - rate * (first_hat / (jnp.sqrt(second_hat) + adam_epsilon) + decay * weight),
        second_new,
    )


MARKS = 128
TILE = 256


def nt_dot(left, right):
    return lax.dot_general(
        left, right, (((1,), (1,)), ((), ())), preferred_element_type=jnp.float32
    )


def nn_dot(left, right):
    return jnp.dot(left, right, preferred_element_type=jnp.float32)


def aligned(start, size):
    return pl.ds(pl.multiple_of(start, 16), size)


def lanes_of(core, width):
    return pl.ds(pl.multiple_of(core * width, 128), width)


class Mover:
    def __init__(self, local_sems, send_sems, recv_sems):
        self.local_sems, self.send_sems, self.recv_sems = local_sems, send_sems, recv_sems
        self.local_count = self.remote_count = 0
        self.sent = []

    def copy(self, source, target):
        moved = pltpu.make_async_copy(source, target, self.local_sems.at[self.local_count])
        self.local_count += 1
        moved.start()
        return moved

    def send(self, source, target, device):
        index = self.remote_count
        self.remote_count += 1
        moved = pltpu.make_async_remote_copy(
            src_ref=source, dst_ref=target, send_sem=self.send_sems.at[index],
            recv_sem=self.recv_sems.at[index], device_id=device, device_id_type=pl.DeviceIdType.MESH,
        )
        moved.start()
        self.sent.append(moved)
        return moved


def greet(core):
    barrier = pltpu.get_barrier_semaphore()
    to_core = {"hid": 1 - core}
    pl.semaphore_signal(barrier, inc=1, device_id=to_core, device_id_type=pl.DeviceIdType.MESH)
    pl.semaphore_wait(barrier, 1)
    return to_core


def attend_rows_kernel(
    teacher_in, hidden_in, teacher_qkv, teacher_out, qkv_weight, out_weight, up_weight, down_weight,
    segment_ref, padding_ref, bias_ref, gain_ref, dim_ref, teacher_bias_ref, teacher_gain_ref, head_gates, layer_gates,
    teacher_part_out, teacher_other_out, teacher_x_out, part_out, x_out, turned_out, query_out, key_out, value_out,
    context_out, context_turned_out, up_out, down_out, out_out, qkv_out,
    log_ref, query_mark_ref, key_mark_ref, valid_ref, vector_ref, teacher_vector_ref, gate_ref, count_ref,
    teacher_x, x_all, turned, query, key, value, context, context_turned, teacher_part, part,
    teacher_qkv_held, teacher_out_held, qkv_wide, out_wide, up_wide, down_wide, qkv_low, out_low, up_low, down_low,
    pack, spread, local_sems, send_sems, recv_sems,
):
    low, wide = jnp.bfloat16, jnp.float32
    core = lax.axis_index("hid")
    mover = Mover(local_sems, send_sems, recv_sems)
    length, width = hidden_in.shape
    here = lanes_of(core, width)
    to_core = greet(core)

    arriving = [mover.copy(teacher_in, teacher_x.at[:, here]), mover.send(teacher_in, teacher_x.at[:, here], to_core)]
    arriving_weights = [mover.copy(teacher_qkv, teacher_qkv_held), mover.copy(teacher_out, teacher_out_held)]
    arriving_student = [mover.copy(hidden_in, x_all.at[:, here]), mover.send(hidden_in, x_all.at[:, here], to_core)]
    casts = [
        (mover.copy(qkv_weight, qkv_wide), qkv_wide, qkv_low, qkv_out),
        (mover.copy(out_weight, out_wide), out_wide, out_low, out_out),
        (mover.copy(up_weight, up_wide), up_wide, up_low, up_out),
        (mover.copy(down_weight, down_wide), down_wide, down_low, down_out),
    ]
    leaving = []

    def cast(index):
        arrived, source, target, output = casts[index]
        arrived.wait()
        target[...] = source[...].astype(low)
        leaving.append(mover.copy(target, output))

    pack[0:4] = bias_ref[2:6]
    pack[4:6] = gain_ref[...]
    pack[6:7] = dim_ref[...].reshape(1, width)
    pack[7:8] = jnp.zeros_like(pack[7:8])
    pack[8:12] = teacher_bias_ref[2:6].astype(wide)
    pack[12:14] = teacher_gain_ref[...].astype(wide)
    pack[14:16] = jnp.zeros_like(pack[14:16])
    pack_flight = mover.send(pack, spread.at[:, here], to_core)
    spread[:, here] = pack[...]

    marks = lax.broadcasted_iota(jnp.int32, (MARKS, length), 0)
    same = jnp.broadcast_to(segment_ref[...], (MARKS, length)) == marks
    padding = jnp.broadcast_to(padding_ref[...], (MARKS, length))
    query_mark_ref[...] = jnp.where(same, 1.0, 0.0).T.astype(low)
    key_mark_ref[...] = jnp.where((same & (padding > 0)) | (marks >= 8), 0.0, masked_score).T.astype(low)
    valid_ref[...] = padding.astype(wide).T
    count_ref[...] = jnp.broadcast_to(jnp.sum(padding[0:8].astype(wide), axis=1, keepdims=True), (8, 128))

    pair = 2 * HEAD
    pairs = width // pair
    block_rows = length // 2
    first_head = lax.broadcasted_iota(jnp.int32, (1, pair), 1) < HEAD
    gate_ref[...] = jnp.zeros_like(gate_ref)
    for number in range(pairs):
        row = jnp.where(first_head, head_gates[2 * number], head_gates[2 * number + 1])
        gate_ref[0:1, number * pair : (number + 1) * pair] = row
        gate_ref[1:2, number * pair : (number + 1) * pair] = 1.0 / row

    def project(x_ref, weights, query_bias, value_bias):
        rows = x_ref[...]
        query[...] = (nn_dot(rows, weights[0]) + query_bias).astype(low)
        key[...] = nn_dot(rows, weights[1]).astype(low)
        value[...] = (nn_dot(rows, weights[2]) + value_bias).astype(low)

    def attend(number, keep):
        lanes = slice(number * pair, (number + 1) * pair)
        scaled = query[:, lanes] * jnp.asarray(HEAD ** (-0.5), low)
        key_wide = jnp.concatenate([key[:, lanes], key_mark_ref[...]], axis=1)
        values = jnp.concatenate([value[:, lanes], jnp.ones((length, pair), low)], axis=1)
        logs = []
        for start in range(0, length, block_rows):
            block = slice(start, start + block_rows)
            outs, columns = [], []
            for head in range(2):
                chosen = jnp.where(first_head if head == 0 else ~first_head, scaled[block], jnp.zeros_like(scaled[block]))
                query_wide = jnp.concatenate([chosen, query_mark_ref[block]], axis=1)
                scores = nt_dot(query_wide, key_wide)
                top = jnp.max(scores, axis=1, keepdims=True)
                weights = jnp.exp(scores - top)
                mixed = nn_dot(weights.astype(low), values)
                sums = mixed[:, pair:]
                outs.append(mixed[:, :pair] * (1.0 / sums))
                if keep:
                    columns.append(top + jnp.log(sums))
            mixed = jnp.where(first_head, outs[0], outs[1])
            if keep:
                mixed = mixed * gate_ref[0:1, lanes]
                logs.append(jnp.where(first_head, columns[0], columns[1]))
            mixed = mixed.astype(low)
            context[block, lanes] = mixed
            if keep:
                context_turned[lanes, block] = mixed.T
        if keep:
            log_turned = jnp.concatenate(logs, axis=0).T
            log_ref[8 * number : 8 * number + 8] = jnp.concatenate(
                [log_turned[0:1], log_turned[HEAD : HEAD + 1], log_turned[0:6]], axis=0
            )

    for moved in arriving[:1] + arriving_weights[:1]:
        moved.wait()
    arriving[1].wait_recv()
    leaving.append(mover.copy(teacher_x, teacher_x_out))
    project(teacher_x, teacher_qkv_held, teacher_bias_ref[0:1].astype(wide), teacher_bias_ref[1:2].astype(wide))
    for number in range(pairs):
        attend(number, False)
        cast(number)
    arriving_weights[1].wait()
    teacher_part[...] = nn_dot(context[...], teacher_out_held[...]).astype(low)
    teacher_flight = mover.send(teacher_part, teacher_other_out, to_core)
    leaving.append(mover.copy(teacher_part, teacher_part_out))

    arriving_student[0].wait()
    arriving_student[1].wait_recv()
    leaving.append(mover.copy(x_all, x_out))
    project(x_all, qkv_low, bias_ref[0:1], bias_ref[1:2])
    leaving.append(mover.copy(query, query_out))
    leaving.append(mover.copy(key, key_out))
    leaving.append(mover.copy(value, value_out))
    turned[...] = x_all[...].T
    leaving.append(mover.copy(turned, turned_out))
    for number in range(pairs):
        attend(number, True)
        if number == 0:
            cast(3)
    part[...] = nn_dot(context[...], out_low[...]).astype(low)
    leaving.append(mover.copy(part, part_out))
    leaving.append(mover.copy(context, context_out))
    leaving.append(mover.copy(context_turned, context_turned_out))

    pack_flight.wait_recv()
    dims = spread[6:7]
    ones = jnp.ones_like(dims)
    for target, rows, scales in (
        (vector_ref, spread[0:8], (layer_gates[0] * dims, layer_gates[1] * dims)),
        (teacher_vector_ref, spread[8:16], (ones, ones)),
    ):
        target[...] = jnp.concatenate(
            [scales[0], rows[0:1], rows[4:5], rows[2:3], scales[1], rows[1:2], rows[5:6], rows[3:4]], axis=0
        )
    teacher_flight.wait_recv()
    for moved in leaving:
        moved.wait()
    for moved in mover.sent:
        moved.wait_send()


def attend_rows_call(teacher_in, hidden_in, teacher_qkv, teacher_out, qkv_weight, out_weight, up_weight, down_weight, segment, padding, biases, gains, dims, teacher_biases, teacher_gains, head_gates, layer_gates):
    low, wide = jnp.bfloat16, jnp.float32
    length, width = hidden_in.shape
    full = 2 * width
    pairs = width // (2 * HEAD)
    hidden = up_weight.shape[1]
    vmem, anywhere = pl.BlockSpec(memory_space=pltpu.VMEM), pl.BlockSpec(memory_space=pl.ANY)
    smem = pl.BlockSpec(memory_space=pltpu.SMEM)
    rows_full, rows_half = (length, full), (length, width)
    far = [rows_full] * 5 + [(full, length)] + [rows_half] * 4 + [(width, length)]
    far += [up_weight.shape, down_weight.shape, out_weight.shape, qkv_weight.shape]
    near = [
        ((8 * pairs, length), wide), ((length, MARKS), low), ((length, MARKS), low), ((length, MARKS), wide),
        ((8, full), wide), ((8, full), wide), ((8, width), wide), ((8, 128), wide),
    ]
    held = [rows_full, rows_full, (full, length), rows_half, rows_half, rows_half, rows_half, (width, length), rows_full, rows_full]
    return pl.pallas_call(
        attend_rows_kernel,
        out_shape=[jax.ShapeDtypeStruct(shape, low) for shape in far] + [jax.ShapeDtypeStruct(*pair) for pair in near],
        in_specs=[anywhere] * 8 + [vmem] * 7 + [smem] * 2,
        out_specs=[anywhere] * len(far) + [vmem] * len(near),
        scratch_shapes=[pltpu.VMEM(shape, low) for shape in held]
        + [pltpu.VMEM(teacher_qkv.shape, low), pltpu.VMEM(teacher_out.shape, low)]
        + [pltpu.VMEM(w.shape, wide) for w in (qkv_weight, out_weight, up_weight, down_weight)]
        + [pltpu.VMEM(w.shape, low) for w in (qkv_weight, out_weight, up_weight, down_weight)]
        + [pltpu.VMEM((16, width), wide), pltpu.VMEM((16, full), wide)]
        + [pltpu.SemaphoreType.DMA((24,)), pltpu.SemaphoreType.DMA((4,)), pltpu.SemaphoreType.DMA((4,))],
        compiler_params=pltpu.CompilerParams(collective_id=1, has_side_effects=True, vmem_limit_bytes=60 * 2**20),
        cost_estimate=pl.CostEstimate(flops=2 * 10**10, bytes_accessed=5 * 10**7, transcendentals=14 * 10**6),
        name="attend_rows",
    )(
        teacher_in, hidden_in, teacher_qkv, teacher_out, qkv_weight, out_weight, up_weight, down_weight,
        segment, padding, biases, gains, dims, teacher_biases, teacher_gains, head_gates, layer_gates,
    )


def norm_parts(resid):
    center = jnp.mean(resid, axis=1, keepdims=True)
    second = jnp.mean(resid * resid, axis=1, keepdims=True)
    inverse = lax.rsqrt(second - center * center + epsilon_norm)
    return (resid - center) * inverse, inverse


def norm_grad(grad_normed, normed, inverse):
    center = jnp.mean(grad_normed, axis=1, keepdims=True)
    crossed = jnp.mean(grad_normed * normed, axis=1, keepdims=True)
    return inverse * (grad_normed - center - normed * crossed)


def column_sum(value):
    return jnp.sum(value, axis=0, keepdims=True)


def feed_rows_kernel(
    teacher_x_in, teacher_part_in, teacher_other_in, x_in, part_in, teacher_up_in, teacher_down_in, up_in, down_in,
    valid_ref, vector_ref, teacher_vector_ref, up_bias_ref, unit_gate_ref, teacher_up_bias_ref,
    other_out, base_out, back_out, activated_out, first_out, reduced_out, expanded_out, block_ref, sums_ref, unit_sums_ref,
    teacher_x, teacher_part, teacher_other, x_all, part, other, teacher_up, teacher_down, up, down,
    teacher_first, first, teacher_reduced, teacher_reduced_other, reduced, reduced_other, slope, activated_turned,
    first_turned, grad_reduced, grad_expanded, base, back, local_sems, send_sems, recv_sems,
):
    low, wide = jnp.bfloat16, jnp.float32
    core = lax.axis_index("hid")
    mover = Mover(local_sems, send_sems, recv_sems)
    length, full = x_in.shape
    half = full // 2
    up_bias, unit_gate, teacher_up_bias = (r[...].astype(wide).reshape(1, r.shape[0]) for r in (up_bias_ref, unit_gate_ref, teacher_up_bias_ref))
    to_core = greet(core)
    part_flight = mover.send(part_in, other, to_core)
    tiles = [slice(start, start + TILE) for start in range(0, length, TILE)]
    teacher_rows = ((teacher_x_in, teacher_x), (teacher_part_in, teacher_part), (teacher_other_in, teacher_other))
    tile_loads = [[mover.copy(source.at[tiles[0]], target.at[tiles[0]]) for source, target in teacher_rows]]
    up_load = mover.copy(teacher_up_in, teacher_up)
    down_load = mover.copy(teacher_down_in, teacher_down)
    rest = slice(TILE, length)
    tile_loads.append([mover.copy(source.at[rest], target.at[rest]) for source, target in teacher_rows])
    loads = [
        mover.copy(source, target) for source, target in ((x_in, x_all), (part_in, part), (up_in, up), (down_in, down))
    ]

    def norm_one(x_ref, own_ref, far_ref, vectors, block):
        branch = own_ref[block].astype(wide) + far_ref[block].astype(wide)
        normed, _ = norm_parts(x_ref[block].astype(wide) + (branch + vectors[1:2]) * vectors[0:1])
        return normed * vectors[2:3] + vectors[3:4]

    def gelu_share(expanded):
        return 0.5 + 0.5 * lax.erf(expanded * (0.5**0.5))

    teacher_flights = []
    for index, block in enumerate(tiles):
        if index < 2:
            for moved in tile_loads[index]:
                moved.wait()
        out = norm_one(teacher_x, teacher_part, teacher_other, teacher_vector_ref, block)
        teacher_first[block] = out
        if index == 0:
            up_load.wait()
        expanded = nn_dot(out.astype(low), teacher_up[...]) + teacher_up_bias
        activated = (expanded * gelu_share(expanded)).astype(low)
        if index == 0:
            down_load.wait()
        teacher_reduced[block] = nn_dot(activated, teacher_down[...]).astype(low)
        teacher_flights.append(mover.send(teacher_reduced.at[block], teacher_reduced_other.at[block], to_core))
    for moved in loads:
        moved.wait()
    part_flight.wait_recv()
    leaving = [mover.copy(other, other_out)]
    flights = []
    for block in tiles:
        out = norm_one(x_all, part, other, vector_ref, block)
        first[block] = out
        out_low = out.astype(low)
        first_turned[:, block] = out_low.T
        expanded = nn_dot(out_low, up[...]) + up_bias
        share = gelu_share(expanded)
        activated = (expanded * share * unit_gate).astype(low)
        reduced[block] = nn_dot(activated, down[...]).astype(low)
        flights.append(mover.send(reduced.at[block], reduced_other.at[block], to_core))
        activated_turned[:, block] = activated.T
        bell = jnp.exp(-0.5 * expanded * expanded)
        slope[block] = ((share + expanded * bell * 0.3989422804014327) * unit_gate).astype(low)
        leaving.append(mover.copy(activated_turned.at[:, block], activated_out.at[:, block]))
        leaving.append(mover.copy(first_turned.at[:, block], first_out.at[:, block]))

    sums_ref[...] = jnp.zeros_like(sums_ref)
    unit_sums_ref[...] = jnp.zeros_like(unit_sums_ref)
    for index, block in enumerate(tiles):
        teacher_flights[index].wait_recv()
        flights[index].wait_recv()
        student_first, target_first = first[block], teacher_first[block]
        branch = reduced[block].astype(wide) + reduced_other[block].astype(wide)
        normed, inverse = norm_parts(student_first + (branch + vector_ref[5:6]) * vector_ref[4:5])
        second = normed * vector_ref[6:7] + vector_ref[7:8]
        target_branch = teacher_reduced[block].astype(wide) + teacher_reduced_other[block].astype(wide)
        target_normed, _ = norm_parts(target_first + target_branch + teacher_vector_ref[5:6])
        target = target_normed * teacher_vector_ref[6:7] + teacher_vector_ref[7:8]
        block_ref[block] = jnp.where(core == 0, second[:, :half], second[:, half:]).astype(low)
        twice = valid_ref[block, 0:1] * 2.0
        grad_second = twice * (second - target)
        grad_resid = norm_grad(grad_second * vector_ref[6:7], normed, inverse)
        grad_branch = grad_resid * vector_ref[4:5]
        sums_ref[0:1] += column_sum(grad_second * normed)
        sums_ref[1:2] += column_sum(grad_second)
        sums_ref[2:3] += column_sum(grad_branch)
        grad_branch_low = grad_branch.astype(low)
        grad_reduced[block] = grad_branch_low
        grad_activated = nt_dot(grad_branch_low, down[...]).astype(low).astype(wide)
        grad_unit = (grad_activated * slope[block].astype(wide)).astype(low)
        grad_expanded[block] = grad_unit
        unit_sums_ref[0:1] += column_sum(grad_unit.astype(wide))
        back[block] = nt_dot(grad_unit, up[...]).astype(low)
        base[block] = twice * (student_first - target_first) + grad_resid
        leaving.append(mover.copy(back.at[block], back_out.at[block]))
        leaving.append(mover.copy(base.at[block], base_out.at[block]))
        leaving.append(mover.copy(grad_reduced.at[block], reduced_out.at[block]))
        leaving.append(mover.copy(grad_expanded.at[block], expanded_out.at[block]))
    for moved in leaving:
        moved.wait()
    for moved in mover.sent:
        moved.wait_send()


def feed_rows_call(teacher_x, teacher_part, teacher_other, x_all, part, teacher_up, teacher_down, up_low, down_low, valid, vectors, teacher_vectors, up_bias, unit_gates, teacher_up_bias):
    low, wide = jnp.bfloat16, jnp.float32
    length, full = x_all.shape
    hidden = up_low.shape[1]
    vmem, anywhere = pl.BlockSpec(memory_space=pltpu.VMEM), pl.BlockSpec(memory_space=pl.ANY)
    rows = (length, full)
    up_shape, down_shape = up_low.shape, down_low.shape
    far = [(rows, low), (rows, wide), (rows, low), ((hidden, length), low), ((full, length), low), (rows, low), ((length, hidden), low)]
    near = [((length, full // 2), low), ((8, full), wide), ((8, hidden), wide)]
    held = [(rows, low)] * 6 + [(up_shape, low), (down_shape, low)] * 2
    held += [(rows, wide)] * 2 + [(rows, low)] * 4 + [((length, hidden), low), ((hidden, length), low), ((full, length), low)]
    held += [(rows, low), ((length, hidden), low), (rows, wide), (rows, low)]
    return pl.pallas_call(
        feed_rows_kernel,
        out_shape=[jax.ShapeDtypeStruct(*pair) for pair in far + near],
        in_specs=[anywhere] * 9 + [vmem] * 6,
        out_specs=[anywhere] * len(far) + [vmem] * len(near),
        scratch_shapes=[pltpu.VMEM(*pair) for pair in held]
        + [pltpu.SemaphoreType.DMA((48,)), pltpu.SemaphoreType.DMA((12,)), pltpu.SemaphoreType.DMA((12,))],
        compiler_params=pltpu.CompilerParams(collective_id=2, has_side_effects=True, vmem_limit_bytes=62 * 2**20),
        cost_estimate=pl.CostEstimate(flops=3 * 10**10, bytes_accessed=5 * 10**7, transcendentals=6 * 10**6),
        name="feed_rows",
    )(
        teacher_x, teacher_part, teacher_other, x_all, part, teacher_up, teacher_down, up_low, down_low,
        valid, vectors, teacher_vectors, up_bias, unit_gates, teacher_up_bias,
    )


def vector_adam_kernel(
    factor_ref, norm_in, block_in, input_grad_in, bias_sum, unit_sum, bias, bias_first, bias_second,
    unit, unit_first, unit_second, gain, gain_first, gain_second,
    norm_out, block_out, input_grad_out, bias_grad, bias_new, bias_second_new, unit_grad, unit_new, unit_second_new, gain_grad, gain_new, gain_second_new,
):
    block_out[...] = block_in[...]
    input_grad_out[...] = input_grad_in[...]
    norm_out[...] = norm_in[...]
    factor = factor_ref[...]
    for total, states, outs in (
        (bias_sum[0:6], (bias, bias_first, bias_second), (bias_grad, bias_new, bias_second_new)),
        (bias_sum[6:8], (gain, gain_first, gain_second), (gain_grad, gain_new, gain_second_new)),
        (unit_sum[0:1], (unit, unit_first, unit_second), (unit_grad, unit_new, unit_second_new)),
    ):
        clipped = total * factor
        values = [state[...].reshape(clipped.shape) for state in states]
        new_weight, new_second = adam_step(*values, clipped, rate_vector, 0.0)
        for target, value in zip(outs, (clipped, new_weight, new_second)):
            target[...] = value.reshape(target.shape)


def vector_adam(*arrays):
    same = [jax.ShapeDtypeStruct(a.shape, a.dtype) for a in arrays[1:4]]
    shapes = [a.shape for a in arrays[6:15:3] for _ in range(3)]
    vmem = pl.BlockSpec(memory_space=pltpu.VMEM)
    return pl.pallas_call(
        vector_adam_kernel,
        out_shape=same + [jax.ShapeDtypeStruct(shape, jnp.float32) for shape in shapes],
        in_specs=[vmem] * 15,
        out_specs=[vmem] * 12,
        cost_estimate=pl.CostEstimate(flops=10**5, bytes_accessed=5 * 10**6, transcendentals=10**4),
        name="vector_adam",
    )(*arrays)


INNER = 16
SMALL_ROWS = 40
COUNT_ROW = 36


class Piece:
    def __init__(self, source, target, first_row, rows, first_column, columns, order, own, halvings):
        self.source, self.target = source, target
        self.first_row, self.rows = first_row, rows
        self.first_column, self.columns = first_column, columns
        self.order, self.own, self.halvings = order, own, halvings


def piece_buffers(rows, columns, halvings):
    low, wide = jnp.bfloat16, jnp.float32
    last = rows // 16 if halvings == 4 else rows // 8
    return [
        pltpu.VMEM((rows // 2, columns), low),
        pltpu.VMEM((rows // 4, columns), low),
        pltpu.VMEM((rows // 8, columns), low),
        pltpu.VMEM((last, columns), low),
        pltpu.VMEM((rows // 4, columns), low),
        pltpu.VMEM((rows // 8, columns), low),
        pltpu.VMEM((last, columns), low),
        pltpu.VMEM((rows // 4, columns), wide),
        pltpu.VMEM((last, columns), low),
    ]


SCHEDULE = (
    "D", 1, 0, "F", 2, "E", "G", "l", 5, "n", "n", 1, 0, "n", "n", 4, 2, "o", 3, "a", 0, 1, "a", "a", 0, 2, 9, 5, 1,
    "a", 4, 8, 0, 2, "a", 1, 3, "a", 0, 9, 2, 4, "q", 5, "q", 6, 8, "q", 7, 1, "i", 3, 4, 5, 2, 3, 0, 9, 1, 4, "i", 7,
    6, 3, 8, "s", 5, "s", 4, 0, 3, 8, 1, 6, 5, 4, "s", 9, 2, 7, 3, "s", 6, 5, 8, 7, 6, 0, 8, 3, 4, 7, 9, 6, 7, 2, 9, 6,
    "S", 7, 8, 4, 9, "S", 6, 5, "S", 7, "S", 2, 1, 9, 8, "S", 3, 5, 7, 6,
)


def backward_kernel(
    outer, unit_t_in, first_t_in, branch_in, expanded_in, back, base_in, x_in, x_t_in, part_in, other_in, context_in, context_t_in, query_in,
    key_in, value_in, query_mark_in, key_mark_in, out_weight_in, qkv_weight_in,
    vector_ref, gate_ref, log_ref, sums_two, unit_sums, count,
    down_sum, up_sum, qkv_sum, out_sum, bias_out, unit_out, factor_out, norm_out, input_grad,
    base, x, part, other, context, context_t, query,
    key, value, query_mark, key_mark, out_weight, qkv_weight,
    unit_t, first_t, branch_grad, expanded, down, up, back_other, back_own, heads_grad, inner_rows, sums_one, turned_keys,
    turned_grad, pair_keys, pair_values, qkv_parts, out_parts, input_send, input_recv, small, small_recv,
    small_outer, squares, square_recv, resid_grad, shard_outer, send_sems, recv_sems, load_sems, shard_sems, *buffers,
):
    low, wide = jnp.bfloat16, jnp.float32
    place = lax.axis_index("rows")
    inside = place % INNER
    group = place // INNER
    core = lax.axis_index("hid")
    bits = {"x": inside % 2, "y": (inside // 2) % 2, "v": (inside // 4) % 2, "w": inside // 8}
    steps = {"x": 1, "y": 2, "v": 4, "w": 8}
    peer = {name: {"rows": place + steps[name] - 2 * steps[name] * bits[name]} for name in bits}
    to_group = [{"rows": inside + INNER * ((group + d) % outer)} for d in range(outer)]
    to_core = {"hid": 1 - core}
    barrier = pltpu.get_barrier_semaphore()
    peers = list(peer.values()) + to_group[1:] + [to_core]
    for there in peers:
        pl.semaphore_signal(barrier, inc=1, device_id=there, device_id_type=pl.DeviceIdType.MESH)
    pl.semaphore_wait(barrier, len(peers))

    counter = [0]
    pending = []

    def send(source, target, device):
        index = counter[0]
        counter[0] += 1
        copy = pltpu.make_async_remote_copy(
            src_ref=source, dst_ref=target, send_sem=send_sems.at[index],
            recv_sem=recv_sems.at[index], device_id=device, device_id_type=pl.DeviceIdType.MESH,
        )
        copy.start()
        pending.append(copy)
        return copy

    loads = []

    def load(source, target):
        copy = pltpu.make_async_copy(source, target, load_sems.at[len(loads)])
        copy.start()
        loads.append(copy)

    def wait_loads(first, last):
        for copy in loads[first:last]:
            copy.wait()

    orders = ("xyvw", "yxvw", "vxyw")
    orders_two = ("xyvw", "yxvw", "vyxw")
    pieces = []

    def add_piece(*fields):
        piece = Piece(*fields)
        piece.index, piece.step = len(pieces), 0
        piece.buffers = buffers[9 * piece.index : 9 * piece.index + 9]
        piece.offsets = [0]
        size = piece.rows
        for name in piece.order[: piece.halvings]:
            size = size // 2
            piece.offsets.append(piece.offsets[-1] + size * bits[name])
        pieces.append(piece)

    for source, target, lanes in ((down, down_sum, orders), (up, up_sum, orders_two)):
        rows = source.shape[0] // 3
        for lane in range(3):
            add_piece(source, target, rows * lane, rows, 0, source.shape[1], lanes[lane], None, 4)
    columns = qkv_parts.shape[1]
    split = qkv_parts.shape[0] * 5 // 9
    add_piece(qkv_parts, qkv_sum, 0, split, 0, columns, orders[0], None, 4)
    add_piece(qkv_parts, qkv_sum, split, qkv_parts.shape[0] - split, 0, columns, orders[1], None, 4)
    split = out_parts.shape[1] // 3
    add_piece(out_parts, out_sum, 0, out_parts.shape[0], 0, split, orders[0], None, 3)
    add_piece(out_parts, out_sum, 0, out_parts.shape[0], split, 2 * split, orders[1], None, 3)

    square_terms = []

    def advance_piece(piece):
        r1, r2, r3, r4, s2, s3, s4, keep, shard = piece.buffers
        step = piece.step
        piece.step += 1
        order, rows = piece.order, piece.rows
        columns = pl.ds(piece.first_column, piece.columns)
        names_done = order[: piece.halvings]

        def own(start, size):
            if piece.own is not None:
                return piece.own[aligned(start, size), :].astype(wide)
            return piece.source[aligned(piece.first_row + piece.offsets[1] + start, size), columns].astype(wide)

        if step == 0:
            start = piece.first_row + rows // 2 * (1 - bits[order[0]])
            piece.flight = send(piece.source.at[aligned(start, rows // 2), columns], r1, peer[order[0]])
        elif step == 1:
            if piece.own is not None:
                wait_loads(piece.loaded, piece.loaded + 1)
            piece.flight.wait_recv()
            bit = bits[order[1]]
            size = rows // 4
            sent = size * (1 - bit)
            s2[...] = (own(sent, size) + r1[aligned(sent, size), :].astype(wide)).astype(low)
            piece.flight = send(s2, r2, peer[order[1]])
            kept = size * bit
            keep[...] = own(kept, size) + r1[aligned(kept, size), :].astype(wide)
        elif step == 2:
            piece.flight.wait_recv()
            keep[...] = keep[...] + r2[...].astype(wide)
            bit = bits[order[2]]
            size = rows // 8
            s3[...] = keep[aligned(size * (1 - bit), size), :].astype(low)
            piece.flight = send(s3, r3, peer[order[2]])
        elif step == 3:
            piece.flight.wait_recv()
            size = rows // 8
            mine = aligned(size * bits[order[2]], size)
            total = keep[mine, :] + r3[...].astype(wide)
            if piece.halvings == 4:
                keep[mine, :] = total
                small_size = size // 2
                sent = size * bits[order[2]] + small_size * (1 - bits[order[3]])
                s4[...] = keep[aligned(sent, small_size), :].astype(low)
            else:
                s4[...] = total.astype(low)
            piece.flight = send(s4, r4, peer[order[3]])
        elif step == 4:
            piece.flight.wait_recv()
            if piece.halvings == 4:
                size = rows // 16
                kept = rows // 8 * bits[order[2]] + size * bits[order[3]]
                total = keep[aligned(kept, size), :] + r4[...].astype(wide)
                weight = 1.0
            else:
                total = s4[...].astype(wide) + r4[...].astype(wide)
                weight = 0.5
            if outer > 1:
                shard[...] = total.astype(low)
                shard_outer[piece.index][0] = shard[...]
                copies = [send(shard, shard_outer[piece.index].at[d], to_group[d]) for d in range(1, outer)]
                for copy in copies:
                    copy.wait()
                    pending[:] = [entry for entry in pending if entry is not copy]
                total = jnp.zeros_like(total)
                for index in range(outer):
                    total = total + shard_outer[piece.index][(group - index + outer) % outer].astype(wide)
            shard[...] = total.astype(low)
            square_terms.append(weight * jnp.sum(jnp.sum(total * total, axis=0, keepdims=True), axis=1, keepdims=True))
            size = rows // 2**piece.halvings
            here = piece.target.at[aligned(piece.first_row + piece.offsets[-1], size), columns]
            piece.local = pltpu.make_async_copy(shard, here, shard_sems.at[piece.index])
            piece.local.start()
            piece.flight = send(shard, here, peer[names_done[-1]])
        elif step < 4 + piece.halvings:
            level = piece.halvings - (step - 4)
            piece.flight.wait_recv()
            if step == 5:
                piece.local.wait()
            size = rows // 2**level
            block = piece.target.at[aligned(piece.first_row + piece.offsets[level], size), columns]
            piece.flight = send(block, block, peer[names_done[level - 1]])
        elif step == 4 + piece.halvings:
            piece.flight.wait_recv()

    back_flight = []
    length, full = x.shape
    half = full // 2
    head_loads = ((base_in, base), (x_in, x), (part_in, part), (other_in, other), (back, back_own), (context_in, context), (out_weight_in, out_weight))
    mid_loads = ((context_t_in, context_t), (query_in, query), (key_in, key), (value_in, value), (query_mark_in, query_mark), (key_mark_in, key_mark))

    def start_loads():
        for pair in ((unit_t_in, unit_t), (branch_in, branch_grad), (first_t_in, first_t), (expanded_in, expanded)):
            load(*pair)
        back_flight.append(send(back, back_other, to_core))
        for pair in head_loads + mid_loads + ((qkv_weight_in, qkv_weight),):
            load(*pair)

    def weight_gradient(first, turned, grads, leaves):
        for piece in pieces[first : first + 3]:
            bit = bits[piece.order[0]]
            size = piece.rows // 2
            block = aligned(piece.first_row + size * (1 - bit if leaves else bit), size)
            piece.source[block, :] = nn_dot(turned[block, :], grads[...]).astype(low)

    def wait_head_loads():
        back_flight[0].wait_recv()
        wait_loads(4, 11)
        sums_one[...] = jnp.zeros_like(sums_one)
        pair_keys[...] = jnp.zeros_like(pair_keys)
        pair_values[...] = jnp.zeros_like(pair_values)

    def norm_back(index):
        block = slice(index * TILE, (index + 1) * TILE)
        returned = (back_own[block, :].astype(wide) + back_other[block, :].astype(wide)).astype(low).astype(wide)
        grad_first = base[block, :] + returned
        branch = part[block, :].astype(wide) + other[block, :].astype(wide)
        resid = x[block, :].astype(wide) + (branch + vector_ref[1:2]) * vector_ref[0:1]
        normed, inverse = norm_parts(resid)
        grad_resid = norm_grad(grad_first * vector_ref[2:3], normed, inverse)
        resid_grad[block, :] = jnp.where(core == 0, grad_resid[:, :half], grad_resid[:, half:])
        grad_attended = grad_resid * vector_ref[0:1]
        sums_one[0:1] += column_sum(grad_first * normed)
        sums_one[1:2] += column_sum(grad_first)
        sums_one[2:3] += column_sum(grad_attended)
        grad_attended_low = grad_attended.astype(low)
        branch_grad[block, :] = grad_attended_low
        grad_heads = (nt_dot(grad_attended_low, out_weight[...]) * gate_ref[0:1]).astype(low)
        heads_grad[block, :] = grad_heads
        product = grad_heads.astype(wide) * context[block, :].astype(wide) * gate_ref[1:2]
        lane = lax.broadcasted_iota(jnp.int32, (1, 128), 1)
        columns = jnp.zeros((TILE, 128), wide)
        for pair in range(half // 128):
            some = product[:, 128 * pair : 128 * pair + 128]
            low_sum = jnp.sum(jnp.where(lane < HEAD, some, 0.0), axis=1, keepdims=True)
            high_sum = jnp.sum(jnp.where(lane < HEAD, 0.0, some), axis=1, keepdims=True)
            columns = jnp.where(lane == 2 * pair, low_sum, jnp.where(lane == 2 * pair + 1, high_sum, columns))
        inner_rows[:, block] = columns.T[0:8]

    def out_gradient():
        wait_loads(11, 17)
        out_parts[...] = nn_dot(context_t[...], branch_grad[...]).astype(low)

    pair_width = 2 * HEAD
    scale = HEAD ** (-0.5)
    vector_rows = [[], []]

    def attend_head(number, head):
        lanes = slice(number * pair_width, (number + 1) * pair_width)
        if head == 0:
            turned_keys[...] = key[:, lanes].T
        lane = lax.broadcasted_iota(jnp.int32, (1, pair_width), 1)
        mask = lane < HEAD if head == 0 else lane >= HEAD
        queries, grads = query[:, lanes], heads_grad[:, lanes]
        query_wide = jnp.concatenate([queries, query_mark[...]], axis=1)
        logs = log_ref[8 * number + head : 8 * number + head + 1, :]
        inner = inner_rows[2 * number + head : 2 * number + head + 1, :]

        for start in range(0, length, TILE):
            block = slice(start, start + TILE)
            zero = jnp.zeros((TILE, pair_width), low)
            chosen = jnp.where(mask, key[block, lanes] * jnp.asarray(scale, low), zero)
            key_wide = jnp.concatenate([chosen, key_mark[block, :]], axis=1)
            probs = jnp.exp(nt_dot(key_wide, query_wide) - logs)
            grad_probs = nt_dot(jnp.where(mask, value[block, lanes], zero), grads)
            grad_raw = (probs * (grad_probs - inner)).astype(low)
            unit_t[block, :] = grad_raw
            pair_keys[block, :] = jnp.where(mask, nn_dot(grad_raw, queries), pair_keys[block, :])
            pair_values[block, :] = jnp.where(mask, nn_dot(probs.astype(low), grads), pair_values[block, :])

        rows = slice(HEAD * head, HEAD * head + HEAD)
        turned_grad[rows, :] = nn_dot(turned_keys[rows, :], unit_t[0:length, :])
        if head == 1:
            query_out = (turned_grad[...].T * scale).astype(low)
            value_out = pair_values[...].astype(low)
            for index, value_here in enumerate((query_out, (pair_keys[...] * scale).astype(low), value_out)):
                expanded[:, index * half + number * pair_width : index * half + (number + 1) * pair_width] = value_here
            vector_rows[0].append(column_sum(query_out.astype(wide)))
            vector_rows[1].append(column_sum(value_out.astype(wide)))

    def proj(index):
        return expanded[:, index * half : (index + 1) * half]

    def projection_gradient(index):
        if index == 0:
            wait_loads(17, 19)
        rows = slice(index * full, (index + 1) * full)
        qkv_parts[rows, :] = nn_dot(first_t[...], proj(index)).astype(low)

    small_flight = []

    def own_half(vector):
        return jnp.where(core == 0, vector[:, :half], vector[:, half:])

    def start_small():
        small[...] = jnp.zeros_like(small)
        vectors = vector_rows[0] + vector_rows[1]
        vectors += [own_half(sums_one[2:3]), own_half(sums_two[2:3]), own_half(sums_one[1:2]), own_half(sums_two[1:2])]
        vectors += [unit_sums[0:1], own_half(sums_one[0:1]), own_half(sums_two[0:1]), count[0:1]]
        row = 0
        for vector in vectors:
            for start in range(0, vector.shape[1], 128):
                small[row : row + 1, :] = vector[:, start : start + 128]
                row += 1
        small_flight.append(send(small, small_recv.at[0], peer["x"]))

    def next_small():
        index = len(small_flight)
        if index == 0:
            start_small()
            return
        small_flight[-1].wait_recv()
        last = small if index == 1 else small_outer.at[index - 2]
        small_outer[index - 1] = last[...] + small_recv[index - 1]
        small_flight.append(send(small_outer.at[index - 1], small_recv.at[index], peer["xyvw"[index]]))

    input_flight = []

    def input_half(side):
        columns = aligned(half * side, half)
        return (
            nt_dot(proj(0), qkv_weight[0, columns, :])
            + nt_dot(proj(1), qkv_weight[1, columns, :])
            + nt_dot(proj(2), qkv_weight[2, columns, :])
        )

    def input_gradient(index):
        if index == 0:
            input_send[...] = input_half(1 - core).astype(low)
            input_flight.append(send(input_send, input_recv, to_core))
        else:
            input_grad[...] = input_half(core)

    small_totals = []
    square_flights = []

    def finish_small():
        small_flight[-1].wait_recv()
        small_total = small_outer[2] + small_recv[3]
        if outer > 1:
            small_outer[3] = small_total
            small_outer[4 + group] = small_total
            copies = [send(small_outer.at[3], small_outer.at[4 + group], to_group[d]) for d in range(1, outer)]
            for copy in copies:
                copy.wait_recv()
            small_total = small_outer[4]
            for index in range(1, outer):
                small_total = small_total + small_outer[4 + index]
        unit = 1.0 / (D * small_total[COUNT_ROW : COUNT_ROW + 1, 0:1])
        for index in range(24):
            row, lane = index // 3, index % 3
            source = 3 * row + lane if row < 6 else 12 + 3 * row + lane
            bias_out[row : row + 1, 128 * lane : 128 * lane + 128] = small_total[source : source + 1]
        for index in range(12):
            unit_out[:, 128 * index : 128 * index + 128] = jnp.broadcast_to(small_total[18 + index : 19 + index], (8, 128))
        inside_small = lax.broadcasted_iota(jnp.int32, small_total.shape, 0) < COUNT_ROW
        square = jnp.sum(
            jnp.sum(jnp.where(inside_small, small_total * small_total, 0.0), axis=0, keepdims=True), axis=1, keepdims=True
        )
        small_totals.extend([unit, square])
        input_flight[0].wait_recv()
        summed = input_grad[...] + input_recv[...].astype(wide)
        input_grad[...] = (summed.astype(low).astype(wide) + resid_grad[...]) * unit

    def next_square():
        index = len(square_flights)
        if index == 0:
            total_square = square_terms[0]
            for term in square_terms[1:]:
                total_square = total_square + term
            squares[0] = jnp.broadcast_to(total_square, (8, 128))
        else:
            square_flights[-1].wait_recv()
            squares[index] = squares[index - 1] + square_recv[index - 1]
        if index == 4:
            squares[4] = squares[4] + jnp.broadcast_to(small_totals[1], (8, 128))
        device = to_core if index == 4 else peer["xyvw"[index]]
        square_flights.append(send(squares.at[index], square_recv.at[index], device))
        if index == 0:
            finish_small()

    start_loads()
    done = {"n": 0, "a": 0, "q": 0, "i": 0}
    for entry in SCHEDULE:
        if isinstance(entry, int):
            advance_piece(pieces[entry])
        elif entry == "D":
            wait_loads(0, 2)
            weight_gradient(0, unit_t, branch_grad, True)
        elif entry == "E":
            weight_gradient(0, unit_t, branch_grad, False)
        elif entry == "F":
            wait_loads(2, 4)
            weight_gradient(3, first_t, expanded, True)
        elif entry == "G":
            weight_gradient(3, first_t, expanded, False)
            load(x_t_in, first_t)
        elif entry == "l":
            wait_head_loads()
        elif entry == "n":
            norm_back(done["n"])
        elif entry == "o":
            out_gradient()
        elif entry == "a":
            attend_head(done["a"] // 2, done["a"] % 2)
        elif entry == "q":
            projection_gradient(done["q"])
        elif entry == "i":
            input_gradient(done["i"])
        elif entry == "s":
            next_small()
        else:
            next_square()
        if entry in done:
            done[entry] += 1
    square_flights[-1].wait_recv()
    norm = jnp.sqrt(squares[4] + square_recv[4]) * small_totals[0]
    factor_out[...] = (small_totals[0] * clip_norm / jnp.maximum(norm, clip_norm))[0:1, 0:1]
    norm_out[...] = norm[0:1, 0:1]
    for copy in pending:
        copy.wait_send()


def backward_call(outer, unit_t, first_t, branch_grad, expanded, back, base, x_all, x_t, part, other, context, context_t, queries, keys_in, values, query_mark, key_mark, out_low, qkv_low, vectors, gates, logs, sums_two, unit_sums, count):
    low, wide = jnp.bfloat16, jnp.float32
    length, full = x_all.shape
    half = full // 2
    qkv_shape = (3 * full, half)
    out_shape = (half, full)
    down_shape, up_shape = (unit_t.shape[0], full), (full, expanded.shape[1])
    big = [unit_t, first_t, branch_grad, expanded, back, base, x_all, x_t, part, other, context, context_t, queries, keys_in, values, query_mark, key_mark, out_low, qkv_low]
    little = [vectors, gates, logs, sums_two, unit_sums, count]
    vmem = pl.BlockSpec(memory_space=pltpu.VMEM)
    hbm = pl.BlockSpec(memory_space=pl.ANY)
    sizes = [(shape[0] // 3, shape[1], 4) for shape in (down_shape, up_shape) for _ in range(3)]
    split = qkv_shape[0] * 5 // 9
    sizes += [(split, half, 4), (qkv_shape[0] - split, half, 4), (half, full // 3, 3), (half, full // 3 * 2, 3)]
    copies = sum(4 + halvings + (outer - 1) for _, _, halvings in sizes) + 2 + 4 + (outer - 1) + 5
    lasts = [(rows // 2**halvings, columns) for rows, columns, halvings in sizes]
    spare = [(outer,) + last if outer > 1 else (1, 8, 128) for last in lasts]
    scratch = [pltpu.VMEM(a.shape, a.dtype) for a in big[5:7] + big[8:]]
    scratch += [pltpu.VMEM(shape, low) for shape in (unit_t.shape, first_t.shape, branch_grad.shape, expanded.shape, down_shape, up_shape)]
    scratch += [
        pltpu.VMEM(back.shape, low),
        pltpu.VMEM(back.shape, low),
        pltpu.VMEM((length, half), low),
        pltpu.VMEM((8, length), wide),
        pltpu.VMEM((8, full), wide),
        pltpu.VMEM((2 * HEAD, length), low),
        pltpu.VMEM((2 * HEAD, length), wide),
        pltpu.VMEM((length, 2 * HEAD), wide),
        pltpu.VMEM((length, 2 * HEAD), wide),
        pltpu.VMEM(qkv_shape, low),
        pltpu.VMEM(out_shape, low),
        pltpu.VMEM((length, half), low),
        pltpu.VMEM((length, half), low),
        pltpu.VMEM((SMALL_ROWS, 128), wide),
        pltpu.VMEM((4, SMALL_ROWS, 128), wide),
        pltpu.VMEM((4 + outer, SMALL_ROWS, 128), wide),
        pltpu.VMEM((5, 8, 128), wide),
        pltpu.VMEM((5, 8, 128), wide),
        pltpu.VMEM((length, half), wide),
        tuple(pltpu.VMEM(shape, low) for shape in spare),
        pltpu.SemaphoreType.DMA((copies,)),
        pltpu.SemaphoreType.DMA((copies,)),
        pltpu.SemaphoreType.DMA((len(big) + 6,)),
        pltpu.SemaphoreType.DMA((12,)),
    ]
    for size in sizes:
        scratch += piece_buffers(*size)
    return pl.pallas_call(
        functools.partial(backward_kernel, outer),
        out_shape=[
            jax.ShapeDtypeStruct(down_shape, low),
            jax.ShapeDtypeStruct(up_shape, low),
            jax.ShapeDtypeStruct(qkv_shape, low),
            jax.ShapeDtypeStruct(out_shape, low),
            jax.ShapeDtypeStruct((8, half), wide),
            jax.ShapeDtypeStruct((8, unit_sums.shape[1]), wide),
            jax.ShapeDtypeStruct((1, 1), wide),
            jax.ShapeDtypeStruct((1, 1), wide),
            jax.ShapeDtypeStruct((length, half), wide),
        ],
        in_specs=[hbm] * len(big) + [vmem] * len(little),
        out_specs=[hbm] * 4 + [vmem] * 5,
        scratch_shapes=scratch,
        compiler_params=pltpu.CompilerParams(
            collective_id=0, has_side_effects=True, vmem_limit_bytes=61 * 2**20
        ),
        cost_estimate=pl.CostEstimate(flops=2 * 10**10, bytes_accessed=3 * 10**8, transcendentals=7 * 10**6),
        name="backward_rows",
    )(*big, *little)


def on_device(
    hidden_in,
    teacher_in,
    segment_ids,
    pad_mask,
    qkv_weight,
    qkv_moment1,
    qkv_moment2,
    out_weight,
    out_moment1,
    out_moment2,
    up_weight,
    up_moment1,
    up_moment2,
    down_weight,
    down_moment1,
    down_moment2,
    bias_vectors,
    bias_moment1,
    bias_moment2,
    up_bias,
    up_bias_moment1,
    up_bias_moment2,
    norm_gains,
    gain_moment1,
    gain_moment2,
    head_gates,
    layer_gates,
    dim_gates,
    unit_gates,
    teacher_qkv,
    teacher_out,
    teacher_up,
    teacher_down,
    teacher_biases,
    teacher_up_bias,
    teacher_gains,
):
    length = segment_ids.shape[1]
    width = hidden_in.shape[2]
    wide = jnp.float32
    (
        teacher_part, teacher_other, teacher_x, part, x_all, x_turned, queries, keys_in, values, context, context_turned,
        up_low, down_low, out_low, qkv_low, logs, query_mark, key_mark, valid, vectors, teacher_vectors, gate_rows, count,
    ) = attend_rows_call(
        teacher_in[0], hidden_in[0], teacher_qkv, teacher_out, qkv_weight, out_weight, up_weight, down_weight,
        segment_ids, pad_mask, bias_vectors, norm_gains, dim_gates, teacher_biases, teacher_gains, head_gates, layer_gates,
    )
    part_other, base, back, activated, first, reduced, expanded, block_out, sums_two, unit_sums = feed_rows_call(
        teacher_x, teacher_part, teacher_other, x_all, part, teacher_up, teacher_down, up_low, down_low,
        valid, vectors, teacher_vectors, up_bias, unit_gates, teacher_up_bias,
    )
    rows_all = lax.axis_size("rows")
    down_sum, up_sum, qkv_sum, out_sum, bias_sum, unit_sum, factor, norm, input_grad = backward_call(
        rows_all // INNER, activated, first, reduced, expanded, back, base, x_all, x_turned, part, part_other, context, context_turned,
        queries, keys_in, values, query_mark, key_mark, out_low, qkv_low, vectors, gate_rows, logs,
        sums_two, unit_sums, count,
    )
    weight_sums = (lax.optimization_barrier(qkv_sum.reshape(qkv_weight.shape)), out_sum, up_sum, down_sum)
    weights = (qkv_weight, out_weight, up_weight, down_weight)
    firsts = (qkv_moment1, out_moment1, up_moment1, down_moment1)
    seconds = (qkv_moment2, out_moment2, up_moment2, down_moment2)
    rates = (rate_attend, rate_output, rate_expand, rate_reduce)
    results = []
    for index in range(4):
        clipped = weight_sums[index].astype(wide) * factor
        new_weight, new_second = adam_step(
            weights[index], firsts[index], seconds[index], clipped, rates[index], weight_decay
        )
        results.append((clipped, new_weight, new_second, new_weight.astype(jnp.bfloat16)))
    late, _ = lax.optimization_barrier((factor, results[3][1][:1, :1]))
    vector_results = vector_adam(
        late, norm, block_out, input_grad, bias_sum, unit_sum, bias_vectors, bias_moment1, bias_moment2, up_bias, up_bias_moment1, up_bias_moment2,
        norm_gains, gain_moment1, gain_moment2,
    )
    norm, block_out, input_grad = vector_results[:3]
    grad_norm = norm.reshape(())
    results += [vector_results[3:6], vector_results[6:9], vector_results[9:12]]
    block_out = block_out.reshape(hidden_in.shape)
    input_grad = input_grad.reshape(hidden_in.shape)
    return (
        block_out,
        input_grad,
        grad_norm,
        results[0][0],
        results[0][1],
        results[0][2],
        results[1][0],
        results[1][1],
        results[1][2],
        results[2][0],
        results[2][1],
        results[2][2],
        results[3][0],
        results[3][1],
        results[3][2],
        results[4][0],
        results[4][1],
        results[4][2],
        results[5][0],
        results[5][1],
        results[5][2],
        results[6][0],
        results[6][1],
        results[6][2],
        results[0][3],
        results[1][3],
        results[2][3],
        results[3][3],
    )


def solution(mesh):
    in_specs = (
        P("rows", None, "hid"),
        P("rows", None, "hid"),
        P("rows", None),
        P("rows", None),
        P(None, None, "hid"),
        P(None, None, "hid"),
        P(None, None, "hid"),
        P("hid", None),
        P("hid", None),
        P("hid", None),
        P(None, "hid"),
        P(None, "hid"),
        P(None, "hid"),
        P("hid", None),
        P("hid", None),
        P("hid", None),
        P(None, "hid"),
        P(None, "hid"),
        P(None, "hid"),
        P("hid"),
        P("hid"),
        P("hid"),
        P(None, "hid"),
        P(None, "hid"),
        P(None, "hid"),
        P("hid"),
        P(),
        P("hid"),
        P("hid"),
        P(None, None, "hid"),
        P("hid", None),
        P(None, "hid"),
        P("hid", None),
        P(None, "hid"),
        P("hid"),
        P(None, "hid"),
    )
    out_specs = (
        P("rows", None, "hid"),
        P("rows", None, "hid"),
        P(),
        P(None, None, "hid"),
        P(None, None, "hid"),
        P(None, None, "hid"),
        P("hid", None),
        P("hid", None),
        P("hid", None),
        P(None, "hid"),
        P(None, "hid"),
        P(None, "hid"),
        P("hid", None),
        P("hid", None),
        P("hid", None),
        P(None, "hid"),
        P(None, "hid"),
        P(None, "hid"),
        P("hid"),
        P("hid"),
        P("hid"),
        P(None, "hid"),
        P(None, "hid"),
        P(None, "hid"),
        P(None, None, "hid"),
        P("hid", None),
        P(None, "hid"),
        P("hid", None),
    )
    return jax.shard_map(
        on_device, mesh=mesh, in_specs=in_specs, out_specs=out_specs, check_vma=False
    )
```
